32 devices in a mesh: tm: 8 (over z, x), dp: 4 (over y, core).
Axes of the slice: x: 2, y: 2, z: 4, core: 2. Of those that a mesh axis runs over, the one named last changes fastest.
Arguments:
- inputs: bfloat16 [4, 4096, 256], P('dp', 'tm'), may hold values from -6 to 6
- grad_stream_out: bfloat16 [4, 4096, 256], P('dp', 'tm'), may hold values from -6 to 6
- grad_skip_out: bfloat16 [4, 4096, 256], P('dp', 'tm'), may hold values from -6 to 6
- sample_weight: float32 [4, 4096], P('dp', 'tm'), may hold values from 0.5 to 6, as said below
- conv_weight: bfloat16 [6, 512, 512], replicated, may hold values from -0.25 to 0.25
- out_weight: bfloat16 [6, 256, 512], replicated, may hold values from -0.375 to 0.375
Outputs:
- grad_inputs: float32 [4, 4096, 256], P('dp', 'tm')
- grad_conv: float32 [6, 512, 512], P(None, 'tm', 'dp')
- grad_out: float32 [6, 256, 512], P(None, 'tm', 'dp')
The draws below stay inside these ranges and needn't reach their ends.
Inputs may be any that keep to these rules, and one draw needn't show every extreme that they name: `sample_weight`: positive loss weights of each sample.
All inputs are finite; a program needn't handle non-finite values.
Results may differ from the reference program's by a relative error of at most 0.02.
Values may be sent and summed in bfloat16 or wider, within the bound.
No kernel may reach another device: no remote copies, remote signals or barrier semaphores. Data moves between devices by JAX's collectives and lax.ppermute only.
A program may use at most 128 MiB of HBM per device.

```python
import jax
import jax.numpy as jnp

C = 256
LAYERS = 6
SAMPLES = 4096
BATCH = 4


def draw_sample_weight(key, part):
    rising = 1.0 + 2.0 * jnp.arange(SAMPLES, dtype=jnp.float32) / (SAMPLES - 1)
    factor = jnp.exp(jax.random.uniform(key, (BATCH, SAMPLES), jnp.float32, -0.69, 0.69))
    return rising[None, :] * factor


def block_levels(stream_key, extent, split, smallest, top_value):
    level, own = 1.0, jax.random.fold_in(stream_key, 6)
    for dim, parts in split:
        draws = jnp.exp(jax.random.uniform(jax.random.fold_in(own, dim), (parts,), jnp.float32, smallest / len(split), top_value / len(split)))
        level = level * jnp.repeat(draws, extent[dim] // parts).reshape([-1 if axis == dim else 1 for axis in range(len(extent))])
    return level


def normal_values(key, shape, spread, most, pieces=(), kind=jnp.bfloat16):
    factor_of = block_levels(key, shape, pieces, -0.22, 0.18) if pieces else 1.0
    values = jax.random.normal(key, shape, jnp.float32) * spread * factor_of
    return jnp.minimum(jnp.maximum(values, -most), most).astype(kind)


def setup_inputs(seed: int = 0) -> dict:
    arg_keys = jax.random.split(jax.random.key(seed), 7)
    return {
        "inputs": normal_values(arg_keys[0], (BATCH, SAMPLES, C), 1.0, 6.0, ((0, 4), (1, 8))),
        "grad_stream_out": normal_values(arg_keys[1], (BATCH, SAMPLES, C), 1.0, 6.0, ((0, 4), (1, 8))),
        "grad_skip_out": normal_values(arg_keys[2], (BATCH, SAMPLES, C), 1.0, 6.0, ((0, 4), (1, 8))),
        "sample_weight": draw_sample_weight(jax.random.fold_in(arg_keys[6], 71), 0),
        "conv_weight": normal_values(arg_keys[4], (LAYERS, 2 * C, 2 * C), (2 * C) ** -0.5, 0.25),
        "out_weight": normal_values(arg_keys[5], (LAYERS, C, 2 * C), C ** -0.5, 0.375),
    }


def flat_dot(operand, matrix):
    lead = operand.shape[:-1]
    result = jnp.dot(operand.reshape(-1, operand.shape[-1]), matrix, preferred_element_type=jnp.float32)
    return result.reshape(lead + (matrix.shape[-1],))


def outer_sum(left_op, right_op):
    return jnp.dot(left_op.reshape(-1, left_op.shape[-1]).T, right_op.reshape(-1, right_op.shape[-1]), preferred_element_type=jnp.float32)


def shift_past(values, dilation):
    return jnp.pad(values, ((0, 0), (dilation, 0), (0, 0)))[:, :values.shape[1]]


def shift_later(values, dilation):
    return jnp.pad(values, ((0, 0), (0, dilation), (0, 0)))[:, dilation:]


def forward_layer(present, earlier, conv_layer, out_layer, channels):
    preact = flat_dot(present, conv_layer[:channels]) + flat_dot(earlier, conv_layer[channels:])
    gated = (jnp.tanh(preact[..., :channels]) * jax.nn.sigmoid(preact[..., channels:])).astype(jnp.bfloat16)
    return preact, gated


def reference(inputs, grad_stream_out, grad_skip_out, sample_weight, conv_weight, out_weight):
    channels = inputs.shape[2]
    samples_all = sample_weight.shape[0] * sample_weight.shape[1]
    weighting = sample_weight * (samples_all / jnp.sum(sample_weight))
    stream = inputs.astype(jnp.float32)
    stored = []
    for layer_index in range(LAYERS):
        dilation = 2 ** layer_index
        present = stream.astype(jnp.bfloat16)
        earlier = shift_past(present, dilation)
        preact, gated = forward_layer(present, earlier, conv_weight[layer_index], out_weight[layer_index], channels)
        projected = flat_dot(gated, out_weight[layer_index])
        stream = stream + projected[..., :channels]
        stored.append(present)
    grad_stream = grad_stream_out.astype(jnp.float32) * weighting[..., None]
    grad_skips = grad_skip_out.astype(jnp.float32) * weighting[..., None]
    conv_grads = [None] * LAYERS
    out_grads = [None] * LAYERS
    for layer_index in reversed(range(LAYERS)):
        dilation = 2 ** layer_index
        present = stored[layer_index]
        earlier = shift_past(present, dilation)
        preact, gated = forward_layer(present, earlier, conv_weight[layer_index], out_weight[layer_index], channels)
        grad_proj = jnp.concatenate([grad_stream, grad_skips], axis=-1).astype(jnp.bfloat16)
        out_grads[layer_index] = outer_sum(gated, grad_proj)
        grad_gated = flat_dot(grad_proj, out_weight[layer_index].T)
        filtered = jnp.tanh(preact[..., :channels])
        opening = jax.nn.sigmoid(preact[..., channels:])
        grad_preact = jnp.concatenate([grad_gated * opening * (1.0 - filtered * filtered), grad_gated * filtered * opening * (1.0 - opening)], axis=-1).astype(jnp.bfloat16)
        conv_grads[layer_index] = jnp.concatenate([outer_sum(present, grad_preact), outer_sum(earlier, grad_preact)], axis=0)
        later_rows = shift_later(grad_preact, dilation)
        grad_stream = grad_stream + flat_dot(grad_preact, conv_weight[layer_index, :channels].T) + flat_dot(later_rows, conv_weight[layer_index, channels:].T)
    return grad_stream, jnp.stack(conv_grads), jnp.stack(out_grads)
```

```python
import functools

import jax
import jax.numpy as jnp
from jax import lax
from jax.experimental import pallas as pl
from jax.experimental.pallas import tpu as pltpu
from jax.sharding import PartitionSpec as P

LANES = 128
VMEM_BYTES = 56 * 1024 * 1024
NN = (((1,), (0,)), ((), ()))
NT = (((1,), (1,)), ((), ()))
TN = (((0,), (0,)), ((), ()))


def dot(left, right, dims):
    return lax.dot_general(left, right, dims, preferred_element_type=jnp.float32)


def shifted(x, axis, by):
    count = lax.axis_size(axis)
    pairs = [(i, i + by) for i in range(count) if 0 <= i + by < count]
    return lax.ppermute(x, axis, pairs)


def column(row, rows):
    return jnp.broadcast_to(row, (LANES, rows)).T


def pack_kernel(head_x, tail_x, head_gs, head_gk, weight, to_next, to_prev):
    halo, channels = tail_x.shape
    to_next[...] = tail_x[...]
    by_row = column(weight[...][:, :LANES], LANES)[:halo]
    by_row = jnp.concatenate([by_row] * (channels // LANES), axis=1)
    to_prev[0:halo] = head_x[...]
    to_prev[halo : 2 * halo] = (head_gs[...].astype(jnp.float32) * by_row).astype(jnp.bfloat16)
    to_prev[2 * halo : 3 * halo] = (head_gk[...].astype(jnp.float32) * by_row).astype(jnp.bfloat16)


def pack(halo, x, grad_stream_out, grad_skip_out, weight):
    length, channels = x.shape
    first = pl.BlockSpec((halo, channels), lambda i: (0, 0))
    last = pl.BlockSpec((halo, channels), lambda i: (length // halo - 1, 0))
    return pl.pallas_call(
        pack_kernel,
        grid=(1,),
        in_specs=[first, last, first, first, pl.BlockSpec((1, length), lambda i: (0, 0))],
        out_specs=[
            pl.BlockSpec((halo, channels), lambda i: (0, 0)),
            pl.BlockSpec((3 * halo, channels), lambda i: (0, 0)),
        ],
        out_shape=[
            jax.ShapeDtypeStruct((halo, channels), jnp.bfloat16),
            jax.ShapeDtypeStruct((3 * halo, channels), jnp.bfloat16),
        ],
        name="pack_borders",
    )(x, x, grad_stream_out, grad_skip_out, weight)


def split_rows(total):
    high = total.astype(jnp.bfloat16).astype(jnp.float32)
    middle = (total - high).astype(jnp.bfloat16).astype(jnp.float32)
    low = total - high - middle
    row = lax.broadcasted_iota(jnp.int32, (16, LANES), 0)
    rows = jnp.where(row == 0, high, jnp.where(row == 1, middle, jnp.where(row == 2, low, 0.0)))
    return rows.astype(jnp.bfloat16)


def joined_rows(rows):
    return jnp.sum(rows.astype(jnp.float32), axis=0, keepdims=True)


def layer_kernel(
    plan, prev_x, own_x, next_rows, own_gs, own_gk, weight, conv_w, out_w,
    grad_in, *rest,
):
    grad_parts = rest[:-8]
    stream, operands, factors, gates, grad_proj, grad_stream, past_part, total = rest[-8:]
    halo, (length, channels) = plan["halo"], own_x.shape
    layers = conv_w.shape[0]
    pad = 2 ** (layers - 1)
    extent = length + 2 * halo
    stream[0:pad] = jnp.zeros((pad, channels), jnp.float32)
    stream[pad : pad + halo] = prev_x[...].astype(jnp.float32)
    stream[pad + halo : pad + halo + length] = own_x[...].astype(jnp.float32)
    stream[pad + halo + length :] = next_rows[0:halo].astype(jnp.float32)
    by_row = column(weight[...], length)
    by_row = jnp.concatenate([by_row] * (channels // LANES), axis=1)
    grad_stream[0:length] = own_gs[...].astype(jnp.float32) * by_row
    grad_stream[length:] = next_rows[halo : 2 * halo].astype(jnp.float32)
    grad_proj[0:length, channels:] = (own_gk[...].astype(jnp.float32) * by_row).astype(jnp.bfloat16)
    grad_proj[length:, channels:] = next_rows[2 * halo : 3 * halo]

    for index in range(layers):
        dilation = 2**index
        start = plan["starts"][index]
        operands[index, start:, :channels] = stream[pad + start :].astype(jnp.bfloat16)
        operands[index, start:, channels:] = stream[
            pad + start - dilation : pad + extent - dilation
        ].astype(jnp.bfloat16)
        preact = dot(operands[index, start:], conv_w[index], NN)
        filtered = jnp.tanh(preact[:, :channels])
        opening = 0.5 + 0.5 * jnp.tanh(0.5 * preact[:, channels:])
        product = filtered * opening
        gates[index, start:] = product.astype(jnp.bfloat16)
        factors[index, start:, :channels] = opening - filtered * product
        factors[index, start:, channels:] = product * (1.0 - opening)
        if index < layers - 1:
            stream[pad + start :] += dot(gates[index, start:], out_w[index, :, :channels], NN)

    for index in reversed(range(layers)):
        dilation = 2**index
        count = plan["counts"][index]
        grad_proj[0:count, :channels] = grad_stream[0:count].astype(jnp.bfloat16)
        grad_gated = dot(grad_proj[0:count], out_w[index], NT)
        own = slice(halo, halo + length)
        total[0:channels] = dot(gates[index, own], grad_proj[0:length], TN)
        plan["store"](total, channels, index, grad_parts, True)
        both = factors[index, halo : halo + count]
        grad_preact = jnp.concatenate(
            [grad_gated * both[:, :channels], grad_gated * both[:, channels:]], axis=1
        ).astype(jnp.bfloat16)
        spread = dot(grad_preact, conv_w[index], NT)
        past_part[0:count] = spread[:, channels:]
        rows = plan["counts"][index - 1] if index else length
        grad_stream[0:rows] += spread[0:rows, :channels] + past_part[dilation : dilation + rows]
        total[...] = dot(operands[index, own], grad_preact[0:length], TN)
        plan["store"](total, 2 * channels, index, grad_parts, False)
    grad_in[...] = grad_stream[0:length]
    plan["finish"](weight, grad_parts)


def store_whole(total, height, index, grad_parts, is_out):
    grad_parts[int(is_out)][index] = total[0:height].astype(jnp.bfloat16)


def finish_whole(weight, grad_parts):
    pass


def finish_shards(weight, grad_parts):
    keep, send = grad_parts[:2]
    own_sum = jnp.broadcast_to(jnp.sum(weight[...], axis=1, keepdims=True), (1, LANES))
    slab = split_rows(own_sum)
    first = keep.shape[2] - 16
    for a in range(keep.shape[0]):
        for b in range(keep.shape[1]):
            keep[a, b, first:] = slab
            send[a, b, first:] = slab


def store_shards(tm, dp, total, height, index, grad_parts, is_out):
    keep, send = grad_parts[2:] if is_out else grad_parts[:2]
    t_at, d_at = lax.axis_index("tm"), lax.axis_index("dp")
    x_at, y_at, z_at, core_at = lax.rem(t_at, 2), lax.div(d_at, 2), lax.div(t_at, 2), lax.rem(d_at, 2)
    depth, rows = tm // 2, height // tm
    at = pl.ds(index * rows, rows)
    for y in range(dp // 2):
        near = total[0 : rows * tm, (2 * y) * LANES : (2 * y + 1) * LANES]
        far = total[0 : rows * tm, (2 * y + 1) * LANES : (2 * y + 2) * LANES]
        mine = jnp.where(core_at == 0, near, far).astype(jnp.bfloat16)
        other = jnp.where(core_at == 0, far, near).astype(jnp.bfloat16)
        y_off = lax.rem(y - y_at + dp // 2, dp // 2)
        for t in range(tm):
            z, x = divmod(t, 2)
            plane = lax.rem(x - x_at + 2, 2) * (dp // 2) + y_off
            along = lax.rem(z - z_at + depth, depth)
            lead = (along, plane) if is_out else (plane, along)
            keep[lead[0], lead[1], at] = mine[t * rows : (t + 1) * rows]
            send[lead[0], lead[1], at] = other[t * rows : (t + 1) * rows]


def run_layers(in_shards, tm, dp, halo, arrays, weight, conv_w, out_w):
    prev_x, own_x, next_rows, own_gs, own_gk = arrays
    length, channels = own_x.shape
    layers = conv_w.shape[0]
    extent = length + 2 * halo
    starts = []
    for index in range(layers):
        need = halo if index == layers - 1 else 2 ** (index + 1)
        starts.append(need // 16 * 16)
    counts = [-(-(length + 2 ** (index + 1) - 1) // 16) * 16 for index in range(layers)]
    plan = {"halo": halo, "starts": starts, "counts": counts}
    if in_shards:
        plan["store"], plan["finish"] = functools.partial(store_shards, tm, dp), finish_shards
        conv_rows, out_rows = layers * 2 * channels // tm + 16, layers * channels // tm
        shapes = 2 * [(dp, tm // 2, conv_rows, LANES)] + 2 * [(tm // 2, dp, out_rows, LANES)]
    else:
        plan["store"], plan["finish"] = store_whole, finish_whole
        shapes = [conv_w.shape, out_w.shape]
    vmem = pl.BlockSpec(memory_space=pltpu.VMEM)
    return pl.pallas_call(
        functools.partial(layer_kernel, plan),
        in_specs=[vmem] * 8,
        out_specs=[vmem] * (1 + len(shapes)),
        out_shape=[jax.ShapeDtypeStruct((length, channels), jnp.float32)]
        + [jax.ShapeDtypeStruct(shape, jnp.bfloat16) for shape in shapes],
        scratch_shapes=[
            pltpu.VMEM((2 ** (layers - 1) + extent, channels), jnp.float32),
            pltpu.VMEM((layers, extent, 2 * channels), jnp.bfloat16),
            pltpu.VMEM((layers, extent, 2 * channels), jnp.float32),
            pltpu.VMEM((layers, extent, channels), jnp.bfloat16),
            pltpu.VMEM((length + halo, 2 * channels), jnp.bfloat16),
            pltpu.VMEM((length + halo, channels), jnp.float32),
            pltpu.VMEM((length + halo, channels), jnp.float32),
            pltpu.VMEM((2 * channels, 2 * channels), jnp.float32),
        ],
        compiler_params=pltpu.CompilerParams(vmem_limit_bytes=VMEM_BYTES),
        name="layers_both_ways",
    )(prev_x, own_x, next_rows, own_gs, own_gk, weight, conv_w, out_w)


def add_kernel(terms, slab_at, *refs):
    outs = refs[sum(len(t) for t in terms) :]
    at = 0
    for out, term in zip(outs, terms):
        parts = refs[at : at + len(term)]
        at += len(term)
        rows = out.shape[-2]
        body = rows if slab_at is None else slab_at
        lead = (slice(None),) * (len(out.shape) - 2)
        value = parts[0][lead + (slice(0, body),)].astype(jnp.float32)
        for part in parts[1:]:
            value = value + part[lead + (slice(0, body),)].astype(jnp.float32)
        out[lead + (slice(0, body),)] = value.astype(out.dtype)
        if slab_at is not None:
            first = (0,) * (len(out.shape) - 2)
            total = joined_rows(parts[0][first + (slice(body, rows),)])
            for part in parts[1:]:
                total = total + joined_rows(part[first + (slice(body, rows),)])
            slab = split_rows(total)
            if len(out.shape) == 2:
                out[body:rows] = slab
            else:
                for i in range(out.shape[0]):
                    out[i, body:rows] = slab


def lead_block(array, index):
    shape = array.shape[1:]
    return pl.BlockSpec((None,) + shape, lambda i: (index,) + (0,) * len(shape))


def add_up(groups, shape, slab_at, name):
    operands = [a for group in groups for a, _ in group]
    specs = [lead_block(a, i) for group in groups for a, i in group]
    zero = (0,) * len(shape)
    return pl.pallas_call(
        functools.partial(add_kernel, [[None] * len(g) for g in groups], slab_at),
        grid=(1,),
        in_specs=specs,
        out_specs=[pl.BlockSpec(shape, lambda i: zero) for _ in groups],
        out_shape=[jax.ShapeDtypeStruct(shape, jnp.bfloat16) for _ in groups],
        compiler_params=pltpu.CompilerParams(vmem_limit_bytes=VMEM_BYTES),
        name=name,
    )(*operands)


def last_kernel(conv_count, out_count, samples_all, *refs):
    conv_parts, refs = refs[:conv_count], refs[conv_count:]
    out_parts, refs = refs[:out_count], refs[out_count:]
    grad_in, grad_inputs, grad_conv, grad_out = refs
    layers, conv_rows, _ = grad_conv.shape
    slab_at = layers * conv_rows
    total = joined_rows(conv_parts[0][slab_at:])
    for part in conv_parts[1:]:
        total = total + joined_rows(part[slab_at:])
    scale = samples_all / total
    for parts, out in ((conv_parts, grad_conv), (out_parts, grad_out)):
        rows = out.shape[1]
        for index in range(layers):
            at = slice(index * rows, (index + 1) * rows)
            value = parts[0][at].astype(jnp.float32)
            for part in parts[1:]:
                value = value + part[at].astype(jnp.float32)
            out[index] = value * scale
    for first in range(0, grad_in.shape[1], LANES):
        grad_inputs[:, first : first + LANES] = grad_in[:, first : first + LANES] * scale


def reduce_shards(tm, dp, keep_conv, send_conv, keep_out, send_out):
    depth, wide = tm // 2, dp // 2
    axes = ("tm", "dp")

    def moved(x, core=0, xs=0, ys=0, zs=0):
        pairs = []
        for t in range(tm):
            for d in range(dp):
                z, a = divmod(t, 2)
                y, c = divmod(d, 2)
                to_t = (z + zs) % depth * 2 + (a + xs) % 2
                to_d = (y + ys) % wide * 2 + (c + core) % 2
                pairs.append((t * dp + d, to_t * dp + to_d))
        return lax.ppermute(x, axes, pairs)

    def plane(x, step):
        return moved(x, xs=step // wide, ys=step % wide)

    def along(x, step):
        return moved(x, zs=step)

    out_there = moved(send_out, core=1)
    conv_there = moved(send_conv, core=1)
    conv_slab = keep_conv.shape[2] - 16
    steps_z, steps_p = range(1, depth), range(1, 2 * wide)
    out_first = add_up(
        [[(keep_out, r), (out_there, r)] for r in steps_z], keep_out.shape[1:], None, "add_out_cores"
    )
    out_z = [along(x, r) for x, r in zip(out_first, steps_z)]
    conv_first = add_up(
        [[(keep_conv, r), (conv_there, r)] for r in steps_p], keep_conv.shape[1:], conv_slab, "add_conv_cores"
    )
    conv_p = [plane(x, r) for x, r in zip(conv_first, steps_p)]
    out_second = add_up(
        [
            [(keep_out.reshape((-1,) + keep_out.shape[2:]), r), (out_there.reshape((-1,) + keep_out.shape[2:]), r)]
            + [(x, r) for x in out_z]
            for r in range(2 * wide)
        ],
        keep_out.shape[2:], None, "add_out_along",
    )
    out_p = [plane(x, r) for x, r in zip(out_second[1:], steps_p)]
    conv_second = add_up(
        [
            [(keep_conv.reshape((-1,) + keep_conv.shape[2:]), r), (conv_there.reshape((-1,) + keep_conv.shape[2:]), r)]
            + [(x, r) for x in conv_p]
            for r in range(depth)
        ],
        keep_conv.shape[2:], conv_slab, "add_conv_plane",
    )
    conv_z = [along(x, r) for x, r in zip(conv_second[1:], steps_z)]
    return [conv_second[0]] + conv_z, [out_second[0]] + out_p


def scattered(part):
    columns = lax.psum_scatter(part, "dp", scatter_dimension=2, tiled=True).astype(jnp.float32)
    return lax.psum_scatter(columns, "tm", scatter_dimension=1, tiled=True)


def body(inputs, grad_stream_out, grad_skip_out, sample_weight, conv_weight, out_weight):
    tm, dp = lax.axis_size("tm"), lax.axis_size("dp")
    batch, length, channels = inputs.shape
    layers = conv_weight.shape[0]
    halo = 2**layers
    samples_all = batch * length * tm * dp
    x, gs, gk = inputs[0], grad_stream_out[0], grad_skip_out[0]
    to_next, to_prev = pack(halo, x, gs, gk, sample_weight)
    prev_x = shifted(to_next, "tm", 1)
    next_rows = shifted(to_prev, "tm", -1)
    in_shards = dp == 4 and tm % 2 == 0 and channels // tm % 16 == 0 and 2 * channels == dp * LANES
    grad_in, *parts = run_layers(
        in_shards, tm, dp, halo, (prev_x, x, next_rows, gs, gk), sample_weight, conv_weight, out_weight
    )
    if not in_shards:
        scale = samples_all / lax.psum(jnp.sum(sample_weight), ("tm", "dp"))
        grad_conv, grad_out = (scattered(part) * scale for part in parts)
        return (grad_in * scale)[None], grad_conv, grad_out
    conv_terms, out_terms = reduce_shards(tm, dp, *parts)
    conv_rows, out_rows = 2 * channels // tm, channels // tm
    grad_inputs, grad_conv, grad_out = pl.pallas_call(
        functools.partial(last_kernel, len(conv_terms), len(out_terms), float(samples_all)),
        out_shape=[
            jax.ShapeDtypeStruct((length, channels), jnp.float32),
            jax.ShapeDtypeStruct((layers, conv_rows, LANES), jnp.float32),
            jax.ShapeDtypeStruct((layers, out_rows, LANES), jnp.float32),
        ],
        name="scale_all",
    )(*conv_terms, *out_terms, grad_in)
    return grad_inputs[None], grad_conv, grad_out


def solution(mesh):
    placed = (
        P("dp", "tm", None),
        P("dp", "tm", None),
        P("dp", "tm", None),
        P("dp", "tm"),
        P(),
        P(),
    )
    return jax.shard_map(
        body,
        mesh=mesh,
        in_specs=placed,
        out_specs=(P("dp", "tm", None), P(None, "tm", "dp"), P(None, "tm", "dp")),
        check_vma=False,
    )
```

```python
import functools

import jax
import jax.numpy as jnp
from jax import lax
from jax.experimental import pallas as pl
from jax.experimental.pallas import tpu as pltpu
from jax.sharding import PartitionSpec as P

LANES = 128
VMEM_BYTES = 36 * 1024 * 1024
ADD_BYTES = 8 * 1024 * 1024
NN = (((1,), (0,)), ((), ()))
NT = (((1,), (1,)), ((), ()))
TN = (((0,), (0,)), ((), ()))


def dot(left, right, dims):
    return lax.dot_general(left, right, dims, preferred_element_type=jnp.float32)


def held(arrays, space=pltpu.VMEM):
    return [pltpu.with_memory_space_constraint(x, space) for x in arrays]


def shifted(x, axis, by):
    count = lax.axis_size(axis)
    pairs = [(i, i + by) for i in range(count) if 0 <= i + by < count]
    return lax.ppermute(x, axis, pairs)


def column(row, rows):
    return jnp.broadcast_to(row, (LANES, rows)).T


def pack_kernel(head_x, tail_x, head_gs, head_gk, weight, to_next, to_prev):
    halo, channels = tail_x.shape
    to_next[...] = tail_x[...]
    by_row = column(weight[...][:, :LANES], LANES)[:halo]
    by_row = jnp.concatenate([by_row] * (channels // LANES), axis=1)
    to_prev[0:halo] = head_x[...]
    to_prev[halo : 2 * halo] = (head_gs[...].astype(jnp.float32) * by_row).astype(jnp.bfloat16)
    to_prev[2 * halo : 3 * halo] = (head_gk[...].astype(jnp.float32) * by_row).astype(jnp.bfloat16)


def pack(halo, x, grad_stream_out, grad_skip_out, weight):
    length, channels = x.shape
    first = pl.BlockSpec((halo, channels), lambda i: (0, 0))
    last = pl.BlockSpec((halo, channels), lambda i: (length // halo - 1, 0))
    return pl.pallas_call(
        pack_kernel,
        grid=(1,),
        in_specs=[first, last, first, first, pl.BlockSpec((1, length), lambda i: (0, 0))],
        out_specs=[
            pl.BlockSpec((halo, channels), lambda i: (0, 0)),
            pl.BlockSpec((3 * halo, channels), lambda i: (0, 0)),
        ],
        out_shape=[
            jax.ShapeDtypeStruct((halo, channels), jnp.bfloat16),
            jax.ShapeDtypeStruct((3 * halo, channels), jnp.bfloat16),
        ],
        compiler_params=pltpu.CompilerParams(vmem_limit_bytes=ADD_BYTES),
        name="pack_borders",
    )(*held((x, x, grad_stream_out, grad_skip_out), pltpu.HBM), weight)


def split_rows(total):
    high = total.astype(jnp.bfloat16).astype(jnp.float32)
    middle = (total - high).astype(jnp.bfloat16).astype(jnp.float32)
    low = total - high - middle
    row = lax.broadcasted_iota(jnp.int32, (16, LANES), 0)
    rows = jnp.where(row == 0, high, jnp.where(row == 1, middle, jnp.where(row == 2, low, 0.0)))
    return rows.astype(jnp.bfloat16)


def joined_rows(rows):
    return jnp.sum(rows.astype(jnp.float32), axis=0, keepdims=True)


def layer_kernel(
    plan, prev_x, own_x, next_rows, own_gs, own_gk, weight, conv_w, out_w,
    grad_in, *rest,
):
    grad_parts = rest[:-8]
    stream, operands, factors, gates, grad_proj, grad_stream, past_part, total = rest[-8:]
    halo, (length, channels) = plan["halo"], own_x.shape
    layers = conv_w.shape[0]
    pad = 2 ** (layers - 1)
    extent = length + 2 * halo
    stream[0:pad] = jnp.zeros((pad, channels), jnp.float32)
    stream[pad : pad + halo] = prev_x[...].astype(jnp.float32)
    stream[pad + halo : pad + halo + length] = own_x[...].astype(jnp.float32)
    stream[pad + halo + length :] = next_rows[0:halo].astype(jnp.float32)
    by_row = column(weight[...], length)
    by_row = jnp.concatenate([by_row] * (channels // LANES), axis=1)
    grad_stream[0:length] = own_gs[...].astype(jnp.float32) * by_row
    grad_stream[length:] = next_rows[halo : 2 * halo].astype(jnp.float32)
    grad_proj[0:length, channels:] = (own_gk[...].astype(jnp.float32) * by_row).astype(jnp.bfloat16)
    grad_proj[length:, channels:] = next_rows[2 * halo : 3 * halo]

    for index in range(layers):
        dilation = 2**index
        start = plan["starts"][index]
        operands[index, start:, :channels] = stream[pad + start :].astype(jnp.bfloat16)
        operands[index, start:, channels:] = stream[
            pad + start - dilation : pad + extent - dilation
        ].astype(jnp.bfloat16)
        preact = dot(operands[index, start:], conv_w[index], NN)
        filtered = jnp.tanh(preact[:, :channels])
        opening = 0.5 + 0.5 * jnp.tanh(0.5 * preact[:, channels:])
        product = filtered * opening
        gates[index, start:] = product.astype(jnp.bfloat16)
        factors[index, start:, :channels] = opening - filtered * product
        factors[index, start:, channels:] = product * (1.0 - opening)
        if index < layers - 1:
            stream[pad + start :] += dot(gates[index, start:], out_w[index, :, :channels], NN)

    for index in reversed(range(layers)):
        dilation = 2**index
        count = plan["counts"][index]
        grad_proj[0:count, :channels] = grad_stream[0:count].astype(jnp.bfloat16)
        grad_gated = dot(grad_proj[0:count], out_w[index], NT)
        own = slice(halo, halo + length)
        total[0:channels] = dot(gates[index, own], grad_proj[0:length], TN)
        plan["store"](total, channels, index, grad_parts, True)
        both = factors[index, halo : halo + count]
        grad_preact = jnp.concatenate(
            [grad_gated * both[:, :channels], grad_gated * both[:, channels:]], axis=1
        ).astype(jnp.bfloat16)
        spread = dot(grad_preact, conv_w[index], NT)
        past_part[0:count] = spread[:, channels:]
        rows = plan["counts"][index - 1] if index else length
        grad_stream[0:rows] += spread[0:rows, :channels] + past_part[dilation : dilation + rows]
        total[...] = dot(operands[index, own], grad_preact[0:length], TN)
        plan["store"](total, 2 * channels, index, grad_parts, False)
    grad_in[...] = grad_stream[0:length]
    plan["finish"](weight, grad_parts)


def store_whole(total, height, index, grad_parts, is_out):
    grad_parts[int(is_out)][index] = total[0:height].astype(jnp.bfloat16)


def finish_whole(weight, grad_parts):
    pass


def finish_shards(weight, grad_parts):
    keep, send = grad_parts[:2]
    own_sum = jnp.broadcast_to(jnp.sum(weight[...], axis=1, keepdims=True), (1, LANES))
    slab = split_rows(own_sum)
    first = keep.shape[2] - 16
    for a in range(keep.shape[0]):
        for b in range(keep.shape[1]):
            keep[a, b, first:] = slab
            send[a, b, first:] = slab


def store_shards(tm, dp, total, height, index, grad_parts, is_out):
    keep, send = grad_parts[2:] if is_out else grad_parts[:2]
    t_at, d_at = lax.axis_index("tm"), lax.axis_index("dp")
    x_at, y_at, z_at, core_at = lax.rem(t_at, 2), lax.div(d_at, 2), lax.div(t_at, 2), lax.rem(d_at, 2)
    depth, rows = tm // 2, height // tm
    at = pl.ds(index * rows, rows)
    for y in range(dp // 2):
        near = total[0 : rows * tm, (2 * y) * LANES : (2 * y + 1) * LANES]
        far = total[0 : rows * tm, (2 * y + 1) * LANES : (2 * y + 2) * LANES]
        mine = jnp.where(core_at == 0, near, far).astype(jnp.bfloat16)
        other = jnp.where(core_at == 0, far, near).astype(jnp.bfloat16)
        y_off = lax.rem(y - y_at + dp // 2, dp // 2)
        for t in range(tm):
            z, x = divmod(t, 2)
            plane = lax.rem(x - x_at + 2, 2) * (dp // 2) + y_off
            along = lax.rem(z - z_at + depth, depth)
            lead = (along, plane) if is_out else (plane, along)
            keep[lead[0], lead[1], at] = mine[t * rows : (t + 1) * rows]
            send[lead[0], lead[1], at] = other[t * rows : (t + 1) * rows]


def run_layers(in_shards, tm, dp, halo, arrays, weight, conv_w, out_w):
    prev_x, own_x, next_rows, own_gs, own_gk = arrays
    length, channels = own_x.shape
    layers = conv_w.shape[0]
    extent = length + 2 * halo
    starts = []
    for index in range(layers):
        need = halo if index == layers - 1 else 2 ** (index + 1)
        starts.append(need // 16 * 16)
    counts = [-(-(length + 2 ** (index + 1) - 1) // 16) * 16 for index in range(layers)]
    plan = {"halo": halo, "starts": starts, "counts": counts}
    if in_shards:
        plan["store"], plan["finish"] = functools.partial(store_shards, tm, dp), finish_shards
        conv_rows, out_rows = layers * 2 * channels // tm + 16, layers * channels // tm
        shapes = 2 * [(dp, tm // 2, conv_rows, LANES)] + 2 * [(tm // 2, dp, out_rows, LANES)]
    else:
        plan["store"], plan["finish"] = store_whole, finish_whole
        shapes = [conv_w.shape, out_w.shape]
    vmem = pl.BlockSpec(memory_space=pltpu.VMEM)
    return pl.pallas_call(
        functools.partial(layer_kernel, plan),
        in_specs=[vmem] * 8,
        out_specs=[vmem] * (1 + len(shapes)),
        out_shape=[pltpu.VMEM((length, channels), jnp.float32)] + [pltpu.VMEM(shape, jnp.bfloat16) for shape in shapes],
        scratch_shapes=[
            pltpu.VMEM((2 ** (layers - 1) + extent, channels), jnp.float32),
            pltpu.VMEM((layers, extent, 2 * channels), jnp.bfloat16),
            pltpu.VMEM((layers, extent, 2 * channels), jnp.float32),
            pltpu.VMEM((layers, extent, channels), jnp.bfloat16),
            pltpu.VMEM((length + halo, 2 * channels), jnp.bfloat16),
            pltpu.VMEM((length + halo, channels), jnp.float32),
            pltpu.VMEM((length + halo, channels), jnp.float32),
            pltpu.VMEM((2 * channels, 2 * channels), jnp.float32),
        ],
        compiler_params=pltpu.CompilerParams(vmem_limit_bytes=VMEM_BYTES),
        name="layers_both_ways",
    )(*held([prev_x]), own_x, *held([next_rows]), own_gs, own_gk, weight, conv_w, out_w)


def add_kernel(count, groups, slab_at, *refs):
    arrays, outs = refs[:count], refs[-len(groups) :]
    for out, group in zip(outs, groups):
        rows, lead = out.shape[-2], (slice(None),) * (len(out.shape) - 2)
        body = rows if slab_at is None else slab_at
        value = 0.0
        for array, at in group:
            value = value + arrays[array][at + lead + (slice(0, body),)].astype(jnp.float32)
        out[lead + (slice(0, body),)] = value.astype(out.dtype)
        if slab_at is not None:
            first = (0,) * len(lead) + (slice(body, rows),)
            total = 0.0
            for array, at in group:
                total = total + joined_rows(arrays[array][at + first])
            slab = split_rows(total)
            for i in range(out.shape[0]) if lead else (None,):
                out[(() if i is None else (i,)) + (slice(body, rows),)] = slab


def add_up(arrays, groups, shape, slab_at, after, name):
    vmem = pl.BlockSpec(memory_space=pltpu.VMEM)
    return pl.pallas_call(
        functools.partial(add_kernel, len(arrays), groups, slab_at),
        in_specs=[vmem] * len(arrays) + [pl.BlockSpec(memory_space=pl.ANY)] * len(after),
        out_specs=[vmem] * len(groups),
        out_shape=[pltpu.VMEM(shape, jnp.bfloat16) for _ in groups],
        compiler_params=pltpu.CompilerParams(vmem_limit_bytes=ADD_BYTES),
        name=name,
    )(*held(arrays), *held(after))


def last_kernel(conv_count, out_count, samples_all, *refs):
    conv_parts, refs = refs[:conv_count], refs[conv_count:]
    out_parts, refs = refs[:out_count], refs[out_count:]
    grad_in, grad_inputs, grad_conv, grad_out = refs
    layers, conv_rows, _ = grad_conv.shape
    slab_at = layers * conv_rows
    total = joined_rows(conv_parts[0][slab_at:])
    for part in conv_parts[1:]:
        total = total + joined_rows(part[slab_at:])
    scale = samples_all / total
    for parts, out in ((conv_parts, grad_conv), (out_parts, grad_out)):
        rows = out.shape[1]
        for index in range(layers):
            at = slice(index * rows, (index + 1) * rows)
            value = parts[0][at].astype(jnp.float32)
            for part in parts[1:]:
                value = value + part[at].astype(jnp.float32)
            out[index] = value * scale
    for first in range(0, grad_in.shape[1], LANES):
        grad_inputs[:, first : first + LANES] = grad_in[:, first : first + LANES] * scale


def reduce_shards(tm, dp, keep_conv, send_conv, keep_out, send_out):
    depth, wide = tm // 2, dp // 2
    axes = ("tm", "dp")

    def moved(x, core=0, xs=0, ys=0, zs=0):
        pairs = []
        for t in range(tm):
            for d in range(dp):
                z, a = divmod(t, 2)
                y, c = divmod(d, 2)
                to_t = (z + zs) % depth * 2 + (a + xs) % 2
                to_d = (y + ys) % wide * 2 + (c + core) % 2
                pairs.append((t * dp + d, to_t * dp + to_d))
        return lax.ppermute(x, axes, pairs)

    def plane(x, step):
        return moved(x, xs=step // wide, ys=step % wide)

    def along(x, step):
        return moved(x, zs=step)

    out_there = moved(send_out, core=1)
    conv_there = moved(send_conv, core=1)
    conv_slab = keep_conv.shape[2] - 16
    steps_z, steps_p = range(1, depth), range(1, 2 * wide)
    out_first = add_up(
        [keep_out, out_there], [[(0, (r,)), (1, (r,))] for r in steps_z], keep_out.shape[1:], None, [],
        "add_out_cores",
    )
    out_z = [along(x, r) for x, r in zip(out_first, steps_z)]
    conv_first = add_up(
        [keep_conv, conv_there], [[(0, (r,)), (1, (r,))] for r in steps_p], keep_conv.shape[1:], conv_slab,
        out_first[:1], "add_conv_cores",
    )
    conv_p = [plane(x, r) for x, r in zip(conv_first, steps_p)]
    out_second = add_up(
        [keep_out, out_there] + out_z,
        [[(0, (0, r)), (1, (0, r))] + [(2 + i, (r,)) for i in range(len(out_z))] for r in range(2 * wide)],
        keep_out.shape[2:], None, [], "add_out_along",
    )
    out_p = [plane(x, r) for x, r in zip(out_second[1:], steps_p)]
    conv_second = add_up(
        [keep_conv, conv_there] + conv_p,
        [[(0, (0, r)), (1, (0, r))] + [(2 + i, (r,)) for i in range(len(conv_p))] for r in range(depth)],
        keep_conv.shape[2:], conv_slab, out_second[:1], "add_conv_plane",
    )
    conv_z = [along(x, r) for x, r in zip(conv_second[1:], steps_z)]
    return [conv_second[0]] + conv_z, [out_second[0]] + out_p


def scattered(part):
    columns = lax.psum_scatter(part, "dp", scatter_dimension=2, tiled=True).astype(jnp.float32)
    return lax.psum_scatter(columns, "tm", scatter_dimension=1, tiled=True)


def body(inputs, grad_stream_out, grad_skip_out, sample_weight, conv_weight, out_weight):
    tm, dp = lax.axis_size("tm"), lax.axis_size("dp")
    batch, length, channels = inputs.shape
    layers = conv_weight.shape[0]
    halo = 2**layers
    samples_all = batch * length * tm * dp
    x, gs, gk = inputs[0], grad_stream_out[0], grad_skip_out[0]
    to_next, to_prev = pack(halo, x, gs, gk, sample_weight)
    prev_x = shifted(to_next, "tm", 1)
    next_rows = shifted(to_prev, "tm", -1)
    in_shards = dp == 4 and tm % 2 == 0 and channels // tm % 16 == 0 and 2 * channels == dp * LANES
    grad_in, *parts = run_layers(
        in_shards, tm, dp, halo, (prev_x, x, next_rows, gs, gk), sample_weight, conv_weight, out_weight
    )
    if not in_shards:
        scale = samples_all / lax.psum(jnp.sum(sample_weight), ("tm", "dp"))
        grad_conv, grad_out = (scattered(part) * scale for part in parts)
        return (grad_in * scale)[None], grad_conv, grad_out
    conv_terms, out_terms = reduce_shards(tm, dp, *parts)
    conv_rows, out_rows = 2 * channels // tm, channels // tm
    grad_inputs, grad_conv, grad_out = pl.pallas_call(
        functools.partial(last_kernel, len(conv_terms), len(out_terms), float(samples_all)),
        out_shape=[
            jax.ShapeDtypeStruct((length, channels), jnp.float32),
            jax.ShapeDtypeStruct((layers, conv_rows, LANES), jnp.float32),
            jax.ShapeDtypeStruct((layers, out_rows, LANES), jnp.float32),
        ],
        compiler_params=pltpu.CompilerParams(vmem_limit_bytes=ADD_BYTES),
        name="scale_all",
    )(*held(conv_terms), *held(out_terms), *held([grad_in]))
    return grad_inputs[None], grad_conv, grad_out


def solution(mesh):
    placed = (
        P("dp", "tm", None),
        P("dp", "tm", None),
        P("dp", "tm", None),
        P("dp", "tm"),
        P(),
        P(),
    )
    return jax.shard_map(
        body,
        mesh=mesh,
        in_specs=placed,
        out_specs=(P("dp", "tm", None), P(None, "tm", "dp"), P(None, "tm", "dp")),
        check_vma=False,
    )
```

```python
import functools

import jax
import jax.numpy as jnp
from jax import lax
from jax.experimental import pallas as pl
from jax.experimental.pallas import tpu as pltpu
from jax.sharding import PartitionSpec as P

LANES = 128
VMEM_BYTES = 24 * 1024 * 1024
ADD_BYTES = 8 * 1024 * 1024
NN = (((1,), (0,)), ((), ()))
NT = (((1,), (1,)), ((), ()))
TN = (((0,), (0,)), ((), ()))


def dot(left, right, dims):
    return lax.dot_general(left, right, dims, preferred_element_type=jnp.float32)


def held(arrays, space=pltpu.VMEM):
    return [pltpu.with_memory_space_constraint(x, space) for x in arrays]


def shifted(x, axis, by):
    count = lax.axis_size(axis)
    pairs = [(i, i + by) for i in range(count) if 0 <= i + by < count]
    return lax.ppermute(x, axis, pairs)


def column(row, rows):
    return jnp.broadcast_to(row, (LANES, rows)).T


def cost(flops, moved):
    return pl.CostEstimate(flops=flops, bytes_accessed=moved, transcendentals=0)


def pack_kernel(head_x, tail_x, head_gs, head_gk, weight, to_next, to_prev):
    halo, channels = tail_x.shape
    to_next[...] = tail_x[...]
    by_row = column(weight[...], LANES)[:halo]
    by_row = jnp.concatenate([by_row] * (channels // LANES), axis=1)
    to_prev[0:halo] = head_x[...]
    to_prev[halo : 2 * halo] = (head_gs[...].astype(jnp.float32) * by_row).astype(jnp.bfloat16)
    to_prev[2 * halo : 3 * halo] = (head_gk[...].astype(jnp.float32) * by_row).astype(jnp.bfloat16)


def pack(halo, x, grad_stream_out, grad_skip_out, weight):
    length, channels = x.shape
    first = pl.BlockSpec((halo, channels), lambda i: (0, 0))
    last = pl.BlockSpec((halo, channels), lambda i: (length // halo - 1, 0))
    return pl.pallas_call(
        pack_kernel,
        grid=(1,),
        in_specs=[first, last, first, first, pl.BlockSpec((1, LANES), lambda i: (0, 0))],
        out_specs=[
            pl.BlockSpec((halo, channels), lambda i: (0, 0)),
            pl.BlockSpec((3 * halo, channels), lambda i: (0, 0)),
        ],
        out_shape=[
            jax.ShapeDtypeStruct((halo, channels), jnp.bfloat16),
            jax.ShapeDtypeStruct((3 * halo, channels), jnp.bfloat16),
        ],
        compiler_params=pltpu.CompilerParams(vmem_limit_bytes=ADD_BYTES),
        name="pack_borders",
    )(*held((x, x, grad_stream_out, grad_skip_out, weight), pltpu.HBM))


def load_kernel(
    x, gs, gk, weight, conv_w, out_w, _, x_here, grad_stream, grad_skip, sums, conv_here, out_here,
    gs_raw, gk_raw, weight_here, sems,
):
    pairs = ((weight, weight_here), (gs, gs_raw), (gk, gk_raw), (x, x_here), (conv_w, conv_here), (out_w, out_here))
    copies = [pltpu.make_async_copy(a, b, sems.at[i]) for i, (a, b) in enumerate(pairs)]
    for copy in copies:
        copy.start()
    for copy in copies[:3]:
        copy.wait()
    length, channels = x_here.shape
    by_row = column(weight_here[...], length)
    by_row = jnp.concatenate([by_row] * (channels // LANES), axis=1)
    grad_stream[...] = gs_raw[...].astype(jnp.float32) * by_row
    grad_skip[...] = (gk_raw[...].astype(jnp.float32) * by_row).astype(jnp.bfloat16)
    own_sum = jnp.broadcast_to(jnp.sum(weight_here[...], axis=1, keepdims=True), (1, LANES))
    sums[...] = split_rows(own_sum)
    for copy in copies[3:]:
        copy.wait()


def load_all(x, gs, gk, weight, conv_w, out_w, after):
    shape = x.shape
    vmem, anywhere = pl.BlockSpec(memory_space=pltpu.VMEM), pl.BlockSpec(memory_space=pl.ANY)
    return pl.pallas_call(
        load_kernel,
        in_specs=[anywhere] * 7,
        out_specs=[vmem] * 6,
        out_shape=[
            pltpu.VMEM(shape, jnp.bfloat16),
            pltpu.VMEM(shape, jnp.float32),
            pltpu.VMEM(shape, jnp.bfloat16),
            pltpu.VMEM((16, LANES), jnp.bfloat16),
            pltpu.VMEM(conv_w.shape, jnp.bfloat16),
            pltpu.VMEM(out_w.shape, jnp.bfloat16),
        ],
        scratch_shapes=[
            pltpu.VMEM(shape, jnp.bfloat16),
            pltpu.VMEM(shape, jnp.bfloat16),
            pltpu.VMEM(weight.shape, jnp.float32),
            pltpu.SemaphoreType.DMA((6,)),
        ],
        compiler_params=pltpu.CompilerParams(vmem_limit_bytes=ADD_BYTES),
        cost_estimate=cost(10**7, 6 * 10**6),
        name="load_all",
    )(*held((x, gs, gk, weight, conv_w, out_w), pltpu.HBM), *held([after]))


def split_rows(total):
    high = total.astype(jnp.bfloat16).astype(jnp.float32)
    middle = (total - high).astype(jnp.bfloat16).astype(jnp.float32)
    low = total - high - middle
    row = lax.broadcasted_iota(jnp.int32, (16, LANES), 0)
    rows = jnp.where(row == 0, high, jnp.where(row == 1, middle, jnp.where(row == 2, low, 0.0)))
    return rows.astype(jnp.bfloat16)


def joined_rows(rows):
    return jnp.sum(rows.astype(jnp.float32), axis=0, keepdims=True)


def backward(plan, layers, refs_of, conv_w, out_w, grad_proj, grad_stream, past_part, total, grad_parts):
    halo, length, channels = plan["halo"], plan["length"], plan["channels"]
    own = slice(halo, halo + length)
    for place, index in enumerate(layers):
        dilation, count = 2**index, plan["counts"][index]
        operands, factors, gates = refs_of(index)
        grad_proj[0:count, :channels] = grad_stream[0:count].astype(jnp.bfloat16)
        grad_gated = dot(grad_proj[0:count], out_w[index], NT)
        total[0:channels] = dot(gates[own], grad_proj[0:length], TN)
        plan["store"](total, channels, place, grad_parts, True)
        both = factors[halo : halo + count]
        grad_preact = jnp.concatenate(
            [grad_gated * both[:, :channels], grad_gated * both[:, channels:]], axis=1
        ).astype(jnp.bfloat16)
        spread = dot(grad_preact, conv_w[index], NT)
        past_part[0:count] = spread[:, channels:]
        rows = plan["counts"][index - 1] if index else length
        grad_stream[0:rows] += spread[0:rows, :channels] + past_part[dilation : dilation + rows]
        total[...] = dot(operands[own], grad_preact[0:length], TN)
        plan["store"](total, 2 * channels, place, grad_parts, False)


def first_kernel(
    plan, prev_x, next_rows, own_x, own_grad, own_skip, conv_w, out_w,
    low_operands, low_factors, low_gates, grad_stream, grad_skip, *rest,
):
    grad_parts = rest[:-7]
    stream, operands, factors, gates, grad_proj, past_part, total = rest[-7:]
    halo, (length, channels) = plan["halo"], own_x.shape
    layers, low = conv_w.shape[0], low_gates.shape[0]
    pad = 2 ** (layers - 1)
    extent = length + 2 * halo
    stream[0:pad] = jnp.zeros((pad, channels), jnp.float32)
    stream[pad : pad + halo] = prev_x[...].astype(jnp.float32)
    stream[pad + halo : pad + halo + length] = own_x[...].astype(jnp.float32)
    stream[pad + halo + length :] = next_rows[0:halo].astype(jnp.float32)

    def refs_of(index):
        if index < low:
            return low_operands.at[index], low_factors.at[index], low_gates.at[index]
        return operands.at[index - low], factors.at[index - low], gates.at[index - low]

    for index in range(layers):
        dilation, start = 2**index, plan["starts"][index]
        operand, factor, gate = refs_of(index)
        operand[start:, :channels] = stream[pad + start :].astype(jnp.bfloat16)
        operand[start:, channels:] = stream[pad + start - dilation : pad + extent - dilation].astype(jnp.bfloat16)
        preact = dot(operand[start:], conv_w[index], NN)
        filtered = jnp.tanh(preact[:, :channels])
        opening = 0.5 + 0.5 * jnp.tanh(0.5 * preact[:, channels:])
        product = filtered * opening
        gate[start:] = product.astype(jnp.bfloat16)
        factor[start:, :channels] = opening - filtered * product
        factor[start:, channels:] = product * (1.0 - opening)
        if index < layers - 1:
            stream[pad + start :] += dot(gate[start:], out_w[index, :, :channels], NN)

    grad_stream[0:length] = own_grad[...]
    grad_stream[length:] = next_rows[halo : 2 * halo].astype(jnp.float32)
    grad_skip[0:length] = own_skip[...]
    grad_skip[length:] = next_rows[2 * halo : 3 * halo]
    grad_proj[:, channels:] = grad_skip[...]
    backward(
        plan, list(reversed(range(low, layers))), refs_of, conv_w, out_w,
        grad_proj, grad_stream, past_part, total, grad_parts,
    )


def second_kernel(
    plan, low_operands, low_factors, low_gates, grad_before, grad_skip, sums, conv_w, out_w, grad_in, *rest
):
    grad_parts = rest[:-4]
    grad_stream, grad_proj, past_part, total = rest[-4:]
    channels, low = plan["channels"], low_gates.shape[0]
    grad_stream[...] = grad_before[...]
    grad_proj[:, channels:] = grad_skip[...]

    def refs_of(index):
        return low_operands.at[index], low_factors.at[index], low_gates.at[index]

    backward(
        plan, list(reversed(range(low))), refs_of, conv_w, out_w, grad_proj, grad_stream, past_part, total, grad_parts
    )
    grad_in[...] = grad_stream[0 : plan["length"]]
    plan["finish"](sums, grad_parts)


def store_whole(total, height, place, grad_parts, is_out):
    grad_parts[int(is_out)][place] = total[0:height].astype(jnp.bfloat16)


def finish_whole(sums, grad_parts):
    pass


def finish_shards(sums, grad_parts):
    for part in grad_parts:
        for a in range(part.shape[0]):
            for b in range(part.shape[1]):
                for c in range(part.shape[2]):
                    part[a, b, c, part.shape[3] - 16 :] = sums[...]


def lead_of_high(place, x, y, z):
    return z, x, y


def lead_of_low(half, place, x, y, z):
    return (x, y, z) if place < half else (y, x, z)


def store_shards(tm, dp, lead_of, total, height, place, grad_parts, is_out):
    keep, send = grad_parts
    t_at, d_at = lax.axis_index("tm"), lax.axis_index("dp")
    x_at, y_at, z_at, core_at = lax.rem(t_at, 2), lax.div(d_at, 2), lax.div(t_at, 2), lax.rem(d_at, 2)
    channels = total.shape[0] // 2
    depth, rows = tm // 2, height // tm
    at = pl.ds(place * 3 * channels // tm + (2 * channels // tm if is_out else 0), rows)
    for y in range(dp // 2):
        near = total[0:height, (2 * y) * LANES : (2 * y + 1) * LANES]
        far = total[0:height, (2 * y + 1) * LANES : (2 * y + 2) * LANES]
        mine = jnp.where(core_at == 0, near, far).astype(jnp.bfloat16)
        other = jnp.where(core_at == 0, far, near).astype(jnp.bfloat16)
        y_off = lax.rem(y - y_at + dp // 2, dp // 2)
        for t in range(tm):
            z, x = divmod(t, 2)
            lead = lead_of(place, lax.rem(x - x_at + 2, 2), y_off, lax.rem(z - z_at + depth, depth))
            keep[lead[0], lead[1], lead[2], at] = mine[t * rows : (t + 1) * rows]
            send[lead[0], lead[1], lead[2], at] = other[t * rows : (t + 1) * rows]


def run_layers(in_shards, tm, dp, halo, prev_x, next_rows, loaded):
    own_x, own_grad, own_skip, sums, conv_w, out_w = loaded
    length, channels = own_x.shape
    layers = conv_w.shape[0]
    low = layers - layers // 3
    extent = length + 2 * halo
    starts = []
    for index in range(layers):
        need = halo if index == layers - 1 else 2 ** (index + 1)
        starts.append(need // 16 * 16)
    counts = [-(-(length + 2 ** (index + 1) - 1) // 16) * 16 for index in range(layers)]
    plan = {"halo": halo, "starts": starts, "counts": counts, "length": length, "channels": channels}
    if in_shards:
        rows = 3 * channels // tm
        high_plan = plan | {"store": functools.partial(store_shards, tm, dp, lead_of_high)}
        low_plan = plan | {
            "store": functools.partial(store_shards, tm, dp, functools.partial(lead_of_low, low // 2)),
            "finish": finish_shards,
        }
        high_shapes = 2 * [(tm // 2, 2, dp // 2, (layers - low) * rows, LANES)]
        low_shapes = 2 * [(2, 2, tm // 2, low * rows + 16, LANES)]
    else:
        high_plan = plan | {"store": store_whole}
        low_plan = high_plan | {"finish": finish_whole}
        high_shapes = [(layers - low,) + conv_w.shape[1:], (layers - low,) + out_w.shape[1:]]
        low_shapes = [(low,) + conv_w.shape[1:], (low,) + out_w.shape[1:]]
    vmem = pl.BlockSpec(memory_space=pltpu.VMEM)
    weight_bytes = 2 * (conv_w.size + out_w.size)
    flops = 2 * length * channels * channels
    border = length + halo
    *kept, grad_stream, grad_skip, a, b = pl.pallas_call(
        functools.partial(first_kernel, high_plan),
        in_specs=[vmem] * 7,
        out_specs=[vmem] * 7,
        out_shape=[
            pltpu.VMEM((low, extent, 2 * channels), jnp.bfloat16),
            pltpu.VMEM((low, extent, 2 * channels), jnp.float32),
            pltpu.VMEM((low, extent, channels), jnp.bfloat16),
            pltpu.VMEM((border, channels), jnp.float32),
            pltpu.VMEM((border, channels), jnp.bfloat16),
        ]
        + [pltpu.VMEM(shape, jnp.bfloat16) for shape in high_shapes],
        scratch_shapes=[
            pltpu.VMEM((2 ** (layers - 1) + extent, channels), jnp.float32),
            pltpu.VMEM((layers - low, extent, 2 * channels), jnp.bfloat16),
            pltpu.VMEM((layers - low, extent, 2 * channels), jnp.float32),
            pltpu.VMEM((layers - low, extent, channels), jnp.bfloat16),
            pltpu.VMEM((border, 2 * channels), jnp.bfloat16),
            pltpu.VMEM((border, channels), jnp.float32),
            pltpu.VMEM((2 * channels, 2 * channels), jnp.float32),
        ],
        compiler_params=pltpu.CompilerParams(vmem_limit_bytes=VMEM_BYTES),
        cost_estimate=cost(flops * (5 * layers + 12 * (layers - low)), weight_bytes),
        name="forward_and_last_layers",
    )(*held((prev_x, next_rows, own_x, own_grad, own_skip, conv_w, out_w)))
    grad_in, *rest = pl.pallas_call(
        functools.partial(second_kernel, low_plan),
        in_specs=[vmem] * 8,
        out_specs=[vmem] * 3,
        out_shape=[pltpu.VMEM((length, channels), jnp.float32)]
        + [pltpu.VMEM(shape, jnp.bfloat16) for shape in low_shapes],
        scratch_shapes=[
            pltpu.VMEM((border, channels), jnp.float32),
            pltpu.VMEM((border, 2 * channels), jnp.bfloat16),
            pltpu.VMEM((border, channels), jnp.float32),
            pltpu.VMEM((2 * channels, 2 * channels), jnp.float32),
        ],
        compiler_params=pltpu.CompilerParams(vmem_limit_bytes=VMEM_BYTES),
        cost_estimate=cost(flops * 12 * low, weight_bytes),
        name="first_layers",
    )(*held((*kept, grad_stream, grad_skip, sums, conv_w, out_w)))
    return grad_in, (a, b), rest


def add_kernel(count, groups, *refs):
    arrays, outs = refs[:count], refs[-len(groups) :]
    for out, pieces in zip(outs, groups):
        lead = (slice(None),) * (len(out.shape) - 2)
        for first, rows, with_total, terms in pieces:
            body = rows - 16 if with_total else rows
            value = 0.0
            for array, at, begin in terms:
                value = value + arrays[array][at + lead + (slice(begin, begin + body),)].astype(jnp.float32)
            out[lead + (slice(first, first + body),)] = value.astype(out.dtype)
            if with_total:
                total = 0.0
                for array, at, begin in terms:
                    rows_at = slice(begin + body, begin + rows)
                    total = total + joined_rows(arrays[array][at + (0,) * len(lead) + (rows_at,)])
                slab = split_rows(total)
                out[lead + (slice(first + body, first + rows),)] = jnp.broadcast_to(slab, out.shape[:-2] + slab.shape)


def add_up(arrays, groups, shapes, after, name):
    vmem = pl.BlockSpec(memory_space=pltpu.VMEM)
    return pl.pallas_call(
        functools.partial(add_kernel, len(arrays), groups),
        in_specs=[vmem] * len(arrays) + [pl.BlockSpec(memory_space=pl.ANY)] * len(after),
        out_specs=[vmem] * len(groups),
        out_shape=[pltpu.VMEM(shape, jnp.bfloat16) for shape in shapes],
        compiler_params=pltpu.CompilerParams(vmem_limit_bytes=ADD_BYTES),
        name=name,
    )(*held(arrays), *held(after))


def last_kernel(low_count, high_count, samples_all, low, *refs):
    low_parts, refs = refs[:low_count], refs[low_count:]
    high_parts, refs = refs[:high_count], refs[high_count:]
    grad_in, grad_inputs, grad_conv, grad_out = refs
    layers, conv_rows, _ = grad_conv.shape
    out_rows = grad_out.shape[1]
    rows = conv_rows + out_rows
    total = 0.0
    for part in low_parts:
        total = total + joined_rows(part[low * rows :])
    scale = samples_all / total
    for index in range(layers):
        parts, place = (low_parts, low - 1 - index) if index < low else (high_parts, layers - 1 - index)
        for out, at in ((grad_conv, 0), (grad_out, conv_rows)):
            first = place * rows + at
            value = 0.0
            for part in parts:
                value = value + part[first : first + out.shape[1]].astype(jnp.float32)
            out[index] = value * scale
    for first in range(0, grad_in.shape[1], LANES):
        grad_inputs[:, first : first + LANES] = grad_in[:, first : first + LANES] * scale


def reduce_shards(tm, dp, layers, high_parts, low_parts):
    depth, wide = tm // 2, dp // 2
    axes = ("tm", "dp")

    def moved(x, core=0, xs=0, ys=0, zs=0):
        pairs = []
        for t in range(tm):
            for d in range(dp):
                z, a = divmod(t, 2)
                y, c = divmod(d, 2)
                to_t = (z + zs) % depth * 2 + (a + xs) % 2
                to_d = (y + ys) % wide * 2 + (c + core) % 2
                pairs.append((t * dp + d, to_t * dp + to_d))
        return lax.ppermute(x, axes, pairs)

    (keep_high, send_high), (keep_low, send_low) = high_parts, low_parts
    high_rows, low_rows = keep_high.shape[3], keep_low.shape[3]
    half = (low_rows - 16) // 2
    steps_z = range(1, depth)
    steps_p = [(x, y) for x in range(2) for y in range(wide)][1:]

    high_there = moved(send_high, core=1)
    low_there = moved(send_low, core=1)
    high_first = add_up(
        [keep_high, high_there], [[(0, high_rows, False, [(0, (r,), 0), (1, (r,), 0)])] for r in steps_z],
        [keep_high.shape[1:]] * len(steps_z), [], "add_last_cores",
    )
    high_z = [moved(x, zs=r) for x, r in zip(high_first, steps_z)]
    a_rows, b_rows = half, low_rows - half
    send_a, send_b = add_up(
        [keep_low, low_there],
        [
            [(0, a_rows, False, [(0, (1,), 0), (1, (1,), 0)])],
            [(0, b_rows, True, [(0, (1,), half), (1, (1,), half)])],
        ],
        [(2, depth, a_rows, LANES), (2, depth, b_rows, LANES)], high_first[:1], "add_first_cores",
    )
    a_x, b_y = moved(send_a, xs=1), moved(send_b, ys=1)
    send_a, send_b = add_up(
        [keep_low, low_there, a_x, b_y],
        [
            [(0, a_rows, False, [(0, (0, 1), 0), (1, (0, 1), 0), (2, (1,), 0)])],
            [(0, b_rows, True, [(0, (0, 1), half), (1, (0, 1), half), (3, (1,), 0)])],
        ],
        [(depth, a_rows, LANES), (depth, b_rows, LANES)], [], "add_first_halves",
    )
    a_y, b_x = moved(send_a, ys=1), moved(send_b, xs=1)
    high_second = add_up(
        [keep_high, high_there] + high_z,
        [
            [(0, high_rows, False, [(0, (0, x, y), 0), (1, (0, x, y), 0)] + [(2 + i, (x, y), 0) for i in range(len(high_z))])]
            for x, y in [(0, 0)] + steps_p
        ],
        [(high_rows, LANES)] * (2 * wide), [send_a], "add_last_along",
    )
    high_p = [moved(v, xs=x, ys=y) for v, (x, y) in zip(high_second[1:], steps_p)]
    low_third = add_up(
        [keep_low, low_there, a_x, b_y, a_y, b_x],
        [
            [
                (0, a_rows, False, [(0, (0, 0, r), 0), (1, (0, 0, r), 0), (2, (0, r), 0), (4, (r,), 0)]),
                (half, b_rows, True, [(0, (0, 0, r), half), (1, (0, 0, r), half), (3, (0, r), 0), (5, (r,), 0)]),
            ]
            for r in range(depth)
        ],
        [(low_rows, LANES)] * depth, high_second[:1], "add_first_quarters",
    )
    low_z = [moved(v, zs=r) for v, r in zip(low_third[1:], steps_z)]
    return [low_third[0]] + low_z, [high_second[0]] + high_p


def scattered(part):
    columns = lax.psum_scatter(part, "dp", scatter_dimension=2, tiled=True).astype(jnp.float32)
    return lax.psum_scatter(columns, "tm", scatter_dimension=1, tiled=True)


def body(inputs, grad_stream_out, grad_skip_out, sample_weight, conv_weight, out_weight):
    tm, dp = lax.axis_size("tm"), lax.axis_size("dp")
    batch, length, channels = inputs.shape
    layers = conv_weight.shape[0]
    low = layers - layers // 3
    halo = 2**layers
    samples_all = batch * length * tm * dp
    x, gs, gk = inputs[0], grad_stream_out[0], grad_skip_out[0]
    to_next, to_prev = pack(halo, x, gs, gk, sample_weight)
    prev_x = shifted(to_next, "tm", 1)
    next_rows = shifted(to_prev, "tm", -1)
    loaded = load_all(x, gs, gk, sample_weight, conv_weight, out_weight, to_next)
    in_shards = dp == 4 and tm % 2 == 0 and channels // tm % 16 == 0 and 2 * channels == dp * LANES and low % 2 == 0
    grad_in, high_parts, low_parts = run_layers(in_shards, tm, dp, halo, prev_x, next_rows, loaded)
    if not in_shards:
        scale = samples_all / lax.psum(jnp.sum(sample_weight), ("tm", "dp"))
        grad_conv, grad_out = (
            scattered(jnp.concatenate([first[::-1], last[::-1]])) * scale for first, last in zip(low_parts, high_parts)
        )
        return (grad_in * scale)[None], grad_conv, grad_out
    low_terms, high_terms = reduce_shards(tm, dp, layers, high_parts, low_parts)
    conv_rows, out_rows = 2 * channels // tm, channels // tm
    grad_inputs, grad_conv, grad_out = pl.pallas_call(
        functools.partial(last_kernel, len(low_terms), len(high_terms), float(samples_all), low),
        out_shape=[
            jax.ShapeDtypeStruct((length, channels), jnp.float32),
            jax.ShapeDtypeStruct((layers, conv_rows, LANES), jnp.float32),
            jax.ShapeDtypeStruct((layers, out_rows, LANES), jnp.float32),
        ],
        compiler_params=pltpu.CompilerParams(vmem_limit_bytes=ADD_BYTES),
        name="scale_all",
    )(*held(low_terms), *held(high_terms), *held([grad_in]))
    return grad_inputs[None], grad_conv, grad_out


def solution(mesh):
    placed = (
        P("dp", "tm", None),
        P("dp", "tm", None),
        P("dp", "tm", None),
        P("dp", "tm"),
        P(),
        P(),
    )
    return jax.shard_map(
        body,
        mesh=mesh,
        in_specs=placed,
        out_specs=(P("dp", "tm", None), P(None, "tm", "dp"), P(None, "tm", "dp")),
        check_vma=False,
    )
```

```python
import functools

import jax
import jax.numpy as jnp
from jax import lax
from jax.experimental import pallas as pl
from jax.experimental.pallas import tpu as pltpu
from jax.sharding import PartitionSpec as P

LANES = 128
VMEM_BYTES = 24 * 1024 * 1024
ADD_BYTES = 8 * 1024 * 1024
EXTRA = (32, 16, 0)
CHAINS = (("x", "y", "z0", "z1"), ("y", "z0", "x", "z1"), ("z0", "x", "y", "z1"))
NN = (((1,), (0,)), ((), ()))
NT = (((1,), (1,)), ((), ()))
TN = (((0,), (0,)), ((), ()))


def dot(left, right, dims):
    return lax.dot_general(left, right, dims, preferred_element_type=jnp.float32)


def held(arrays, space=pltpu.VMEM):
    return [pltpu.with_memory_space_constraint(x, space) for x in arrays]


def shifted(x, axis, by):
    count = lax.axis_size(axis)
    pairs = [(i, i + by) for i in range(count) if 0 <= i + by < count]
    return lax.ppermute(x, axis, pairs)


def column(row, rows):
    return jnp.broadcast_to(row, (LANES, rows)).T


def cost(flops, moved):
    return pl.CostEstimate(flops=flops, bytes_accessed=moved, transcendentals=0)


def pack_kernel(head_x, tail_x, head_gs, head_gk, weight, to_next, to_prev):
    halo, channels = tail_x.shape
    to_next[...] = tail_x[...]
    by_row = column(weight[...], LANES)[:halo]
    by_row = jnp.concatenate([by_row] * (channels // LANES), axis=1)
    to_prev[0:halo] = head_x[...]
    to_prev[halo : 2 * halo] = (head_gs[...].astype(jnp.float32) * by_row).astype(jnp.bfloat16)
    to_prev[2 * halo : 3 * halo] = (head_gk[...].astype(jnp.float32) * by_row).astype(jnp.bfloat16)


def pack(halo, x, grad_stream_out, grad_skip_out, weight):
    length, channels = x.shape
    first = pl.BlockSpec((halo, channels), lambda i: (0, 0))
    last = pl.BlockSpec((halo, channels), lambda i: (length // halo - 1, 0))
    return pl.pallas_call(
        pack_kernel,
        grid=(1,),
        in_specs=[first, last, first, first, pl.BlockSpec((1, LANES), lambda i: (0, 0))],
        out_specs=[
            pl.BlockSpec((halo, channels), lambda i: (0, 0)),
            pl.BlockSpec((3 * halo, channels), lambda i: (0, 0)),
        ],
        out_shape=[
            jax.ShapeDtypeStruct((halo, channels), jnp.bfloat16),
            jax.ShapeDtypeStruct((3 * halo, channels), jnp.bfloat16),
        ],
        compiler_params=pltpu.CompilerParams(vmem_limit_bytes=ADD_BYTES),
        name="pack_borders",
    )(*held((x, x, grad_stream_out, grad_skip_out, weight), pltpu.HBM))


def load_kernel(
    x, gs, gk, weight, conv_w, out_w, _, x_here, grad_stream, grad_skip, sums, conv_here, out_here,
    gs_raw, gk_raw, weight_here, sems,
):
    some = pl.ds(0, conv_here.shape[0])
    pairs = (
        (weight, weight_here), (gs, gs_raw), (gk, gk_raw), (x, x_here),
        (conv_w.at[some], conv_here), (out_w.at[some], out_here),
    )
    copies = [pltpu.make_async_copy(a, b, sems.at[i]) for i, (a, b) in enumerate(pairs)]
    for copy in copies:
        copy.start()
    for copy in copies[:3]:
        copy.wait()
    length, channels = x_here.shape
    by_row = column(weight_here[...], length)
    by_row = jnp.concatenate([by_row] * (channels // LANES), axis=1)
    grad_stream[...] = gs_raw[...].astype(jnp.float32) * by_row
    grad_skip[...] = (gk_raw[...].astype(jnp.float32) * by_row).astype(jnp.bfloat16)
    own_sum = jnp.broadcast_to(jnp.sum(weight_here[...], axis=1, keepdims=True), (1, LANES))
    sums[...] = split_rows(own_sum)
    for copy in copies[3:]:
        copy.wait()


def load_some(third, x, gs, gk, weight, conv_w, out_w, after):
    shape = x.shape
    vmem, anywhere = pl.BlockSpec(memory_space=pltpu.VMEM), pl.BlockSpec(memory_space=pl.ANY)
    return pl.pallas_call(
        load_kernel,
        in_specs=[anywhere] * 7,
        out_specs=[vmem] * 6,
        out_shape=[
            pltpu.VMEM(shape, jnp.bfloat16),
            pltpu.VMEM(shape, jnp.float32),
            pltpu.VMEM(shape, jnp.bfloat16),
            pltpu.VMEM((16, LANES), jnp.bfloat16),
            pltpu.VMEM((third,) + conv_w.shape[1:], jnp.bfloat16),
            pltpu.VMEM((third,) + out_w.shape[1:], jnp.bfloat16),
        ],
        scratch_shapes=[
            pltpu.VMEM(shape, jnp.bfloat16),
            pltpu.VMEM(shape, jnp.bfloat16),
            pltpu.VMEM(weight.shape, jnp.float32),
            pltpu.SemaphoreType.DMA((6,)),
        ],
        compiler_params=pltpu.CompilerParams(vmem_limit_bytes=ADD_BYTES),
        cost_estimate=cost(10**7, 4 * 10**6),
        name="load_some",
    )(*held((x, gs, gk, weight, conv_w, out_w), pltpu.HBM), *held([after]))


def split_rows(total):
    high = total.astype(jnp.bfloat16).astype(jnp.float32)
    middle = (total - high).astype(jnp.bfloat16).astype(jnp.float32)
    low = total - high - middle
    row = lax.broadcasted_iota(jnp.int32, (16, LANES), 0)
    rows = jnp.where(row == 0, high, jnp.where(row == 1, middle, jnp.where(row == 2, low, 0.0)))
    return rows.astype(jnp.bfloat16)


def joined_rows(rows):
    return jnp.sum(rows.astype(jnp.float32), axis=0, keepdims=True)


def backward(plan, layers, refs_of, weights_of, grad_proj, grad_stream, past_part, total, grad_parts):
    halo, length, channels = plan["halo"], plan["length"], plan["channels"]
    own = slice(halo, halo + length)
    for place, index in enumerate(layers):
        dilation, count = 2**index, plan["counts"][index]
        operands, factors, gates = refs_of(index)
        conv_layer, out_layer = weights_of(index)
        grad_proj[0:count, :channels] = grad_stream[0:count].astype(jnp.bfloat16)
        grad_gated = dot(grad_proj[0:count], out_layer[...], NT)
        total[0:channels] = dot(gates[own], grad_proj[0:length], TN)
        plan["store"](total, channels, place, grad_parts, True)
        both = factors[halo : halo + count]
        grad_preact = jnp.concatenate(
            [grad_gated * both[:, :channels], grad_gated * both[:, channels:]], axis=1
        ).astype(jnp.bfloat16)
        spread = dot(grad_preact, conv_layer[...], NT)
        past_part[0:count] = spread[:, channels:]
        rows = plan["counts"][index - 1] if index else length
        grad_stream[0:rows] += spread[0:rows, :channels] + past_part[dilation : dilation + rows]
        total[...] = dot(operands[own], grad_preact[0:length], TN)
        plan["store"](total, 2 * channels, place, grad_parts, False)


def first_kernel(
    plan, prev_x, next_rows, own_x, own_grad, own_skip, sums, conv_low, out_low, conv_w, out_w,
    low_operands, low_factors, low_gates, grad_stream, grad_skip, conv_high, out_high, *rest,
):
    grad_parts = rest[:-8]
    stream, operands, factors, gates, grad_proj, past_part, total, sems = rest[-8:]
    halo, (length, channels) = plan["halo"], own_x.shape
    layers, low, third = conv_w.shape[0], low_gates.shape[0], conv_low.shape[0]
    copies = {}
    for index in range(third, layers):
        at = 2 * (index - third)
        copies[index] = (
            pltpu.make_async_copy(conv_w.at[index], conv_high.at[index - third], sems.at[at]),
            pltpu.make_async_copy(out_w.at[index], out_high.at[index - third], sems.at[at + 1]),
        )
        for copy in copies[index]:
            copy.start()
    pad = 2 ** (layers - 1)
    extent = length + 2 * halo
    stream[0:pad] = jnp.zeros((pad, channels), jnp.float32)
    stream[pad : pad + halo] = prev_x[...].astype(jnp.float32)
    stream[pad + halo : pad + halo + length] = own_x[...].astype(jnp.float32)
    stream[pad + halo + length :] = next_rows[0:halo].astype(jnp.float32)

    def refs_of(index):
        if index < low:
            return low_operands.at[index], low_factors.at[index], low_gates.at[index]
        return operands.at[index - low], factors.at[index - low], gates.at[index - low]

    def weights_of(index):
        if index < third:
            return conv_low.at[index], out_low.at[index]
        return conv_high.at[index - third], out_high.at[index - third]

    for index in range(layers):
        dilation, start = 2**index, plan["starts"][index]
        operand, factor, gate = refs_of(index)
        conv_layer, out_layer = weights_of(index)
        operand[start:, :channels] = stream[pad + start :].astype(jnp.bfloat16)
        operand[start:, channels:] = stream[pad + start - dilation : pad + extent - dilation].astype(jnp.bfloat16)
        for copy in copies.get(index, ()):
            copy.wait()
        preact = dot(operand[start:], conv_layer[...], NN)
        filtered = jnp.tanh(preact[:, :channels])
        opening = 0.5 + 0.5 * jnp.tanh(0.5 * preact[:, channels:])
        product = filtered * opening
        gate[start:] = product.astype(jnp.bfloat16)
        factor[start:, :channels] = opening - filtered * product
        factor[start:, channels:] = product * (1.0 - opening)
        if index < layers - 1:
            stream[pad + start :] += dot(gate[start:], out_layer[:, :channels], NN)

    grad_stream[0:length] = own_grad[...]
    grad_stream[length:] = next_rows[halo : 2 * halo].astype(jnp.float32)
    grad_skip[0:length] = own_skip[...]
    grad_skip[length:] = next_rows[2 * halo : 3 * halo]
    grad_proj[:, channels:] = grad_skip[...]
    backward(
        plan, list(reversed(range(low, layers))), refs_of, weights_of,
        grad_proj, grad_stream, past_part, total, grad_parts,
    )
    plan["finish"](sums, grad_parts)


def later_kernel(
    plan, first, third, low_operands, low_factors, low_gates, grad_before, grad_skip, sums, conv_w, out_w, *rest
):
    grad_after, *grad_parts, grad_stream, grad_proj, past_part, total = rest[-7:]
    channels = plan["channels"]
    grad_stream[...] = grad_before[...]
    grad_proj[:, channels:] = grad_skip[...]

    def refs_of(index):
        return low_operands.at[index], low_factors.at[index], low_gates.at[index]

    def weights_of(index):
        return conv_w.at[index - first], out_w.at[index - first]

    backward(
        plan, list(reversed(range(first, first + third))), refs_of, weights_of,
        grad_proj, grad_stream, past_part, total, grad_parts,
    )
    grad_after[...] = grad_stream[0 : grad_after.shape[0]]
    plan["finish"](sums, grad_parts)


def store_whole(total, height, place, grad_parts, is_out):
    grad_parts[int(is_out)][place] = total[0:height].astype(jnp.bfloat16)


def finish_whole(sums, grad_parts):
    pass


def finish_shards(extra, sums, grad_parts):
    for part in grad_parts:
        lead, rows = part.shape[:-2], part.shape[-2]
        for first in range(rows - extra, rows, 16):
            part[(slice(None),) * len(lead) + (slice(first, first + 16),)] = jnp.broadcast_to(
                sums[...], lead + sums.shape
            )


def store_shards(tm, dp, order, total, height, place, grad_parts, is_out):
    keep, send = grad_parts
    t_at, d_at = lax.axis_index("tm"), lax.axis_index("dp")
    core_at = lax.rem(d_at, 2)
    channels = total.shape[0] // 2
    rows = height // tm
    at = pl.ds(place * 3 * channels // tm + (2 * channels // tm if is_out else 0), rows)
    at_bits = bits_of(t_at, d_at, lax.rem, lax.div)
    for y in range(dp // 2):
        near = total[0:height, (2 * y) * LANES : (2 * y + 1) * LANES]
        far = total[0:height, (2 * y + 1) * LANES : (2 * y + 2) * LANES]
        mine = jnp.where(core_at == 0, near, far).astype(jnp.bfloat16)
        other = jnp.where(core_at == 0, far, near).astype(jnp.bfloat16)
        for t in range(tm):
            bits = bits_of(t, 2 * y, lambda a, b: a % b, lambda a, b: a // b)
            lead = tuple(lax.rem(bits[name] + at_bits[name], 2) for name in order)
            keep[lead + (at,)] = mine[t * rows : (t + 1) * rows]
            send[lead + (at,)] = other[t * rows : (t + 1) * rows]


def bits_of(t, d, rem, div):
    return {"x": rem(t, 2), "z0": rem(div(t, 2), 2), "z1": div(t, 4), "y": div(d, 2)}


def run_layers(in_shards, tm, dp, halo, prev_x, next_rows, loaded, conv_w, out_w):
    own_x, own_grad, own_skip, sums, conv_low, out_low = loaded
    length, channels = own_x.shape
    layers, third = conv_w.shape[0], conv_low.shape[0]
    low = layers - third
    extent, border = length + 2 * halo, length + halo
    starts = []
    for index in range(layers):
        need = halo if index == layers - 1 else 2 ** (index + 1)
        starts.append(need // 16 * 16)
    counts = [-(-(length + 2 ** (index + 1) - 1) // 16) * 16 for index in range(layers)]
    plan = {"halo": halo, "starts": starts, "counts": counts, "length": length, "channels": channels}
    if in_shards:
        rows = third * 3 * channels // tm
        plans = [
            plan
            | {
                "store": functools.partial(store_shards, tm, dp, order),
                "finish": functools.partial(finish_shards, extra),
            }
            for order, extra in zip(CHAINS, EXTRA)
        ]
        shapes = [2 * [(2,) * len(order) + (rows + extra, LANES)] for order, extra in zip(CHAINS, EXTRA)]
    else:
        plans = [plan | {"store": store_whole, "finish": finish_whole}] * len(CHAINS)
        shapes = [[(third,) + conv_w.shape[1:], (third,) + out_w.shape[1:]]] * len(CHAINS)
    vmem, anywhere = pl.BlockSpec(memory_space=pltpu.VMEM), pl.BlockSpec(memory_space=pl.ANY)
    weight_bytes = 2 * (conv_w.size + out_w.size)
    flops = 2 * length * channels * channels
    *kept, grad_stream, grad_skip, conv_high, out_high, keep, send = pl.pallas_call(
        functools.partial(first_kernel, plans[0]),
        in_specs=[vmem] * 8 + [anywhere] * 2,
        out_specs=[vmem] * 9,
        out_shape=[
            pltpu.VMEM((low, extent, 2 * channels), jnp.bfloat16),
            pltpu.VMEM((low, extent, 2 * channels), jnp.float32),
            pltpu.VMEM((low, extent, channels), jnp.bfloat16),
            pltpu.VMEM((border, channels), jnp.float32),
            pltpu.VMEM((border, channels), jnp.bfloat16),
            pltpu.VMEM((low,) + conv_w.shape[1:], jnp.bfloat16),
            pltpu.VMEM((low,) + out_w.shape[1:], jnp.bfloat16),
        ]
        + [pltpu.VMEM(shape, jnp.bfloat16) for shape in shapes[0]],
        scratch_shapes=[
            pltpu.VMEM((2 ** (layers - 1) + extent, channels), jnp.float32),
            pltpu.VMEM((third, extent, 2 * channels), jnp.bfloat16),
            pltpu.VMEM((third, extent, 2 * channels), jnp.float32),
            pltpu.VMEM((third, extent, channels), jnp.bfloat16),
            pltpu.VMEM((border, 2 * channels), jnp.bfloat16),
            pltpu.VMEM((border, channels), jnp.float32),
            pltpu.VMEM((2 * channels, 2 * channels), jnp.float32),
            pltpu.SemaphoreType.DMA((2 * low,)),
        ],
        compiler_params=pltpu.CompilerParams(vmem_limit_bytes=VMEM_BYTES),
        cost_estimate=cost(flops * (5 * layers + 12 * third), weight_bytes),
        name="forward_and_last_third",
    )(
        *held((prev_x, next_rows, own_x, own_grad, own_skip, sums, conv_low, out_low)),
        *held((conv_w, out_w), pltpu.HBM),
    )
    parts = [Chunk(tm, dp, 0, keep, send) if in_shards else (keep, send)]
    for step in (1, 2):
        first = layers - (step + 1) * third
        last = step == 2
        weights = (conv_low, out_low) if last else (conv_high, out_high)
        after = [parts[0].next_message()] if last and in_shards else []
        grad_stream, keep, send = pl.pallas_call(
            functools.partial(later_kernel, plans[step], first, third),
            in_specs=[vmem] * 8 + [anywhere] * len(after),
            out_specs=[vmem] * 3,
            out_shape=[pltpu.VMEM((length if last else border, channels), jnp.float32)]
            + [pltpu.VMEM(shape, jnp.bfloat16) for shape in shapes[step]],
            scratch_shapes=[
                pltpu.VMEM((border, channels), jnp.float32),
                pltpu.VMEM((border, 2 * channels), jnp.bfloat16),
                pltpu.VMEM((border, channels), jnp.float32),
                pltpu.VMEM((2 * channels, 2 * channels), jnp.float32),
            ],
            compiler_params=pltpu.CompilerParams(vmem_limit_bytes=VMEM_BYTES),
            cost_estimate=cost(flops * 12 * third, weight_bytes),
            name="first_third" if last else "middle_third",
        )(*held((*kept, grad_stream, grad_skip, sums, *weights, *after)))
        parts.append(Chunk(tm, dp, step, keep, send) if in_shards else (keep, send))
    return grad_stream, parts


def add_kernel(count, groups, *refs):
    arrays, outs = refs[:count], refs[-len(groups) :]
    for out, pieces in zip(outs, groups):
        lead = (slice(None),) * (len(out.shape) - 2)
        for first, rows, with_total, terms in pieces:
            body = rows - 16 if with_total else rows
            value = 0.0
            for array, at, begin in terms:
                value = value + arrays[array][at + lead + (slice(begin, begin + body),)].astype(jnp.float32)
            out[lead + (slice(first, first + body),)] = value.astype(out.dtype)
            if with_total:
                total = 0.0
                for array, at, begin in terms:
                    rows_at = slice(begin + body, begin + rows)
                    total = total + joined_rows(arrays[array][at + (0,) * len(lead) + (rows_at,)])
                slab = split_rows(total)
                out[lead + (slice(first + body, first + rows),)] = jnp.broadcast_to(slab, out.shape[:-2] + slab.shape)


def add_up(arrays, groups, shapes, after, name):
    vmem = pl.BlockSpec(memory_space=pltpu.VMEM)
    return pl.pallas_call(
        functools.partial(add_kernel, len(arrays), groups),
        in_specs=[vmem] * len(arrays) + [pl.BlockSpec(memory_space=pl.ANY)] * len(after),
        out_specs=[vmem] * len(groups),
        out_shape=[pltpu.VMEM(shape, jnp.bfloat16) for shape in shapes],
        compiler_params=pltpu.CompilerParams(vmem_limit_bytes=ADD_BYTES),
        name=name,
    )(*held(arrays), *held(after))


def last_kernel(counts, samples_all, third, *refs):
    parts = []
    for count in counts:
        parts.append(refs[:count])
        refs = refs[count:]
    grad_in, grad_inputs, grad_conv, grad_out = refs
    layers, conv_rows, _ = grad_conv.shape
    out_rows = grad_out.shape[1]
    rows = conv_rows + out_rows
    total = 0.0
    for part in parts[0]:
        total = total + joined_rows(part[(0,) * (len(part.shape) - 2) + (slice(part.shape[-2] - 16, part.shape[-2]),)])
    scale = samples_all / total
    for chunk, terms in enumerate(parts):
        for place in range(third):
            index = layers - 1 - chunk * third - place
            for out, at in ((grad_conv, place * rows), (grad_out, place * rows + conv_rows)):
                value = 0.0
                for part in terms:
                    own = (0,) * (len(part.shape) - 2) + (slice(at, at + out.shape[1]),)
                    value = value + part[own].astype(jnp.float32)
                out[index] = value * scale
    for first in range(0, grad_in.shape[1], LANES):
        grad_inputs[:, first : first + LANES] = grad_in[:, first : first + LANES] * scale


class Chunk:
    def __init__(self, tm, dp, chunk, keep, send):
        self.tm, self.dp, self.chunk, self.rows = tm, dp, chunk, keep.shape[-2]
        self.message = None
        self.terms = [keep, self.swapped(send, "core")]

    def swapped(self, value, name):
        over_t, over_d = {"core": (0, 1), "y": (0, 2), "x": (1, 0), "z0": (2, 0), "z1": (4, 0)}[name]
        tm, dp = self.tm, self.dp
        pairs = [(t * dp + d, (t ^ over_t) * dp + (d ^ over_d)) for t in range(tm) for d in range(dp)]
        return lax.ppermute(value, ("tm", "dp"), pairs)

    def next_message(self):
        if self.message is None:
            left = len(CHAINS[self.chunk]) + 2 - len(self.terms)
            leads = [(0,) * (len(v.shape) - 2 - left) + (1,) for v in self.terms]
            pieces = [(0, self.rows, self.chunk == 0, [(i, at, 0) for i, at in enumerate(leads)])]
            (self.message,) = add_up(
                self.terms, [pieces], [(2,) * (left - 1) + (self.rows, LANES)], [],
                "add_chunk%d_step%d" % (self.chunk, len(self.terms) - 1),
            )
        return self.message

    def finished(self):
        for name in CHAINS[self.chunk]:
            self.terms.append(self.swapped(self.next_message(), name))
            self.message = None
        return self.terms


def scattered(part):
    columns = lax.psum_scatter(part, "dp", scatter_dimension=2, tiled=True).astype(jnp.float32)
    return lax.psum_scatter(columns, "tm", scatter_dimension=1, tiled=True)


def body(inputs, grad_stream_out, grad_skip_out, sample_weight, conv_weight, out_weight):
    tm, dp = lax.axis_size("tm"), lax.axis_size("dp")
    batch, length, channels = inputs.shape
    layers = conv_weight.shape[0]
    third = layers // len(CHAINS)
    halo = 2**layers
    samples_all = batch * length * tm * dp
    x, gs, gk = inputs[0], grad_stream_out[0], grad_skip_out[0]
    to_next, to_prev = pack(halo, x, gs, gk, sample_weight)
    prev_x = shifted(to_next, "tm", 1)
    next_rows = shifted(to_prev, "tm", -1)
    loaded = load_some(third, x, gs, gk, sample_weight, conv_weight, out_weight, to_next)
    in_shards = tm == 8 and dp == 4 and channels // tm % 16 == 0 and 2 * channels == dp * LANES
    grad_in, parts = run_layers(in_shards, tm, dp, halo, prev_x, next_rows, loaded, conv_weight, out_weight)
    if not in_shards:
        scale = samples_all / lax.psum(jnp.sum(sample_weight), ("tm", "dp"))
        grad_conv, grad_out = (
            scattered(jnp.concatenate([part[i][::-1] for part in reversed(parts)])) * scale for i in range(2)
        )
        return (grad_in * scale)[None], grad_conv, grad_out
    terms = [part.finished() for part in parts]
    conv_rows, out_rows = 2 * channels // tm, channels // tm
    grad_inputs, grad_conv, grad_out = pl.pallas_call(
        functools.partial(last_kernel, [len(group) for group in terms], float(samples_all), third),
        out_shape=[
            jax.ShapeDtypeStruct((length, channels), jnp.float32),
            jax.ShapeDtypeStruct((layers, conv_rows, LANES), jnp.float32),
            jax.ShapeDtypeStruct((layers, out_rows, LANES), jnp.float32),
        ],
        compiler_params=pltpu.CompilerParams(vmem_limit_bytes=ADD_BYTES),
        name="scale_all",
    )(*held([value for group in terms for value in group]), *held([grad_in]))
    return grad_inputs[None], grad_conv, grad_out


def solution(mesh):
    placed = (
        P("dp", "tm", None),
        P("dp", "tm", None),
        P("dp", "tm", None),
        P("dp", "tm"),
        P(),
        P(),
    )
    return jax.shard_map(
        body,
        mesh=mesh,
        in_specs=placed,
        out_specs=(P("dp", "tm", None), P(None, "tm", "dp"), P(None, "tm", "dp")),
        check_vma=False,
    )
```

```python
import functools

import jax
import jax.numpy as jnp
from jax import lax
from jax.experimental import pallas as pl
from jax.experimental.pallas import tpu as pltpu
from jax.sharding import PartitionSpec as P

LANES = 128
VMEM_BYTES = 24 * 1024 * 1024
ADD_BYTES = 8 * 1024 * 1024
CHAINS = (("x", "y", "z0", "z1"), ("y", "z0", "x", "z1"), ("z0", "x", "y", "z1"))
EXTRA = (16, 0, 0)
NN = (((1,), (0,)), ((), ()))
NT = (((1,), (1,)), ((), ()))
TN = (((0,), (0,)), ((), ()))


def dot(left, right, dims):
    return lax.dot_general(left, right, dims, preferred_element_type=jnp.float32)


def held(arrays, space=pltpu.VMEM):
    return [pltpu.with_memory_space_constraint(x, space) for x in arrays]


def around(x, axis, by):
    count = lax.axis_size(axis)
    return lax.ppermute(x, axis, [(i, (i + by) % count) for i in range(count)])


def column(row, rows):
    return jnp.broadcast_to(row, (LANES, rows)).T


def cost(flops, moved):
    return pl.CostEstimate(flops=flops, bytes_accessed=moved, transcendentals=0)


def pack_kernel(tail_x, tail_gs, tail_gk, weight, message):
    halo, channels = tail_gs.shape
    by_row = column(weight[...], LANES)[LANES - halo :]
    by_row = jnp.concatenate([by_row] * (channels // LANES), axis=1)
    message[0 : 2 * halo] = tail_x[...]
    message[2 * halo : 3 * halo] = (tail_gs[...].astype(jnp.float32) * by_row).astype(jnp.bfloat16)
    message[3 * halo :] = (tail_gk[...].astype(jnp.float32) * by_row).astype(jnp.bfloat16)


def pack(halo, x, grad_stream_out, grad_skip_out, weight):
    length, channels = x.shape

    def last(rows):
        return pl.BlockSpec((rows, channels), lambda i: (length // rows - 1, 0))

    return pl.pallas_call(
        pack_kernel,
        grid=(1,),
        in_specs=[last(2 * halo), last(halo), last(halo), pl.BlockSpec((1, LANES), lambda i: (0, length // LANES - 1))],
        out_specs=pl.BlockSpec((4 * halo, channels), lambda i: (0, 0)),
        out_shape=jax.ShapeDtypeStruct((4 * halo, channels), jnp.bfloat16),
        compiler_params=pltpu.CompilerParams(vmem_limit_bytes=ADD_BYTES),
        name="pack_borders",
    )(*held((x, grad_stream_out, grad_skip_out, weight), pltpu.HBM))


def load_kernel(
    x, gs, gk, weight, conv_w, out_w, _, x_here, grad_stream, grad_skip, sums, conv_here, out_here,
    gs_raw, gk_raw, weight_here, sems,
):
    some = pl.ds(0, conv_here.shape[0])
    pairs = (
        (weight, weight_here), (gs, gs_raw), (gk, gk_raw), (x, x_here),
        (conv_w.at[some], conv_here), (out_w.at[some], out_here),
    )
    copies = [pltpu.make_async_copy(a, b, sems.at[i]) for i, (a, b) in enumerate(pairs)]
    for copy in copies:
        copy.start()
    for copy in copies[:3]:
        copy.wait()
    length, channels = x_here.shape
    by_row = column(weight_here[...], length)
    by_row = jnp.concatenate([by_row] * (channels // LANES), axis=1)
    grad_stream[...] = gs_raw[...].astype(jnp.float32) * by_row
    grad_skip[...] = (gk_raw[...].astype(jnp.float32) * by_row).astype(jnp.bfloat16)
    own_sum = jnp.broadcast_to(jnp.sum(weight_here[...], axis=1, keepdims=True), (1, LANES))
    sums[...] = split_rows(own_sum)
    for copy in copies[3:]:
        copy.wait()


def load_some(low, x, gs, gk, weight, conv_w, out_w, after):
    shape = x.shape
    vmem, anywhere = pl.BlockSpec(memory_space=pltpu.VMEM), pl.BlockSpec(memory_space=pl.ANY)
    return pl.pallas_call(
        load_kernel,
        in_specs=[anywhere] * 7,
        out_specs=[vmem] * 6,
        out_shape=[
            pltpu.VMEM(shape, jnp.bfloat16),
            pltpu.VMEM(shape, jnp.float32),
            pltpu.VMEM(shape, jnp.bfloat16),
            pltpu.VMEM((16, LANES), jnp.bfloat16),
            pltpu.VMEM((low,) + conv_w.shape[1:], jnp.bfloat16),
            pltpu.VMEM((low,) + out_w.shape[1:], jnp.bfloat16),
        ],
        scratch_shapes=[
            pltpu.VMEM(shape, jnp.bfloat16),
            pltpu.VMEM(shape, jnp.bfloat16),
            pltpu.VMEM(weight.shape, jnp.float32),
            pltpu.SemaphoreType.DMA((6,)),
        ],
        compiler_params=pltpu.CompilerParams(vmem_limit_bytes=ADD_BYTES),
        cost_estimate=cost(10**7, 5 * 10**6),
        name="load_some",
    )(*held((x, gs, gk, weight, conv_w, out_w), pltpu.HBM), *held([after]))


def split_rows(total):
    high = total.astype(jnp.bfloat16).astype(jnp.float32)
    middle = (total - high).astype(jnp.bfloat16).astype(jnp.float32)
    low = total - high - middle
    row = lax.broadcasted_iota(jnp.int32, (16, LANES), 0)
    rows = jnp.where(row == 0, high, jnp.where(row == 1, middle, jnp.where(row == 2, low, 0.0)))
    return rows.astype(jnp.bfloat16)


def joined_rows(rows):
    return jnp.sum(rows.astype(jnp.float32), axis=0, keepdims=True)


def cut_off(rows, dilation):
    row = lax.broadcasted_iota(jnp.int32, rows.shape, 0)
    return jnp.where(jnp.logical_and(row < dilation, lax.axis_index("tm") == 0), 0.0, rows)


def items_of(layers, chunk):
    third = layers // len(CHAINS)
    high = layers - chunk * third
    items = []
    for index in reversed(range(high - third, high)):
        items.append((index, False))
        if chunk == 0 or index < high - 1:
            items.append((index, True))
    return items + ([(high - third - 1, True)] if high > third else [])


def backward(plan, layers, refs_of, weights_of, grad_proj, grad_stream, past_part, total, grad_parts):
    halo, length, channels = plan["halo"], plan["length"], plan["channels"]
    own = slice(halo, halo + length)
    items = plan["items"]

    def out_grad(index):
        if (index, True) in items:
            total[0:channels] = dot(refs_of(index)[2][own], grad_proj[0:length], TN)
            plan["store"](total, channels, items.index((index, True)), grad_parts)

    for index in layers:
        dilation, count = 2**index, plan["counts"][index]
        operands, factors, _ = refs_of(index)
        conv_layer, out_layer = weights_of(index)
        grad_proj[0:count, :channels] = grad_stream[0:count].astype(jnp.bfloat16)
        grad_gated = dot(grad_proj[0:count], out_layer[...], NT)
        out_grad(index)
        both = factors[halo : halo + count]
        grad_preact = jnp.concatenate(
            [grad_gated * both[:, :channels], grad_gated * both[:, channels:]], axis=1
        ).astype(jnp.bfloat16)
        spread = dot(grad_preact, conv_layer[...], NT)
        past_part[0:count] = spread[:, channels:]
        cut = slice(halo, halo + max(dilation, 8))
        past_part[cut] = cut_off(past_part[cut], dilation)
        rows = plan["counts"][index - 1] if index else length
        grad_stream[0:rows] += spread[0:rows, :channels] + past_part[dilation : dilation + rows]
        total[...] = dot(operands[own], grad_preact[0:length], TN)
        plan["store"](total, 2 * channels, items.index((index, False)), grad_parts)
    after = layers[-1] - 1
    if (after, True) in items:
        grad_proj[0:length, :channels] = grad_stream[0:length].astype(jnp.bfloat16)
        out_grad(after)


def first_kernel(
    plan, prev_rows, own_x, own_grad, own_skip, sums, conv_low, out_low, conv_w, out_w,
    low_operands, low_factors, low_gates, grad_stream, grad_skip, *rest,
):
    grad_parts = rest[:-10]
    stream, operands, factors, gates, grad_proj, past_part, total, conv_high, out_high, sems = rest[-10:]
    halo, (length, channels) = plan["halo"], own_x.shape
    layers, low = conv_w.shape[0], low_gates.shape[0]
    copies = {}
    for index in range(low, layers):
        at = 2 * (index - low)
        copies[index] = (
            pltpu.make_async_copy(conv_w.at[index], conv_high.at[index - low], sems.at[at]),
            pltpu.make_async_copy(out_w.at[index], out_high.at[index - low], sems.at[at + 1]),
        )
        for copy in copies[index]:
            copy.start()
    pad = 2 ** (layers - 1)
    extent = length + 2 * halo
    begin = 2 * halo
    stream[0:pad] = jnp.zeros((pad, channels), jnp.float32)
    stream[pad : pad + begin] = prev_rows[0:begin].astype(jnp.float32)
    stream[pad + begin :] = own_x[...].astype(jnp.float32)

    def refs_of(index):
        if index < low:
            return low_operands.at[index], low_factors.at[index], low_gates.at[index]
        return operands.at[index - low], factors.at[index - low], gates.at[index - low]

    def weights_of(index):
        if index < low:
            return conv_low.at[index], out_low.at[index]
        return conv_high.at[index - low], out_high.at[index - low]

    for index in range(layers):
        dilation, start = 2**index, plan["starts"][index]
        operand, factor, gate = refs_of(index)
        conv_layer, out_layer = weights_of(index)
        operand[start:, :channels] = stream[pad + start :].astype(jnp.bfloat16)
        operand[start:, channels:] = stream[pad + start - dilation : pad + extent - dilation].astype(jnp.bfloat16)
        slab = max(dilation, 16)
        earlier = stream[pad + begin - dilation : pad + begin - dilation + slab]
        operand[begin : begin + slab, channels:] = cut_off(earlier, dilation).astype(jnp.bfloat16)
        for copy in copies.get(index, ()):
            copy.wait()
        preact = dot(operand[start:], conv_layer[...], NN)
        filtered = jnp.tanh(preact[:, :channels])
        opening = 0.5 + 0.5 * jnp.tanh(0.5 * preact[:, channels:])
        product = filtered * opening
        gate[start:] = product.astype(jnp.bfloat16)
        factor[start:, :channels] = opening - filtered * product
        factor[start:, channels:] = product * (1.0 - opening)
        if index < layers - 1:
            stream[pad + start :] += dot(gate[start:], out_layer[:, :channels], NN)

    grad_stream[0:halo] = prev_rows[2 * halo : 3 * halo].astype(jnp.float32)
    grad_stream[halo:] = own_grad[...]
    grad_skip[0:halo] = prev_rows[3 * halo :]
    grad_skip[halo:] = own_skip[...]
    grad_proj[:, channels:] = grad_skip[...]
    backward(
        plan, list(reversed(range(low, layers))), refs_of, weights_of,
        grad_proj, grad_stream, past_part, total, grad_parts,
    )
    plan["finish"](sums, grad_parts)


def later_kernel(
    plan, first, third, low_operands, low_factors, low_gates, grad_before, grad_skip, conv_w, out_w, *rest
):
    *outs, keep, send, grad_stream, grad_proj, past_part, total = rest[plan["unused"] :]
    channels = plan["channels"]
    grad_stream[...] = grad_before[...]
    grad_proj[:, channels:] = grad_skip[...]

    def refs_of(index):
        return low_operands.at[index], low_factors.at[index], low_gates.at[index]

    def weights_of(index):
        return conv_w.at[index], out_w.at[index]

    backward(
        plan, list(reversed(range(first, first + third))), refs_of, weights_of,
        grad_proj, grad_stream, past_part, total, (keep, send),
    )
    at = 0
    for out in outs:
        out[...] = grad_stream[at : at + out.shape[0]]
        at += out.shape[0]


def store_whole(items, total, height, item, grad_parts):
    is_out = items[item][1]
    place = sum(kind == is_out for _, kind in items[:item])
    grad_parts[int(is_out)][place] = total[0:height].astype(jnp.bfloat16)


def finish_whole(sums, grad_parts):
    pass


def finish_shards(extra, sums, grad_parts):
    for part in grad_parts:
        lead, rows = part.shape[:-2], part.shape[-2]
        for first in range(rows - extra, rows, 16):
            part[(slice(None),) * len(lead) + (slice(first, first + 16),)] = jnp.broadcast_to(
                sums[...], lead + sums.shape
            )


def store_shards(tm, dp, order, bases, total, height, item, grad_parts):
    keep, send = grad_parts
    t_at, d_at = lax.axis_index("tm"), lax.axis_index("dp")
    core_at = lax.rem(d_at, 2)
    rows = height // tm
    at = pl.ds(bases[item], rows)
    at_bits = bits_of(t_at, d_at, lax.rem, lax.div)
    for y in range(dp // 2):
        near = total[0:height, (2 * y) * LANES : (2 * y + 1) * LANES]
        far = total[0:height, (2 * y + 1) * LANES : (2 * y + 2) * LANES]
        mine = jnp.where(core_at == 0, near, far).astype(jnp.bfloat16)
        other = jnp.where(core_at == 0, far, near).astype(jnp.bfloat16)
        for t in range(tm):
            bits = bits_of(t, 2 * y, lambda a, b: a % b, lambda a, b: a // b)
            lead = tuple(lax.rem(bits[name] + at_bits[name], 2) for name in order)
            keep[lead + (at,)] = mine[t * rows : (t + 1) * rows]
            send[lead + (at,)] = other[t * rows : (t + 1) * rows]


def bits_of(t, d, rem, div):
    return {"x": rem(t, 2), "z0": rem(div(t, 2), 2), "z1": div(t, 4), "y": div(d, 2)}


def bases_of(items, tm, channels):
    ends = [0]
    for _, is_out in items:
        ends.append(ends[-1] + (1 if is_out else 2) * channels // tm)
    return ends[:-1], ends[-1]


def run_layers(in_shards, tm, dp, halo, prev_rows, loaded, conv_w, out_w):
    own_x, own_grad, own_skip, sums, conv_low, out_low = loaded
    length, channels = own_x.shape
    layers, low = conv_w.shape[0], conv_low.shape[0]
    third = layers - low
    extent, border = length + 2 * halo, length + halo
    starts = []
    for index in range(layers):
        need = halo if index == layers - 1 else 2 ** (index + 1)
        starts.append(need // 16 * 16)
    counts = [-(-(length + 2 ** (index + 1) - 1) // 16) * 16 for index in range(layers)]
    plan = {"halo": halo, "starts": starts, "counts": counts, "length": length, "channels": channels, "unused": 0}
    plans, shapes = [], []
    for chunk, order in enumerate(CHAINS):
        items = items_of(layers, chunk)
        bases, rows = bases_of(items, tm, channels)
        if in_shards:
            store = functools.partial(store_shards, tm, dp, order, bases)
            finish = functools.partial(finish_shards, EXTRA[chunk])
            shapes.append(2 * [(2,) * len(order) + (rows + EXTRA[chunk], LANES)])
        else:
            store, finish = functools.partial(store_whole, items), finish_whole
            outs = sum(is_out for _, is_out in items)
            shapes.append([(len(items) - outs,) + conv_w.shape[1:], (outs,) + out_w.shape[1:]])
        plans.append(plan | {"items": items, "store": store, "finish": finish})
    vmem, anywhere = pl.BlockSpec(memory_space=pltpu.VMEM), pl.BlockSpec(memory_space=pl.ANY)
    weight_bytes = 2 * (conv_w.size + out_w.size)
    flops = 2 * length * channels * channels
    *kept, grad_stream, grad_skip, keep, send = pl.pallas_call(
        functools.partial(first_kernel, plans[0]),
        in_specs=[vmem] * 7 + [anywhere] * 2,
        out_specs=[vmem] * 7,
        out_shape=[
            pltpu.VMEM((low, extent, 2 * channels), jnp.bfloat16),
            pltpu.VMEM((low, extent, 2 * channels), jnp.float32),
            pltpu.VMEM((low, extent, channels), jnp.bfloat16),
            pltpu.VMEM((border, channels), jnp.float32),
            pltpu.VMEM((border, channels), jnp.bfloat16),
        ]
        + [pltpu.VMEM(shape, jnp.bfloat16) for shape in shapes[0]],
        scratch_shapes=[
            pltpu.VMEM((2 ** (layers - 1) + extent, channels), jnp.float32),
            pltpu.VMEM((third, extent, 2 * channels), jnp.bfloat16),
            pltpu.VMEM((third, extent, 2 * channels), jnp.float32),
            pltpu.VMEM((third, extent, channels), jnp.bfloat16),
            pltpu.VMEM((border, 2 * channels), jnp.bfloat16),
            pltpu.VMEM((border, channels), jnp.float32),
            pltpu.VMEM((2 * channels, 2 * channels), jnp.float32),
            pltpu.VMEM((third,) + conv_w.shape[1:], jnp.bfloat16),
            pltpu.VMEM((third,) + out_w.shape[1:], jnp.bfloat16),
            pltpu.SemaphoreType.DMA((2 * third,)),
        ],
        compiler_params=pltpu.CompilerParams(vmem_limit_bytes=VMEM_BYTES),
        cost_estimate=cost(flops * (5 * layers + 12 * third), weight_bytes),
        name="forward_and_last_third",
    )(*held((prev_rows, own_x, own_grad, own_skip, sums, conv_low, out_low)), *held((conv_w, out_w), pltpu.HBM))

    def later(step, outs, after):
        return pl.pallas_call(
            functools.partial(later_kernel, plans[step] | {"unused": len(after)}, layers - (step + 1) * third, third),
            in_specs=[vmem] * 7 + [anywhere] * len(after),
            out_specs=[vmem] * (len(outs) + 2),
            out_shape=[pltpu.VMEM((rows, channels), jnp.float32) for rows in outs]
            + [pltpu.VMEM(shape, jnp.bfloat16) for shape in shapes[step]],
            scratch_shapes=[
                pltpu.VMEM((border, channels), jnp.float32),
                pltpu.VMEM((border, 2 * channels), jnp.bfloat16),
                pltpu.VMEM((border, channels), jnp.float32),
                pltpu.VMEM((2 * channels, 2 * channels), jnp.float32),
            ],
            compiler_params=pltpu.CompilerParams(vmem_limit_bytes=VMEM_BYTES),
            cost_estimate=cost(flops * 12 * third, weight_bytes),
            name="middle_third" if step == 1 else "first_third",
        )(*held((*kept, grad_stream, grad_skip, conv_low, out_low, *after)))

    parts = [(keep, send)]
    if in_shards:
        parts[0] = Chunk(tm, dp, 0, keep, send)
    grad_stream, *middle = later(1, [border], [])
    other, own, *last = later(2, [halo, length - halo], [parts[0].next_message()] if in_shards else [])
    parts += [middle, last]
    if in_shards:
        for step in (1, 2):
            parts[step] = Chunk(tm, dp, step, *parts[step])
    return other, own, parts


def add_kernel(count, groups, *refs):
    arrays, outs = refs[:count], refs[-len(groups) :]
    for out, pieces in zip(outs, groups):
        lead = (slice(None),) * (len(out.shape) - 2)
        for first, rows, with_total, terms in pieces:
            body = rows - 16 if with_total else rows
            value = 0.0
            for array, at, begin in terms:
                value = value + arrays[array][at + lead + (slice(begin, begin + body),)].astype(jnp.float32)
            out[lead + (slice(first, first + body),)] = value.astype(out.dtype)
            if with_total:
                total = 0.0
                for array, at, begin in terms:
                    rows_at = slice(begin + body, begin + rows)
                    total = total + joined_rows(arrays[array][at + (0,) * len(lead) + (rows_at,)])
                slab = split_rows(total)
                out[lead + (slice(first + body, first + rows),)] = jnp.broadcast_to(slab, out.shape[:-2] + slab.shape)


def add_up(arrays, groups, shapes, after, name):
    vmem = pl.BlockSpec(memory_space=pltpu.VMEM)
    return pl.pallas_call(
        functools.partial(add_kernel, len(arrays), groups),
        in_specs=[vmem] * len(arrays) + [pl.BlockSpec(memory_space=pl.ANY)] * len(after),
        out_specs=[vmem] * len(groups),
        out_shape=[pltpu.VMEM(shape, jnp.bfloat16) for shape in shapes],
        compiler_params=pltpu.CompilerParams(vmem_limit_bytes=ADD_BYTES),
        name=name,
    )(*held(arrays), *held(after))


def first_block(array, first, rows):
    return array[(0,) * (len(array.shape) - 2) + (slice(first, first + rows),)].astype(jnp.float32)


def first_block(array, first, rows):
    return array[(0,) * (len(array.shape) - 2) + (slice(first, first + rows),)].astype(jnp.float32)


def last_kernel(counts, samples_all, tm, *refs):
    chunks = []
    for count in counts:
        chunks.append(refs[:count])
        refs = refs[count:]
    other, own, grad_inputs, grad_conv, grad_out = refs
    layers, channels = grad_conv.shape[0], own.shape[1]
    total = 0.0
    for term in chunks[0]:
        total = total + jnp.sum(first_block(term, term.shape[-2] - 16, 16), axis=0, keepdims=True)
    scale = samples_all / total
    for chunk, terms in enumerate(chunks):
        items = items_of(layers, chunk)
        for (index, is_out), base in zip(items, bases_of(items, tm, channels)[0]):
            out = grad_out if is_out else grad_conv
            value = 0.0
            for term in terms:
                value = value + first_block(term, base, out.shape[1])
            out[index] = value * scale
    for first in range(0, channels, LANES):
        lanes = slice(first, first + LANES)
        grad_inputs[0 : own.shape[0], lanes] = own[:, lanes] * scale
        grad_inputs[own.shape[0] :, lanes] = other[:, lanes] * scale


class Chunk:
    def __init__(self, tm, dp, chunk, keep, send):
        self.tm, self.dp, self.chunk, self.rows = tm, dp, chunk, keep.shape[-2]
        self.message = None
        self.terms = [keep, swapped(tm, dp, send, "core")]

    def next_message(self, after=()):
        if self.message is None:
            left = len(CHAINS[self.chunk]) + 2 - len(self.terms)
            pieces = []
            for i, v in enumerate(self.terms):
                pieces.append((i, (0,) * (len(v.shape) - 2 - left) + (1,), 0))
            (self.message,) = add_up(
                self.terms, [[(0, self.rows, self.chunk == 0, pieces)]], [(2,) * (left - 1) + (self.rows, LANES)], after,
                "add_chunk%d_step%d" % (self.chunk, len(self.terms) - 1),
            )
        return self.message

    def run_chain(self, after=()):
        for step, name in enumerate(CHAINS[self.chunk]):
            self.terms.append(swapped(self.tm, self.dp, self.next_message(after if step == 1 else ()), name))
            self.message = None
        return self.terms


def swapped(tm, dp, value, name):
    over_t, over_d = {"core": (0, 1), "y": (0, 2), "x": (1, 0), "z0": (2, 0), "z1": (4, 0)}[name]
    pairs = [(t * dp + d, (t ^ over_t) * dp + (d ^ over_d)) for t in range(tm) for d in range(dp)]
    return lax.ppermute(value, ("tm", "dp"), pairs)


def scattered(part):
    columns = lax.psum_scatter(part, "dp", scatter_dimension=2, tiled=True).astype(jnp.float32)
    return lax.psum_scatter(columns, "tm", scatter_dimension=1, tiled=True)


def body(inputs, grad_stream_out, grad_skip_out, sample_weight, conv_weight, out_weight):
    tm, dp = lax.axis_size("tm"), lax.axis_size("dp")
    batch, length, channels = inputs.shape
    layers = conv_weight.shape[0]
    third = layers // len(CHAINS)
    halo = 2**layers
    samples_all = batch * length * tm * dp
    x, gs, gk = inputs[0], grad_stream_out[0], grad_skip_out[0]
    message = pack(halo, x, gs, gk, sample_weight)
    prev_rows = around(message, "tm", 1)
    loaded = load_some(layers - third, x, gs, gk, sample_weight, conv_weight, out_weight, message)
    in_shards = tm == 8 and dp == 4 and channels // tm % 16 == 0 and 2 * channels == dp * LANES
    other, own, parts = run_layers(in_shards, tm, dp, halo, prev_rows, loaded, conv_weight, out_weight)
    other = around(other, "tm", -1)
    if not in_shards:
        scale = samples_all / lax.psum(jnp.sum(sample_weight), ("tm", "dp"))
        found = {}
        for chunk, part in enumerate(parts):
            items = items_of(layers, chunk)
            for is_out in (False, True):
                for place, item in enumerate(item for item in items if item[1] == is_out):
                    found[item] = part[int(is_out)][place]
        grad_conv, grad_out = (
            scattered(jnp.stack([found[index, is_out] for index in range(layers)])) * scale for is_out in (False, True)
        )
        return (jnp.concatenate([own, other]) * scale)[None], grad_conv, grad_out
    chunks = [part.run_chain([other] if part is parts[0] else ()) for part in parts]
    conv_rows, out_rows = 2 * channels // tm, channels // tm
    grad_inputs, grad_conv, grad_out = pl.pallas_call(
        functools.partial(last_kernel, [len(terms) for terms in chunks], float(samples_all), tm),
        out_shape=[
            jax.ShapeDtypeStruct((length, channels), jnp.float32),
            jax.ShapeDtypeStruct((layers, conv_rows, LANES), jnp.float32),
            jax.ShapeDtypeStruct((layers, out_rows, LANES), jnp.float32),
        ],
        compiler_params=pltpu.CompilerParams(vmem_limit_bytes=ADD_BYTES),
        name="scale_all",
    )(*held([term for terms in chunks for term in terms]), *held([other, own]))
    return grad_inputs[None], grad_conv, grad_out


def solution(mesh):
    placed = (
        P("dp", "tm", None),
        P("dp", "tm", None),
        P("dp", "tm", None),
        P("dp", "tm"),
        P(),
        P(),
    )
    return jax.shard_map(
        body,
        mesh=mesh,
        in_specs=placed,
        out_specs=(P("dp", "tm", None), P(None, "tm", "dp"), P(None, "tm", "dp")),
        check_vma=False,
    )
```

```python
import functools

import jax
import jax.numpy as jnp
from jax import lax
from jax.experimental import pallas as pl
from jax.experimental.pallas import tpu as pltpu
from jax.sharding import PartitionSpec as P

LANES = 128
VMEM_BYTES = 24 * 1024 * 1024
ADD_BYTES = 8 * 1024 * 1024
CHAINS = (("x", "y", "z0", "z1"), ("y", "z0", "x", "z1"), ("z0", "x", "y", "z1"))
EXTRA = (16, 0, 0)
NN = (((1,), (0,)), ((), ()))
NT = (((1,), (1,)), ((), ()))
TN = (((0,), (0,)), ((), ()))


def dot(left, right, dims):
    return lax.dot_general(left, right, dims, preferred_element_type=jnp.float32)


def held(arrays, space=pltpu.VMEM):
    return [pltpu.with_memory_space_constraint(x, space) for x in arrays]


def shifted(x, axis, by):
    count = lax.axis_size(axis)
    return lax.ppermute(x, axis, [(i, i + by) for i in range(count) if 0 <= i + by < count])


def is_last():
    return lax.axis_index("tm") == lax.axis_size("tm") - 1


def column(row, rows):
    return jnp.broadcast_to(row, (LANES, rows)).T


def cost(flops, moved):
    return pl.CostEstimate(flops=flops, bytes_accessed=moved, transcendentals=0)


def pack_kernel(tail_x, tail_gs, tail_gk, weight, message):
    halo, channels = tail_gs.shape
    by_row = column(weight[...], LANES)[LANES - halo :]
    by_row = jnp.concatenate([by_row] * (channels // LANES), axis=1)
    message[0 : 2 * halo] = tail_x[...]
    message[2 * halo : 3 * halo] = (tail_gs[...].astype(jnp.float32) * by_row).astype(jnp.bfloat16)
    message[3 * halo :] = (tail_gk[...].astype(jnp.float32) * by_row).astype(jnp.bfloat16)


def pack(halo, x, grad_stream_out, grad_skip_out, weight):
    length, channels = x.shape

    def last(rows):
        return pl.BlockSpec((rows, channels), lambda i: (length // rows - 1, 0))

    return pl.pallas_call(
        pack_kernel,
        grid=(1,),
        in_specs=[last(2 * halo), last(halo), last(halo), pl.BlockSpec((1, LANES), lambda i: (0, length // LANES - 1))],
        out_specs=pl.BlockSpec((4 * halo, channels), lambda i: (0, 0)),
        out_shape=jax.ShapeDtypeStruct((4 * halo, channels), jnp.bfloat16),
        compiler_params=pltpu.CompilerParams(vmem_limit_bytes=ADD_BYTES),
        name="pack_borders",
    )(*held((x, grad_stream_out, grad_skip_out, weight), pltpu.HBM))


def load_kernel(
    x, gs, gk, weight, conv_w, out_w, _, x_here, grad_stream, grad_skip, sums, conv_here, out_here,
    gs_raw, gk_raw, weight_here, sems,
):
    pairs = ((weight, weight_here), (gs, gs_raw), (gk, gk_raw), (x, x_here), (conv_w, conv_here), (out_w, out_here))
    copies = [pltpu.make_async_copy(a, b, sems.at[i]) for i, (a, b) in enumerate(pairs)]
    for copy in copies:
        copy.start()
    for copy in copies[:3]:
        copy.wait()
    length, channels = x_here.shape
    by_row = column(weight_here[...], length)
    by_row = jnp.concatenate([by_row] * (channels // LANES), axis=1)
    grad_stream[...] = gs_raw[...].astype(jnp.float32) * by_row
    grad_skip[...] = (gk_raw[...].astype(jnp.float32) * by_row).astype(jnp.bfloat16)
    own_sum = jnp.broadcast_to(jnp.sum(weight_here[...], axis=1, keepdims=True), (1, LANES))
    sums[...] = split_rows(own_sum)
    for copy in copies[3:]:
        copy.wait()


def load_all(x, gs, gk, weight, conv_w, out_w, after):
    shape = x.shape
    vmem, anywhere = pl.BlockSpec(memory_space=pltpu.VMEM), pl.BlockSpec(memory_space=pl.ANY)
    return pl.pallas_call(
        load_kernel,
        in_specs=[anywhere] * 7,
        out_specs=[vmem] * 6,
        out_shape=[
            pltpu.VMEM(shape, jnp.bfloat16),
            pltpu.VMEM(shape, jnp.float32),
            pltpu.VMEM(shape, jnp.bfloat16),
            pltpu.VMEM((16, LANES), jnp.bfloat16),
            pltpu.VMEM(conv_w.shape, jnp.bfloat16),
            pltpu.VMEM(out_w.shape, jnp.bfloat16),
        ],
        scratch_shapes=[
            pltpu.VMEM(shape, jnp.bfloat16),
            pltpu.VMEM(shape, jnp.bfloat16),
            pltpu.VMEM(weight.shape, jnp.float32),
            pltpu.SemaphoreType.DMA((6,)),
        ],
        compiler_params=pltpu.CompilerParams(vmem_limit_bytes=ADD_BYTES),
        cost_estimate=cost(10**7, 6 * 10**6),
        name="load_all",
    )(*held((x, gs, gk, weight, conv_w, out_w), pltpu.HBM), *held([after]))


def split_rows(total):
    high = total.astype(jnp.bfloat16).astype(jnp.float32)
    middle = (total - high).astype(jnp.bfloat16).astype(jnp.float32)
    low = total - high - middle
    row = lax.broadcasted_iota(jnp.int32, (16, LANES), 0)
    rows = jnp.where(row == 0, high, jnp.where(row == 1, middle, jnp.where(row == 2, low, 0.0)))
    return rows.astype(jnp.bfloat16)


def joined_rows(rows):
    return jnp.sum(rows.astype(jnp.float32), axis=0, keepdims=True)


def items_of(layers, chunk):
    third = layers // len(CHAINS)
    high = layers - chunk * third
    items = []
    for index in reversed(range(high - third, high)):
        items.append((index, False))
        if chunk == 0 or index < high - 1:
            items.append((index, True))
    return items + ([(high - third - 1, True)] if high > third else [])


def backward(plan, layers, refs_of, conv_w, out_w, grad_stream, scratch, grad_parts):
    grad_proj, grad_preact, past_part, conv_total, *out_totals = scratch
    halo, length, channels = plan["halo"], plan["length"], plan["channels"]
    border = length + halo
    items = plan["items"]
    past_part[border:] = jnp.zeros((past_part.shape[0] - border, channels), jnp.float32)
    grad_proj[:, :channels] = grad_stream[...].astype(jnp.bfloat16)

    def add_rows(at, to, index):
        rows = slice(halo + at, halo + to)
        operands, _, gates = refs_of(index)
        yield conv_total, (index, False), operands[rows], grad_preact[at:to]
        if (index - 1, True) in items:
            yield out_totals[0], (index - 1, True), refs_of(index - 1)[2][rows], grad_proj[at:to]

    for index in layers:
        dilation = 2**index
        _, factors, gates = refs_of(index)
        grad_gated = dot(grad_proj[...], out_w[index], NT)
        first = index == layers[0] and (index, True) in items
        if first:
            out_totals[1][...] = dot(gates[halo:border], grad_proj[0:length], TN)

            @pl.when(is_last())
            def _():
                out_totals[1][...] += dot(gates[border:], grad_proj[length:], TN)

            plan["store"](out_totals[1], items.index((index, True)), grad_parts)
        both = factors[halo:]
        grad_preact[...] = jnp.concatenate(
            [grad_gated * both[:, :channels], grad_gated * both[:, channels:]], axis=1
        ).astype(jnp.bfloat16)
        spread = dot(grad_preact[...], conv_w[index], NT)
        past_part[0:border] = spread[:, channels:]
        grad_stream[...] += spread[:, :channels] + past_part[dilation : dilation + border]
        if index:
            grad_proj[:, :channels] = grad_stream[...].astype(jnp.bfloat16)
        for total, _, left, right in add_rows(0, length, index):
            total[...] = dot(left, right, TN)

        @pl.when(is_last())
        def _():
            for total, _, left, right in add_rows(length, border, index):
                total[...] += dot(left, right, TN)

        for total, item, _, _ in add_rows(0, 0, index):
            plan["store"](total, items.index(item), grad_parts)


def first_kernel(
    plan, prev_rows, own_x, own_grad, own_skip, sums, conv_w, out_w,
    low_operands, low_factors, low_gates, grad_stream, grad_skip, *rest,
):
    *grad_parts, stream, operands, factors, gates = rest[: 4 + 2]
    scratch = rest[6:]
    halo, (length, channels) = plan["halo"], own_x.shape
    layers, low = conv_w.shape[0], low_gates.shape[0]
    pad = 2 ** (layers - 1)
    extent = length + 2 * halo
    begin = 2 * halo
    stream[0:pad] = jnp.zeros((pad, channels), jnp.float32)
    stream[pad : pad + begin] = prev_rows[0:begin].astype(jnp.float32)
    stream[pad + begin :] = own_x[...].astype(jnp.float32)

    def refs_of(index):
        if index < low:
            return low_operands.at[index], low_factors.at[index], low_gates.at[index]
        return operands.at[index - low], factors.at[index - low], gates.at[index - low]

    for index in range(layers):
        dilation, start = 2**index, plan["starts"][index]
        operand, factor, gate = refs_of(index)
        operand[start:, :channels] = stream[pad + start :].astype(jnp.bfloat16)
        operand[start:, channels:] = stream[pad + start - dilation : pad + extent - dilation].astype(jnp.bfloat16)
        preact = dot(operand[start:], conv_w[index], NN)
        filtered = jnp.tanh(preact[:, :channels])
        opening = 0.5 + 0.5 * jnp.tanh(0.5 * preact[:, channels:])
        product = filtered * opening
        gate[start:] = product.astype(jnp.bfloat16)
        factor[start:, :channels] = opening - filtered * product
        factor[start:, channels:] = product * (1.0 - opening)
        if index < layers - 1:
            stream[pad + start :] += dot(gate[start:], out_w[index, :, :channels], NN)

    grad_stream[0:halo] = prev_rows[2 * halo : 3 * halo].astype(jnp.float32)
    grad_stream[halo:] = own_grad[...]
    grad_skip[0:halo] = prev_rows[3 * halo :]
    grad_skip[halo:] = own_skip[...]
    scratch[0][:, channels:] = grad_skip[...]
    backward(plan, list(reversed(range(low, layers))), refs_of, conv_w, out_w, grad_stream, scratch, grad_parts)
    plan["finish"](sums, grad_parts)


def later_kernel(
    plan, first, third, low_operands, low_factors, low_gates, grad_before, grad_skip, conv_w, out_w, *rest
):
    outs = rest[plan["unused"] : plan["unused"] + plan["outs"]]
    keep, send, grad_stream, *scratch = rest[plan["unused"] + plan["outs"] :]
    grad_stream[...] = grad_before[...]
    scratch[0][:, plan["channels"] :] = grad_skip[...]

    def refs_of(index):
        return low_operands.at[index], low_factors.at[index], low_gates.at[index]

    layers = list(reversed(range(first, first + third)))
    backward(plan, layers, refs_of, conv_w, out_w, grad_stream, scratch, (keep, send))
    at = 0
    for out in outs:
        out[...] = grad_stream[at : at + out.shape[0]]
        at += out.shape[0]


def store_whole(items, total, item, grad_parts):
    is_out = items[item][1]
    place = sum(kind == is_out for _, kind in items[:item])
    grad_parts[int(is_out)][place] = total[...].astype(jnp.bfloat16)


def finish_whole(sums, grad_parts):
    pass


def finish_shards(extra, sums, grad_parts):
    for part in grad_parts:
        lead, rows = part.shape[:-2], part.shape[-2]
        for first in range(rows - extra, rows, 16):
            part[(slice(None),) * len(lead) + (slice(first, first + 16),)] = jnp.broadcast_to(
                sums[...], lead + sums.shape
            )


def store_shards(tm, dp, order, bases, total, item, grad_parts):
    keep, send = grad_parts
    t_at, d_at = lax.axis_index("tm"), lax.axis_index("dp")
    core_at = lax.rem(d_at, 2)
    rows = total.shape[0] // tm
    at = pl.ds(bases[item], rows)
    at_bits = bits_of(t_at, d_at, lax.rem, lax.div)
    for y in range(dp // 2):
        near = total[:, (2 * y) * LANES : (2 * y + 1) * LANES]
        far = total[:, (2 * y + 1) * LANES : (2 * y + 2) * LANES]
        mine = jnp.where(core_at == 0, near, far).astype(jnp.bfloat16)
        other = jnp.where(core_at == 0, far, near).astype(jnp.bfloat16)
        for t in range(tm):
            bits = bits_of(t, 2 * y, lambda a, b: a % b, lambda a, b: a // b)
            lead = tuple(lax.rem(bits[name] + at_bits[name], 2) for name in order)
            keep[lead + (at,)] = mine[t * rows : (t + 1) * rows]
            send[lead + (at,)] = other[t * rows : (t + 1) * rows]


def bits_of(t, d, rem, div):
    return {"x": rem(t, 2), "z0": rem(div(t, 2), 2), "z1": div(t, 4), "y": div(d, 2)}


def bases_of(items, tm, channels):
    ends = [0]
    for _, is_out in items:
        ends.append(ends[-1] + (1 if is_out else 2) * channels // tm)
    return ends[:-1], ends[-1]


def run_layers(in_shards, tm, dp, halo, prev_rows, loaded):
    own_x, own_grad, own_skip, sums, conv_w, out_w = loaded
    length, channels = own_x.shape
    layers = conv_w.shape[0]
    third = layers // len(CHAINS)
    low = layers - third
    extent, border = length + 2 * halo, length + halo
    starts = []
    for index in range(layers):
        need = halo if index == layers - 1 else 2 ** (index + 1)
        starts.append(need // 16 * 16)
    plan = {"halo": halo, "starts": starts, "length": length, "channels": channels}
    plans, shapes = [], []
    for chunk, order in enumerate(CHAINS):
        items = items_of(layers, chunk)
        bases, rows = bases_of(items, tm, channels)
        if in_shards:
            store = functools.partial(store_shards, tm, dp, order, bases)
            finish = functools.partial(finish_shards, EXTRA[chunk])
            shapes.append(2 * [(2,) * len(order) + (rows + EXTRA[chunk], LANES)])
        else:
            store, finish = functools.partial(store_whole, items), finish_whole
            outs = sum(is_out for _, is_out in items)
            shapes.append([(len(items) - outs,) + conv_w.shape[1:], (outs,) + out_w.shape[1:]])
        plans.append(plan | {"items": items, "store": store, "finish": finish})
    vmem, anywhere = pl.BlockSpec(memory_space=pltpu.VMEM), pl.BlockSpec(memory_space=pl.ANY)
    weight_bytes = 2 * (conv_w.size + out_w.size)
    flops = 2 * length * channels * channels
    scratch = [
        pltpu.VMEM((border, 2 * channels), jnp.bfloat16),
        pltpu.VMEM((border, 2 * channels), jnp.bfloat16),
        pltpu.VMEM((border + 2 ** (layers - 1), channels), jnp.float32),
        pltpu.VMEM((2 * channels, 2 * channels), jnp.float32),
        pltpu.VMEM((channels, 2 * channels), jnp.float32),
        pltpu.VMEM((channels, 2 * channels), jnp.float32),
    ]
    *kept, grad_stream, grad_skip, keep, send = pl.pallas_call(
        functools.partial(first_kernel, plans[0]),
        in_specs=[vmem] * 7,
        out_specs=[vmem] * 7,
        out_shape=[
            pltpu.VMEM((low, extent, 2 * channels), jnp.bfloat16),
            pltpu.VMEM((low, extent, 2 * channels), jnp.float32),
            pltpu.VMEM((low, extent, channels), jnp.bfloat16),
            pltpu.VMEM((border, channels), jnp.float32),
            pltpu.VMEM((border, channels), jnp.bfloat16),
        ]
        + [pltpu.VMEM(shape, jnp.bfloat16) for shape in shapes[0]],
        scratch_shapes=[
            pltpu.VMEM((2 ** (layers - 1) + extent, channels), jnp.float32),
            pltpu.VMEM((third, extent, 2 * channels), jnp.bfloat16),
            pltpu.VMEM((third, extent, 2 * channels), jnp.float32),
            pltpu.VMEM((third, extent, channels), jnp.bfloat16),
        ]
        + scratch,
        compiler_params=pltpu.CompilerParams(vmem_limit_bytes=VMEM_BYTES),
        cost_estimate=cost(flops * (5 * layers + 12 * third), weight_bytes),
        name="forward_and_last_third",
    )(*held((prev_rows, *loaded)))

    def later(step, outs, after):
        more = {"unused": len(after), "outs": len(outs)}
        return pl.pallas_call(
            functools.partial(later_kernel, plans[step] | more, layers - (step + 1) * third, third),
            in_specs=[vmem] * 7 + [anywhere] * len(after),
            out_specs=[vmem] * (len(outs) + 2),
            out_shape=[pltpu.VMEM((rows, channels), jnp.float32) for rows in outs]
            + [pltpu.VMEM(shape, jnp.bfloat16) for shape in shapes[step]],
            scratch_shapes=[pltpu.VMEM((border, channels), jnp.float32)] + scratch,
            compiler_params=pltpu.CompilerParams(vmem_limit_bytes=VMEM_BYTES),
            cost_estimate=cost(flops * 12 * third, weight_bytes),
            name="middle_third" if step == 1 else "first_third",
        )(*held((*kept, grad_stream, grad_skip, conv_w, out_w, *after)))

    parts = [(keep, send)]
    if in_shards:
        parts[0] = Chunk(tm, dp, 0, keep, send)
    grad_stream, *middle = later(1, [border], [])
    other, own, tail, *last = later(2, [halo, length - halo, halo], [parts[0].next_message()] if in_shards else [])
    parts += [middle, last]
    if in_shards:
        for step in (1, 2):
            parts[step] = Chunk(tm, dp, step, *parts[step])
    return other, own, tail, parts


def add_kernel(count, groups, *refs):
    arrays, outs = refs[:count], refs[-len(groups) :]
    for out, pieces in zip(outs, groups):
        lead = (slice(None),) * (len(out.shape) - 2)
        for first, rows, with_total, terms in pieces:
            body = rows - 16 if with_total else rows
            value = 0.0
            for array, at, begin in terms:
                value = value + arrays[array][at + lead + (slice(begin, begin + body),)].astype(jnp.float32)
            out[lead + (slice(first, first + body),)] = value.astype(out.dtype)
            if with_total:
                total = 0.0
                for array, at, begin in terms:
                    rows_at = slice(begin + body, begin + rows)
                    total = total + joined_rows(arrays[array][at + (0,) * len(lead) + (rows_at,)])
                slab = split_rows(total)
                out[lead + (slice(first + body, first + rows),)] = jnp.broadcast_to(slab, out.shape[:-2] + slab.shape)


def add_up(arrays, groups, shapes, after, name):
    vmem = pl.BlockSpec(memory_space=pltpu.VMEM)
    return pl.pallas_call(
        functools.partial(add_kernel, len(arrays), groups),
        in_specs=[vmem] * len(arrays) + [pl.BlockSpec(memory_space=pl.ANY)] * len(after),
        out_specs=[vmem] * len(groups),
        out_shape=[pltpu.VMEM(shape, jnp.bfloat16) for shape in shapes],
        compiler_params=pltpu.CompilerParams(vmem_limit_bytes=ADD_BYTES),
        name=name,
    )(*held(arrays), *held(after))


def first_block(array, first, rows):
    return array[(0,) * (len(array.shape) - 2) + (slice(first, first + rows),)].astype(jnp.float32)


def first_block(array, first, rows):
    return array[(0,) * (len(array.shape) - 2) + (slice(first, first + rows),)].astype(jnp.float32)


def last_kernel(counts, samples_all, tm, *refs):
    chunks = []
    for count in counts:
        chunks.append(refs[:count])
        refs = refs[count:]
    other, own, tail, grad_inputs, grad_conv, grad_out = refs
    layers, channels = grad_conv.shape[0], own.shape[1]
    total = 0.0
    for term in chunks[0]:
        total = total + jnp.sum(first_block(term, term.shape[-2] - 16, 16), axis=0, keepdims=True)
    scale = samples_all / total
    for chunk, terms in enumerate(chunks):
        items = items_of(layers, chunk)
        for (index, is_out), base in zip(items, bases_of(items, tm, channels)[0]):
            out = grad_out if is_out else grad_conv
            value = 0.0
            for term in terms:
                value = value + first_block(term, base, out.shape[1])
            out[index] = value * scale
    for first in range(0, channels, LANES):
        lanes = slice(first, first + LANES)
        grad_inputs[0 : own.shape[0], lanes] = own[:, lanes] * scale
        grad_inputs[own.shape[0] :, lanes] = jnp.where(is_last(), tail[:, lanes], other[:, lanes]) * scale


class Chunk:
    def __init__(self, tm, dp, chunk, keep, send):
        self.tm, self.dp, self.chunk, self.rows = tm, dp, chunk, keep.shape[-2]
        self.message = None
        self.terms = [keep, swapped(tm, dp, send, "core")]

    def next_message(self, after=()):
        if self.message is None:
            left = len(CHAINS[self.chunk]) + 2 - len(self.terms)
            pieces = []
            for i, v in enumerate(self.terms):
                pieces.append((i, (0,) * (len(v.shape) - 2 - left) + (1,), 0))
            (self.message,) = add_up(
                self.terms, [[(0, self.rows, self.chunk == 0, pieces)]], [(2,) * (left - 1) + (self.rows, LANES)], after,
                "add_chunk%d_step%d" % (self.chunk, len(self.terms) - 1),
            )
        return self.message

    def run_chain(self, after=()):
        for step, name in enumerate(CHAINS[self.chunk]):
            self.terms.append(swapped(self.tm, self.dp, self.next_message(after if step == 1 else ()), name))
            self.message = None
        return self.terms


def swapped(tm, dp, value, name):
    over_t, over_d = {"core": (0, 1), "y": (0, 2), "x": (1, 0), "z0": (2, 0), "z1": (4, 0)}[name]
    pairs = [(t * dp + d, (t ^ over_t) * dp + (d ^ over_d)) for t in range(tm) for d in range(dp)]
    return lax.ppermute(value, ("tm", "dp"), pairs)


def scattered(part):
    columns = lax.psum_scatter(part, "dp", scatter_dimension=2, tiled=True).astype(jnp.float32)
    return lax.psum_scatter(columns, "tm", scatter_dimension=1, tiled=True)


def body(inputs, grad_stream_out, grad_skip_out, sample_weight, conv_weight, out_weight):
    tm, dp = lax.axis_size("tm"), lax.axis_size("dp")
    batch, length, channels = inputs.shape
    layers = conv_weight.shape[0]
    third = layers // len(CHAINS)
    halo = 2**layers
    samples_all = batch * length * tm * dp
    x, gs, gk = inputs[0], grad_stream_out[0], grad_skip_out[0]
    message = pack(halo, x, gs, gk, sample_weight)
    prev_rows = shifted(message, "tm", 1)
    loaded = load_all(x, gs, gk, sample_weight, conv_weight, out_weight, message)
    in_shards = tm == 8 and dp == 4 and channels // tm % 16 == 0 and 2 * channels == dp * LANES
    other, own, tail, parts = run_layers(in_shards, tm, dp, halo, prev_rows, loaded)
    other = shifted(other, "tm", -1)
    if not in_shards:
        scale = samples_all / lax.psum(jnp.sum(sample_weight), ("tm", "dp"))
        found = {}
        for chunk, part in enumerate(parts):
            items = items_of(layers, chunk)
            for is_out in (False, True):
                for place, item in enumerate(item for item in items if item[1] == is_out):
                    found[item] = part[int(is_out)][place]
        grad_conv, grad_out = (
            scattered(jnp.stack([found[index, is_out] for index in range(layers)])) * scale for is_out in (False, True)
        )
        ends = jnp.where(is_last(), tail, other)
        return (jnp.concatenate([own, ends]) * scale)[None], grad_conv, grad_out
    chunks = [part.run_chain([other] if part is parts[0] else ()) for part in parts]
    conv_rows, out_rows = 2 * channels // tm, channels // tm
    grad_inputs, grad_conv, grad_out = pl.pallas_call(
        functools.partial(last_kernel, [len(terms) for terms in chunks], float(samples_all), tm),
        out_shape=[
            jax.ShapeDtypeStruct((length, channels), jnp.float32),
            jax.ShapeDtypeStruct((layers, conv_rows, LANES), jnp.float32),
            jax.ShapeDtypeStruct((layers, out_rows, LANES), jnp.float32),
        ],
        compiler_params=pltpu.CompilerParams(vmem_limit_bytes=ADD_BYTES),
        name="scale_all",
    )(*held([term for terms in chunks for term in terms]), *held([other, own, tail]))
    return grad_inputs[None], grad_conv, grad_out


def solution(mesh):
    placed = (
        P("dp", "tm", None),
        P("dp", "tm", None),
        P("dp", "tm", None),
        P("dp", "tm"),
        P(),
        P(),
    )
    return jax.shard_map(
        body,
        mesh=mesh,
        in_specs=placed,
        out_specs=(P("dp", "tm", None), P(None, "tm", "dp"), P(None, "tm", "dp")),
        check_vma=False,
    )
```

```python
import functools

import jax
import jax.numpy as jnp
from jax import lax
from jax.experimental import pallas as pl
from jax.experimental.pallas import tpu as pltpu
from jax.sharding import PartitionSpec as P

LANES = 128
VMEM_BYTES = 24 * 1024 * 1024
ADD_BYTES = 8 * 1024 * 1024
CHAINS = (("x", "y", "z0", "z1"), ("y", "z0", "x", "z1"), ("z0", "x", "y", "z1"))
EXTRA = (16, 0, 0)
NN = (((1,), (0,)), ((), ()))
NT = (((1,), (1,)), ((), ()))
TN = (((0,), (0,)), ((), ()))


def dot(left, right, dims):
    return lax.dot_general(left, right, dims, preferred_element_type=jnp.float32)


def held(arrays, space=pltpu.VMEM):
    return [pltpu.with_memory_space_constraint(x, space) for x in arrays]


def neighbours_swapped(x, axis, even_first):
    count = lax.axis_size(axis)
    pairs = []
    for i in range(count):
        j = i + 1 if i % 2 == (0 if even_first else 1) else i - 1
        pairs.append((i, j if 0 <= j < count else i))
    return lax.ppermute(x, axis, pairs)


def column(row, rows):
    return jnp.broadcast_to(row, (LANES, rows)).T


def cost(flops, moved):
    return pl.CostEstimate(flops=flops, bytes_accessed=moved, transcendentals=0)


def pack_kernel(head_x, tail_x, head_gs, head_gk, weight, message_a, message_b):
    halo, channels = head_x.shape
    by_row = column(weight[...], LANES)[:halo]
    by_row = jnp.concatenate([by_row] * (channels // LANES), axis=1)
    for_prev = jnp.concatenate([
        head_x[...],
        (head_gs[...].astype(jnp.float32) * by_row).astype(jnp.bfloat16),
        (head_gk[...].astype(jnp.float32) * by_row).astype(jnp.bfloat16),
    ])
    for_next = jnp.concatenate([tail_x[...], jnp.zeros((2 * halo, channels), jnp.bfloat16)])
    odd = lax.rem(lax.axis_index("tm"), 2) == 1
    message_a[...] = jnp.where(odd, for_prev, for_next)
    message_b[...] = jnp.where(odd, for_next, for_prev)


def pack(halo, x, grad_stream_out, grad_skip_out, weight):
    length, channels = x.shape
    first = pl.BlockSpec((halo, channels), lambda i: (0, 0))
    last = pl.BlockSpec((halo, channels), lambda i: (length // halo - 1, 0))
    message = jax.ShapeDtypeStruct((3 * halo, channels), jnp.bfloat16)
    return pl.pallas_call(
        pack_kernel,
        grid=(1,),
        in_specs=[first, last, first, first, pl.BlockSpec((1, LANES), lambda i: (0, 0))],
        out_specs=[pl.BlockSpec(message.shape, lambda i: (0, 0))] * 2,
        out_shape=[message] * 2,
        compiler_params=pltpu.CompilerParams(vmem_limit_bytes=ADD_BYTES),
        name="pack_borders",
    )(*held((x, x, grad_stream_out, grad_skip_out, weight), pltpu.HBM))


def load_kernel(
    x, gs, gk, weight, conv_w, out_w, _, x_here, grad_stream, grad_skip, sums, conv_here, out_here,
    gs_raw, gk_raw, weight_here, sems,
):
    pairs = ((weight, weight_here), (gs, gs_raw), (gk, gk_raw), (x, x_here), (conv_w, conv_here), (out_w, out_here))
    copies = [pltpu.make_async_copy(a, b, sems.at[i]) for i, (a, b) in enumerate(pairs)]
    for copy in copies:
        copy.start()
    for copy in copies[:3]:
        copy.wait()
    length, channels = x_here.shape
    by_row = column(weight_here[...], length)
    by_row = jnp.concatenate([by_row] * (channels // LANES), axis=1)
    grad_stream[...] = gs_raw[...].astype(jnp.float32) * by_row
    grad_skip[...] = (gk_raw[...].astype(jnp.float32) * by_row).astype(jnp.bfloat16)
    own_sum = jnp.broadcast_to(jnp.sum(weight_here[...], axis=1, keepdims=True), (1, LANES))
    sums[...] = split_rows(own_sum)
    for copy in copies[3:]:
        copy.wait()


def load_all(x, gs, gk, weight, conv_w, out_w, after):
    shape = x.shape
    vmem, anywhere = pl.BlockSpec(memory_space=pltpu.VMEM), pl.BlockSpec(memory_space=pl.ANY)
    return pl.pallas_call(
        load_kernel,
        in_specs=[anywhere] * 7,
        out_specs=[vmem] * 6,
        out_shape=[
            pltpu.VMEM(shape, jnp.bfloat16),
            pltpu.VMEM(shape, jnp.float32),
            pltpu.VMEM(shape, jnp.bfloat16),
            pltpu.VMEM((16, LANES), jnp.bfloat16),
            pltpu.VMEM(conv_w.shape, jnp.bfloat16),
            pltpu.VMEM(out_w.shape, jnp.bfloat16),
        ],
        scratch_shapes=[
            pltpu.VMEM(shape, jnp.bfloat16),
            pltpu.VMEM(shape, jnp.bfloat16),
            pltpu.VMEM(weight.shape, jnp.float32),
            pltpu.SemaphoreType.DMA((6,)),
        ],
        compiler_params=pltpu.CompilerParams(vmem_limit_bytes=ADD_BYTES),
        cost_estimate=cost(10**7, 6 * 10**6),
        name="load_all",
    )(*held((x, gs, gk, weight, conv_w, out_w), pltpu.HBM), *held([after]))


def split_rows(total):
    high = total.astype(jnp.bfloat16).astype(jnp.float32)
    middle = (total - high).astype(jnp.bfloat16).astype(jnp.float32)
    low = total - high - middle
    row = lax.broadcasted_iota(jnp.int32, (16, LANES), 0)
    rows = jnp.where(row == 0, high, jnp.where(row == 1, middle, jnp.where(row == 2, low, 0.0)))
    return rows.astype(jnp.bfloat16)


def joined_rows(rows):
    return jnp.sum(rows.astype(jnp.float32), axis=0, keepdims=True)


def items_of(layers, chunk):
    third = layers // len(CHAINS)
    high = layers - chunk * third
    items = []
    for index in reversed(range(high - third, high)):
        items.append((index, False))
        if chunk == 0 or index < high - 1:
            items.append((index, True))
    return items + ([(high - third - 1, True)] if high > third else [])


def backward(plan, layers, refs_of, conv_w, out_w, grad_stream, scratch, grad_parts):
    grad_proj, past_part, total = scratch
    halo, length, channels = plan["halo"], plan["length"], plan["channels"]
    own = slice(halo, halo + length)
    items = plan["items"]

    def out_grad(index):
        if (index, True) in items:
            total[0:channels] = dot(refs_of(index)[2][own], grad_proj[0:length], TN)
            plan["store"](total, items.index((index, True)), grad_parts)

    for index in layers:
        dilation, count = 2**index, plan["counts"][index]
        operands, factors, _ = refs_of(index)
        grad_proj[0:count, :channels] = grad_stream[0:count].astype(jnp.bfloat16)
        grad_gated = dot(grad_proj[0:count], out_w[index], NT)
        out_grad(index)
        both = factors[halo : halo + count]
        grad_preact = jnp.concatenate(
            [grad_gated * both[:, :channels], grad_gated * both[:, channels:]], axis=1
        ).astype(jnp.bfloat16)
        spread = dot(grad_preact, conv_w[index], NT)
        past_part[0:count] = spread[:, channels:]
        rows = plan["counts"][index - 1] if index else length
        grad_stream[0:rows] += spread[0:rows, :channels] + past_part[dilation : dilation + rows]
        total[...] = dot(operands[own], grad_preact[0:length], TN)
        plan["store"](total, items.index((index, False)), grad_parts)
    after = layers[-1] - 1
    if (after, True) in items:
        grad_proj[0:length, :channels] = grad_stream[0:length].astype(jnp.bfloat16)
        out_grad(after)


def first_kernel(
    plan, message_a, message_b, own_x, own_grad, own_skip, sums, conv_w, out_w,
    low_operands, low_factors, low_gates, grad_stream, grad_skip, *rest,
):
    *grad_parts, stream, operands, factors, gates = rest[:6]
    scratch = rest[6:]
    halo, (length, channels) = plan["halo"], own_x.shape
    layers, low = conv_w.shape[0], low_gates.shape[0]
    pad = 2 ** (layers - 1)
    extent = length + 2 * halo
    at = lax.axis_index("tm")
    odd, is_first, is_last = lax.rem(at, 2) == 1, at == 0, at == lax.axis_size("tm") - 1

    def from_prev(rows):
        chosen = jnp.where(odd, message_a[rows], message_b[rows])
        return jnp.where(is_first, jnp.zeros_like(chosen), chosen)

    def from_next(rows):
        chosen = jnp.where(odd, message_b[rows], message_a[rows])
        return jnp.where(is_last, jnp.zeros_like(chosen), chosen)

    stream[0:pad] = jnp.zeros((pad, channels), jnp.float32)
    stream[pad : pad + halo] = from_prev(slice(0, halo)).astype(jnp.float32)
    stream[pad + halo : pad + halo + length] = own_x[...].astype(jnp.float32)
    stream[pad + halo + length :] = from_next(slice(0, halo)).astype(jnp.float32)

    def refs_of(index):
        if index < low:
            return low_operands.at[index], low_factors.at[index], low_gates.at[index]
        return operands.at[index - low], factors.at[index - low], gates.at[index - low]

    for index in range(layers):
        dilation, start = 2**index, plan["starts"][index]
        operand, factor, gate = refs_of(index)
        operand[start:, :channels] = stream[pad + start :].astype(jnp.bfloat16)
        operand[start:, channels:] = stream[pad + start - dilation : pad + extent - dilation].astype(jnp.bfloat16)
        preact = dot(operand[start:], conv_w[index], NN)
        filtered = jnp.tanh(preact[:, :channels])
        opening = 0.5 + 0.5 * jnp.tanh(0.5 * preact[:, channels:])
        product = filtered * opening
        gate[start:] = product.astype(jnp.bfloat16)
        factor[start:, :channels] = opening - filtered * product
        factor[start:, channels:] = product * (1.0 - opening)
        if index < layers - 1:
            stream[pad + start :] += dot(gate[start:], out_w[index, :, :channels], NN)

    grad_stream[0:length] = own_grad[...]
    grad_stream[length:] = from_next(slice(halo, 2 * halo)).astype(jnp.float32)
    grad_skip[0:length] = own_skip[...]
    grad_skip[length:] = from_next(slice(2 * halo, 3 * halo))
    scratch[0][:, channels:] = grad_skip[...]
    backward(plan, list(reversed(range(low, layers))), refs_of, conv_w, out_w, grad_stream, scratch, grad_parts)
    plan["finish"](sums, grad_parts)


def later_kernel(
    plan, first, third, low_operands, low_factors, low_gates, grad_before, grad_skip, conv_w, out_w, *rest
):
    grad_after, keep, send, grad_stream, *scratch = rest[plan["unused"] :]
    grad_stream[...] = grad_before[...]
    scratch[0][:, plan["channels"] :] = grad_skip[...]

    def refs_of(index):
        return low_operands.at[index], low_factors.at[index], low_gates.at[index]

    layers = list(reversed(range(first, first + third)))
    backward(plan, layers, refs_of, conv_w, out_w, grad_stream, scratch, (keep, send))
    grad_after[...] = grad_stream[0 : grad_after.shape[0]]


def store_whole(items, total, item, grad_parts):
    is_out = items[item][1]
    place = sum(kind == is_out for _, kind in items[:item])
    part = grad_parts[int(is_out)]
    part[place] = total[0 : part.shape[1]].astype(jnp.bfloat16)


def finish_whole(sums, grad_parts):
    pass


def finish_shards(extra, sums, grad_parts):
    for part in grad_parts:
        lead, rows = part.shape[:-2], part.shape[-2]
        for first in range(rows - extra, rows, 16):
            part[(slice(None),) * len(lead) + (slice(first, first + 16),)] = jnp.broadcast_to(
                sums[...], lead + sums.shape
            )


def store_shards(tm, dp, order, items, bases, total, item, grad_parts):
    keep, send = grad_parts
    t_at, d_at = lax.axis_index("tm"), lax.axis_index("dp")
    core_at = lax.rem(d_at, 2)
    height = total.shape[0] // (2 if items[item][1] else 1)
    rows = height // tm
    at = pl.ds(bases[item], rows)
    at_bits = bits_of(t_at, d_at, lax.rem, lax.div)
    for y in range(dp // 2):
        near = total[0:height, (2 * y) * LANES : (2 * y + 1) * LANES]
        far = total[0:height, (2 * y + 1) * LANES : (2 * y + 2) * LANES]
        mine = jnp.where(core_at == 0, near, far).astype(jnp.bfloat16)
        other = jnp.where(core_at == 0, far, near).astype(jnp.bfloat16)
        for t in range(tm):
            bits = bits_of(t, 2 * y, lambda a, b: a % b, lambda a, b: a // b)
            lead = tuple(lax.rem(bits[name] + at_bits[name], 2) for name in order)
            keep[lead + (at,)] = mine[t * rows : (t + 1) * rows]
            send[lead + (at,)] = other[t * rows : (t + 1) * rows]


def bits_of(t, d, rem, div):
    return {"x": rem(t, 2), "z0": rem(div(t, 2), 2), "z1": div(t, 4), "y": div(d, 2)}


def bases_of(items, tm, channels):
    ends = [0]
    for _, is_out in items:
        ends.append(ends[-1] + (1 if is_out else 2) * channels // tm)
    return ends[:-1], ends[-1]


def run_layers(in_shards, tm, dp, halo, messages, loaded):
    own_x, own_grad, own_skip, sums, conv_w, out_w = loaded
    length, channels = own_x.shape
    layers = conv_w.shape[0]
    third = layers // len(CHAINS)
    low = layers - third
    extent, border = length + 2 * halo, length + halo
    starts = []
    for index in range(layers):
        need = halo if index == layers - 1 else 2 ** (index + 1)
        starts.append(need // 16 * 16)
    counts = [-(-(length + 2 ** (index + 1) - 1) // 16) * 16 for index in range(layers)]
    plan = {"halo": halo, "starts": starts, "counts": counts, "length": length, "channels": channels}
    plans, shapes = [], []
    for chunk, order in enumerate(CHAINS):
        items = items_of(layers, chunk)
        bases, rows = bases_of(items, tm, channels)
        if in_shards:
            store = functools.partial(store_shards, tm, dp, order, items, bases)
            finish = functools.partial(finish_shards, EXTRA[chunk])
            shapes.append(2 * [(2,) * len(order) + (rows + EXTRA[chunk], LANES)])
        else:
            store, finish = functools.partial(store_whole, items), finish_whole
            outs = sum(is_out for _, is_out in items)
            shapes.append([(len(items) - outs,) + conv_w.shape[1:], (outs,) + out_w.shape[1:]])
        plans.append(plan | {"items": items, "store": store, "finish": finish})
    vmem, anywhere = pl.BlockSpec(memory_space=pltpu.VMEM), pl.BlockSpec(memory_space=pl.ANY)
    weight_bytes = 2 * (conv_w.size + out_w.size)
    flops = 2 * length * channels * channels
    scratch = [
        pltpu.VMEM((border, 2 * channels), jnp.bfloat16),
        pltpu.VMEM((border, channels), jnp.float32),
        pltpu.VMEM((2 * channels, 2 * channels), jnp.float32),
    ]
    *kept, grad_stream, grad_skip, keep, send = pl.pallas_call(
        functools.partial(first_kernel, plans[0]),
        in_specs=[vmem] * 8,
        out_specs=[vmem] * 7,
        out_shape=[
            pltpu.VMEM((low, extent, 2 * channels), jnp.bfloat16),
            pltpu.VMEM((low, extent, 2 * channels), jnp.float32),
            pltpu.VMEM((low, extent, channels), jnp.bfloat16),
            pltpu.VMEM((border, channels), jnp.float32),
            pltpu.VMEM((border, channels), jnp.bfloat16),
        ]
        + [pltpu.VMEM(shape, jnp.bfloat16) for shape in shapes[0]],
        scratch_shapes=[
            pltpu.VMEM((2 ** (layers - 1) + extent, channels), jnp.float32),
            pltpu.VMEM((third, extent, 2 * channels), jnp.bfloat16),
            pltpu.VMEM((third, extent, 2 * channels), jnp.float32),
            pltpu.VMEM((third, extent, channels), jnp.bfloat16),
        ]
        + scratch,
        compiler_params=pltpu.CompilerParams(vmem_limit_bytes=VMEM_BYTES),
        cost_estimate=cost(flops * (5 * layers + 12 * third), weight_bytes),
        name="forward_and_last_third",
    )(*held((*messages, *loaded)))

    def later(step, rows, after):
        more = {"unused": len(after)}
        return pl.pallas_call(
            functools.partial(later_kernel, plans[step] | more, layers - (step + 1) * third, third),
            in_specs=[vmem] * 7 + [anywhere] * len(after),
            out_specs=[vmem] * 3,
            out_shape=[pltpu.VMEM((rows, channels), jnp.float32)]
            + [pltpu.VMEM(shape, jnp.bfloat16) for shape in shapes[step]],
            scratch_shapes=[pltpu.VMEM((border, channels), jnp.float32)] + scratch,
            compiler_params=pltpu.CompilerParams(vmem_limit_bytes=VMEM_BYTES),
            cost_estimate=cost(flops * 12 * third, weight_bytes),
            name="middle_third" if step == 1 else "first_third",
        )(*held((*kept, grad_stream, grad_skip, conv_w, out_w, *after)))

    parts = [(keep, send)]
    if in_shards:
        parts[0] = Chunk(tm, dp, 0, keep, send)
    grad_stream, *middle = later(1, border, [])
    grad_in, *last = later(2, length, [parts[0].next_message()] if in_shards else [])
    parts += [middle, last]
    if in_shards:
        for step in (1, 2):
            parts[step] = Chunk(tm, dp, step, *parts[step])
    return grad_in, parts


def add_kernel(count, groups, *refs):
    arrays, outs = refs[:count], refs[-len(groups) :]
    for out, pieces in zip(outs, groups):
        lead = (slice(None),) * (len(out.shape) - 2)
        for first, rows, with_total, terms in pieces:
            body = rows - 16 if with_total else rows
            value = 0.0
            for array, at, begin in terms:
                value = value + arrays[array][at + lead + (slice(begin, begin + body),)].astype(jnp.float32)
            out[lead + (slice(first, first + body),)] = value.astype(out.dtype)
            if with_total:
                total = 0.0
                for array, at, begin in terms:
                    rows_at = slice(begin + body, begin + rows)
                    total = total + joined_rows(arrays[array][at + (0,) * len(lead) + (rows_at,)])
                slab = split_rows(total)
                out[lead + (slice(first + body, first + rows),)] = jnp.broadcast_to(slab, out.shape[:-2] + slab.shape)


def add_up(arrays, groups, shapes, name):
    vmem = pl.BlockSpec(memory_space=pltpu.VMEM)
    return pl.pallas_call(
        functools.partial(add_kernel, len(arrays), groups),
        in_specs=[vmem] * len(arrays),
        out_specs=[vmem] * len(groups),
        out_shape=[pltpu.VMEM(shape, jnp.bfloat16) for shape in shapes],
        compiler_params=pltpu.CompilerParams(vmem_limit_bytes=ADD_BYTES),
        name=name,
    )(*held(arrays))


def first_block(array, first, rows):
    return array[(0,) * (len(array.shape) - 2) + (slice(first, first + rows),)].astype(jnp.float32)


def first_block(array, first, rows):
    return array[(0,) * (len(array.shape) - 2) + (slice(first, first + rows),)].astype(jnp.float32)


def last_kernel(counts, samples_all, tm, *refs):
    chunks = []
    for count in counts:
        chunks.append(refs[:count])
        refs = refs[count:]
    grad_in, grad_inputs, grad_conv, grad_out = refs
    layers, channels = grad_conv.shape[0], grad_in.shape[1]
    total = 0.0
    for term in chunks[0]:
        total = total + jnp.sum(first_block(term, term.shape[-2] - 16, 16), axis=0, keepdims=True)
    scale = samples_all / total
    for chunk, terms in enumerate(chunks):
        items = items_of(layers, chunk)
        for (index, is_out), base in zip(items, bases_of(items, tm, channels)[0]):
            out = grad_out if is_out else grad_conv
            value = 0.0
            for term in terms:
                value = value + first_block(term, base, out.shape[1])
            out[index] = value * scale
    for first in range(0, channels, LANES):
        lanes = slice(first, first + LANES)
        grad_inputs[:, lanes] = grad_in[:, lanes] * scale


class Chunk:
    def __init__(self, tm, dp, chunk, keep, send):
        self.tm, self.dp, self.chunk, self.rows = tm, dp, chunk, keep.shape[-2]
        self.message = None
        self.terms = [keep, swapped(tm, dp, send, "core")]

    def next_message(self):
        if self.message is None:
            left = len(CHAINS[self.chunk]) + 2 - len(self.terms)
            pieces = []
            for i, v in enumerate(self.terms):
                pieces.append((i, (0,) * (len(v.shape) - 2 - left) + (1,), 0))
            (self.message,) = add_up(
                self.terms, [[(0, self.rows, self.chunk == 0, pieces)]], [(2,) * (left - 1) + (self.rows, LANES)],
                "add_chunk%d_step%d" % (self.chunk, len(self.terms) - 1),
            )
        return self.message

    def run_chain(self):
        for name in CHAINS[self.chunk]:
            self.terms.append(swapped(self.tm, self.dp, self.next_message(), name))
            self.message = None
        return self.terms


def swapped(tm, dp, value, name):
    over_t, over_d = {"core": (0, 1), "y": (0, 2), "x": (1, 0), "z0": (2, 0), "z1": (4, 0)}[name]
    pairs = [(t * dp + d, (t ^ over_t) * dp + (d ^ over_d)) for t in range(tm) for d in range(dp)]
    return lax.ppermute(value, ("tm", "dp"), pairs)


def scattered(part):
    columns = lax.psum_scatter(part, "dp", scatter_dimension=2, tiled=True).astype(jnp.float32)
    return lax.psum_scatter(columns, "tm", scatter_dimension=1, tiled=True)


def body(inputs, grad_stream_out, grad_skip_out, sample_weight, conv_weight, out_weight):
    tm, dp = lax.axis_size("tm"), lax.axis_size("dp")
    batch, length, channels = inputs.shape
    layers = conv_weight.shape[0]
    third = layers // len(CHAINS)
    halo = 2**layers
    samples_all = batch * length * tm * dp
    x, gs, gk = inputs[0], grad_stream_out[0], grad_skip_out[0]
    message_a, message_b = pack(halo, x, gs, gk, sample_weight)
    messages = [neighbours_swapped(message_a, "tm", True), neighbours_swapped(message_b, "tm", False)]
    loaded = load_all(x, gs, gk, sample_weight, conv_weight, out_weight, message_a)
    in_shards = tm == 8 and dp == 4 and channels // tm % 16 == 0 and 2 * channels == dp * LANES
    grad_in, parts = run_layers(in_shards, tm, dp, halo, messages, loaded)
    if not in_shards:
        scale = samples_all / lax.psum(jnp.sum(sample_weight), ("tm", "dp"))
        found = {}
        for chunk, part in enumerate(parts):
            items = items_of(layers, chunk)
            for is_out in (False, True):
                for place, item in enumerate(item for item in items if item[1] == is_out):
                    found[item] = part[int(is_out)][place]
        grad_conv, grad_out = (
            scattered(jnp.stack([found[index, is_out] for index in range(layers)])) * scale for is_out in (False, True)
        )
        return (grad_in * scale)[None], grad_conv, grad_out
    chunks = [part.run_chain() for part in parts]
    conv_rows, out_rows = 2 * channels // tm, channels // tm
    grad_inputs, grad_conv, grad_out = pl.pallas_call(
        functools.partial(last_kernel, [len(terms) for terms in chunks], float(samples_all), tm),
        out_shape=[
            jax.ShapeDtypeStruct((length, channels), jnp.float32),
            jax.ShapeDtypeStruct((layers, conv_rows, LANES), jnp.float32),
            jax.ShapeDtypeStruct((layers, out_rows, LANES), jnp.float32),
        ],
        compiler_params=pltpu.CompilerParams(vmem_limit_bytes=ADD_BYTES),
        name="scale_all",
    )(*held([term for terms in chunks for term in terms]), *held([grad_in]))
    return grad_inputs[None], grad_conv, grad_out


def solution(mesh):
    placed = (
        P("dp", "tm", None),
        P("dp", "tm", None),
        P("dp", "tm", None),
        P("dp", "tm"),
        P(),
        P(),
    )
    return jax.shard_map(
        body,
        mesh=mesh,
        in_specs=placed,
        out_specs=(P("dp", "tm", None), P(None, "tm", "dp"), P(None, "tm", "dp")),
        check_vma=False,
    )
```

```python
import functools

import jax
import jax.numpy as jnp
from jax import lax
from jax.experimental import pallas as pl
from jax.experimental.pallas import tpu as pltpu
from jax.sharding import PartitionSpec as P

LANES = 128
VMEM_BYTES = 24 * 1024 * 1024
ADD_BYTES = 8 * 1024 * 1024
CHAINS = (("x", "y", "z0", "z1"), ("y", "z0", "x", "z1"), ("z0", "x", "y", "z1"))
EXTRA = (0, 0, 16)
NN = (((1,), (0,)), ((), ()))
NT = (((1,), (1,)), ((), ()))
TN = (((0,), (0,)), ((), ()))


def dot(left, right, dims):
    return lax.dot_general(left, right, dims, preferred_element_type=jnp.float32)


def held(arrays, space=pltpu.VMEM):
    return [pltpu.with_memory_space_constraint(x, space) for x in arrays]


def around(x, axis, by):
    count = lax.axis_size(axis)
    return lax.ppermute(x, axis, [(i, (i + by) % count) for i in range(count)])


def column(row, rows):
    return jnp.broadcast_to(row, (LANES, rows)).T


def cost(flops, moved):
    return pl.CostEstimate(flops=flops, bytes_accessed=moved, transcendentals=0)


def pack_kernel(tail_x, tail_gs, tail_gk, weight, message):
    halo, channels = tail_gs.shape
    by_row = column(weight[...], LANES)[LANES - halo :]
    by_row = jnp.concatenate([by_row] * (channels // LANES), axis=1)
    message[0 : 2 * halo] = tail_x[...]
    message[2 * halo : 3 * halo] = (tail_gs[...].astype(jnp.float32) * by_row).astype(jnp.bfloat16)
    message[3 * halo :] = (tail_gk[...].astype(jnp.float32) * by_row).astype(jnp.bfloat16)


def pack(halo, x, grad_stream_out, grad_skip_out, weight):
    length, channels = x.shape

    def last(rows):
        return pl.BlockSpec((rows, channels), lambda i: (length // rows - 1, 0))

    return pl.pallas_call(
        pack_kernel,
        grid=(1,),
        in_specs=[last(2 * halo), last(halo), last(halo), pl.BlockSpec((1, LANES), lambda i: (0, length // LANES - 1))],
        out_specs=pl.BlockSpec((4 * halo, channels), lambda i: (0, 0)),
        out_shape=jax.ShapeDtypeStruct((4 * halo, channels), jnp.bfloat16),
        compiler_params=pltpu.CompilerParams(vmem_limit_bytes=ADD_BYTES),
        name="pack_borders",
    )(*held((x, grad_stream_out, grad_skip_out, weight), pltpu.HBM))


def load_kernel(
    x, gs, gk, weight, conv_w, out_w, _, x_here, grad_stream, grad_skip, sums, conv_here, out_here,
    gs_raw, gk_raw, weight_here, sems,
):
    pairs = ((weight, weight_here), (gs, gs_raw), (gk, gk_raw), (x, x_here), (conv_w, conv_here), (out_w, out_here))
    copies = [pltpu.make_async_copy(a, b, sems.at[i]) for i, (a, b) in enumerate(pairs)]
    for copy in copies:
        copy.start()
    for copy in copies[:3]:
        copy.wait()
    length, channels = x_here.shape
    by_row = column(weight_here[...], length)
    by_row = jnp.concatenate([by_row] * (channels // LANES), axis=1)
    grad_stream[...] = gs_raw[...].astype(jnp.float32) * by_row
    grad_skip[...] = (gk_raw[...].astype(jnp.float32) * by_row).astype(jnp.bfloat16)
    own_sum = jnp.broadcast_to(jnp.sum(weight_here[...], axis=1, keepdims=True), (1, LANES))
    sums[...] = split_rows(own_sum)
    for copy in copies[3:]:
        copy.wait()


def load_all(x, gs, gk, weight, conv_w, out_w, after):
    shape = x.shape
    vmem, anywhere = pl.BlockSpec(memory_space=pltpu.VMEM), pl.BlockSpec(memory_space=pl.ANY)
    return pl.pallas_call(
        load_kernel,
        in_specs=[anywhere] * 7,
        out_specs=[vmem] * 6,
        out_shape=[
            pltpu.VMEM(shape, jnp.bfloat16),
            pltpu.VMEM(shape, jnp.float32),
            pltpu.VMEM(shape, jnp.bfloat16),
            pltpu.VMEM((16, LANES), jnp.bfloat16),
            pltpu.VMEM(conv_w.shape, jnp.bfloat16),
            pltpu.VMEM(out_w.shape, jnp.bfloat16),
        ],
        scratch_shapes=[
            pltpu.VMEM(shape, jnp.bfloat16),
            pltpu.VMEM(shape, jnp.bfloat16),
            pltpu.VMEM(weight.shape, jnp.float32),
            pltpu.SemaphoreType.DMA((6,)),
        ],
        compiler_params=pltpu.CompilerParams(vmem_limit_bytes=ADD_BYTES),
        cost_estimate=cost(10**7, 6 * 10**6),
        name="load_all",
    )(*held((x, gs, gk, weight, conv_w, out_w), pltpu.HBM), *held([after]))


def split_rows(total):
    high = total.astype(jnp.bfloat16).astype(jnp.float32)
    middle = (total - high).astype(jnp.bfloat16).astype(jnp.float32)
    low = total - high - middle
    row = lax.broadcasted_iota(jnp.int32, (16, LANES), 0)
    rows = jnp.where(row == 0, high, jnp.where(row == 1, middle, jnp.where(row == 2, low, 0.0)))
    return rows.astype(jnp.bfloat16)


def joined_rows(rows):
    return jnp.sum(rows.astype(jnp.float32), axis=0, keepdims=True)


def cut_off(rows, dilation):
    row = lax.broadcasted_iota(jnp.int32, rows.shape, 0)
    return jnp.where(jnp.logical_and(row < dilation, lax.axis_index("tm") == 0), 0.0, rows)


def items_of(layers, chunk):
    third = layers // len(CHAINS)
    high = layers - chunk * third
    items = []
    for index in reversed(range(high - third, high)):
        items.append((index, False))
        if chunk == 0 or index < high - 1:
            items.append((index, True))
    return items + ([(high - third - 1, True)] if high > third else [])


def backward(plan, layers, refs_of, conv_w, out_w, grad_proj, grad_stream, past_part, total, grad_parts):
    halo, length, channels = plan["halo"], plan["length"], plan["channels"]
    own = slice(halo, halo + length)
    items = plan["items"]

    def out_grad(index):
        if (index, True) in items:
            total[0:channels] = dot(refs_of(index)[2][own], grad_proj[0:length], TN)
            plan["store"](total, channels, items.index((index, True)), grad_parts)

    for index in layers:
        dilation, count = 2**index, plan["counts"][index]
        operands, factors, _ = refs_of(index)
        grad_proj[0:count, :channels] = grad_stream[0:count].astype(jnp.bfloat16)
        grad_gated = dot(grad_proj[0:count], out_w[index], NT)
        out_grad(index)
        both = factors[halo : halo + count]
        grad_preact = jnp.concatenate(
            [grad_gated * both[:, :channels], grad_gated * both[:, channels:]], axis=1
        ).astype(jnp.bfloat16)
        spread = dot(grad_preact, conv_w[index], NT)
        past_part[0:count] = spread[:, channels:]
        cut = slice(halo, halo + max(dilation, 8))
        past_part[cut] = cut_off(past_part[cut], dilation)
        rows = plan["counts"][index - 1] if index else length
        grad_stream[0:rows] += spread[0:rows, :channels] + past_part[dilation : dilation + rows]
        total[...] = dot(operands[own], grad_preact[0:length], TN)
        plan["store"](total, 2 * channels, items.index((index, False)), grad_parts)
    after = layers[-1] - 1
    if (after, True) in items:
        grad_proj[0:length, :channels] = grad_stream[0:length].astype(jnp.bfloat16)
        out_grad(after)


def first_kernel(
    plan, prev_rows, own_x, own_grad, own_skip, conv_w, out_w,
    low_operands, low_factors, low_gates, grad_stream, grad_skip, *rest,
):
    *grad_parts, stream, operands, factors, gates, grad_proj, past_part, total = rest
    halo, (length, channels) = plan["halo"], own_x.shape
    layers, low = conv_w.shape[0], low_gates.shape[0]
    pad = 2 ** (layers - 1)
    extent = length + 2 * halo
    begin = 2 * halo
    stream[0:pad] = jnp.zeros((pad, channels), jnp.float32)
    stream[pad : pad + begin] = prev_rows[0:begin].astype(jnp.float32)
    stream[pad + begin :] = own_x[...].astype(jnp.float32)

    def refs_of(index):
        if index < low:
            return low_operands.at[index], low_factors.at[index], low_gates.at[index]
        return operands.at[index - low], factors.at[index - low], gates.at[index - low]

    for index in range(layers):
        dilation, start = 2**index, plan["starts"][index]
        operand, factor, gate = refs_of(index)
        operand[start:, :channels] = stream[pad + start :].astype(jnp.bfloat16)
        operand[start:, channels:] = stream[pad + start - dilation : pad + extent - dilation].astype(jnp.bfloat16)
        slab = max(dilation, 16)
        earlier = stream[pad + begin - dilation : pad + begin - dilation + slab]
        operand[begin : begin + slab, channels:] = cut_off(earlier, dilation).astype(jnp.bfloat16)
        preact = dot(operand[start:], conv_w[index], NN)
        filtered = jnp.tanh(preact[:, :channels])
        opening = 0.5 + 0.5 * jnp.tanh(0.5 * preact[:, channels:])
        product = filtered * opening
        gate[start:] = product.astype(jnp.bfloat16)
        factor[start:, :channels] = opening - filtered * product
        factor[start:, channels:] = product * (1.0 - opening)
        if index < layers - 1:
            stream[pad + start :] += dot(gate[start:], out_w[index, :, :channels], NN)

    grad_stream[0:halo] = prev_rows[2 * halo : 3 * halo].astype(jnp.float32)
    grad_stream[halo:] = own_grad[...]
    grad_skip[0:halo] = prev_rows[3 * halo :]
    grad_skip[halo:] = own_skip[...]
    grad_proj[:, channels:] = grad_skip[...]
    backward(
        plan, list(reversed(range(low, layers))), refs_of, conv_w, out_w,
        grad_proj, grad_stream, past_part, total, grad_parts,
    )


def later_kernel(
    plan, first, third, low_operands, low_factors, low_gates, grad_before, grad_skip, sums, conv_w, out_w, *rest
):
    *outs, keep, send, grad_stream, grad_proj, past_part, total = rest[plan["unused"] :]
    channels = plan["channels"]
    grad_stream[...] = grad_before[...]
    grad_proj[:, channels:] = grad_skip[...]

    def refs_of(index):
        return low_operands.at[index], low_factors.at[index], low_gates.at[index]

    backward(
        plan, list(reversed(range(first, first + third))), refs_of, conv_w, out_w,
        grad_proj, grad_stream, past_part, total, (keep, send),
    )
    at = 0
    for out in outs:
        out[...] = grad_stream[at : at + out.shape[0]]
        at += out.shape[0]
    plan["finish"](sums, (keep, send))


def store_whole(items, total, height, item, grad_parts):
    is_out = items[item][1]
    place = sum(kind == is_out for _, kind in items[:item])
    grad_parts[int(is_out)][place] = total[0:height].astype(jnp.bfloat16)


def finish_whole(sums, grad_parts):
    pass


def finish_shards(extra, sums, grad_parts):
    for part in grad_parts:
        lead, rows = part.shape[:-2], part.shape[-2]
        for first in range(rows - extra, rows, 16):
            part[(slice(None),) * len(lead) + (slice(first, first + 16),)] = jnp.broadcast_to(
                sums[...], lead + sums.shape
            )


def store_shards(tm, dp, order, bases, total, height, item, grad_parts):
    keep, send = grad_parts
    t_at, d_at = lax.axis_index("tm"), lax.axis_index("dp")
    core_at = lax.rem(d_at, 2)
    rows = height // tm
    at = pl.ds(bases[item], rows)
    at_bits = bits_of(t_at, d_at, lax.rem, lax.div)
    for y in range(dp // 2):
        near = total[0:height, (2 * y) * LANES : (2 * y + 1) * LANES]
        far = total[0:height, (2 * y + 1) * LANES : (2 * y + 2) * LANES]
        mine = jnp.where(core_at == 0, near, far).astype(jnp.bfloat16)
        other = jnp.where(core_at == 0, far, near).astype(jnp.bfloat16)
        for t in range(tm):
            bits = bits_of(t, 2 * y, lambda a, b: a % b, lambda a, b: a // b)
            lead = tuple(lax.rem(bits[name] + at_bits[name], 2) for name in order)
            keep[lead + (at,)] = mine[t * rows : (t + 1) * rows]
            send[lead + (at,)] = other[t * rows : (t + 1) * rows]


def bits_of(t, d, rem, div):
    return {"x": rem(t, 2), "z0": rem(div(t, 2), 2), "z1": div(t, 4), "y": div(d, 2)}


def bases_of(items, tm, channels):
    ends = [0]
    for _, is_out in items:
        ends.append(ends[-1] + (1 if is_out else 2) * channels // tm)
    return ends[:-1], ends[-1]


def run_layers(in_shards, tm, dp, halo, prev_rows, loaded):
    own_x, own_grad, own_skip, sums, conv_w, out_w = loaded
    length, channels = own_x.shape
    layers = conv_w.shape[0]
    third = layers // len(CHAINS)
    low = layers - third
    extent, border = length + 2 * halo, length + halo
    starts = []
    for index in range(layers):
        need = halo if index == layers - 1 else 2 ** (index + 1)
        starts.append(need // 16 * 16)
    counts = [-(-(length + 2 ** (index + 1) - 1) // 16) * 16 for index in range(layers)]
    plan = {"halo": halo, "starts": starts, "counts": counts, "length": length, "channels": channels, "unused": 0}
    plans, shapes = [], []
    for chunk, order in enumerate(CHAINS):
        items = items_of(layers, chunk)
        bases, rows = bases_of(items, tm, channels)
        if in_shards:
            store = functools.partial(store_shards, tm, dp, order, bases)
            finish = functools.partial(finish_shards, EXTRA[chunk])
            shapes.append(2 * [(2,) * len(order) + (rows + EXTRA[chunk], LANES)])
        else:
            store, finish = functools.partial(store_whole, items), finish_whole
            outs = sum(is_out for _, is_out in items)
            shapes.append([(len(items) - outs,) + conv_w.shape[1:], (outs,) + out_w.shape[1:]])
        plans.append(plan | {"items": items, "store": store, "finish": finish})
    vmem, anywhere = pl.BlockSpec(memory_space=pltpu.VMEM), pl.BlockSpec(memory_space=pl.ANY)
    weight_bytes = 2 * (conv_w.size + out_w.size)
    flops = 2 * length * channels * channels
    *kept, grad_stream, grad_skip, keep, send = pl.pallas_call(
        functools.partial(first_kernel, plans[0]),
        in_specs=[vmem] * 6,
        out_specs=[vmem] * 7,
        out_shape=[
            pltpu.VMEM((low, extent, 2 * channels), jnp.bfloat16),
            pltpu.VMEM((low, extent, 2 * channels), jnp.float32),
            pltpu.VMEM((low, extent, channels), jnp.bfloat16),
            pltpu.VMEM((border, channels), jnp.float32),
            pltpu.VMEM((border, channels), jnp.bfloat16),
        ]
        + [pltpu.VMEM(shape, jnp.bfloat16) for shape in shapes[0]],
        scratch_shapes=[
            pltpu.VMEM((2 ** (layers - 1) + extent, channels), jnp.float32),
            pltpu.VMEM((third, extent, 2 * channels), jnp.bfloat16),
            pltpu.VMEM((third, extent, 2 * channels), jnp.float32),
            pltpu.VMEM((third, extent, channels), jnp.bfloat16),
            pltpu.VMEM((border, 2 * channels), jnp.bfloat16),
            pltpu.VMEM((border, channels), jnp.float32),
            pltpu.VMEM((2 * channels, 2 * channels), jnp.float32),
        ],
        compiler_params=pltpu.CompilerParams(vmem_limit_bytes=VMEM_BYTES),
        cost_estimate=cost(flops * (5 * layers + 12 * third), weight_bytes),
        name="forward_and_last_third",
    )(*held((prev_rows, own_x, own_grad, own_skip, conv_w, out_w)))

    def later(step, outs, after):
        return pl.pallas_call(
            functools.partial(later_kernel, plans[step] | {"unused": len(after)}, layers - (step + 1) * third, third),
            in_specs=[vmem] * 8 + [anywhere] * len(after),
            out_specs=[vmem] * (len(outs) + 2),
            out_shape=[pltpu.VMEM((rows, channels), jnp.float32) for rows in outs]
            + [pltpu.VMEM(shape, jnp.bfloat16) for shape in shapes[step]],
            scratch_shapes=[
                pltpu.VMEM((border, channels), jnp.float32),
                pltpu.VMEM((border, 2 * channels), jnp.bfloat16),
                pltpu.VMEM((border, channels), jnp.float32),
                pltpu.VMEM((2 * channels, 2 * channels), jnp.float32),
            ],
            compiler_params=pltpu.CompilerParams(vmem_limit_bytes=VMEM_BYTES),
            cost_estimate=cost(flops * 12 * third, weight_bytes),
            name="middle_third" if step == 1 else "first_third",
        )(*held((*kept, grad_stream, grad_skip, sums, conv_w, out_w, *after)))

    parts = [(keep, send)]
    if in_shards:
        parts[0] = Chunk(tm, dp, 0, keep, send)
    grad_stream, *middle = later(1, [border], [])
    other, own, *last = later(2, [halo, length - halo], [parts[0].next_message()] if in_shards else [])
    parts += [middle, last]
    if in_shards:
        for step in (1, 2):
            parts[step] = Chunk(tm, dp, step, *parts[step])
    return other, own, parts


def add_kernel(count, groups, *refs):
    arrays, outs = refs[:count], refs[-len(groups) :]
    for out, pieces in zip(outs, groups):
        lead = (slice(None),) * (len(out.shape) - 2)
        for first, rows, with_total, terms in pieces:
            body = rows - 16 if with_total else rows
            value = 0.0
            for array, at, begin in terms:
                value = value + arrays[array][at + lead + (slice(begin, begin + body),)].astype(jnp.float32)
            out[lead + (slice(first, first + body),)] = value.astype(out.dtype)
            if with_total:
                total = 0.0
                for array, at, begin in terms:
                    rows_at = slice(begin + body, begin + rows)
                    total = total + joined_rows(arrays[array][at + (0,) * len(lead) + (rows_at,)])
                slab = split_rows(total)
                out[lead + (slice(first + body, first + rows),)] = jnp.broadcast_to(slab, out.shape[:-2] + slab.shape)


def add_up(arrays, groups, shapes, after, name):
    vmem = pl.BlockSpec(memory_space=pltpu.VMEM)
    return pl.pallas_call(
        functools.partial(add_kernel, len(arrays), groups),
        in_specs=[vmem] * len(arrays) + [pl.BlockSpec(memory_space=pl.ANY)] * len(after),
        out_specs=[vmem] * len(groups),
        out_shape=[pltpu.VMEM(shape, jnp.bfloat16) for shape in shapes],
        compiler_params=pltpu.CompilerParams(vmem_limit_bytes=ADD_BYTES),
        name=name,
    )(*held(arrays), *held(after))


def first_block(array, first, rows):
    return array[(0,) * (len(array.shape) - 2) + (slice(first, first + rows),)].astype(jnp.float32)


def first_block(array, first, rows):
    return array[(0,) * (len(array.shape) - 2) + (slice(first, first + rows),)].astype(jnp.float32)


def last_kernel(counts, samples_all, tm, *refs):
    chunks = []
    for count in counts:
        chunks.append(refs[:count])
        refs = refs[count:]
    other, own, grad_inputs, grad_conv, grad_out = refs
    layers, channels = grad_conv.shape[0], own.shape[1]
    total = 0.0
    for term in chunks[-1]:
        total = total + jnp.sum(first_block(term, term.shape[-2] - 16, 16), axis=0, keepdims=True)
    scale = samples_all / total
    for chunk, terms in enumerate(chunks):
        items = items_of(layers, chunk)
        for (index, is_out), base in zip(items, bases_of(items, tm, channels)[0]):
            out = grad_out if is_out else grad_conv
            value = 0.0
            for term in terms:
                value = value + first_block(term, base, out.shape[1])
            out[index] = value * scale
    for first in range(0, channels, LANES):
        lanes = slice(first, first + LANES)
        grad_inputs[0 : own.shape[0], lanes] = own[:, lanes] * scale
        grad_inputs[own.shape[0] :, lanes] = other[:, lanes] * scale


class Chunk:
    def __init__(self, tm, dp, chunk, keep, send):
        self.tm, self.dp, self.chunk, self.rows = tm, dp, chunk, keep.shape[-2]
        self.message = None
        self.terms = [keep, swapped(tm, dp, send, "core")]

    def next_message(self, after=()):
        if self.message is None:
            left = len(CHAINS[self.chunk]) + 2 - len(self.terms)
            pieces = []
            for i, v in enumerate(self.terms):
                pieces.append((i, (0,) * (len(v.shape) - 2 - left) + (1,), 0))
            (self.message,) = add_up(
                self.terms, [[(0, self.rows, EXTRA[self.chunk] > 0, pieces)]], [(2,) * (left - 1) + (self.rows, LANES)], after,
                "add_chunk%d_step%d" % (self.chunk, len(self.terms) - 1),
            )
        return self.message

    def run_chain(self, after=()):
        for step, name in enumerate(CHAINS[self.chunk]):
            self.terms.append(swapped(self.tm, self.dp, self.next_message(after if step == 2 else ()), name))
            self.message = None
        return self.terms


def swapped(tm, dp, value, name):
    over_t, over_d = {"core": (0, 1), "y": (0, 2), "x": (1, 0), "z0": (2, 0), "z1": (4, 0)}[name]
    pairs = [(t * dp + d, (t ^ over_t) * dp + (d ^ over_d)) for t in range(tm) for d in range(dp)]
    return lax.ppermute(value, ("tm", "dp"), pairs)


def scattered(part):
    columns = lax.psum_scatter(part, "dp", scatter_dimension=2, tiled=True).astype(jnp.float32)
    return lax.psum_scatter(columns, "tm", scatter_dimension=1, tiled=True)


def body(inputs, grad_stream_out, grad_skip_out, sample_weight, conv_weight, out_weight):
    tm, dp = lax.axis_size("tm"), lax.axis_size("dp")
    batch, length, channels = inputs.shape
    layers = conv_weight.shape[0]
    third = layers // len(CHAINS)
    halo = 2**layers
    samples_all = batch * length * tm * dp
    x, gs, gk = inputs[0], grad_stream_out[0], grad_skip_out[0]
    message = pack(halo, x, gs, gk, sample_weight)
    prev_rows = around(message, "tm", 1)
    loaded = load_all(x, gs, gk, sample_weight, conv_weight, out_weight, message)
    in_shards = tm == 8 and dp == 4 and channels // tm % 16 == 0 and 2 * channels == dp * LANES
    other, own, parts = run_layers(in_shards, tm, dp, halo, prev_rows, loaded)
    other = around(other, "tm", -1)
    if not in_shards:
        scale = samples_all / lax.psum(jnp.sum(sample_weight), ("tm", "dp"))
        found = {}
        for chunk, part in enumerate(parts):
            items = items_of(layers, chunk)
            for is_out in (False, True):
                for place, item in enumerate(item for item in items if item[1] == is_out):
                    found[item] = part[int(is_out)][place]
        grad_conv, grad_out = (
            scattered(jnp.stack([found[index, is_out] for index in range(layers)])) * scale for is_out in (False, True)
        )
        return (jnp.concatenate([own, other]) * scale)[None], grad_conv, grad_out
    chunks = [part.run_chain([other] if part is parts[0] else ()) for part in parts]
    conv_rows, out_rows = 2 * channels // tm, channels // tm
    grad_inputs, grad_conv, grad_out = pl.pallas_call(
        functools.partial(last_kernel, [len(terms) for terms in chunks], float(samples_all), tm),
        out_shape=[
            jax.ShapeDtypeStruct((length, channels), jnp.float32),
            jax.ShapeDtypeStruct((layers, conv_rows, LANES), jnp.float32),
            jax.ShapeDtypeStruct((layers, out_rows, LANES), jnp.float32),
        ],
        compiler_params=pltpu.CompilerParams(vmem_limit_bytes=ADD_BYTES),
        name="scale_all",
    )(*held([term for terms in chunks for term in terms]), *held([other, own]))
    return grad_inputs[None], grad_conv, grad_out


def solution(mesh):
    placed = (
        P("dp", "tm", None),
        P("dp", "tm", None),
        P("dp", "tm", None),
        P("dp", "tm"),
        P(),
        P(),
    )
    return jax.shard_map(
        body,
        mesh=mesh,
        in_specs=placed,
        out_specs=(P("dp", "tm", None), P(None, "tm", "dp"), P(None, "tm", "dp")),
        check_vma=False,
    )
```

```python
import functools

import jax
import jax.numpy as jnp
from jax import lax
from jax.experimental import pallas as pl
from jax.experimental.pallas import tpu as pltpu
from jax.sharding import PartitionSpec as P

LANES = 128
VMEM_BYTES = 24 * 1024 * 1024
ADD_BYTES = 8 * 1024 * 1024
CHAINS = (("y", "x", "z0", "z1"), ("x", "z0", "y", "z1"), ("z0", "y", "x", "z1"))
EXTRA = (0, 0, 16)
NN = (((1,), (0,)), ((), ()))
NT = (((1,), (1,)), ((), ()))
TN = (((0,), (0,)), ((), ()))


def dot(left, right, dims):
    return lax.dot_general(left, right, dims, preferred_element_type=jnp.float32)


def held(arrays, space=pltpu.VMEM):
    return [pltpu.with_memory_space_constraint(x, space) for x in arrays]


def around(x, axis, by):
    count = lax.axis_size(axis)
    return lax.ppermute(x, axis, [(i, (i + by) % count) for i in range(count)])


def column(row, rows):
    return jnp.broadcast_to(row, (LANES, rows)).T


def cost(flops, moved):
    return pl.CostEstimate(flops=flops, bytes_accessed=moved, transcendentals=0)


def pack_kernel(tail_x, tail_gs, tail_gk, weight, message):
    halo, channels = tail_gs.shape
    by_row = column(weight[...], LANES)[LANES - halo :]
    by_row = jnp.concatenate([by_row] * (channels // LANES), axis=1)
    message[0 : 2 * halo] = tail_x[...]
    message[2 * halo : 3 * halo] = (tail_gs[...].astype(jnp.float32) * by_row).astype(jnp.bfloat16)
    message[3 * halo :] = (tail_gk[...].astype(jnp.float32) * by_row).astype(jnp.bfloat16)


def pack(halo, x, grad_stream_out, grad_skip_out, weight):
    length, channels = x.shape

    def last(rows):
        return pl.BlockSpec((rows, channels), lambda i: (length // rows - 1, 0))

    return pl.pallas_call(
        pack_kernel,
        grid=(1,),
        in_specs=[last(2 * halo), last(halo), last(halo), pl.BlockSpec((1, LANES), lambda i: (0, length // LANES - 1))],
        out_specs=pl.BlockSpec((4 * halo, channels), lambda i: (0, 0)),
        out_shape=jax.ShapeDtypeStruct((4 * halo, channels), jnp.bfloat16),
        compiler_params=pltpu.CompilerParams(vmem_limit_bytes=ADD_BYTES),
        name="pack_borders",
    )(*held((x, grad_stream_out, grad_skip_out, weight), pltpu.HBM))


def load_kernel(
    x, gs, gk, weight, conv_w, out_w, _, x_here, grad_stream, grad_skip, sums, conv_here, out_here,
    gs_raw, gk_raw, weight_here, sems,
):
    pairs = ((weight, weight_here), (gs, gs_raw), (gk, gk_raw), (x, x_here), (conv_w, conv_here), (out_w, out_here))
    copies = [pltpu.make_async_copy(a, b, sems.at[i]) for i, (a, b) in enumerate(pairs)]
    for copy in copies:
        copy.start()
    for copy in copies[:3]:
        copy.wait()
    length, channels = x_here.shape
    by_row = column(weight_here[...], length)
    by_row = jnp.concatenate([by_row] * (channels // LANES), axis=1)
    grad_stream[...] = gs_raw[...].astype(jnp.float32) * by_row
    grad_skip[...] = (gk_raw[...].astype(jnp.float32) * by_row).astype(jnp.bfloat16)
    own_sum = jnp.broadcast_to(jnp.sum(weight_here[...], axis=1, keepdims=True), (1, LANES))
    sums[...] = split_rows(own_sum)
    for copy in copies[3:]:
        copy.wait()


def load_all(x, gs, gk, weight, conv_w, out_w, after):
    shape = x.shape
    vmem, anywhere = pl.BlockSpec(memory_space=pltpu.VMEM), pl.BlockSpec(memory_space=pl.ANY)
    return pl.pallas_call(
        load_kernel,
        in_specs=[anywhere] * 7,
        out_specs=[vmem] * 6,
        out_shape=[
            pltpu.VMEM(shape, jnp.bfloat16),
            pltpu.VMEM(shape, jnp.float32),
            pltpu.VMEM(shape, jnp.bfloat16),
            pltpu.VMEM((16, LANES), jnp.bfloat16),
            pltpu.VMEM(conv_w.shape, jnp.bfloat16),
            pltpu.VMEM(out_w.shape, jnp.bfloat16),
        ],
        scratch_shapes=[
            pltpu.VMEM(shape, jnp.bfloat16),
            pltpu.VMEM(shape, jnp.bfloat16),
            pltpu.VMEM(weight.shape, jnp.float32),
            pltpu.SemaphoreType.DMA((6,)),
        ],
        compiler_params=pltpu.CompilerParams(vmem_limit_bytes=ADD_BYTES),
        cost_estimate=cost(10**7, 6 * 10**6),
        name="load_all",
    )(*held((x, gs, gk, weight, conv_w, out_w), pltpu.HBM), *held([after]))


def split_rows(total):
    high = total.astype(jnp.bfloat16).astype(jnp.float32)
    middle = (total - high).astype(jnp.bfloat16).astype(jnp.float32)
    low = total - high - middle
    row = lax.broadcasted_iota(jnp.int32, (16, LANES), 0)
    rows = jnp.where(row == 0, high, jnp.where(row == 1, middle, jnp.where(row == 2, low, 0.0)))
    return rows.astype(jnp.bfloat16)


def joined_rows(rows):
    return jnp.sum(rows.astype(jnp.float32), axis=0, keepdims=True)


def cut_off(rows, dilation):
    row = lax.broadcasted_iota(jnp.int32, rows.shape, 0)
    return jnp.where(jnp.logical_and(row < dilation, lax.axis_index("tm") == 0), 0.0, rows)


def items_of(layers, chunk):
    third = layers // len(CHAINS)
    high = layers - chunk * third
    items = []
    for index in reversed(range(high - third, high)):
        items.append((index, False))
        if chunk == 0 or index < high - 1:
            items.append((index, True))
    return items + ([(high - third - 1, True)] if high > third else [])


def earlier_rows(plan, index, present, first, last):
    dilation, begin = 2**index, 2 * plan["halo"]
    cut = cut_off(present[begin - dilation : begin], dilation)
    return jnp.concatenate([present[first - dilation : begin - dilation], cut, present[begin : last - dilation]])


def backward(plan, layers, refs_of, conv_w, out_w, grad_proj, grad_stream, past_part, grad_parts):
    halo, length, channels = plan["halo"], plan["length"], plan["channels"]
    own = slice(halo, halo + length)
    items = plan["items"]

    def out_grad(index):
        if (index, True) in items:
            total = dot(refs_of(index)[3][own], grad_proj[0:length], TN)
            plan["store"](total, items.index((index, True)), grad_parts)

    for index in layers:
        dilation, count = 2**index, plan["counts"][index]
        present, earlier, factors, _ = refs_of(index)
        grad_proj[0:count, :channels] = grad_stream[0:count].astype(jnp.bfloat16)
        grad_gated = dot(grad_proj[0:count], out_w[index], NT)
        out_grad(index)
        both = factors[halo : halo + count].astype(jnp.float32)
        grad_preact = jnp.concatenate(
            [grad_gated * both[:, :channels], grad_gated * both[:, channels:]], axis=1
        ).astype(jnp.bfloat16)
        spread = dot(grad_preact, conv_w[index], NT)
        past_part[0:count] = spread[:, channels:]
        cut = slice(halo, halo + max(dilation, 8))
        past_part[cut] = cut_off(past_part[cut], dilation)
        rows = plan["counts"][index - 1] if index else length
        grad_stream[0:rows] += spread[0:rows, :channels] + past_part[dilation : dilation + rows]
        past = earlier_rows(plan, index, present, halo, halo + length) if earlier is None else earlier[own]
        total = dot(jnp.concatenate([present[own], past], axis=1), grad_preact[0:length], TN)
        plan["store"](total, items.index((index, False)), grad_parts)
    after = layers[-1] - 1
    if (after, True) in items:
        grad_proj[0:length, :channels] = grad_stream[0:length].astype(jnp.bfloat16)
        out_grad(after)


def first_kernel(
    plan, prev_rows, own_x, own_grad, own_skip, conv_w, out_w,
    low_present, low_earlier, low_factors, low_gates, grad_stream, grad_skip, *rest,
):
    *grad_parts, stream, high_present, high_factors, high_gates, grad_proj, past_part = rest
    halo, (length, channels) = plan["halo"], own_x.shape
    layers, low = conv_w.shape[0], low_gates.shape[0]
    pad = 2 ** (layers - 1)
    extent = length + 2 * halo
    begin = 2 * halo
    stream[0:pad] = jnp.zeros((pad, channels), jnp.float32)
    stream[pad : pad + begin] = prev_rows[0:begin].astype(jnp.float32)
    stream[pad + begin :] = own_x[...].astype(jnp.float32)

    def refs_of(index):
        if index < low:
            return low_present.at[index], low_earlier.at[index], low_factors.at[index], low_gates.at[index]
        at = index - low
        return high_present.at[at], None, high_factors.at[at], high_gates.at[at]

    refs_of(0)[0][0:begin] = prev_rows[0:begin]
    refs_of(0)[0][begin:] = own_x[...]
    for index in range(layers):
        dilation, start = 2**index, plan["starts"][index]
        present, earlier, factor, gate = refs_of(index)
        if earlier is None:
            past = earlier_rows(plan, index, present, start, extent)
        else:
            past = stream[pad + start - dilation : pad + extent - dilation]
            cut = cut_off(past[begin - start : begin - start + 16], dilation)
            past = jnp.concatenate([past[: begin - start], cut, past[begin - start + 16 :]]).astype(jnp.bfloat16)
            earlier[start:] = past
        preact = dot(jnp.concatenate([present[start:], past], axis=1), conv_w[index], NN)
        filtered = jnp.tanh(preact[:, :channels])
        opening = 0.5 + 0.5 * jnp.tanh(0.5 * preact[:, channels:])
        product = filtered * opening
        gated = product.astype(jnp.bfloat16)
        gate[start:] = gated
        factor[start:, :channels] = (opening - filtered * product).astype(jnp.bfloat16)
        factor[start:, channels:] = (product * (1.0 - opening)).astype(jnp.bfloat16)
        if index < layers - 1:
            after = stream[pad + start :] + dot(gated, out_w[index, :, :channels], NN)
            refs_of(index + 1)[0][start:] = after.astype(jnp.bfloat16)
            if index < layers - 2:
                stream[pad + start :] = after

    grad_stream[0:halo] = prev_rows[2 * halo : 3 * halo].astype(jnp.float32)
    grad_stream[halo:] = own_grad[...]
    grad_skip[0:halo] = prev_rows[3 * halo :]
    grad_skip[halo:] = own_skip[...]
    grad_proj[:, channels:] = grad_skip[...]
    backward(
        plan, list(reversed(range(low, layers))), refs_of, conv_w, out_w, grad_proj, grad_stream, past_part, grad_parts
    )


def later_kernel(
    plan, first, third, present, earlier, factors, gates, grad_before, grad_skip, sums, conv_w, out_w, *rest
):
    *outs, keep, send, grad_stream, grad_proj, past_part = rest[plan["unused"] :]
    channels = plan["channels"]
    grad_stream[...] = grad_before[...]
    grad_proj[:, channels:] = grad_skip[...]

    def refs_of(index):
        return present.at[index], earlier.at[index], factors.at[index], gates.at[index]

    backward(
        plan, list(reversed(range(first, first + third))), refs_of, conv_w, out_w,
        grad_proj, grad_stream, past_part, (keep, send),
    )
    at = 0
    for out in outs:
        out[...] = grad_stream[at : at + out.shape[0]].astype(out.dtype)
        at += out.shape[0]
    plan["finish"](sums, (keep, send))


def store_whole(items, total, item, grad_parts):
    is_out = items[item][1]
    place = sum(kind == is_out for _, kind in items[:item])
    grad_parts[int(is_out)][place] = total.astype(jnp.bfloat16)


def finish_whole(sums, grad_parts):
    pass


def finish_shards(extra, sums, grad_parts):
    for part in grad_parts:
        lead, rows = part.shape[:-2], part.shape[-2]
        for first in range(rows - extra, rows, 16):
            part[(slice(None),) * len(lead) + (slice(first, first + 16),)] = jnp.broadcast_to(
                sums[...], lead + sums.shape
            )


def store_shards(tm, dp, order, bases, total, item, grad_parts):
    keep, send = grad_parts
    t_at, d_at = lax.axis_index("tm"), lax.axis_index("dp")
    core_at = lax.rem(d_at, 2)
    rows = total.shape[0] // tm
    at = pl.ds(bases[item], rows)
    at_bits = bits_of(t_at, d_at, lax.rem, lax.div)
    for y in range(dp // 2):
        near = total[:, (2 * y) * LANES : (2 * y + 1) * LANES]
        far = total[:, (2 * y + 1) * LANES : (2 * y + 2) * LANES]
        mine = jnp.where(core_at == 0, near, far).astype(jnp.bfloat16)
        other = jnp.where(core_at == 0, far, near).astype(jnp.bfloat16)
        for t in range(tm):
            bits = bits_of(t, 2 * y, lambda a, b: a % b, lambda a, b: a // b)
            lead = tuple(lax.rem(bits[name] + at_bits[name], 2) for name in order)
            keep[lead + (at,)] = mine[t * rows : (t + 1) * rows]
            send[lead + (at,)] = other[t * rows : (t + 1) * rows]


def bits_of(t, d, rem, div):
    return {"x": rem(t, 2), "z0": rem(div(t, 2), 2), "z1": div(t, 4), "y": div(d, 2)}


def bases_of(items, tm, channels):
    ends = [0]
    for _, is_out in items:
        ends.append(ends[-1] + (1 if is_out else 2) * channels // tm)
    return ends[:-1], ends[-1]


def run_layers(in_shards, tm, dp, halo, prev_rows, loaded):
    own_x, own_grad, own_skip, sums, conv_w, out_w = loaded
    length, channels = own_x.shape
    layers = conv_w.shape[0]
    third = layers // len(CHAINS)
    low = layers - third
    extent, border = length + 2 * halo, length + halo
    starts = []
    for index in range(layers):
        need = halo if index == layers - 1 else 2 ** (index + 1)
        starts.append(need // 16 * 16)
    counts = [-(-(length + 2 ** (index + 1) - 1) // 16) * 16 for index in range(layers)]
    plan = {"halo": halo, "starts": starts, "counts": counts, "length": length, "channels": channels, "unused": 0}
    plans, shapes = [], []
    for chunk, order in enumerate(CHAINS):
        items = items_of(layers, chunk)
        bases, rows = bases_of(items, tm, channels)
        if in_shards:
            store = functools.partial(store_shards, tm, dp, order, bases)
            finish = functools.partial(finish_shards, EXTRA[chunk])
            shapes.append(2 * [(2,) * len(order) + (rows + EXTRA[chunk], LANES)])
        else:
            store, finish = functools.partial(store_whole, items), finish_whole
            outs = sum(is_out for _, is_out in items)
            shapes.append([(len(items) - outs,) + conv_w.shape[1:], (outs,) + out_w.shape[1:]])
        plans.append(plan | {"items": items, "store": store, "finish": finish})
    vmem, anywhere = pl.BlockSpec(memory_space=pltpu.VMEM), pl.BlockSpec(memory_space=pl.ANY)
    weight_bytes = 2 * (conv_w.size + out_w.size)
    flops = 2 * length * channels * channels
    *kept, grad_stream, grad_skip, keep, send = pl.pallas_call(
        functools.partial(first_kernel, plans[0]),
        in_specs=[vmem] * 6,
        out_specs=[vmem] * 8,
        out_shape=[
            pltpu.VMEM((low, extent, channels), jnp.bfloat16),
            pltpu.VMEM((low, extent, channels), jnp.bfloat16),
            pltpu.VMEM((low, extent, 2 * channels), jnp.bfloat16),
            pltpu.VMEM((low, extent, channels), jnp.bfloat16),
            pltpu.VMEM((border, channels), jnp.float32),
            pltpu.VMEM((border, channels), jnp.bfloat16),
        ]
        + [pltpu.VMEM(shape, jnp.bfloat16) for shape in shapes[0]],
        scratch_shapes=[
            pltpu.VMEM((2 ** (layers - 1) + extent, channels), jnp.float32),
            pltpu.VMEM((third, extent, channels), jnp.bfloat16),
            pltpu.VMEM((third, extent, 2 * channels), jnp.bfloat16),
            pltpu.VMEM((third, extent, channels), jnp.bfloat16),
            pltpu.VMEM((border, 2 * channels), jnp.bfloat16),
            pltpu.VMEM((border, channels), jnp.float32),
        ],
        compiler_params=pltpu.CompilerParams(vmem_limit_bytes=VMEM_BYTES),
        cost_estimate=cost(flops * (5 * layers + 12 * third), weight_bytes),
        name="forward_and_last_third",
    )(*held((prev_rows, own_x, own_grad, own_skip, conv_w, out_w)))

    def later(step, outs, after):
        return pl.pallas_call(
            functools.partial(later_kernel, plans[step] | {"unused": len(after)}, layers - (step + 1) * third, third),
            in_specs=[vmem] * 9 + [anywhere] * len(after),
            out_specs=[vmem] * (len(outs) + 2),
            out_shape=[pltpu.VMEM((rows, channels), kind) for rows, kind in outs]
            + [pltpu.VMEM(shape, jnp.bfloat16) for shape in shapes[step]],
            scratch_shapes=[
                pltpu.VMEM((border, channels), jnp.float32),
                pltpu.VMEM((border, 2 * channels), jnp.bfloat16),
                pltpu.VMEM((border, channels), jnp.float32),
            ],
            compiler_params=pltpu.CompilerParams(vmem_limit_bytes=VMEM_BYTES),
            cost_estimate=cost(flops * 12 * third, weight_bytes),
            name="middle_third" if step == 1 else "first_third",
        )(*held((*kept, grad_stream, grad_skip, sums, conv_w, out_w, *after)))

    parts = [(keep, send)]
    if in_shards:
        parts[0] = Chunk(tm, dp, 0, keep, send)
    grad_stream, *middle = later(1, [(border, jnp.float32)], [])
    other, own, *last = later(
        2, [(halo, jnp.bfloat16), (length - halo, jnp.float32)], [parts[0].next_message()] if in_shards else []
    )
    parts += [middle, last]
    if in_shards:
        for step in (1, 2):
            parts[step] = Chunk(tm, dp, step, *parts[step])
    return other, own, parts


def add_kernel(count, groups, *refs):
    arrays, outs = refs[:count], refs[-len(groups) :]
    for out, pieces in zip(outs, groups):
        lead = (slice(None),) * (len(out.shape) - 2)
        for first, rows, with_total, terms in pieces:
            body = rows - 16 if with_total else rows
            value = 0.0
            for array, at, begin in terms:
                value = value + arrays[array][at + lead + (slice(begin, begin + body),)].astype(jnp.float32)
            out[lead + (slice(first, first + body),)] = value.astype(out.dtype)
            if with_total:
                total = 0.0
                for array, at, begin in terms:
                    rows_at = slice(begin + body, begin + rows)
                    total = total + joined_rows(arrays[array][at + (0,) * len(lead) + (rows_at,)])
                slab = split_rows(total)
                out[lead + (slice(first + body, first + rows),)] = jnp.broadcast_to(slab, out.shape[:-2] + slab.shape)


def add_up(arrays, groups, shapes, after, name):
    vmem = pl.BlockSpec(memory_space=pltpu.VMEM)
    return pl.pallas_call(
        functools.partial(add_kernel, len(arrays), groups),
        in_specs=[vmem] * len(arrays) + [pl.BlockSpec(memory_space=pl.ANY)] * len(after),
        out_specs=[vmem] * len(groups),
        out_shape=[pltpu.VMEM(shape, jnp.bfloat16) for shape in shapes],
        compiler_params=pltpu.CompilerParams(vmem_limit_bytes=ADD_BYTES),
        name=name,
    )(*held(arrays), *held(after))


def first_block(array, first, rows):
    return array[(0,) * (len(array.shape) - 2) + (slice(first, first + rows),)].astype(jnp.float32)


def first_block(array, first, rows):
    return array[(0,) * (len(array.shape) - 2) + (slice(first, first + rows),)].astype(jnp.float32)


def last_kernel(counts, samples_all, tm, *refs):
    chunks = []
    for count in counts:
        chunks.append(refs[:count])
        refs = refs[count:]
    other, own, grad_inputs, grad_conv, grad_out = refs
    layers, channels = grad_conv.shape[0], own.shape[1]
    total = 0.0
    for term in chunks[-1]:
        total = total + jnp.sum(first_block(term, term.shape[-2] - 16, 16), axis=0, keepdims=True)
    scale = samples_all / total
    for chunk, terms in enumerate(chunks):
        items = items_of(layers, chunk)
        for (index, is_out), base in zip(items, bases_of(items, tm, channels)[0]):
            out = grad_out if is_out else grad_conv
            value = 0.0
            for term in terms:
                value = value + first_block(term, base, out.shape[1])
            out[index] = value * scale
    for first in range(0, channels, LANES):
        lanes = slice(first, first + LANES)
        grad_inputs[0 : own.shape[0], lanes] = own[:, lanes] * scale
        grad_inputs[own.shape[0] :, lanes] = other[:, lanes].astype(jnp.float32) * scale


class Chunk:
    def __init__(self, tm, dp, chunk, keep, send):
        self.tm, self.dp, self.chunk, self.rows = tm, dp, chunk, keep.shape[-2]
        self.message = None
        self.terms = [keep, swapped(tm, dp, send, "core")]

    def next_message(self, after=()):
        if self.message is None:
            left = len(CHAINS[self.chunk]) + 2 - len(self.terms)
            pieces = []
            for i, v in enumerate(self.terms):
                pieces.append((i, (0,) * (len(v.shape) - 2 - left) + (1,), 0))
            (self.message,) = add_up(
                self.terms, [[(0, self.rows, EXTRA[self.chunk] > 0, pieces)]], [(2,) * (left - 1) + (self.rows, LANES)], after,
                "add_chunk%d_step%d" % (self.chunk, len(self.terms) - 1),
            )
        return self.message

    def run_chain(self, after=()):
        for step, name in enumerate(CHAINS[self.chunk]):
            self.terms.append(swapped(self.tm, self.dp, self.next_message(after if step == 1 else ()), name))
            self.message = None
        return self.terms


def swapped(tm, dp, value, name):
    over_t, over_d = {"core": (0, 1), "y": (0, 2), "x": (1, 0), "z0": (2, 0), "z1": (4, 0)}[name]
    pairs = [(t * dp + d, (t ^ over_t) * dp + (d ^ over_d)) for t in range(tm) for d in range(dp)]
    return lax.ppermute(value, ("tm", "dp"), pairs)


def scattered(part):
    columns = lax.psum_scatter(part, "dp", scatter_dimension=2, tiled=True).astype(jnp.float32)
    return lax.psum_scatter(columns, "tm", scatter_dimension=1, tiled=True)


def body(inputs, grad_stream_out, grad_skip_out, sample_weight, conv_weight, out_weight):
    tm, dp = lax.axis_size("tm"), lax.axis_size("dp")
    batch, length, channels = inputs.shape
    layers = conv_weight.shape[0]
    third = layers // len(CHAINS)
    halo = 2**layers
    samples_all = batch * length * tm * dp
    x, gs, gk = inputs[0], grad_stream_out[0], grad_skip_out[0]
    message = pack(halo, x, gs, gk, sample_weight)
    prev_rows = around(message, "tm", 1)
    loaded = load_all(x, gs, gk, sample_weight, conv_weight, out_weight, message)
    in_shards = tm == 8 and dp == 4 and channels // tm % 16 == 0 and 2 * channels == dp * LANES
    other, own, parts = run_layers(in_shards, tm, dp, halo, prev_rows, loaded)
    other = around(other, "tm", -1)
    if not in_shards:
        scale = samples_all / lax.psum(jnp.sum(sample_weight), ("tm", "dp"))
        found = {}
        for chunk, part in enumerate(parts):
            items = items_of(layers, chunk)
            for is_out in (False, True):
                for place, item in enumerate(item for item in items if item[1] == is_out):
                    found[item] = part[int(is_out)][place]
        grad_conv, grad_out = (
            scattered(jnp.stack([found[index, is_out] for index in range(layers)])) * scale for is_out in (False, True)
        )
        return (jnp.concatenate([own, other]) * scale)[None], grad_conv, grad_out
    chunks = [part.run_chain([other] if part is parts[0] else ()) for part in parts]
    conv_rows, out_rows = 2 * channels // tm, channels // tm
    grad_inputs, grad_conv, grad_out = pl.pallas_call(
        functools.partial(last_kernel, [len(terms) for terms in chunks], float(samples_all), tm),
        out_shape=[
            jax.ShapeDtypeStruct((length, channels), jnp.float32),
            jax.ShapeDtypeStruct((layers, conv_rows, LANES), jnp.float32),
            jax.ShapeDtypeStruct((layers, out_rows, LANES), jnp.float32),
        ],
        compiler_params=pltpu.CompilerParams(vmem_limit_bytes=ADD_BYTES),
        name="scale_all",
    )(*held([term for terms in chunks for term in terms]), *held([other, own]))
    return grad_inputs[None], grad_conv, grad_out


def solution(mesh):
    placed = (
        P("dp", "tm", None),
        P("dp", "tm", None),
        P("dp", "tm", None),
        P("dp", "tm"),
        P(),
        P(),
    )
    return jax.shard_map(
        body,
        mesh=mesh,
        in_specs=placed,
        out_specs=(P("dp", "tm", None), P(None, "tm", "dp"), P(None, "tm", "dp")),
        check_vma=False,
    )
```

```python
import functools

import jax
import jax.numpy as jnp
from jax import lax
from jax.experimental import pallas as pl
from jax.experimental.pallas import tpu as pltpu
from jax.sharding import PartitionSpec as P

LANES = 128
VMEM_BYTES = 24 * 1024 * 1024
ADD_BYTES = 8 * 1024 * 1024
CHAINS = (("y", "x", "z0", "z1"), ("x", "z0", "y", "z1"), ("z0", "y", "x", "z1"))
EXTRA = (0, 0, 16)
NN = (((1,), (0,)), ((), ()))
NT = (((1,), (1,)), ((), ()))
TN = (((0,), (0,)), ((), ()))


def dot(left, right, dims):
    return lax.dot_general(left, right, dims, preferred_element_type=jnp.float32)


def held(arrays, space=pltpu.VMEM):
    return [pltpu.with_memory_space_constraint(x, space) for x in arrays]


def around(x, axis, by):
    count = lax.axis_size(axis)
    return lax.ppermute(x, axis, [(i, (i + by) % count) for i in range(count)])


def column(row, rows):
    return jnp.broadcast_to(row, (LANES, rows)).T


def cost(flops, moved):
    return pl.CostEstimate(flops=flops, bytes_accessed=moved, transcendentals=0)


def pack_kernel(tail_x, tail_gs, tail_gk, weight, message):
    halo, channels = tail_gs.shape
    by_row = column(weight[...], LANES)[LANES - halo :]
    by_row = jnp.concatenate([by_row] * (channels // LANES), axis=1)
    message[0 : 2 * halo] = tail_x[...]
    message[2 * halo : 3 * halo] = (tail_gs[...].astype(jnp.float32) * by_row).astype(jnp.bfloat16)
    message[3 * halo :] = (tail_gk[...].astype(jnp.float32) * by_row).astype(jnp.bfloat16)


def pack(halo, x, grad_stream_out, grad_skip_out, weight):
    length, channels = x.shape

    def last(rows):
        return pl.BlockSpec((rows, channels), lambda i: (length // rows - 1, 0))

    return pl.pallas_call(
        pack_kernel,
        grid=(1,),
        in_specs=[last(2 * halo), last(halo), last(halo), pl.BlockSpec((1, LANES), lambda i: (0, length // LANES - 1))],
        out_specs=pl.BlockSpec((4 * halo, channels), lambda i: (0, 0)),
        out_shape=jax.ShapeDtypeStruct((4 * halo, channels), jnp.bfloat16),
        compiler_params=pltpu.CompilerParams(vmem_limit_bytes=ADD_BYTES),
        name="pack_borders",
    )(*held((x, grad_stream_out, grad_skip_out, weight), pltpu.HBM))


def load_kernel(
    x, gs, gk, weight, conv_w, out_w, _, x_here, grad_stream, grad_skip, sums, conv_here, out_here,
    gs_raw, gk_raw, weight_here, sems,
):
    pairs = ((weight, weight_here), (gs, gs_raw), (gk, gk_raw), (x, x_here), (conv_w, conv_here), (out_w, out_here))
    copies = [pltpu.make_async_copy(a, b, sems.at[i]) for i, (a, b) in enumerate(pairs)]
    for copy in copies:
        copy.start()
    for copy in copies[:3]:
        copy.wait()
    length, channels = x_here.shape
    by_row = column(weight_here[...], length)
    by_row = jnp.concatenate([by_row] * (channels // LANES), axis=1)
    grad_stream[...] = gs_raw[...].astype(jnp.float32) * by_row
    grad_skip[...] = (gk_raw[...].astype(jnp.float32) * by_row).astype(jnp.bfloat16)
    own_sum = jnp.broadcast_to(jnp.sum(weight_here[...], axis=1, keepdims=True), (1, LANES))
    sums[...] = split_rows(own_sum)
    for copy in copies[3:]:
        copy.wait()


def load_all(x, gs, gk, weight, conv_w, out_w, after):
    shape = x.shape
    vmem, anywhere = pl.BlockSpec(memory_space=pltpu.VMEM), pl.BlockSpec(memory_space=pl.ANY)
    return pl.pallas_call(
        load_kernel,
        in_specs=[anywhere] * 7,
        out_specs=[vmem] * 6,
        out_shape=[
            pltpu.VMEM(shape, jnp.bfloat16),
            pltpu.VMEM(shape, jnp.float32),
            pltpu.VMEM(shape, jnp.bfloat16),
            pltpu.VMEM((16, LANES), jnp.bfloat16),
            pltpu.VMEM(conv_w.shape, jnp.bfloat16),
            pltpu.VMEM(out_w.shape, jnp.bfloat16),
        ],
        scratch_shapes=[
            pltpu.VMEM(shape, jnp.bfloat16),
            pltpu.VMEM(shape, jnp.bfloat16),
            pltpu.VMEM(weight.shape, jnp.float32),
            pltpu.SemaphoreType.DMA((6,)),
        ],
        compiler_params=pltpu.CompilerParams(vmem_limit_bytes=ADD_BYTES),
        cost_estimate=cost(10**7, 6 * 10**6),
        name="load_all",
    )(*held((x, gs, gk, weight, conv_w, out_w), pltpu.HBM), *held([after]))


def split_rows(total):
    high = total.astype(jnp.bfloat16).astype(jnp.float32)
    middle = (total - high).astype(jnp.bfloat16).astype(jnp.float32)
    low = total - high - middle
    row = lax.broadcasted_iota(jnp.int32, (16, LANES), 0)
    rows = jnp.where(row == 0, high, jnp.where(row == 1, middle, jnp.where(row == 2, low, 0.0)))
    return rows.astype(jnp.bfloat16)


def joined_rows(rows):
    return jnp.sum(rows.astype(jnp.float32), axis=0, keepdims=True)


def cut_off(rows, dilation):
    row = lax.broadcasted_iota(jnp.int32, rows.shape, 0)
    return jnp.where(jnp.logical_and(row < dilation, lax.axis_index("tm") == 0), 0.0, rows)


def items_of(layers, chunk):
    third = layers // len(CHAINS)
    high = layers - chunk * third
    items = []
    for index in reversed(range(high - third, high)):
        items.append((index, False))
        if chunk == 0 or index < high - 1:
            items.append((index, True))
    return items + ([(high - third - 1, True)] if high > third else [])


def earlier_rows(plan, index, present, first, last):
    dilation, begin = 2**index, 2 * plan["halo"]
    cut = cut_off(present[begin - dilation : begin], dilation)
    return jnp.concatenate([present[first - dilation : begin - dilation], cut, present[begin : last - dilation]])


def backward(plan, layers, refs_of, conv_w, out_w, grad_proj, grad_stream, past_part, grad_parts):
    halo, length, channels = plan["halo"], plan["length"], plan["channels"]
    own = slice(halo, halo + length)
    items = plan["items"]

    def out_grad(index):
        if (index, True) in items:
            total = dot(refs_of(index)[3][own], grad_proj[0:length], TN)
            plan["store"](total, items.index((index, True)), grad_parts)

    for index in layers:
        dilation, count = 2**index, plan["counts"][index]
        present, earlier, factors, _ = refs_of(index)
        grad_proj[0:count, :channels] = grad_stream[0:count].astype(jnp.bfloat16)
        grad_gated = dot(grad_proj[0:count], out_w[index], NT)
        out_grad(index)
        both = factors[halo : halo + count].astype(jnp.float32)
        grad_preact = jnp.concatenate(
            [grad_gated * both[:, :channels], grad_gated * both[:, channels:]], axis=1
        ).astype(jnp.bfloat16)
        spread = dot(grad_preact, conv_w[index], NT)
        past_part[0:count] = spread[:, channels:]
        cut = slice(halo, halo + max(dilation, 8))
        past_part[cut] = cut_off(past_part[cut], dilation)
        rows = plan["counts"][index - 1] if index else length
        grad_stream[0:rows] += spread[0:rows, :channels] + past_part[dilation : dilation + rows]
        past = earlier_rows(plan, index, present, halo, halo + length) if earlier is None else earlier[own]
        total = dot(jnp.concatenate([present[own], past], axis=1), grad_preact[0:length], TN)
        plan["store"](total, items.index((index, False)), grad_parts)
    after = layers[-1] - 1
    if (after, True) in items:
        grad_proj[0:length, :channels] = grad_stream[0:length].astype(jnp.bfloat16)
        out_grad(after)


def first_kernel(
    plan, prev_rows, own_x, own_grad, own_skip, conv_w, out_w,
    low_present, low_earlier, low_factors, low_gates, grad_stream, grad_skip, *rest,
):
    *grad_parts, stream, high_present, high_factors, high_gates, grad_proj, past_part = rest
    halo, (length, channels) = plan["halo"], own_x.shape
    layers, low = conv_w.shape[0], low_gates.shape[0]
    pad = 2 ** (layers - 1)
    extent = length + 2 * halo
    begin = 2 * halo
    stream[0:pad] = jnp.zeros((pad, channels), jnp.float32)
    stream[pad : pad + begin] = prev_rows[0:begin].astype(jnp.float32)
    stream[pad + begin :] = own_x[...].astype(jnp.float32)

    def refs_of(index):
        if index < low:
            return low_present.at[index], low_earlier.at[index], low_factors.at[index], low_gates.at[index]
        at = index - low
        return high_present.at[at], None, high_factors.at[at], high_gates.at[at]

    refs_of(0)[0][0:begin] = prev_rows[0:begin]
    refs_of(0)[0][begin:] = own_x[...]
    for index in range(layers):
        dilation, start = 2**index, plan["starts"][index]
        present, earlier, factor, gate = refs_of(index)
        if earlier is None:
            past = earlier_rows(plan, index, present, start, extent)
        else:
            past = stream[pad + start - dilation : pad + extent - dilation]
            cut = cut_off(past[begin - start : begin - start + 16], dilation)
            past = jnp.concatenate([past[: begin - start], cut, past[begin - start + 16 :]]).astype(jnp.bfloat16)
            earlier[start:] = past
        preact = dot(jnp.concatenate([present[start:], past], axis=1), conv_w[index], NN)
        filtered = jnp.tanh(preact[:, :channels])
        opening = 0.5 + 0.5 * jnp.tanh(0.5 * preact[:, channels:])
        product = filtered * opening
        gated = product.astype(jnp.bfloat16)
        gate[start:] = gated
        factor[start:, :channels] = (opening - filtered * product).astype(jnp.bfloat16)
        factor[start:, channels:] = (product * (1.0 - opening)).astype(jnp.bfloat16)
        if index < layers - 1:
            after = stream[pad + start :] + dot(gated, out_w[index, :, :channels], NN)
            refs_of(index + 1)[0][start:] = after.astype(jnp.bfloat16)
            if index < layers - 2:
                stream[pad + start :] = after

    grad_stream[0:halo] = prev_rows[2 * halo : 3 * halo].astype(jnp.float32)
    grad_stream[halo:] = own_grad[...]
    grad_skip[0:halo] = prev_rows[3 * halo :]
    grad_skip[halo:] = own_skip[...]
    grad_proj[:, channels:] = grad_skip[...]
    backward(
        plan, list(reversed(range(low, layers))), refs_of, conv_w, out_w, grad_proj, grad_stream, past_part, grad_parts
    )


def later_kernel(
    plan, first, third, present, earlier, factors, gates, grad_before, grad_skip, sums, conv_w, out_w, *rest
):
    *outs, keep, send, grad_stream, grad_proj, past_part = rest[plan["unused"] :]
    channels = plan["channels"]
    halves = outs[plan["outs"] :]
    outs = outs[: plan["outs"]]
    grad_stream[...] = grad_before[...]
    grad_proj[:, channels:] = grad_skip[...]

    def refs_of(index):
        return present.at[index], earlier.at[index], factors.at[index], gates.at[index]

    backward(
        plan, list(reversed(range(first, first + third))), refs_of, conv_w, out_w,
        grad_proj, grad_stream, past_part, (keep, send),
    )
    at = 0
    for out in outs:
        out[...] = grad_stream[at : at + out.shape[0]].astype(out.dtype)
        at += out.shape[0]
    plan["finish"](sums, (keep, send))
    for i, half in enumerate(halves):
        half[...] = send[i]


def store_whole(items, total, item, grad_parts):
    is_out = items[item][1]
    place = sum(kind == is_out for _, kind in items[:item])
    grad_parts[int(is_out)][place] = total.astype(jnp.bfloat16)


def finish_whole(sums, grad_parts):
    pass


def finish_shards(extra, sums, grad_parts):
    for part in grad_parts:
        lead, rows = part.shape[:-2], part.shape[-2]
        for first in range(rows - extra, rows, 16):
            part[(slice(None),) * len(lead) + (slice(first, first + 16),)] = jnp.broadcast_to(
                sums[...], lead + sums.shape
            )


def store_shards(tm, dp, order, bases, total, item, grad_parts):
    keep, send = grad_parts
    t_at, d_at = lax.axis_index("tm"), lax.axis_index("dp")
    core_at = lax.rem(d_at, 2)
    rows = total.shape[0] // tm
    at = pl.ds(bases[item], rows)
    at_bits = bits_of(t_at, d_at, lax.rem, lax.div)
    for y in range(dp // 2):
        near = total[:, (2 * y) * LANES : (2 * y + 1) * LANES]
        far = total[:, (2 * y + 1) * LANES : (2 * y + 2) * LANES]
        mine = jnp.where(core_at == 0, near, far).astype(jnp.bfloat16)
        other = jnp.where(core_at == 0, far, near).astype(jnp.bfloat16)
        for t in range(tm):
            bits = bits_of(t, 2 * y, lambda a, b: a % b, lambda a, b: a // b)
            lead = tuple(lax.rem(bits[name] + at_bits[name], 2) for name in order)
            keep[lead + (at,)] = mine[t * rows : (t + 1) * rows]
            send[lead + (at,)] = other[t * rows : (t + 1) * rows]


def bits_of(t, d, rem, div):
    return {"x": rem(t, 2), "z0": rem(div(t, 2), 2), "z1": div(t, 4), "y": div(d, 2)}


def bases_of(items, tm, channels):
    ends = [0]
    for _, is_out in items:
        ends.append(ends[-1] + (1 if is_out else 2) * channels // tm)
    return ends[:-1], ends[-1]


def run_layers(in_shards, tm, dp, halo, prev_rows, loaded):
    own_x, own_grad, own_skip, sums, conv_w, out_w = loaded
    length, channels = own_x.shape
    layers = conv_w.shape[0]
    third = layers // len(CHAINS)
    low = layers - third
    extent, border = length + 2 * halo, length + halo
    starts = []
    for index in range(layers):
        need = halo if index == layers - 1 else 2 ** (index + 1)
        starts.append(need // 16 * 16)
    counts = [-(-(length + 2 ** (index + 1) - 1) // 16) * 16 for index in range(layers)]
    plan = {"halo": halo, "starts": starts, "counts": counts, "length": length, "channels": channels, "unused": 0}
    plans, shapes = [], []
    for chunk, order in enumerate(CHAINS):
        items = items_of(layers, chunk)
        bases, rows = bases_of(items, tm, channels)
        if in_shards:
            store = functools.partial(store_shards, tm, dp, order, bases)
            finish = functools.partial(finish_shards, EXTRA[chunk])
            shapes.append(2 * [(2,) * len(order) + (rows + EXTRA[chunk], LANES)])
        else:
            store, finish = functools.partial(store_whole, items), finish_whole
            outs = sum(is_out for _, is_out in items)
            shapes.append([(len(items) - outs,) + conv_w.shape[1:], (outs,) + out_w.shape[1:]])
        plans.append(plan | {"items": items, "store": store, "finish": finish})
    vmem, anywhere = pl.BlockSpec(memory_space=pltpu.VMEM), pl.BlockSpec(memory_space=pl.ANY)
    weight_bytes = 2 * (conv_w.size + out_w.size)
    flops = 2 * length * channels * channels
    *kept, grad_stream, grad_skip, keep, send = pl.pallas_call(
        functools.partial(first_kernel, plans[0]),
        in_specs=[vmem] * 6,
        out_specs=[vmem] * 8,
        out_shape=[
            pltpu.VMEM((low, extent, channels), jnp.bfloat16),
            pltpu.VMEM((low, extent, channels), jnp.bfloat16),
            pltpu.VMEM((low, extent, 2 * channels), jnp.bfloat16),
            pltpu.VMEM((low, extent, channels), jnp.bfloat16),
            pltpu.VMEM((border, channels), jnp.float32),
            pltpu.VMEM((border, channels), jnp.bfloat16),
        ]
        + [pltpu.VMEM(shape, jnp.bfloat16) for shape in shapes[0]],
        scratch_shapes=[
            pltpu.VMEM((2 ** (layers - 1) + extent, channels), jnp.float32),
            pltpu.VMEM((third, extent, channels), jnp.bfloat16),
            pltpu.VMEM((third, extent, 2 * channels), jnp.bfloat16),
            pltpu.VMEM((third, extent, channels), jnp.bfloat16),
            pltpu.VMEM((border, 2 * channels), jnp.bfloat16),
            pltpu.VMEM((border, channels), jnp.float32),
        ],
        compiler_params=pltpu.CompilerParams(vmem_limit_bytes=VMEM_BYTES),
        cost_estimate=cost(flops * (5 * layers + 12 * third), weight_bytes),
        name="forward_and_last_third",
    )(*held((prev_rows, own_x, own_grad, own_skip, conv_w, out_w)))

    def later(step, outs, after):
        more = {"unused": len(after), "outs": len(outs)}
        split = in_shards and step == len(CHAINS) - 1
        keep, send = (pltpu.VMEM(shape, jnp.bfloat16) for shape in shapes[step])
        halves = [pltpu.VMEM(shapes[step][1][1:], jnp.bfloat16)] * 2
        return pl.pallas_call(
            functools.partial(later_kernel, plans[step] | more, layers - (step + 1) * third, third),
            in_specs=[vmem] * 9 + [anywhere] * len(after),
            out_specs=[vmem] * (len(outs) + (3 if split else 2)),
            out_shape=[pltpu.VMEM((rows, channels), kind) for rows, kind in outs]
            + (halves + [keep] if split else [keep, send]),
            scratch_shapes=([send] if split else [])
            + [
                pltpu.VMEM((border, channels), jnp.float32),
                pltpu.VMEM((border, 2 * channels), jnp.bfloat16),
                pltpu.VMEM((border, channels), jnp.float32),
            ],
            compiler_params=pltpu.CompilerParams(vmem_limit_bytes=VMEM_BYTES),
            cost_estimate=cost(flops * 12 * third, weight_bytes),
            name="middle_third" if step == 1 else "first_third",
        )(*held((*kept, grad_stream, grad_skip, sums, conv_w, out_w, *after)))

    parts = [(keep, send)]
    if in_shards:
        parts[0] = Chunk(tm, dp, 0, keep, [send])
    grad_stream, *middle = later(1, [(border, jnp.float32)], [])
    other, own, *last = later(
        2, [(halo, jnp.bfloat16), (length - halo, jnp.float32)], [parts[0].next_message()] if in_shards else []
    )
    parts += [middle, last]
    if in_shards:
        parts[1] = Chunk(tm, dp, 1, middle[0], middle[1:])
        parts[2] = Chunk(tm, dp, 2, last[-1], last[:-1])
    return other, own, parts


def add_kernel(count, groups, *refs):
    arrays, outs = refs[:count], refs[-len(groups) :]
    for out, pieces in zip(outs, groups):
        lead = (slice(None),) * (len(out.shape) - 2)
        for first, rows, with_total, terms in pieces:
            body = rows - 16 if with_total else rows
            value = 0.0
            for array, at, begin in terms:
                value = value + arrays[array][at + lead + (slice(begin, begin + body),)].astype(jnp.float32)
            out[lead + (slice(first, first + body),)] = value.astype(out.dtype)
            if with_total:
                total = 0.0
                for array, at, begin in terms:
                    rows_at = slice(begin + body, begin + rows)
                    total = total + joined_rows(arrays[array][at + (0,) * len(lead) + (rows_at,)])
                slab = split_rows(total)
                out[lead + (slice(first + body, first + rows),)] = jnp.broadcast_to(slab, out.shape[:-2] + slab.shape)


def add_up(arrays, groups, shapes, after, name):
    vmem = pl.BlockSpec(memory_space=pltpu.VMEM)
    return pl.pallas_call(
        functools.partial(add_kernel, len(arrays), groups),
        in_specs=[vmem] * len(arrays) + [pl.BlockSpec(memory_space=pl.ANY)] * len(after),
        out_specs=[vmem] * len(groups),
        out_shape=[pltpu.VMEM(shape, jnp.bfloat16) for shape in shapes],
        compiler_params=pltpu.CompilerParams(vmem_limit_bytes=ADD_BYTES),
        name=name,
    )(*held(arrays), *held(after))


def first_block(array, first, rows):
    return array[(0,) * (len(array.shape) - 2) + (slice(first, first + rows),)].astype(jnp.float32)


def first_block(array, first, rows):
    return array[(0,) * (len(array.shape) - 2) + (slice(first, first + rows),)].astype(jnp.float32)


def last_kernel(counts, samples_all, tm, *refs):
    chunks = []
    for count in counts:
        chunks.append(refs[:count])
        refs = refs[count:]
    other, own, grad_inputs, grad_conv, grad_out = refs
    layers, channels = grad_conv.shape[0], own.shape[1]
    total = 0.0
    for term in chunks[-1]:
        total = total + jnp.sum(first_block(term, term.shape[-2] - 16, 16), axis=0, keepdims=True)
    scale = samples_all / total
    for chunk, terms in enumerate(chunks):
        items = items_of(layers, chunk)
        for (index, is_out), base in zip(items, bases_of(items, tm, channels)[0]):
            out = grad_out if is_out else grad_conv
            value = 0.0
            for term in terms:
                value = value + first_block(term, base, out.shape[1])
            out[index] = value * scale
    for first in range(0, channels, LANES):
        lanes = slice(first, first + LANES)
        grad_inputs[0 : own.shape[0], lanes] = own[:, lanes] * scale
        grad_inputs[own.shape[0] :, lanes] = other[:, lanes].astype(jnp.float32) * scale


class Chunk:
    def __init__(self, tm, dp, chunk, keep, sends):
        self.tm, self.dp, self.chunk, self.rows = tm, dp, chunk, keep.shape[-2]
        self.message = None
        there = [swapped(tm, dp, send, "core") for send in reversed(sends)]
        self.terms = [keep, there[-1]]
        self.first_terms = [keep, there[0]]

    def next_message(self, after=()):
        if self.message is None:
            left = len(CHAINS[self.chunk]) + 2 - len(self.terms)
            terms = self.first_terms if len(self.terms) == 2 else self.terms
            pieces = []
            for i, v in enumerate(terms):
                more = len(v.shape) - 2 - left
                pieces.append((i, () if more < 0 else (0,) * more + (1,), 0))
            (self.message,) = add_up(
                terms, [[(0, self.rows, EXTRA[self.chunk] > 0, pieces)]], [(2,) * (left - 1) + (self.rows, LANES)], after,
                "add_chunk%d_step%d" % (self.chunk, len(self.terms) - 1),
            )
        return self.message

    def run_chain(self, after=()):
        for step, name in enumerate(CHAINS[self.chunk]):
            self.terms.append(swapped(self.tm, self.dp, self.next_message(after if step == 1 else ()), name))
            self.message = None
        return self.terms


def swapped(tm, dp, value, name):
    over_t, over_d = {"core": (0, 1), "y": (0, 2), "x": (1, 0), "z0": (2, 0), "z1": (4, 0)}[name]
    pairs = [(t * dp + d, (t ^ over_t) * dp + (d ^ over_d)) for t in range(tm) for d in range(dp)]
    return lax.ppermute(value, ("tm", "dp"), pairs)


def scattered(part):
    columns = lax.psum_scatter(part, "dp", scatter_dimension=2, tiled=True).astype(jnp.float32)
    return lax.psum_scatter(columns, "tm", scatter_dimension=1, tiled=True)


def body(inputs, grad_stream_out, grad_skip_out, sample_weight, conv_weight, out_weight):
    tm, dp = lax.axis_size("tm"), lax.axis_size("dp")
    batch, length, channels = inputs.shape
    layers = conv_weight.shape[0]
    third = layers // len(CHAINS)
    halo = 2**layers
    samples_all = batch * length * tm * dp
    x, gs, gk = inputs[0], grad_stream_out[0], grad_skip_out[0]
    message = pack(halo, x, gs, gk, sample_weight)
    prev_rows = around(message, "tm", 1)
    loaded = load_all(x, gs, gk, sample_weight, conv_weight, out_weight, message)
    in_shards = tm == 8 and dp == 4 and channels // tm % 16 == 0 and 2 * channels == dp * LANES
    other, own, parts = run_layers(in_shards, tm, dp, halo, prev_rows, loaded)
    other = around(other, "tm", -1)
    if not in_shards:
        scale = samples_all / lax.psum(jnp.sum(sample_weight), ("tm", "dp"))
        found = {}
        for chunk, part in enumerate(parts):
            items = items_of(layers, chunk)
            for is_out in (False, True):
                for place, item in enumerate(item for item in items if item[1] == is_out):
                    found[item] = part[int(is_out)][place]
        grad_conv, grad_out = (
            scattered(jnp.stack([found[index, is_out] for index in range(layers)])) * scale for is_out in (False, True)
        )
        return (jnp.concatenate([own, other]) * scale)[None], grad_conv, grad_out
    chunks = [part.run_chain([other] if part is parts[0] else ()) for part in parts]
    conv_rows, out_rows = 2 * channels // tm, channels // tm
    grad_inputs, grad_conv, grad_out = pl.pallas_call(
        functools.partial(last_kernel, [len(terms) for terms in chunks], float(samples_all), tm),
        out_shape=[
            jax.ShapeDtypeStruct((length, channels), jnp.float32),
            jax.ShapeDtypeStruct((layers, conv_rows, LANES), jnp.float32),
            jax.ShapeDtypeStruct((layers, out_rows, LANES), jnp.float32),
        ],
        compiler_params=pltpu.CompilerParams(vmem_limit_bytes=ADD_BYTES),
        name="scale_all",
    )(*held([term for terms in chunks for term in terms]), *held([other, own]))
    return grad_inputs[None], grad_conv, grad_out


def solution(mesh):
    placed = (
        P("dp", "tm", None),
        P("dp", "tm", None),
        P("dp", "tm", None),
        P("dp", "tm"),
        P(),
        P(),
    )
    return jax.shard_map(
        body,
        mesh=mesh,
        in_specs=placed,
        out_specs=(P("dp", "tm", None), P(None, "tm", "dp"), P(None, "tm", "dp")),
        check_vma=False,
    )
```

```python
import functools

import jax
import jax.numpy as jnp
from jax import lax
from jax.experimental import pallas as pl
from jax.experimental.pallas import tpu as pltpu
from jax.sharding import PartitionSpec as P

LANES = 128
VMEM_BYTES = 24 * 1024 * 1024
ADD_BYTES = 8 * 1024 * 1024
CHAINS = (("y", "x", "z0", "z1"), ("x", "z0", "y", "z1"), ("z0", "y", "x", "z1"))
EXTRA = (0, 0, 16)
NN = (((1,), (0,)), ((), ()))
NT = (((1,), (1,)), ((), ()))
TN = (((0,), (0,)), ((), ()))


def dot(left, right, dims):
    return lax.dot_general(left, right, dims, preferred_element_type=jnp.float32)


def held(arrays, space=pltpu.VMEM):
    return [pltpu.with_memory_space_constraint(x, space) for x in arrays]


def around(x, axis, by):
    count = lax.axis_size(axis)
    return lax.ppermute(x, axis, [(i, (i + by) % count) for i in range(count)])


def column(row, rows):
    return jnp.broadcast_to(row, (LANES, rows)).T


def cost(flops, moved):
    return pl.CostEstimate(flops=flops, bytes_accessed=moved, transcendentals=0)


def pack_kernel(tail_x, tail_gs, tail_gk, weight, message):
    halo, channels = tail_gs.shape
    by_row = column(weight[...], LANES)[LANES - halo :]
    by_row = jnp.concatenate([by_row] * (channels // LANES), axis=1)
    message[0 : 2 * halo] = tail_x[...]
    message[2 * halo : 3 * halo] = (tail_gs[...].astype(jnp.float32) * by_row).astype(jnp.bfloat16)
    message[3 * halo :] = (tail_gk[...].astype(jnp.float32) * by_row).astype(jnp.bfloat16)


def pack(halo, x, grad_stream_out, grad_skip_out, weight):
    length, channels = x.shape

    def last(rows):
        return pl.BlockSpec((rows, channels), lambda i: (length // rows - 1, 0))

    return pl.pallas_call(
        pack_kernel,
        grid=(1,),
        in_specs=[last(2 * halo), last(halo), last(halo), pl.BlockSpec((1, LANES), lambda i: (0, length // LANES - 1))],
        out_specs=pl.BlockSpec((4 * halo, channels), lambda i: (0, 0)),
        out_shape=jax.ShapeDtypeStruct((4 * halo, channels), jnp.bfloat16),
        compiler_params=pltpu.CompilerParams(vmem_limit_bytes=ADD_BYTES),
        name="pack_borders",
    )(*held((x, grad_stream_out, grad_skip_out, weight), pltpu.HBM))


def load_kernel(
    x, gs, gk, weight, conv_w, out_w, _, x_here, grad_stream, grad_skip, sums, conv_here, out_here,
    gs_raw, gk_raw, weight_here, sems,
):
    pairs = ((weight, weight_here), (gs, gs_raw), (gk, gk_raw), (x, x_here), (conv_w, conv_here), (out_w, out_here))
    copies = [pltpu.make_async_copy(a, b, sems.at[i]) for i, (a, b) in enumerate(pairs)]
    for copy in copies:
        copy.start()
    for copy in copies[:3]:
        copy.wait()
    length, channels = x_here.shape
    by_row = column(weight_here[...], length)
    by_row = jnp.concatenate([by_row] * (channels // LANES), axis=1)
    grad_stream[...] = gs_raw[...].astype(jnp.float32) * by_row
    grad_skip[...] = (gk_raw[...].astype(jnp.float32) * by_row).astype(jnp.bfloat16)
    own_sum = jnp.broadcast_to(jnp.sum(weight_here[...], axis=1, keepdims=True), (1, LANES))
    sums[...] = split_rows(own_sum)
    for copy in copies[3:]:
        copy.wait()


def load_all(x, gs, gk, weight, conv_w, out_w, after):
    shape = x.shape
    vmem, anywhere = pl.BlockSpec(memory_space=pltpu.VMEM), pl.BlockSpec(memory_space=pl.ANY)
    return pl.pallas_call(
        load_kernel,
        in_specs=[anywhere] * 7,
        out_specs=[vmem] * 6,
        out_shape=[
            pltpu.VMEM(shape, jnp.bfloat16),
            pltpu.VMEM(shape, jnp.float32),
            pltpu.VMEM(shape, jnp.bfloat16),
            pltpu.VMEM((16, LANES), jnp.bfloat16),
            pltpu.VMEM(conv_w.shape, jnp.bfloat16),
            pltpu.VMEM(out_w.shape, jnp.bfloat16),
        ],
        scratch_shapes=[
            pltpu.VMEM(shape, jnp.bfloat16),
            pltpu.VMEM(shape, jnp.bfloat16),
            pltpu.VMEM(weight.shape, jnp.float32),
            pltpu.SemaphoreType.DMA((6,)),
        ],
        compiler_params=pltpu.CompilerParams(vmem_limit_bytes=ADD_BYTES),
        cost_estimate=cost(10**7, 6 * 10**6),
        name="load_all",
    )(*held((x, gs, gk, weight, conv_w, out_w), pltpu.HBM), *held([after]))


def split_rows(total):
    high = total.astype(jnp.bfloat16).astype(jnp.float32)
    middle = (total - high).astype(jnp.bfloat16).astype(jnp.float32)
    low = total - high - middle
    row = lax.broadcasted_iota(jnp.int32, (16, LANES), 0)
    rows = jnp.where(row == 0, high, jnp.where(row == 1, middle, jnp.where(row == 2, low, 0.0)))
    return rows.astype(jnp.bfloat16)


def joined_rows(rows):
    return jnp.sum(rows.astype(jnp.float32), axis=0, keepdims=True)


def cut_off(rows, dilation):
    row = lax.broadcasted_iota(jnp.int32, rows.shape, 0)
    return jnp.where(jnp.logical_and(row < dilation, lax.axis_index("tm") == 0), 0.0, rows)


def items_of(layers, chunk):
    third = layers // len(CHAINS)
    high = layers - chunk * third
    items = []
    for index in reversed(range(high - third, high)):
        items.append((index, False))
        if chunk == 0 or index < high - 1:
            items.append((index, True))
    return items + ([(high - third - 1, True)] if high > third else [])


def row_blocks(first, last):
    middle = first + (last - first) // 32 * 16
    return ((middle, last), (first, middle))


def earlier_rows(plan, index, present, first, last):
    dilation, begin = 2**index, 2 * plan["halo"]
    if first >= begin + dilation or last <= begin:
        return present[first - dilation : last - dilation]
    cut = cut_off(present[begin - dilation : begin], dilation)
    return jnp.concatenate([present[first - dilation : begin - dilation], cut, present[begin : last - dilation]])


def backward(plan, layers, refs_of, conv_w, out_w, grad_proj, grad_preact, grad_stream, past_part, grad_parts):
    halo, length, channels = plan["halo"], plan["length"], plan["channels"]
    own = slice(halo, halo + length)
    items = plan["items"]

    def out_grad(index):
        if (index, True) in items:
            total = dot(refs_of(index)[3][own], grad_proj[0:length], TN)
            plan["store"](total, items.index((index, True)), grad_parts)

    for index in layers:
        dilation, count = 2**index, plan["counts"][index]
        rows = plan["counts"][index - 1] if index else length
        present, earlier, factors, _ = refs_of(index)
        for a, b in row_blocks(0, count):
            grad_proj[a:b, :channels] = grad_stream[a:b].astype(jnp.bfloat16)
            grad_gated = dot(grad_proj[a:b], out_w[index], NT)
            both = factors[halo + a : halo + b].astype(jnp.float32)
            grad_preact[a:b] = jnp.concatenate(
                [grad_gated * both[:, :channels], grad_gated * both[:, channels:]], axis=1
            ).astype(jnp.bfloat16)
            spread = dot(grad_preact[a:b], conv_w[index], NT)
            past_part[a:b] = spread[:, channels:]
            if a <= halo < b:
                cut = slice(halo, halo + max(dilation, 8))
                past_part[cut] = cut_off(past_part[cut], dilation)
            c = min(b, rows)
            grad_stream[a:c] += spread[0 : c - a, :channels] + past_part[a + dilation : c + dilation]
        out_grad(index)
        past = earlier_rows(plan, index, present, halo, halo + length) if earlier is None else earlier[own]
        total = dot(jnp.concatenate([present[own], past], axis=1), grad_preact[0:length], TN)
        plan["store"](total, items.index((index, False)), grad_parts)
    after = layers[-1] - 1
    if (after, True) in items:
        grad_proj[0:length, :channels] = grad_stream[0:length].astype(jnp.bfloat16)
        out_grad(after)


def first_kernel(
    plan, prev_rows, own_x, own_grad, own_skip, conv_w, out_w,
    low_present, low_earlier, low_factors, low_gates, grad_stream, grad_skip, *rest,
):
    *grad_parts, stream, high_present, high_factors, high_gates, grad_proj, grad_preact, past_part = rest
    halo, (length, channels) = plan["halo"], own_x.shape
    layers, low = conv_w.shape[0], low_gates.shape[0]
    pad = 2 ** (layers - 1)
    extent = length + 2 * halo
    begin = 2 * halo
    stream[0:pad] = jnp.zeros((pad, channels), jnp.float32)
    stream[pad : pad + begin] = prev_rows[0:begin].astype(jnp.float32)
    stream[pad + begin :] = own_x[...].astype(jnp.float32)

    def refs_of(index):
        if index < low:
            return low_present.at[index], low_earlier.at[index], low_factors.at[index], low_gates.at[index]
        at = index - low
        return high_present.at[at], None, high_factors.at[at], high_gates.at[at]

    refs_of(0)[0][0:begin] = prev_rows[0:begin]
    refs_of(0)[0][begin:] = own_x[...]
    for index in range(layers):
        dilation = 2**index
        present, earlier, factor, gate = refs_of(index)
        for a, b in row_blocks(plan["starts"][index], extent):
            if earlier is None:
                past = earlier_rows(plan, index, present, a, b)
            else:
                past = stream[pad + a - dilation : pad + b - dilation]
                if a <= begin < b:
                    cut = cut_off(past[begin - a : begin - a + 16], dilation)
                    past = jnp.concatenate([past[: begin - a], cut, past[begin - a + 16 :]])
                past = past.astype(jnp.bfloat16)
                earlier[a:b] = past
            preact = dot(jnp.concatenate([present[a:b], past], axis=1), conv_w[index], NN)
            filtered = jnp.tanh(preact[:, :channels])
            opening = 0.5 + 0.5 * jnp.tanh(0.5 * preact[:, channels:])
            product = filtered * opening
            gated = product.astype(jnp.bfloat16)
            gate[a:b] = gated
            factor[a:b, :channels] = (opening - filtered * product).astype(jnp.bfloat16)
            factor[a:b, channels:] = (product * (1.0 - opening)).astype(jnp.bfloat16)
            if index < layers - 1:
                after = stream[pad + a : pad + b] + dot(gated, out_w[index, :, :channels], NN)
                refs_of(index + 1)[0][a:b] = after.astype(jnp.bfloat16)
                if index < layers - 2:
                    stream[pad + a : pad + b] = after

    grad_stream[0:halo] = prev_rows[2 * halo : 3 * halo].astype(jnp.float32)
    grad_stream[halo:] = own_grad[...]
    grad_skip[0:halo] = prev_rows[3 * halo :]
    grad_skip[halo:] = own_skip[...]
    grad_proj[:, channels:] = grad_skip[...]
    backward(
        plan, list(reversed(range(low, layers))), refs_of, conv_w, out_w,
        grad_proj, grad_preact, grad_stream, past_part, grad_parts,
    )


def later_kernel(
    plan, first, third, present, earlier, factors, gates, grad_before, grad_skip, sums, conv_w, out_w, *rest
):
    *outs, keep, send, grad_stream, grad_proj, grad_preact, past_part = rest[plan["unused"] :]
    channels = plan["channels"]
    grad_stream[...] = grad_before[...]
    grad_proj[:, channels:] = grad_skip[...]

    def refs_of(index):
        return present.at[index], earlier.at[index], factors.at[index], gates.at[index]

    backward(
        plan, list(reversed(range(first, first + third))), refs_of, conv_w, out_w,
        grad_proj, grad_preact, grad_stream, past_part, (keep, send),
    )
    at = 0
    for out in outs:
        out[...] = grad_stream[at : at + out.shape[0]].astype(out.dtype)
        at += out.shape[0]
    plan["finish"](sums, (keep, send))


def store_whole(items, total, item, grad_parts):
    is_out = items[item][1]
    place = sum(kind == is_out for _, kind in items[:item])
    grad_parts[int(is_out)][place] = total.astype(jnp.bfloat16)


def finish_whole(sums, grad_parts):
    pass


def finish_shards(extra, sums, grad_parts):
    for part in grad_parts:
        lead, rows = part.shape[:-2], part.shape[-2]
        for first in range(rows - extra, rows, 16):
            part[(slice(None),) * len(lead) + (slice(first, first + 16),)] = jnp.broadcast_to(
                sums[...], lead + sums.shape
            )


def store_shards(tm, dp, order, bases, total, item, grad_parts):
    keep, send = grad_parts
    t_at, d_at = lax.axis_index("tm"), lax.axis_index("dp")
    core_at = lax.rem(d_at, 2)
    rows = total.shape[0] // tm
    at = pl.ds(bases[item], rows)
    at_bits = bits_of(t_at, d_at, lax.rem, lax.div)
    for y in range(dp // 2):
        near = total[:, (2 * y) * LANES : (2 * y + 1) * LANES]
        far = total[:, (2 * y + 1) * LANES : (2 * y + 2) * LANES]
        mine = jnp.where(core_at == 0, near, far).astype(jnp.bfloat16)
        other = jnp.where(core_at == 0, far, near).astype(jnp.bfloat16)
        for t in range(tm):
            bits = bits_of(t, 2 * y, lambda a, b: a % b, lambda a, b: a // b)
            lead = tuple(lax.rem(bits[name] + at_bits[name], 2) for name in order)
            keep[lead + (at,)] = mine[t * rows : (t + 1) * rows]
            send[lead + (at,)] = other[t * rows : (t + 1) * rows]


def bits_of(t, d, rem, div):
    return {"x": rem(t, 2), "z0": rem(div(t, 2), 2), "z1": div(t, 4), "y": div(d, 2)}


def bases_of(items, tm, channels):
    ends = [0]
    for _, is_out in items:
        ends.append(ends[-1] + (1 if is_out else 2) * channels // tm)
    return ends[:-1], ends[-1]


def run_layers(in_shards, tm, dp, halo, prev_rows, loaded):
    own_x, own_grad, own_skip, sums, conv_w, out_w = loaded
    length, channels = own_x.shape
    layers = conv_w.shape[0]
    third = layers // len(CHAINS)
    low = layers - third
    extent, border = length + 2 * halo, length + halo
    starts = []
    for index in range(layers):
        need = halo if index == layers - 1 else 2 ** (index + 1)
        starts.append(need // 16 * 16)
    counts = [-(-(length + 2 ** (index + 1) - 1) // 16) * 16 for index in range(layers)]
    plan = {"halo": halo, "starts": starts, "counts": counts, "length": length, "channels": channels, "unused": 0}
    plans, shapes = [], []
    for chunk, order in enumerate(CHAINS):
        items = items_of(layers, chunk)
        bases, rows = bases_of(items, tm, channels)
        if in_shards:
            store = functools.partial(store_shards, tm, dp, order, bases)
            finish = functools.partial(finish_shards, EXTRA[chunk])
            shapes.append(2 * [(2,) * len(order) + (rows + EXTRA[chunk], LANES)])
        else:
            store, finish = functools.partial(store_whole, items), finish_whole
            outs = sum(is_out for _, is_out in items)
            shapes.append([(len(items) - outs,) + conv_w.shape[1:], (outs,) + out_w.shape[1:]])
        plans.append(plan | {"items": items, "store": store, "finish": finish})
    vmem, anywhere = pl.BlockSpec(memory_space=pltpu.VMEM), pl.BlockSpec(memory_space=pl.ANY)
    weight_bytes = 2 * (conv_w.size + out_w.size)
    flops = 2 * length * channels * channels
    *kept, grad_stream, grad_skip, keep, send = pl.pallas_call(
        functools.partial(first_kernel, plans[0]),
        in_specs=[vmem] * 6,
        out_specs=[vmem] * 8,
        out_shape=[
            pltpu.VMEM((low, extent, channels), jnp.bfloat16),
            pltpu.VMEM((low, extent, channels), jnp.bfloat16),
            pltpu.VMEM((low, extent, 2 * channels), jnp.bfloat16),
            pltpu.VMEM((low, extent, channels), jnp.bfloat16),
            pltpu.VMEM((border, channels), jnp.float32),
            pltpu.VMEM((border, channels), jnp.bfloat16),
        ]
        + [pltpu.VMEM(shape, jnp.bfloat16) for shape in shapes[0]],
        scratch_shapes=[
            pltpu.VMEM((2 ** (layers - 1) + extent, channels), jnp.float32),
            pltpu.VMEM((third, extent, channels), jnp.bfloat16),
            pltpu.VMEM((third, extent, 2 * channels), jnp.bfloat16),
            pltpu.VMEM((third, extent, channels), jnp.bfloat16),
            pltpu.VMEM((border, 2 * channels), jnp.bfloat16),
            pltpu.VMEM((border, 2 * channels), jnp.bfloat16),
            pltpu.VMEM((border, channels), jnp.float32),
        ],
        compiler_params=pltpu.CompilerParams(vmem_limit_bytes=VMEM_BYTES),
        cost_estimate=cost(flops * (5 * layers + 12 * third), weight_bytes),
        name="forward_and_last_third",
    )(*held((prev_rows, own_x, own_grad, own_skip, conv_w, out_w)))

    def later(step, outs, after):
        return pl.pallas_call(
            functools.partial(later_kernel, plans[step] | {"unused": len(after)}, layers - (step + 1) * third, third),
            in_specs=[vmem] * 9 + [anywhere] * len(after),
            out_specs=[vmem] * (len(outs) + 2),
            out_shape=[pltpu.VMEM((rows, channels), kind) for rows, kind in outs]
            + [pltpu.VMEM(shape, jnp.bfloat16) for shape in shapes[step]],
            scratch_shapes=[
                pltpu.VMEM((border, channels), jnp.float32),
                pltpu.VMEM((border, 2 * channels), jnp.bfloat16),
                pltpu.VMEM((border, 2 * channels), jnp.bfloat16),
                pltpu.VMEM((border, channels), jnp.float32),
            ],
            compiler_params=pltpu.CompilerParams(vmem_limit_bytes=VMEM_BYTES),
            cost_estimate=cost(flops * 12 * third, weight_bytes),
            name="middle_third" if step == 1 else "first_third",
        )(*held((*kept, grad_stream, grad_skip, sums, conv_w, out_w, *after)))

    parts = [(keep, send)]
    if in_shards:
        parts[0] = Chunk(tm, dp, 0, keep, send)
    grad_stream, *middle = later(1, [(border, jnp.float32)], [])
    other, own, *last = later(
        2, [(halo, jnp.bfloat16), (length - halo, jnp.float32)], [parts[0].next_message()] if in_shards else []
    )
    parts += [middle, last]
    if in_shards:
        for step in (1, 2):
            parts[step] = Chunk(tm, dp, step, *parts[step])
    return other, own, parts


def add_kernel(count, groups, *refs):
    arrays, outs = refs[:count], refs[-len(groups) :]
    for out, pieces in zip(outs, groups):
        lead = (slice(None),) * (len(out.shape) - 2)
        for first, rows, with_total, terms in pieces:
            body = rows - 16 if with_total else rows
            value = 0.0
            for array, at, begin in terms:
                value = value + arrays[array][at + lead + (slice(begin, begin + body),)].astype(jnp.float32)
            out[lead + (slice(first, first + body),)] = value.astype(out.dtype)
            if with_total:
                total = 0.0
                for array, at, begin in terms:
                    rows_at = slice(begin + body, begin + rows)
                    total = total + joined_rows(arrays[array][at + (0,) * len(lead) + (rows_at,)])
                slab = split_rows(total)
                out[lead + (slice(first + body, first + rows),)] = jnp.broadcast_to(slab, out.shape[:-2] + slab.shape)


def add_up(arrays, groups, shapes, after, name):
    vmem = pl.BlockSpec(memory_space=pltpu.VMEM)
    return pl.pallas_call(
        functools.partial(add_kernel, len(arrays), groups),
        in_specs=[vmem] * len(arrays) + [pl.BlockSpec(memory_space=pl.ANY)] * len(after),
        out_specs=[vmem] * len(groups),
        out_shape=[pltpu.VMEM(shape, jnp.bfloat16) for shape in shapes],
        compiler_params=pltpu.CompilerParams(vmem_limit_bytes=ADD_BYTES),
        name=name,
    )(*held(arrays), *held(after))


def first_block(array, first, rows):
    return array[(0,) * (len(array.shape) - 2) + (slice(first, first + rows),)].astype(jnp.float32)


def first_block(array, first, rows):
    return array[(0,) * (len(array.shape) - 2) + (slice(first, first + rows),)].astype(jnp.float32)


def last_kernel(counts, samples_all, tm, *refs):
    chunks = []
    for count in counts:
        chunks.append(refs[:count])
        refs = refs[count:]
    other, own, grad_inputs, grad_conv, grad_out = refs
    layers, channels = grad_conv.shape[0], own.shape[1]
    total = 0.0
    for term in chunks[-1]:
        total = total + jnp.sum(first_block(term, term.shape[-2] - 16, 16), axis=0, keepdims=True)
    scale = samples_all / total
    for chunk, terms in enumerate(chunks):
        items = items_of(layers, chunk)
        for (index, is_out), base in zip(items, bases_of(items, tm, channels)[0]):
            out = grad_out if is_out else grad_conv
            value = 0.0
            for term in terms:
                value = value + first_block(term, base, out.shape[1])
            out[index] = value * scale
    for first in range(0, channels, LANES):
        lanes = slice(first, first + LANES)
        grad_inputs[0 : own.shape[0], lanes] = own[:, lanes] * scale
        grad_inputs[own.shape[0] :, lanes] = other[:, lanes].astype(jnp.float32) * scale


class Chunk:
    def __init__(self, tm, dp, chunk, keep, send):
        self.tm, self.dp, self.chunk, self.rows = tm, dp, chunk, keep.shape[-2]
        self.message = None
        self.terms = [keep, swapped(tm, dp, send, "core")]

    def next_message(self, after=()):
        if self.message is None:
            left = len(CHAINS[self.chunk]) + 2 - len(self.terms)
            pieces = []
            for i, v in enumerate(self.terms):
                pieces.append((i, (0,) * (len(v.shape) - 2 - left) + (1,), 0))
            (self.message,) = add_up(
                self.terms, [[(0, self.rows, EXTRA[self.chunk] > 0, pieces)]], [(2,) * (left - 1) + (self.rows, LANES)], after,
                "add_chunk%d_step%d" % (self.chunk, len(self.terms) - 1),
            )
        return self.message

    def run_chain(self, after=()):
        for step, name in enumerate(CHAINS[self.chunk]):
            self.terms.append(swapped(self.tm, self.dp, self.next_message(after if step == 1 else ()), name))
            self.message = None
        return self.terms


def swapped(tm, dp, value, name):
    over_t, over_d = {"core": (0, 1), "y": (0, 2), "x": (1, 0), "z0": (2, 0), "z1": (4, 0)}[name]
    pairs = [(t * dp + d, (t ^ over_t) * dp + (d ^ over_d)) for t in range(tm) for d in range(dp)]
    return lax.ppermute(value, ("tm", "dp"), pairs)


def scattered(part):
    columns = lax.psum_scatter(part, "dp", scatter_dimension=2, tiled=True).astype(jnp.float32)
    return lax.psum_scatter(columns, "tm", scatter_dimension=1, tiled=True)


def body(inputs, grad_stream_out, grad_skip_out, sample_weight, conv_weight, out_weight):
    tm, dp = lax.axis_size("tm"), lax.axis_size("dp")
    batch, length, channels = inputs.shape
    layers = conv_weight.shape[0]
    third = layers // len(CHAINS)
    halo = 2**layers
    samples_all = batch * length * tm * dp
    x, gs, gk = inputs[0], grad_stream_out[0], grad_skip_out[0]
    message = pack(halo, x, gs, gk, sample_weight)
    prev_rows = around(message, "tm", 1)
    loaded = load_all(x, gs, gk, sample_weight, conv_weight, out_weight, message)
    in_shards = tm == 8 and dp == 4 and channels // tm % 16 == 0 and 2 * channels == dp * LANES
    other, own, parts = run_layers(in_shards, tm, dp, halo, prev_rows, loaded)
    other = around(other, "tm", -1)
    if not in_shards:
        scale = samples_all / lax.psum(jnp.sum(sample_weight), ("tm", "dp"))
        found = {}
        for chunk, part in enumerate(parts):
            items = items_of(layers, chunk)
            for is_out in (False, True):
                for place, item in enumerate(item for item in items if item[1] == is_out):
                    found[item] = part[int(is_out)][place]
        grad_conv, grad_out = (
            scattered(jnp.stack([found[index, is_out] for index in range(layers)])) * scale for is_out in (False, True)
        )
        return (jnp.concatenate([own, other]) * scale)[None], grad_conv, grad_out
    chunks = [part.run_chain([other] if part is parts[0] else ()) for part in parts]
    conv_rows, out_rows = 2 * channels // tm, channels // tm
    grad_inputs, grad_conv, grad_out = pl.pallas_call(
        functools.partial(last_kernel, [len(terms) for terms in chunks], float(samples_all), tm),
        out_shape=[
            jax.ShapeDtypeStruct((length, channels), jnp.float32),
            jax.ShapeDtypeStruct((layers, conv_rows, LANES), jnp.float32),
            jax.ShapeDtypeStruct((layers, out_rows, LANES), jnp.float32),
        ],
        compiler_params=pltpu.CompilerParams(vmem_limit_bytes=ADD_BYTES),
        name="scale_all",
    )(*held([term for terms in chunks for term in terms]), *held([other, own]))
    return grad_inputs[None], grad_conv, grad_out


def solution(mesh):
    placed = (
        P("dp", "tm", None),
        P("dp", "tm", None),
        P("dp", "tm", None),
        P("dp", "tm"),
        P(),
        P(),
    )
    return jax.shard_map(
        body,
        mesh=mesh,
        in_specs=placed,
        out_specs=(P("dp", "tm", None), P(None, "tm", "dp"), P(None, "tm", "dp")),
        check_vma=False,
    )
```

```python
import functools

import jax
import jax.numpy as jnp
from jax import lax
from jax.experimental import pallas as pl
from jax.experimental.pallas import tpu as pltpu
from jax.sharding import PartitionSpec as P

LANES = 128
VMEM_BYTES = 24 * 1024 * 1024
ADD_BYTES = 8 * 1024 * 1024
CHAINS = (("y", "x", "z0", "z1"), ("x", "z0", "y", "z1"), ("z0", "y", "x", "z1"))
EXTRA = (16, 0, 0)
NN = (((1,), (0,)), ((), ()))
NT = (((1,), (1,)), ((), ()))
TN = (((0,), (0,)), ((), ()))


def dot(left, right, dims):
    return lax.dot_general(left, right, dims, preferred_element_type=jnp.float32)


def held(arrays, space=pltpu.VMEM):
    return [pltpu.with_memory_space_constraint(x, space) for x in arrays]


def around(x, axis, by):
    count = lax.axis_size(axis)
    return lax.ppermute(x, axis, [(i, (i + by) % count) for i in range(count)])


def column(row, rows):
    return jnp.broadcast_to(row, (LANES, rows)).T


def cost(flops, moved):
    return pl.CostEstimate(flops=flops, bytes_accessed=moved, transcendentals=0)


def pack_kernel(tail_x, tail_gs, tail_gk, weight, message):
    halo, channels = tail_gs.shape
    by_row = column(weight[...], LANES)[LANES - halo :]
    by_row = jnp.concatenate([by_row] * (channels // LANES), axis=1)
    message[0 : 2 * halo] = tail_x[...]
    message[2 * halo : 3 * halo] = (tail_gs[...].astype(jnp.float32) * by_row).astype(jnp.bfloat16)
    message[3 * halo :] = (tail_gk[...].astype(jnp.float32) * by_row).astype(jnp.bfloat16)


def pack(halo, x, grad_stream_out, grad_skip_out, weight):
    length, channels = x.shape

    def last(rows):
        return pl.BlockSpec((rows, channels), lambda i: (length // rows - 1, 0))

    return pl.pallas_call(
        pack_kernel,
        grid=(1,),
        in_specs=[last(2 * halo), last(halo), last(halo), pl.BlockSpec((1, LANES), lambda i: (0, length // LANES - 1))],
        out_specs=pl.BlockSpec((4 * halo, channels), lambda i: (0, 0)),
        out_shape=jax.ShapeDtypeStruct((4 * halo, channels), jnp.bfloat16),
        compiler_params=pltpu.CompilerParams(vmem_limit_bytes=ADD_BYTES),
        name="pack_borders",
    )(*held((x, grad_stream_out, grad_skip_out, weight), pltpu.HBM))


def load_kernel(
    x, gs, gk, weight, conv_w, out_w, _, x_here, grad_stream, grad_skip, sums, conv_here, out_here,
    gs_raw, gk_raw, weight_here, sems,
):
    pairs = ((weight, weight_here), (gs, gs_raw), (gk, gk_raw), (x, x_here), (conv_w, conv_here), (out_w, out_here))
    copies = [pltpu.make_async_copy(a, b, sems.at[i]) for i, (a, b) in enumerate(pairs)]
    for copy in copies:
        copy.start()
    for copy in copies[:3]:
        copy.wait()
    length, channels = x_here.shape
    by_row = column(weight_here[...], length)
    by_row = jnp.concatenate([by_row] * (channels // LANES), axis=1)
    grad_stream[...] = gs_raw[...].astype(jnp.float32) * by_row
    grad_skip[...] = (gk_raw[...].astype(jnp.float32) * by_row).astype(jnp.bfloat16)
    own_sum = jnp.broadcast_to(jnp.sum(weight_here[...], axis=1, keepdims=True), (1, LANES))
    sums[...] = split_rows(own_sum)
    for copy in copies[3:]:
        copy.wait()


def load_all(x, gs, gk, weight, conv_w, out_w, after):
    shape = x.shape
    vmem, anywhere = pl.BlockSpec(memory_space=pltpu.VMEM), pl.BlockSpec(memory_space=pl.ANY)
    return pl.pallas_call(
        load_kernel,
        in_specs=[anywhere] * 7,
        out_specs=[vmem] * 6,
        out_shape=[
            pltpu.VMEM(shape, jnp.bfloat16),
            pltpu.VMEM(shape, jnp.float32),
            pltpu.VMEM(shape, jnp.bfloat16),
            pltpu.VMEM((16, LANES), jnp.bfloat16),
            pltpu.VMEM(conv_w.shape, jnp.bfloat16),
            pltpu.VMEM(out_w.shape, jnp.bfloat16),
        ],
        scratch_shapes=[
            pltpu.VMEM(shape, jnp.bfloat16),
            pltpu.VMEM(shape, jnp.bfloat16),
            pltpu.VMEM(weight.shape, jnp.float32),
            pltpu.SemaphoreType.DMA((6,)),
        ],
        compiler_params=pltpu.CompilerParams(vmem_limit_bytes=ADD_BYTES),
        cost_estimate=cost(10**7, 6 * 10**6),
        name="load_all",
    )(*held((x, gs, gk, weight, conv_w, out_w), pltpu.HBM), *held([after]))


def split_rows(total):
    high = total.astype(jnp.bfloat16).astype(jnp.float32)
    middle = (total - high).astype(jnp.bfloat16).astype(jnp.float32)
    low = total - high - middle
    row = lax.broadcasted_iota(jnp.int32, (16, LANES), 0)
    rows = jnp.where(row == 0, high, jnp.where(row == 1, middle, jnp.where(row == 2, low, 0.0)))
    return rows.astype(jnp.bfloat16)


def joined_rows(rows):
    return jnp.sum(rows.astype(jnp.float32), axis=0, keepdims=True)


def cut_off(rows, dilation):
    row = lax.broadcasted_iota(jnp.int32, rows.shape, 0)
    return jnp.where(jnp.logical_and(row < dilation, lax.axis_index("tm") == 0), 0.0, rows)


def items_of(layers, chunk):
    third = layers // len(CHAINS)
    high = layers - chunk * third
    return [(index, is_out) for index in reversed(range(high - third, high)) for is_out in (False, True)]


def earlier_rows(plan, index, present, first, last):
    dilation, begin = 2**index, 2 * plan["halo"]
    cut = cut_off(present[begin - dilation : begin], dilation)
    return jnp.concatenate([present[first - dilation : begin - dilation], cut, present[begin : last - dilation]])


def backward(plan, layers, refs_of, conv_w, out_w, grad_proj, grad_stream, past_part, grad_parts):
    halo, length, channels = plan["halo"], plan["length"], plan["channels"]
    own = slice(halo, halo + length)
    items = plan["items"]

    for index in layers:
        dilation, count = 2**index, plan["counts"][index]
        present, earlier, factors, gates = refs_of(index)
        grad_proj[0:count, :channels] = grad_stream[0:count].astype(jnp.bfloat16)
        grad_gated = dot(grad_proj[0:count], out_w[index], NT)
        total = dot(gates[own], grad_proj[0:length], TN)
        plan["store"](total, items.index((index, True)), grad_parts)
        both = factors[halo : halo + count].astype(jnp.float32)
        grad_preact = jnp.concatenate(
            [grad_gated * both[:, :channels], grad_gated * both[:, channels:]], axis=1
        ).astype(jnp.bfloat16)
        spread = dot(grad_preact, conv_w[index], NT)
        past_part[0:count] = spread[:, channels:]
        cut = slice(halo, halo + max(dilation, 8))
        past_part[cut] = cut_off(past_part[cut], dilation)
        rows = plan["counts"][index - 1] if index else length
        grad_stream[0:rows] += spread[0:rows, :channels] + past_part[dilation : dilation + rows]
        past = earlier_rows(plan, index, present, halo, halo + length) if earlier is None else earlier[own]
        total = dot(jnp.concatenate([present[own], past], axis=1), grad_preact[0:length], TN)
        plan["store"](total, items.index((index, False)), grad_parts)


def first_kernel(
    plan, prev_rows, own_x, own_grad, own_skip, sums, conv_w, out_w,
    low_present, low_earlier, low_factors, low_gates, grad_stream, grad_skip, *rest,
):
    *grad_parts, stream, high_present, high_factors, high_gates, grad_proj, past_part = rest
    halo, (length, channels) = plan["halo"], own_x.shape
    layers, low = conv_w.shape[0], low_gates.shape[0]
    pad = 2 ** (layers - 1)
    extent = length + 2 * halo
    begin = 2 * halo
    stream[0:pad] = jnp.zeros((pad, channels), jnp.float32)
    stream[pad : pad + begin] = prev_rows[0:begin].astype(jnp.float32)
    stream[pad + begin :] = own_x[...].astype(jnp.float32)

    def refs_of(index):
        if index < low:
            return low_present.at[index], low_earlier.at[index], low_factors.at[index], low_gates.at[index]
        at = index - low
        return high_present.at[at], None, high_factors.at[at], high_gates.at[at]

    refs_of(0)[0][0:begin] = prev_rows[0:begin]
    refs_of(0)[0][begin:] = own_x[...]
    for index in range(layers):
        dilation, start = 2**index, plan["starts"][index]
        present, earlier, factor, gate = refs_of(index)
        if earlier is None:
            past = earlier_rows(plan, index, present, start, extent)
        else:
            past = stream[pad + start - dilation : pad + extent - dilation]
            cut = cut_off(past[begin - start : begin - start + 16], dilation)
            past = jnp.concatenate([past[: begin - start], cut, past[begin - start + 16 :]]).astype(jnp.bfloat16)
            earlier[start:] = past
        preact = dot(jnp.concatenate([present[start:], past], axis=1), conv_w[index], NN)
        filtered = jnp.tanh(preact[:, :channels])
        opening = 0.5 + 0.5 * jnp.tanh(0.5 * preact[:, channels:])
        product = filtered * opening
        gated = product.astype(jnp.bfloat16)
        gate[start:] = gated
        factor[start:, :channels] = (opening - filtered * product).astype(jnp.bfloat16)
        factor[start:, channels:] = (product * (1.0 - opening)).astype(jnp.bfloat16)
        if index < layers - 1:
            after = stream[pad + start :] + dot(gated, out_w[index, :, :channels], NN)
            refs_of(index + 1)[0][start:] = after.astype(jnp.bfloat16)
            if index < layers - 2:
                stream[pad + start :] = after

    grad_stream[0:halo] = prev_rows[2 * halo : 3 * halo].astype(jnp.float32)
    grad_stream[halo:] = own_grad[...]
    grad_skip[0:halo] = prev_rows[3 * halo :]
    grad_skip[halo:] = own_skip[...]
    grad_proj[:, channels:] = grad_skip[...]
    backward(
        plan, list(reversed(range(low, layers))), refs_of, conv_w, out_w, grad_proj, grad_stream, past_part, grad_parts
    )
    plan["finish"](sums, grad_parts)


def later_kernel(
    plan, first, third, present, earlier, factors, gates, grad_before, grad_skip, conv_w, out_w, *rest
):
    *outs, keep, send, grad_stream, grad_proj, past_part = rest[plan["unused"] :]
    channels = plan["channels"]
    grad_stream[...] = grad_before[...]
    grad_proj[:, channels:] = grad_skip[...]

    def refs_of(index):
        return present.at[index], earlier.at[index], factors.at[index], gates.at[index]

    backward(
        plan, list(reversed(range(first, first + third))), refs_of, conv_w, out_w,
        grad_proj, grad_stream, past_part, (keep, send),
    )
    at = 0
    for out in outs:
        out[...] = grad_stream[at : at + out.shape[0]].astype(out.dtype)
        at += out.shape[0]


def store_whole(items, total, item, grad_parts):
    is_out = items[item][1]
    place = sum(kind == is_out for _, kind in items[:item])
    grad_parts[int(is_out)][place] = total.astype(jnp.bfloat16)


def finish_whole(sums, grad_parts):
    pass


def finish_shards(extra, sums, grad_parts):
    for part in grad_parts:
        lead, rows = part.shape[:-2], part.shape[-2]
        for first in range(rows - extra, rows, 16):
            part[(slice(None),) * len(lead) + (slice(first, first + 16),)] = jnp.broadcast_to(
                sums[...], lead + sums.shape
            )


def store_shards(tm, dp, order, bases, total, item, grad_parts):
    keep, send = grad_parts
    t_at, d_at = lax.axis_index("tm"), lax.axis_index("dp")
    core_at = lax.rem(d_at, 2)
    rows = total.shape[0] // tm
    at = pl.ds(bases[item], rows)
    at_bits = bits_of(t_at, d_at, lax.rem, lax.div)
    for y in range(dp // 2):
        near = total[:, (2 * y) * LANES : (2 * y + 1) * LANES]
        far = total[:, (2 * y + 1) * LANES : (2 * y + 2) * LANES]
        mine = jnp.where(core_at == 0, near, far).astype(jnp.bfloat16)
        other = jnp.where(core_at == 0, far, near).astype(jnp.bfloat16)
        for t in range(tm):
            bits = bits_of(t, 2 * y, lambda a, b: a % b, lambda a, b: a // b)
            lead = tuple(lax.rem(bits[name] + at_bits[name], 2) for name in order)
            keep[lead + (at,)] = mine[t * rows : (t + 1) * rows]
            send[lead + (at,)] = other[t * rows : (t + 1) * rows]


def bits_of(t, d, rem, div):
    return {"x": rem(t, 2), "z0": rem(div(t, 2), 2), "z1": div(t, 4), "y": div(d, 2)}


def bases_of(items, tm, channels):
    ends = [0]
    for _, is_out in items:
        ends.append(ends[-1] + (1 if is_out else 2) * channels // tm)
    return ends[:-1], ends[-1]


def run_layers(in_shards, tm, dp, halo, prev_rows, loaded):
    own_x, own_grad, own_skip, sums, conv_w, out_w = loaded
    length, channels = own_x.shape
    layers = conv_w.shape[0]
    third = layers // len(CHAINS)
    low = layers - third
    extent, border = length + 2 * halo, length + halo
    starts = []
    for index in range(layers):
        need = halo if index == layers - 1 else 2 ** (index + 1)
        starts.append(need // 16 * 16)
    counts = [-(-(length + 2 ** (index + 1) - 1) // 16) * 16 for index in range(layers)]
    plan = {"halo": halo, "starts": starts, "counts": counts, "length": length, "channels": channels, "unused": 0}
    plans, shapes = [], []
    for chunk, order in enumerate(CHAINS):
        items = items_of(layers, chunk)
        bases, rows = bases_of(items, tm, channels)
        if in_shards:
            store = functools.partial(store_shards, tm, dp, order, bases)
            finish = functools.partial(finish_shards, EXTRA[chunk])
            shapes.append(2 * [(2,) * len(order) + (rows + EXTRA[chunk], LANES)])
        else:
            store, finish = functools.partial(store_whole, items), finish_whole
            outs = sum(is_out for _, is_out in items)
            shapes.append([(len(items) - outs,) + conv_w.shape[1:], (outs,) + out_w.shape[1:]])
        plans.append(plan | {"items": items, "store": store, "finish": finish})
    vmem, anywhere = pl.BlockSpec(memory_space=pltpu.VMEM), pl.BlockSpec(memory_space=pl.ANY)
    weight_bytes = 2 * (conv_w.size + out_w.size)
    flops = 2 * length * channels * channels
    *kept, grad_stream, grad_skip, keep, send = pl.pallas_call(
        functools.partial(first_kernel, plans[0]),
        in_specs=[vmem] * 7,
        out_specs=[vmem] * 8,
        out_shape=[
            pltpu.VMEM((low, extent, channels), jnp.bfloat16),
            pltpu.VMEM((low, extent, channels), jnp.bfloat16),
            pltpu.VMEM((low, extent, 2 * channels), jnp.bfloat16),
            pltpu.VMEM((low, extent, channels), jnp.bfloat16),
            pltpu.VMEM((border, channels), jnp.float32),
            pltpu.VMEM((border, channels), jnp.bfloat16),
        ]
        + [pltpu.VMEM(shape, jnp.bfloat16) for shape in shapes[0]],
        scratch_shapes=[
            pltpu.VMEM((2 ** (layers - 1) + extent, channels), jnp.float32),
            pltpu.VMEM((third, extent, channels), jnp.bfloat16),
            pltpu.VMEM((third, extent, 2 * channels), jnp.bfloat16),
            pltpu.VMEM((third, extent, channels), jnp.bfloat16),
            pltpu.VMEM((border, 2 * channels), jnp.bfloat16),
            pltpu.VMEM((border, channels), jnp.float32),
        ],
        compiler_params=pltpu.CompilerParams(vmem_limit_bytes=VMEM_BYTES),
        cost_estimate=cost(flops * (5 * layers + 12 * third), weight_bytes),
        name="forward_and_last_third",
    )(*held((prev_rows, *loaded)))

    def later(step, outs, after):
        return pl.pallas_call(
            functools.partial(later_kernel, plans[step] | {"unused": len(after)}, layers - (step + 1) * third, third),
            in_specs=[vmem] * 8 + [anywhere] * len(after),
            out_specs=[vmem] * (len(outs) + 2),
            out_shape=[pltpu.VMEM((rows, channels), kind) for rows, kind in outs]
            + [pltpu.VMEM(shape, jnp.bfloat16) for shape in shapes[step]],
            scratch_shapes=[
                pltpu.VMEM((border, channels), jnp.float32),
                pltpu.VMEM((border, 2 * channels), jnp.bfloat16),
                pltpu.VMEM((border, channels), jnp.float32),
            ],
            compiler_params=pltpu.CompilerParams(vmem_limit_bytes=VMEM_BYTES),
            cost_estimate=cost(flops * 12 * third, weight_bytes),
            name="middle_third" if step == 1 else "first_third",
        )(*held((*kept, grad_stream, grad_skip, conv_w, out_w, *after)))

    parts = [(keep, send)]
    if in_shards:
        parts[0] = Chunk(tm, dp, 0, keep, send)
    grad_stream, *middle = later(1, [(border, jnp.float32)], [])
    other, own, *last = later(
        2, [(halo, jnp.bfloat16), (length - halo, jnp.float32)], [parts[0].next_message()] if in_shards else []
    )
    parts += [middle, last]
    if in_shards:
        for step in (1, 2):
            parts[step] = Chunk(tm, dp, step, *parts[step])
    return other, own, parts


def add_kernel(count, groups, *refs):
    arrays, outs = refs[:count], refs[-len(groups) :]
    for out, pieces in zip(outs, groups):
        lead = (slice(None),) * (len(out.shape) - 2)
        for first, rows, with_total, terms in pieces:
            body = rows - 16 if with_total else rows
            value = 0.0
            for array, at, begin in terms:
                value = value + arrays[array][at + lead + (slice(begin, begin + body),)].astype(jnp.float32)
            out[lead + (slice(first, first + body),)] = value.astype(out.dtype)
            if with_total:
                total = 0.0
                for array, at, begin in terms:
                    rows_at = slice(begin + body, begin + rows)
                    total = total + joined_rows(arrays[array][at + (0,) * len(lead) + (rows_at,)])
                slab = split_rows(total)
                out[lead + (slice(first + body, first + rows),)] = jnp.broadcast_to(slab, out.shape[:-2] + slab.shape)


def add_up(arrays, groups, shapes, after, name):
    vmem = pl.BlockSpec(memory_space=pltpu.VMEM)
    return pl.pallas_call(
        functools.partial(add_kernel, len(arrays), groups),
        in_specs=[vmem] * len(arrays) + [pl.BlockSpec(memory_space=pl.ANY)] * len(after),
        out_specs=[vmem] * len(groups),
        out_shape=[pltpu.VMEM(shape, jnp.bfloat16) for shape in shapes],
        compiler_params=pltpu.CompilerParams(vmem_limit_bytes=ADD_BYTES),
        name=name,
    )(*held(arrays), *held(after))


def first_block(array, first, rows):
    return array[(0,) * (len(array.shape) - 2) + (slice(first, first + rows),)].astype(jnp.float32)


def first_block(array, first, rows):
    return array[(0,) * (len(array.shape) - 2) + (slice(first, first + rows),)].astype(jnp.float32)


def last_kernel(counts, samples_all, tm, *refs):
    chunks = []
    for count in counts:
        chunks.insert(0, refs[:count])
        refs = refs[count:]
    other, own, grad_inputs, grad_conv, grad_out = refs
    layers, channels = grad_conv.shape[0], own.shape[1]
    total = 0.0
    for term in chunks[0]:
        total = total + jnp.sum(first_block(term, term.shape[-2] - 16, 16), axis=0, keepdims=True)
    scale = samples_all / total
    for chunk, terms in enumerate(chunks):
        items = items_of(layers, chunk)
        for (index, is_out), base in zip(items, bases_of(items, tm, channels)[0]):
            out = grad_out if is_out else grad_conv
            value = 0.0
            for term in terms:
                value = value + first_block(term, base, out.shape[1])
            out[index] = value * scale
    for first in range(0, channels, LANES):
        lanes = slice(first, first + LANES)
        grad_inputs[0 : own.shape[0], lanes] = own[:, lanes] * scale
        grad_inputs[own.shape[0] :, lanes] = other[:, lanes].astype(jnp.float32) * scale


class Chunk:
    def __init__(self, tm, dp, chunk, keep, send):
        self.tm, self.dp, self.chunk, self.rows = tm, dp, chunk, keep.shape[-2]
        self.message = None
        self.terms = [keep, swapped(tm, dp, send, "core")]

    def next_message(self, after=()):
        if self.message is None:
            left = len(CHAINS[self.chunk]) + 2 - len(self.terms)
            pieces = []
            for i, v in enumerate(self.terms):
                pieces.append((i, (0,) * (len(v.shape) - 2 - left) + (1,), 0))
            (self.message,) = add_up(
                self.terms, [[(0, self.rows, EXTRA[self.chunk] > 0, pieces)]], [(2,) * (left - 1) + (self.rows, LANES)], after,
                "add_chunk%d_step%d" % (self.chunk, len(self.terms) - 1),
            )
        return self.message

    def run_chain(self, after=()):
        for step, name in enumerate(CHAINS[self.chunk]):
            self.terms.append(swapped(self.tm, self.dp, self.next_message(after if step == 1 else ()), name))
            self.message = None
        return self.terms


def swapped(tm, dp, value, name):
    over_t, over_d = {"core": (0, 1), "y": (0, 2), "x": (1, 0), "z0": (2, 0), "z1": (4, 0)}[name]
    pairs = [(t * dp + d, (t ^ over_t) * dp + (d ^ over_d)) for t in range(tm) for d in range(dp)]
    return lax.ppermute(value, ("tm", "dp"), pairs)


def scattered(part):
    columns = lax.psum_scatter(part, "dp", scatter_dimension=2, tiled=True).astype(jnp.float32)
    return lax.psum_scatter(columns, "tm", scatter_dimension=1, tiled=True)


def body(inputs, grad_stream_out, grad_skip_out, sample_weight, conv_weight, out_weight):
    tm, dp = lax.axis_size("tm"), lax.axis_size("dp")
    batch, length, channels = inputs.shape
    layers = conv_weight.shape[0]
    third = layers // len(CHAINS)
    halo = 2**layers
    samples_all = batch * length * tm * dp
    x, gs, gk = inputs[0], grad_stream_out[0], grad_skip_out[0]
    message = pack(halo, x, gs, gk, sample_weight)
    prev_rows = around(message, "tm", 1)
    loaded = load_all(x, gs, gk, sample_weight, conv_weight, out_weight, message)
    in_shards = tm == 8 and dp == 4 and channels // tm % 16 == 0 and 2 * channels == dp * LANES
    other, own, parts = run_layers(in_shards, tm, dp, halo, prev_rows, loaded)
    other = around(other, "tm", -1)
    if not in_shards:
        scale = samples_all / lax.psum(jnp.sum(sample_weight), ("tm", "dp"))
        found = {}
        for chunk, part in enumerate(parts):
            items = items_of(layers, chunk)
            for is_out in (False, True):
                for place, item in enumerate(item for item in items if item[1] == is_out):
                    found[item] = part[int(is_out)][place]
        grad_conv, grad_out = (
            scattered(jnp.stack([found[index, is_out] for index in range(layers)])) * scale for is_out in (False, True)
        )
        return (jnp.concatenate([own, other]) * scale)[None], grad_conv, grad_out
    chunks = [part.run_chain([other] if part is parts[0] else ()) for part in parts]
    conv_rows, out_rows = 2 * channels // tm, channels // tm
    grad_inputs, grad_conv, grad_out = pl.pallas_call(
        functools.partial(last_kernel, [len(terms) for terms in reversed(chunks)], float(samples_all), tm),
        out_shape=[
            jax.ShapeDtypeStruct((length, channels), jnp.float32),
            jax.ShapeDtypeStruct((layers, conv_rows, LANES), jnp.float32),
            jax.ShapeDtypeStruct((layers, out_rows, LANES), jnp.float32),
        ],
        compiler_params=pltpu.CompilerParams(vmem_limit_bytes=ADD_BYTES),
        name="scale_all",
    )(*held([term for terms in reversed(chunks) for term in terms]), *held([other, own]))
    return grad_inputs[None], grad_conv, grad_out


def solution(mesh):
    placed = (
        P("dp", "tm", None),
        P("dp", "tm", None),
        P("dp", "tm", None),
        P("dp", "tm"),
        P(),
        P(),
    )
    return jax.shard_map(
        body,
        mesh=mesh,
        in_specs=placed,
        out_specs=(P("dp", "tm", None), P(None, "tm", "dp"), P(None, "tm", "dp")),
        check_vma=False,
    )
```

```python
import functools

import jax
import jax.numpy as jnp
from jax import lax
from jax.experimental import pallas as pl
from jax.experimental.pallas import tpu as pltpu
from jax.sharding import PartitionSpec as P

LANES = 128
VMEM_BYTES = 24 * 1024 * 1024
ADD_BYTES = 8 * 1024 * 1024
CHAINS = (("y", "x", "z0", "z1"), ("x", "z0", "y", "z1"), ("z0", "y", "x", "z1"))
EXTRA = (16, 0, 0)
NN = (((1,), (0,)), ((), ()))
NT = (((1,), (1,)), ((), ()))
TN = (((0,), (0,)), ((), ()))


def dot(left, right, dims):
    return lax.dot_general(left, right, dims, preferred_element_type=jnp.float32)


def held(arrays, space=pltpu.VMEM):
    return [pltpu.with_memory_space_constraint(x, space) for x in arrays]


def around(x, axis, by):
    count = lax.axis_size(axis)
    return lax.ppermute(x, axis, [(i, (i + by) % count) for i in range(count)])


def column(row, rows):
    return jnp.broadcast_to(row, (LANES, rows)).T


def cost(flops, moved):
    return pl.CostEstimate(flops=flops, bytes_accessed=moved, transcendentals=0)


def pack_kernel(head_x, tail_x, head_gs, head_gk, weight, for_next, for_prev):
    halo, channels = head_x.shape
    by_row = column(weight[...], LANES)[:halo]
    by_row = jnp.concatenate([by_row] * (channels // LANES), axis=1)
    for_next[...] = tail_x[...]
    for_prev[0:halo] = head_x[...]
    for_prev[halo : 2 * halo] = (head_gs[...].astype(jnp.float32) * by_row).astype(jnp.bfloat16)
    for_prev[2 * halo :] = (head_gk[...].astype(jnp.float32) * by_row).astype(jnp.bfloat16)


def pack(halo, x, grad_stream_out, grad_skip_out, weight):
    length, channels = x.shape
    first = pl.BlockSpec((halo, channels), lambda i: (0, 0))
    last = pl.BlockSpec((halo, channels), lambda i: (length // halo - 1, 0))
    shapes = [(halo, channels), (3 * halo, channels)]
    return pl.pallas_call(
        pack_kernel,
        grid=(1,),
        in_specs=[first, last, first, first, pl.BlockSpec((1, LANES), lambda i: (0, 0))],
        out_specs=[pl.BlockSpec(shape, lambda i: (0, 0)) for shape in shapes],
        out_shape=[jax.ShapeDtypeStruct(shape, jnp.bfloat16) for shape in shapes],
        compiler_params=pltpu.CompilerParams(vmem_limit_bytes=ADD_BYTES),
        name="pack_borders",
    )(*held((x, x, grad_stream_out, grad_skip_out, weight), pltpu.HBM))


def load_kernel(
    x, gs, gk, weight, conv_w, out_w, _, x_here, grad_stream, grad_skip, sums, conv_here, out_here,
    gs_raw, gk_raw, weight_here, sems,
):
    pairs = ((weight, weight_here), (gs, gs_raw), (gk, gk_raw), (x, x_here), (conv_w, conv_here), (out_w, out_here))
    copies = [pltpu.make_async_copy(a, b, sems.at[i]) for i, (a, b) in enumerate(pairs)]
    for copy in copies:
        copy.start()
    for copy in copies[:3]:
        copy.wait()
    length, channels = x_here.shape
    by_row = column(weight_here[...], length)
    by_row = jnp.concatenate([by_row] * (channels // LANES), axis=1)
    grad_stream[...] = gs_raw[...].astype(jnp.float32) * by_row
    grad_skip[...] = (gk_raw[...].astype(jnp.float32) * by_row).astype(jnp.bfloat16)
    own_sum = jnp.broadcast_to(jnp.sum(weight_here[...], axis=1, keepdims=True), (1, LANES))
    sums[...] = split_rows(own_sum)
    for copy in copies[3:]:
        copy.wait()


def load_all(x, gs, gk, weight, conv_w, out_w, after):
    shape = x.shape
    vmem, anywhere = pl.BlockSpec(memory_space=pltpu.VMEM), pl.BlockSpec(memory_space=pl.ANY)
    return pl.pallas_call(
        load_kernel,
        in_specs=[anywhere] * 7,
        out_specs=[vmem] * 6,
        out_shape=[
            pltpu.VMEM(shape, jnp.bfloat16),
            pltpu.VMEM(shape, jnp.float32),
            pltpu.VMEM(shape, jnp.bfloat16),
            pltpu.VMEM((16, LANES), jnp.bfloat16),
            pltpu.VMEM(conv_w.shape, jnp.bfloat16),
            pltpu.VMEM(out_w.shape, jnp.bfloat16),
        ],
        scratch_shapes=[
            pltpu.VMEM(shape, jnp.bfloat16),
            pltpu.VMEM(shape, jnp.bfloat16),
            pltpu.VMEM(weight.shape, jnp.float32),
            pltpu.SemaphoreType.DMA((6,)),
        ],
        compiler_params=pltpu.CompilerParams(vmem_limit_bytes=ADD_BYTES),
        cost_estimate=cost(10**7, 6 * 10**6),
        name="load_all",
    )(*held((x, gs, gk, weight, conv_w, out_w), pltpu.HBM), *held([after]))


def split_rows(total):
    high = total.astype(jnp.bfloat16).astype(jnp.float32)
    middle = (total - high).astype(jnp.bfloat16).astype(jnp.float32)
    low = total - high - middle
    row = lax.broadcasted_iota(jnp.int32, (16, LANES), 0)
    rows = jnp.where(row == 0, high, jnp.where(row == 1, middle, jnp.where(row == 2, low, 0.0)))
    return rows.astype(jnp.bfloat16)


def joined_rows(rows):
    return jnp.sum(rows.astype(jnp.float32), axis=0, keepdims=True)


def items_of(layers, chunk):
    third = layers // len(CHAINS)
    high = layers - chunk * third
    return [(index, is_out) for index in reversed(range(high - third, high)) for is_out in (False, True)]


def backward(plan, layers, refs_of, conv_w, out_w, grad_proj, grad_stream, past_part, grad_parts):
    halo, length, channels = plan["halo"], plan["length"], plan["channels"]
    own = slice(halo, halo + length)
    items = plan["items"]

    for index in layers:
        dilation, count = 2**index, plan["counts"][index]
        present, earlier, factors, gates = refs_of(index)
        grad_proj[0:count, :channels] = grad_stream[0:count].astype(jnp.bfloat16)
        grad_gated = dot(grad_proj[0:count], out_w[index], NT)
        total = dot(gates[own], grad_proj[0:length], TN)
        plan["store"](total, items.index((index, True)), grad_parts)
        both = factors[halo : halo + count].astype(jnp.float32)
        grad_preact = jnp.concatenate(
            [grad_gated * both[:, :channels], grad_gated * both[:, channels:]], axis=1
        ).astype(jnp.bfloat16)
        spread = dot(grad_preact, conv_w[index], NT)
        past_part[0:count] = spread[:, channels:]
        rows = plan["counts"][index - 1] if index else length
        grad_stream[0:rows] += spread[0:rows, :channels] + past_part[dilation : dilation + rows]
        past = present[halo - dilation : halo + length - dilation] if earlier is None else earlier[own]
        total = dot(jnp.concatenate([present[own], past], axis=1), grad_preact[0:length], TN)
        plan["store"](total, items.index((index, False)), grad_parts)


def first_kernel(
    plan, prev_rows, next_rows, own_x, own_grad, own_skip, sums, conv_w, out_w,
    low_present, low_earlier, low_factors, low_gates, grad_stream, grad_skip, *rest,
):
    *grad_parts, stream, high_present, high_factors, high_gates, grad_proj, past_part = rest
    halo, (length, channels) = plan["halo"], own_x.shape
    layers, low = conv_w.shape[0], low_gates.shape[0]
    pad = 2 ** (layers - 1)
    extent = length + 2 * halo
    at = lax.axis_index("tm")

    def unless(is_end, rows):
        return jnp.where(is_end, jnp.zeros_like(rows), rows)

    before = unless(at == 0, prev_rows[...])
    after = unless(at == lax.axis_size("tm") - 1, next_rows[...])
    stream[0:pad] = jnp.zeros((pad, channels), jnp.float32)
    stream[pad : pad + halo] = before.astype(jnp.float32)
    stream[pad + halo : pad + halo + length] = own_x[...].astype(jnp.float32)
    stream[pad + halo + length :] = after[0:halo].astype(jnp.float32)

    def refs_of(index):
        if index < low:
            return low_present.at[index], low_earlier.at[index], low_factors.at[index], low_gates.at[index]
        at = index - low
        return high_present.at[at], None, high_factors.at[at], high_gates.at[at]

    refs_of(0)[0][0:halo] = before
    refs_of(0)[0][halo : halo + length] = own_x[...]
    refs_of(0)[0][halo + length :] = after[0:halo]
    for index in range(layers):
        dilation, start = 2**index, plan["starts"][index]
        present, earlier, factor, gate = refs_of(index)
        if earlier is None:
            past = present[start - dilation : extent - dilation]
        else:
            past = stream[pad + start - dilation : pad + extent - dilation].astype(jnp.bfloat16)
            earlier[start:] = past
        preact = dot(jnp.concatenate([present[start:], past], axis=1), conv_w[index], NN)
        filtered = jnp.tanh(preact[:, :channels])
        opening = 0.5 + 0.5 * jnp.tanh(0.5 * preact[:, channels:])
        product = filtered * opening
        gated = product.astype(jnp.bfloat16)
        gate[start:] = gated
        factor[start:, :channels] = (opening - filtered * product).astype(jnp.bfloat16)
        factor[start:, channels:] = (product * (1.0 - opening)).astype(jnp.bfloat16)
        if index < layers - 1:
            moved_on = stream[pad + start :] + dot(gated, out_w[index, :, :channels], NN)
            refs_of(index + 1)[0][start:] = moved_on.astype(jnp.bfloat16)
            if index < layers - 2:
                stream[pad + start :] = moved_on

    grad_stream[0:length] = own_grad[...]
    grad_stream[length:] = after[halo : 2 * halo].astype(jnp.float32)
    grad_skip[0:length] = own_skip[...]
    grad_skip[length:] = after[2 * halo :]
    grad_proj[:, channels:] = grad_skip[...]
    backward(
        plan, list(reversed(range(low, layers))), refs_of, conv_w, out_w, grad_proj, grad_stream, past_part, grad_parts
    )
    plan["finish"](sums, grad_parts)


def later_kernel(
    plan, first, third, present, earlier, factors, gates, grad_before, grad_skip, conv_w, out_w, *rest
):
    grad_after, keep, send, grad_stream, grad_proj, past_part = rest[plan["unused"] :]
    channels = plan["channels"]
    grad_stream[...] = grad_before[...]
    grad_proj[:, channels:] = grad_skip[...]

    def refs_of(index):
        return present.at[index], earlier.at[index], factors.at[index], gates.at[index]

    backward(
        plan, list(reversed(range(first, first + third))), refs_of, conv_w, out_w,
        grad_proj, grad_stream, past_part, (keep, send),
    )
    grad_after[...] = grad_stream[0 : grad_after.shape[0]]


def store_whole(items, total, item, grad_parts):
    is_out = items[item][1]
    place = sum(kind == is_out for _, kind in items[:item])
    grad_parts[int(is_out)][place] = total.astype(jnp.bfloat16)


def finish_whole(sums, grad_parts):
    pass


def finish_shards(extra, sums, grad_parts):
    for part in grad_parts:
        lead, rows = part.shape[:-2], part.shape[-2]
        for first in range(rows - extra, rows, 16):
            part[(slice(None),) * len(lead) + (slice(first, first + 16),)] = jnp.broadcast_to(
                sums[...], lead + sums.shape
            )


def store_shards(tm, dp, order, bases, total, item, grad_parts):
    keep, send = grad_parts
    t_at, d_at = lax.axis_index("tm"), lax.axis_index("dp")
    core_at = lax.rem(d_at, 2)
    rows = total.shape[0] // tm
    at = pl.ds(bases[item], rows)
    at_bits = bits_of(t_at, d_at, lax.rem, lax.div)
    for y in range(dp // 2):
        near = total[:, (2 * y) * LANES : (2 * y + 1) * LANES]
        far = total[:, (2 * y + 1) * LANES : (2 * y + 2) * LANES]
        mine = jnp.where(core_at == 0, near, far).astype(jnp.bfloat16)
        other = jnp.where(core_at == 0, far, near).astype(jnp.bfloat16)
        for t in range(tm):
            bits = bits_of(t, 2 * y, lambda a, b: a % b, lambda a, b: a // b)
            lead = tuple(lax.rem(bits[name] + at_bits[name], 2) for name in order)
            keep[lead + (at,)] = mine[t * rows : (t + 1) * rows]
            send[lead + (at,)] = other[t * rows : (t + 1) * rows]


def bits_of(t, d, rem, div):
    return {"x": rem(t, 2), "z0": rem(div(t, 2), 2), "z1": div(t, 4), "y": div(d, 2)}


def bases_of(items, tm, channels):
    ends = [0]
    for _, is_out in items:
        ends.append(ends[-1] + (1 if is_out else 2) * channels // tm)
    return ends[:-1], ends[-1]


def run_layers(in_shards, tm, dp, halo, borders, loaded):
    own_x, own_grad, own_skip, sums, conv_w, out_w = loaded
    length, channels = own_x.shape
    layers = conv_w.shape[0]
    third = layers // len(CHAINS)
    low = layers - third
    extent, border = length + 2 * halo, length + halo
    starts = []
    for index in range(layers):
        need = halo if index == layers - 1 else 2 ** (index + 1)
        starts.append(need // 16 * 16)
    counts = [-(-(length + 2 ** (index + 1) - 1) // 16) * 16 for index in range(layers)]
    plan = {"halo": halo, "starts": starts, "counts": counts, "length": length, "channels": channels, "unused": 0}
    plans, shapes = [], []
    for chunk, order in enumerate(CHAINS):
        items = items_of(layers, chunk)
        bases, rows = bases_of(items, tm, channels)
        if in_shards:
            store = functools.partial(store_shards, tm, dp, order, bases)
            finish = functools.partial(finish_shards, EXTRA[chunk])
            shapes.append(2 * [(2,) * len(order) + (rows + EXTRA[chunk], LANES)])
        else:
            store, finish = functools.partial(store_whole, items), finish_whole
            outs = sum(is_out for _, is_out in items)
            shapes.append([(len(items) - outs,) + conv_w.shape[1:], (outs,) + out_w.shape[1:]])
        plans.append(plan | {"items": items, "store": store, "finish": finish})
    vmem, anywhere = pl.BlockSpec(memory_space=pltpu.VMEM), pl.BlockSpec(memory_space=pl.ANY)
    weight_bytes = 2 * (conv_w.size + out_w.size)
    flops = 2 * length * channels * channels
    *kept, grad_stream, grad_skip, keep, send = pl.pallas_call(
        functools.partial(first_kernel, plans[0]),
        in_specs=[vmem] * 8,
        out_specs=[vmem] * 8,
        out_shape=[
            pltpu.VMEM((low, extent, channels), jnp.bfloat16),
            pltpu.VMEM((low, extent, channels), jnp.bfloat16),
            pltpu.VMEM((low, extent, 2 * channels), jnp.bfloat16),
            pltpu.VMEM((low, extent, channels), jnp.bfloat16),
            pltpu.VMEM((border, channels), jnp.float32),
            pltpu.VMEM((border, channels), jnp.bfloat16),
        ]
        + [pltpu.VMEM(shape, jnp.bfloat16) for shape in shapes[0]],
        scratch_shapes=[
            pltpu.VMEM((2 ** (layers - 1) + extent, channels), jnp.float32),
            pltpu.VMEM((third, extent, channels), jnp.bfloat16),
            pltpu.VMEM((third, extent, 2 * channels), jnp.bfloat16),
            pltpu.VMEM((third, extent, channels), jnp.bfloat16),
            pltpu.VMEM((border, 2 * channels), jnp.bfloat16),
            pltpu.VMEM((border, channels), jnp.float32),
        ],
        compiler_params=pltpu.CompilerParams(vmem_limit_bytes=VMEM_BYTES),
        cost_estimate=cost(flops * (5 * layers + 12 * third), weight_bytes),
        name="forward_and_last_third",
    )(*held((*borders, *loaded)))

    def later(step, rows, after):
        return pl.pallas_call(
            functools.partial(later_kernel, plans[step] | {"unused": len(after)}, layers - (step + 1) * third, third),
            in_specs=[vmem] * 8 + [anywhere] * len(after),
            out_specs=[vmem] * 3,
            out_shape=[pltpu.VMEM((rows, channels), jnp.float32)]
            + [pltpu.VMEM(shape, jnp.bfloat16) for shape in shapes[step]],
            scratch_shapes=[
                pltpu.VMEM((border, channels), jnp.float32),
                pltpu.VMEM((border, 2 * channels), jnp.bfloat16),
                pltpu.VMEM((border, channels), jnp.float32),
            ],
            compiler_params=pltpu.CompilerParams(vmem_limit_bytes=VMEM_BYTES),
            cost_estimate=cost(flops * 12 * third, weight_bytes),
            name="middle_third" if step == 1 else "first_third",
        )(*held((*kept, grad_stream, grad_skip, conv_w, out_w, *after)))

    parts = [(keep, send)]
    if in_shards:
        parts[0] = Chunk(tm, dp, 0, keep, send)
    grad_stream, *middle = later(1, border, [])
    grad_in, *last = later(2, length, [parts[0].next_message()] if in_shards else [])
    parts += [middle, last]
    if in_shards:
        for step in (1, 2):
            parts[step] = Chunk(tm, dp, step, *parts[step])
    return grad_in, parts


def add_kernel(count, groups, *refs):
    arrays, outs = refs[:count], refs[-len(groups) :]
    for out, pieces in zip(outs, groups):
        lead = (slice(None),) * (len(out.shape) - 2)
        for first, rows, with_total, terms in pieces:
            body = rows - 16 if with_total else rows
            value = 0.0
            for array, at, begin in terms:
                value = value + arrays[array][at + lead + (slice(begin, begin + body),)].astype(jnp.float32)
            out[lead + (slice(first, first + body),)] = value.astype(out.dtype)
            if with_total:
                total = 0.0
                for array, at, begin in terms:
                    rows_at = slice(begin + body, begin + rows)
                    total = total + joined_rows(arrays[array][at + (0,) * len(lead) + (rows_at,)])
                slab = split_rows(total)
                out[lead + (slice(first + body, first + rows),)] = jnp.broadcast_to(slab, out.shape[:-2] + slab.shape)


def add_up(arrays, groups, shapes, name):
    vmem = pl.BlockSpec(memory_space=pltpu.VMEM)
    return pl.pallas_call(
        functools.partial(add_kernel, len(arrays), groups),
        in_specs=[vmem] * len(arrays),
        out_specs=[vmem] * len(groups),
        out_shape=[pltpu.VMEM(shape, jnp.bfloat16) for shape in shapes],
        compiler_params=pltpu.CompilerParams(vmem_limit_bytes=ADD_BYTES),
        name=name,
    )(*held(arrays))


def first_block(array, first, rows):
    return array[(0,) * (len(array.shape) - 2) + (slice(first, first + rows),)].astype(jnp.float32)


def first_block(array, first, rows):
    return array[(0,) * (len(array.shape) - 2) + (slice(first, first + rows),)].astype(jnp.float32)


def last_kernel(counts, samples_all, tm, *refs):
    chunks = []
    for count in counts:
        chunks.insert(0, refs[:count])
        refs = refs[count:]
    grad_in, grad_inputs, grad_conv, grad_out = refs
    layers, channels = grad_conv.shape[0], grad_in.shape[1]
    total = 0.0
    for term in chunks[0]:
        total = total + jnp.sum(first_block(term, term.shape[-2] - 16, 16), axis=0, keepdims=True)
    scale = samples_all / total
    for chunk, terms in enumerate(chunks):
        items = items_of(layers, chunk)
        for (index, is_out), base in zip(items, bases_of(items, tm, channels)[0]):
            out = grad_out if is_out else grad_conv
            value = 0.0
            for term in terms:
                value = value + first_block(term, base, out.shape[1])
            out[index] = value * scale
    for first in range(0, channels, LANES):
        lanes = slice(first, first + LANES)
        grad_inputs[:, lanes] = grad_in[:, lanes] * scale


class Chunk:
    def __init__(self, tm, dp, chunk, keep, send):
        self.tm, self.dp, self.chunk, self.rows = tm, dp, chunk, keep.shape[-2]
        self.message = None
        self.terms = [keep, swapped(tm, dp, send, "core")]

    def next_message(self):
        if self.message is None:
            left = len(CHAINS[self.chunk]) + 2 - len(self.terms)
            pieces = []
            for i, v in enumerate(self.terms):
                pieces.append((i, (0,) * (len(v.shape) - 2 - left) + (1,), 0))
            (self.message,) = add_up(
                self.terms, [[(0, self.rows, EXTRA[self.chunk] > 0, pieces)]], [(2,) * (left - 1) + (self.rows, LANES)],
                "add_chunk%d_step%d" % (self.chunk, len(self.terms) - 1),
            )
        return self.message

    def run_chain(self):
        for name in CHAINS[self.chunk]:
            self.terms.append(swapped(self.tm, self.dp, self.next_message(), name))
            self.message = None
        return self.terms


def swapped(tm, dp, value, name):
    over_t, over_d = {"core": (0, 1), "y": (0, 2), "x": (1, 0), "z0": (2, 0), "z1": (4, 0)}[name]
    pairs = [(t * dp + d, (t ^ over_t) * dp + (d ^ over_d)) for t in range(tm) for d in range(dp)]
    return lax.ppermute(value, ("tm", "dp"), pairs)


def scattered(part):
    columns = lax.psum_scatter(part, "dp", scatter_dimension=2, tiled=True).astype(jnp.float32)
    return lax.psum_scatter(columns, "tm", scatter_dimension=1, tiled=True)


def body(inputs, grad_stream_out, grad_skip_out, sample_weight, conv_weight, out_weight):
    tm, dp = lax.axis_size("tm"), lax.axis_size("dp")
    batch, length, channels = inputs.shape
    layers = conv_weight.shape[0]
    third = layers // len(CHAINS)
    halo = 2**layers
    samples_all = batch * length * tm * dp
    x, gs, gk = inputs[0], grad_stream_out[0], grad_skip_out[0]
    for_next, for_prev = pack(halo, x, gs, gk, sample_weight)
    borders = [around(for_next, "tm", 1), around(for_prev, "tm", -1)]
    loaded = load_all(x, gs, gk, sample_weight, conv_weight, out_weight, for_next)
    in_shards = tm == 8 and dp == 4 and channels // tm % 16 == 0 and 2 * channels == dp * LANES
    grad_in, parts = run_layers(in_shards, tm, dp, halo, borders, loaded)
    if not in_shards:
        scale = samples_all / lax.psum(jnp.sum(sample_weight), ("tm", "dp"))
        found = {}
        for chunk, part in enumerate(parts):
            items = items_of(layers, chunk)
            for is_out in (False, True):
                for place, item in enumerate(item for item in items if item[1] == is_out):
                    found[item] = part[int(is_out)][place]
        grad_conv, grad_out = (
            scattered(jnp.stack([found[index, is_out] for index in range(layers)])) * scale for is_out in (False, True)
        )
        return (grad_in * scale)[None], grad_conv, grad_out
    chunks = [part.run_chain() for part in parts]
    conv_rows, out_rows = 2 * channels // tm, channels // tm
    grad_inputs, grad_conv, grad_out = pl.pallas_call(
        functools.partial(last_kernel, [len(terms) for terms in reversed(chunks)], float(samples_all), tm),
        out_shape=[
            jax.ShapeDtypeStruct((length, channels), jnp.float32),
            jax.ShapeDtypeStruct((layers, conv_rows, LANES), jnp.float32),
            jax.ShapeDtypeStruct((layers, out_rows, LANES), jnp.float32),
        ],
        compiler_params=pltpu.CompilerParams(vmem_limit_bytes=ADD_BYTES),
        name="scale_all",
    )(*held([term for terms in reversed(chunks) for term in terms]), *held([grad_in]))
    return grad_inputs[None], grad_conv, grad_out


def solution(mesh):
    placed = (
        P("dp", "tm", None),
        P("dp", "tm", None),
        P("dp", "tm", None),
        P("dp", "tm"),
        P(),
        P(),
    )
    return jax.shard_map(
        body,
        mesh=mesh,
        in_specs=placed,
        out_specs=(P("dp", "tm", None), P(None, "tm", "dp"), P(None, "tm", "dp")),
        check_vma=False,
    )
```

```python
import functools

import jax
import jax.numpy as jnp
from jax import lax
from jax.experimental import pallas as pl
from jax.experimental.pallas import tpu as pltpu
from jax.sharding import PartitionSpec as P

LANES = 128
VMEM_BYTES = 24 * 1024 * 1024
ADD_BYTES = 8 * 1024 * 1024
CHAINS = (("y", "x", "z0", "z1"), ("x", "z0", "y", "z1"), ("z0", "y", "x", "z1"))
EXTRA = (16, 0, 0)
NN = (((1,), (0,)), ((), ()))
NT = (((1,), (1,)), ((), ()))
TN = (((0,), (0,)), ((), ()))


def dot(left, right, dims):
    return lax.dot_general(left, right, dims, preferred_element_type=jnp.float32)


def held(arrays, space=pltpu.VMEM):
    return [pltpu.with_memory_space_constraint(x, space) for x in arrays]


def around(x, axis, by):
    count = lax.axis_size(axis)
    return lax.ppermute(x, axis, [(i, (i + by) % count) for i in range(count)])


def column(row, rows):
    return jnp.broadcast_to(row, (LANES, rows)).T


def cost(flops, moved):
    return pl.CostEstimate(flops=flops, bytes_accessed=moved, transcendentals=0)


def pack_kernel(tail_x, tail_gs, tail_gk, weight, x_rows, grad_rows):
    halo, channels = tail_gs.shape
    by_row = column(weight[...], LANES)[LANES - halo :]
    by_row = jnp.concatenate([by_row] * (channels // LANES), axis=1)
    x_rows[...] = tail_x[...]
    grad_rows[0:halo] = (tail_gs[...].astype(jnp.float32) * by_row).astype(jnp.bfloat16)
    grad_rows[halo:] = (tail_gk[...].astype(jnp.float32) * by_row).astype(jnp.bfloat16)


def pack(halo, x, grad_stream_out, grad_skip_out, weight):
    length, channels = x.shape

    def last(rows):
        return pl.BlockSpec((rows, channels), lambda i: (length // rows - 1, 0))

    message = jax.ShapeDtypeStruct((2 * halo, channels), jnp.bfloat16)
    return pl.pallas_call(
        pack_kernel,
        grid=(1,),
        in_specs=[last(2 * halo), last(halo), last(halo), pl.BlockSpec((1, LANES), lambda i: (0, length // LANES - 1))],
        out_specs=[pl.BlockSpec(message.shape, lambda i: (0, 0))] * 2,
        out_shape=[message] * 2,
        compiler_params=pltpu.CompilerParams(vmem_limit_bytes=ADD_BYTES),
        name="pack_borders",
    )(*held((x, grad_stream_out, grad_skip_out, weight), pltpu.HBM))


def load_kernel(
    x, gs, gk, weight, conv_w, out_w, _, x_here, grad_stream, grad_skip, sums, conv_here, out_here,
    gs_raw, gk_raw, weight_here, sems,
):
    pairs = ((weight, weight_here), (gs, gs_raw), (gk, gk_raw), (x, x_here), (conv_w, conv_here), (out_w, out_here))
    copies = [pltpu.make_async_copy(a, b, sems.at[i]) for i, (a, b) in enumerate(pairs)]
    for copy in copies:
        copy.start()
    for copy in copies[:3]:
        copy.wait()
    length, channels = x_here.shape
    by_row = column(weight_here[...], length)
    by_row = jnp.concatenate([by_row] * (channels // LANES), axis=1)
    grad_stream[...] = gs_raw[...].astype(jnp.float32) * by_row
    grad_skip[...] = (gk_raw[...].astype(jnp.float32) * by_row).astype(jnp.bfloat16)
    own_sum = jnp.broadcast_to(jnp.sum(weight_here[...], axis=1, keepdims=True), (1, LANES))
    sums[...] = split_rows(own_sum)
    for copy in copies[3:]:
        copy.wait()


def load_all(x, gs, gk, weight, conv_w, out_w, after):
    shape = x.shape
    vmem, anywhere = pl.BlockSpec(memory_space=pltpu.VMEM), pl.BlockSpec(memory_space=pl.ANY)
    return pl.pallas_call(
        load_kernel,
        in_specs=[anywhere] * 7,
        out_specs=[vmem] * 6,
        out_shape=[
            pltpu.VMEM(shape, jnp.bfloat16),
            pltpu.VMEM(shape, jnp.float32),
            pltpu.VMEM(shape, jnp.bfloat16),
            pltpu.VMEM((16, LANES), jnp.bfloat16),
            pltpu.VMEM(conv_w.shape, jnp.bfloat16),
            pltpu.VMEM(out_w.shape, jnp.bfloat16),
        ],
        scratch_shapes=[
            pltpu.VMEM(shape, jnp.bfloat16),
            pltpu.VMEM(shape, jnp.bfloat16),
            pltpu.VMEM(weight.shape, jnp.float32),
            pltpu.SemaphoreType.DMA((6,)),
        ],
        compiler_params=pltpu.CompilerParams(vmem_limit_bytes=ADD_BYTES),
        cost_estimate=cost(10**7, 6 * 10**6),
        name="load_all",
    )(*held((x, gs, gk, weight, conv_w, out_w), pltpu.HBM), *held([after]))


def split_rows(total):
    high = total.astype(jnp.bfloat16).astype(jnp.float32)
    middle = (total - high).astype(jnp.bfloat16).astype(jnp.float32)
    low = total - high - middle
    row = lax.broadcasted_iota(jnp.int32, (16, LANES), 0)
    rows = jnp.where(row == 0, high, jnp.where(row == 1, middle, jnp.where(row == 2, low, 0.0)))
    return rows.astype(jnp.bfloat16)


def joined_rows(rows):
    return jnp.sum(rows.astype(jnp.float32), axis=0, keepdims=True)


def cut_off(rows, dilation):
    row = lax.broadcasted_iota(jnp.int32, rows.shape, 0)
    return jnp.where(jnp.logical_and(row < dilation, lax.axis_index("tm") == 0), 0.0, rows)


def items_of(layers, chunk):
    third = layers // len(CHAINS)
    high = layers - chunk * third
    return [(index, is_out) for index in reversed(range(high - third, high)) for is_out in (False, True)]


def earlier_rows(plan, index, present, first, last):
    dilation, begin = 2**index, 2 * plan["halo"]
    cut = cut_off(present[begin - dilation : begin], dilation)
    return jnp.concatenate([present[first - dilation : begin - dilation], cut, present[begin : last - dilation]])


def backward(plan, layers, refs_of, conv_w, out_w, grad_proj, grad_stream, past_part, grad_parts):
    halo, length, channels = plan["halo"], plan["length"], plan["channels"]
    own = slice(halo, halo + length)
    items = plan["items"]

    for index in layers:
        dilation, count = 2**index, plan["counts"][index]
        present, earlier, factors, gates = refs_of(index)
        grad_proj[0:count, :channels] = grad_stream[0:count].astype(jnp.bfloat16)
        grad_gated = dot(grad_proj[0:count], out_w[index], NT)
        total = dot(gates[own], grad_proj[0:length], TN)
        plan["store"](total, items.index((index, True)), grad_parts)
        both = factors[halo : halo + count].astype(jnp.float32)
        grad_preact = jnp.concatenate(
            [grad_gated * both[:, :channels], grad_gated * both[:, channels:]], axis=1
        ).astype(jnp.bfloat16)
        spread = dot(grad_preact, conv_w[index], NT)
        past_part[0:count] = spread[:, channels:]
        cut = slice(halo, halo + max(dilation, 8))
        past_part[cut] = cut_off(past_part[cut], dilation)
        rows = plan["counts"][index - 1] if index else length
        grad_stream[0:rows] += spread[0:rows, :channels] + past_part[dilation : dilation + rows]
        past = earlier_rows(plan, index, present, halo, halo + length) if earlier is None else earlier[own]
        total = dot(jnp.concatenate([present[own], past], axis=1), grad_preact[0:length], TN)
        plan["store"](total, items.index((index, False)), grad_parts)


def forward_kernel(plan, prev_x, own_x, conv_w, out_w, all_present, all_earlier, all_factors, all_gates, stream):
    halo, (length, channels) = plan["halo"], own_x.shape
    layers, low = conv_w.shape[0], all_earlier.shape[0]
    pad = 2 ** (layers - 1)
    extent = length + 2 * halo
    begin = 2 * halo
    stream[0:pad] = jnp.zeros((pad, channels), jnp.float32)
    stream[pad : pad + begin] = prev_x[...].astype(jnp.float32)
    stream[pad + begin :] = own_x[...].astype(jnp.float32)
    all_present[0, 0:begin] = prev_x[...]
    all_present[0, begin:] = own_x[...]
    for index in range(layers):
        dilation, start = 2**index, plan["starts"][index]
        present = all_present.at[index]
        if index >= low:
            past = earlier_rows(plan, index, present, start, extent)
        else:
            past = stream[pad + start - dilation : pad + extent - dilation]
            cut = cut_off(past[begin - start : begin - start + 16], dilation)
            past = jnp.concatenate([past[: begin - start], cut, past[begin - start + 16 :]]).astype(jnp.bfloat16)
            all_earlier[index, start:] = past
        preact = dot(jnp.concatenate([present[start:], past], axis=1), conv_w[index], NN)
        filtered = jnp.tanh(preact[:, :channels])
        opening = 0.5 + 0.5 * jnp.tanh(0.5 * preact[:, channels:])
        product = filtered * opening
        gated = product.astype(jnp.bfloat16)
        all_gates[index, start:] = gated
        all_factors[index, start:, :channels] = (opening - filtered * product).astype(jnp.bfloat16)
        all_factors[index, start:, channels:] = (product * (1.0 - opening)).astype(jnp.bfloat16)
        if index < layers - 1:
            after = stream[pad + start :] + dot(gated, out_w[index, :, :channels], NN)
            all_present[index + 1, start:] = after.astype(jnp.bfloat16)
            if index < layers - 2:
                stream[pad + start :] = after


def backward_kernel(plan, first, third, all_present, all_earlier, all_factors, all_gates, conv_w, out_w, *rest):
    refs = rest[: plan["inputs"]]
    *outs, keep, send, grad_stream, grad_proj, past_part = rest[plan["inputs"] + plan["unused"] :]
    halo, length, channels, low = plan["halo"], plan["length"], plan["channels"], all_earlier.shape[0]
    if plan["inputs"] == 4:
        prev_rows, own_grad, own_skip, sums = refs
        *outs, grad_skip = outs
        grad_stream[0:halo] = prev_rows[0:halo].astype(jnp.float32)
        grad_stream[halo:] = own_grad[...]
        grad_skip[0:halo] = prev_rows[halo:]
        grad_skip[halo:] = own_skip[...]
    else:
        grad_before, grad_skip = refs
        grad_stream[...] = grad_before[...]
    grad_proj[:, channels:] = grad_skip[...]

    def refs_of(index):
        earlier = all_earlier.at[index] if index < low else None
        return all_present.at[index], earlier, all_factors.at[index], all_gates.at[index]

    backward(
        plan, list(reversed(range(first, first + third))), refs_of, conv_w, out_w,
        grad_proj, grad_stream, past_part, (keep, send),
    )
    at = 0
    for out in outs:
        out[...] = grad_stream[at : at + out.shape[0]].astype(out.dtype)
        at += out.shape[0]
    if plan["inputs"] == 4:
        plan["finish"](sums, (keep, send))


def store_whole(items, total, item, grad_parts):
    is_out = items[item][1]
    place = sum(kind == is_out for _, kind in items[:item])
    grad_parts[int(is_out)][place] = total.astype(jnp.bfloat16)


def finish_whole(sums, grad_parts):
    pass


def finish_shards(extra, sums, grad_parts):
    for part in grad_parts:
        lead, rows = part.shape[:-2], part.shape[-2]
        for first in range(rows - extra, rows, 16):
            part[(slice(None),) * len(lead) + (slice(first, first + 16),)] = jnp.broadcast_to(
                sums[...], lead + sums.shape
            )


def store_shards(tm, dp, order, bases, total, item, grad_parts):
    keep, send = grad_parts
    t_at, d_at = lax.axis_index("tm"), lax.axis_index("dp")
    core_at = lax.rem(d_at, 2)
    rows = total.shape[0] // tm
    at = pl.ds(bases[item], rows)
    at_bits = bits_of(t_at, d_at, lax.rem, lax.div)
    for y in range(dp // 2):
        near = total[:, (2 * y) * LANES : (2 * y + 1) * LANES]
        far = total[:, (2 * y + 1) * LANES : (2 * y + 2) * LANES]
        mine = jnp.where(core_at == 0, near, far).astype(jnp.bfloat16)
        other = jnp.where(core_at == 0, far, near).astype(jnp.bfloat16)
        for t in range(tm):
            bits = bits_of(t, 2 * y, lambda a, b: a % b, lambda a, b: a // b)
            lead = tuple(lax.rem(bits[name] + at_bits[name], 2) for name in order)
            keep[lead + (at,)] = mine[t * rows : (t + 1) * rows]
            send[lead + (at,)] = other[t * rows : (t + 1) * rows]


def bits_of(t, d, rem, div):
    return {"x": rem(t, 2), "z0": rem(div(t, 2), 2), "z1": div(t, 4), "y": div(d, 2)}


def bases_of(items, tm, channels):
    ends = [0]
    for _, is_out in items:
        ends.append(ends[-1] + (1 if is_out else 2) * channels // tm)
    return ends[:-1], ends[-1]


def run_layers(in_shards, tm, dp, halo, borders, loaded):
    own_x, own_grad, own_skip, sums, conv_w, out_w = loaded
    length, channels = own_x.shape
    layers = conv_w.shape[0]
    third = layers // len(CHAINS)
    low = layers - third
    extent, border = length + 2 * halo, length + halo
    starts = []
    for index in range(layers):
        need = halo if index == layers - 1 else 2 ** (index + 1)
        starts.append(need // 16 * 16)
    counts = [-(-(length + 2 ** (index + 1) - 1) // 16) * 16 for index in range(layers)]
    plan = {"halo": halo, "starts": starts, "counts": counts, "length": length, "channels": channels, "unused": 0}
    plans, shapes = [], []
    for chunk, order in enumerate(CHAINS):
        items = items_of(layers, chunk)
        bases, rows = bases_of(items, tm, channels)
        if in_shards:
            store = functools.partial(store_shards, tm, dp, order, bases)
            finish = functools.partial(finish_shards, EXTRA[chunk])
            shapes.append(2 * [(2,) * len(order) + (rows + EXTRA[chunk], LANES)])
        else:
            store, finish = functools.partial(store_whole, items), finish_whole
            outs = sum(is_out for _, is_out in items)
            shapes.append([(len(items) - outs,) + conv_w.shape[1:], (outs,) + out_w.shape[1:]])
        plans.append(plan | {"items": items, "store": store, "finish": finish})
    vmem, anywhere = pl.BlockSpec(memory_space=pltpu.VMEM), pl.BlockSpec(memory_space=pl.ANY)
    weight_bytes = 2 * (conv_w.size + out_w.size)
    flops = 2 * length * channels * channels
    kept = pl.pallas_call(
        functools.partial(forward_kernel, plan),
        in_specs=[vmem] * 4,
        out_specs=[vmem] * 4,
        out_shape=[
            pltpu.VMEM((layers, extent, channels), jnp.bfloat16),
            pltpu.VMEM((low, extent, channels), jnp.bfloat16),
            pltpu.VMEM((layers, extent, 2 * channels), jnp.bfloat16),
            pltpu.VMEM((layers, extent, channels), jnp.bfloat16),
        ],
        scratch_shapes=[pltpu.VMEM((2 ** (layers - 1) + extent, channels), jnp.float32)],
        compiler_params=pltpu.CompilerParams(vmem_limit_bytes=VMEM_BYTES),
        cost_estimate=cost(flops * 5 * layers, weight_bytes),
        name="forward",
    )(*held((borders[0], own_x, conv_w, out_w)))

    def backward_of(step, inputs, outs, after):
        more = {"inputs": len(inputs), "unused": len(after)}
        return pl.pallas_call(
            functools.partial(backward_kernel, plans[step] | more, layers - (step + 1) * third, third),
            in_specs=[vmem] * (6 + len(inputs)) + [anywhere] * len(after),
            out_specs=[vmem] * (len(outs) + 2),
            out_shape=[pltpu.VMEM((rows, channels), kind) for rows, kind in outs]
            + [pltpu.VMEM(shape, jnp.bfloat16) for shape in shapes[step]],
            scratch_shapes=[
                pltpu.VMEM((border, channels), jnp.float32),
                pltpu.VMEM((border, 2 * channels), jnp.bfloat16),
                pltpu.VMEM((border, channels), jnp.float32),
            ],
            compiler_params=pltpu.CompilerParams(vmem_limit_bytes=VMEM_BYTES),
            cost_estimate=cost(flops * 12 * third, weight_bytes),
            name=("last_third", "middle_third", "first_third")[step],
        )(*held((*kept, conv_w, out_w, *inputs, *after)))

    whole = (border, jnp.float32)
    grad_stream, grad_skip, *last = backward_of(
        0, (borders[1], own_grad, own_skip, sums), [whole, (border, jnp.bfloat16)], []
    )
    parts = [last]
    if in_shards:
        parts[0] = Chunk(tm, dp, 0, *last)
    grad_stream, *middle = backward_of(1, (grad_stream, grad_skip), [whole], [])
    other, own, *first = backward_of(
        2, (grad_stream, grad_skip), [(halo, jnp.bfloat16), (length - halo, jnp.float32)],
        [parts[0].next_message()] if in_shards else [],
    )
    parts += [middle, first]
    if in_shards:
        for step in (1, 2):
            parts[step] = Chunk(tm, dp, step, *parts[step])
    return other, own, parts


def add_kernel(count, groups, *refs):
    arrays, outs = refs[:count], refs[-len(groups) :]
    for out, pieces in zip(outs, groups):
        lead = (slice(None),) * (len(out.shape) - 2)
        for first, rows, with_total, terms in pieces:
            body = rows - 16 if with_total else rows
            value = 0.0
            for array, at, begin in terms:
                value = value + arrays[array][at + lead + (slice(begin, begin + body),)].astype(jnp.float32)
            out[lead + (slice(first, first + body),)] = value.astype(out.dtype)
            if with_total:
                total = 0.0
                for array, at, begin in terms:
                    rows_at = slice(begin + body, begin + rows)
                    total = total + joined_rows(arrays[array][at + (0,) * len(lead) + (rows_at,)])
                slab = split_rows(total)
                out[lead + (slice(first + body, first + rows),)] = jnp.broadcast_to(slab, out.shape[:-2] + slab.shape)


def add_up(arrays, groups, shapes, after, name):
    vmem = pl.BlockSpec(memory_space=pltpu.VMEM)
    return pl.pallas_call(
        functools.partial(add_kernel, len(arrays), groups),
        in_specs=[vmem] * len(arrays) + [pl.BlockSpec(memory_space=pl.ANY)] * len(after),
        out_specs=[vmem] * len(groups),
        out_shape=[pltpu.VMEM(shape, jnp.bfloat16) for shape in shapes],
        compiler_params=pltpu.CompilerParams(vmem_limit_bytes=ADD_BYTES),
        name=name,
    )(*held(arrays), *held(after))


def first_block(array, first, rows):
    return array[(0,) * (len(array.shape) - 2) + (slice(first, first + rows),)].astype(jnp.float32)


def first_block(array, first, rows):
    return array[(0,) * (len(array.shape) - 2) + (slice(first, first + rows),)].astype(jnp.float32)


def last_kernel(counts, samples_all, tm, *refs):
    chunks = []
    for count in counts:
        chunks.insert(0, refs[:count])
        refs = refs[count:]
    other, own, grad_inputs, grad_conv, grad_out = refs
    layers, channels = grad_conv.shape[0], own.shape[1]
    total = 0.0
    for term in chunks[0]:
        total = total + jnp.sum(first_block(term, term.shape[-2] - 16, 16), axis=0, keepdims=True)
    scale = samples_all / total
    for chunk, terms in enumerate(chunks):
        items = items_of(layers, chunk)
        for (index, is_out), base in zip(items, bases_of(items, tm, channels)[0]):
            out = grad_out if is_out else grad_conv
            value = 0.0
            for term in terms:
                value = value + first_block(term, base, out.shape[1])
            out[index] = value * scale
    for first in range(0, channels, LANES):
        lanes = slice(first, first + LANES)
        grad_inputs[0 : own.shape[0], lanes] = own[:, lanes] * scale
        grad_inputs[own.shape[0] :, lanes] = other[:, lanes].astype(jnp.float32) * scale


class Chunk:
    def __init__(self, tm, dp, chunk, keep, send):
        self.tm, self.dp, self.chunk, self.rows = tm, dp, chunk, keep.shape[-2]
        self.message = None
        self.terms = [keep, swapped(tm, dp, send, "core")]

    def next_message(self, after=()):
        if self.message is None:
            left = len(CHAINS[self.chunk]) + 2 - len(self.terms)
            pieces = []
            for i, v in enumerate(self.terms):
                pieces.append((i, (0,) * (len(v.shape) - 2 - left) + (1,), 0))
            (self.message,) = add_up(
                self.terms, [[(0, self.rows, EXTRA[self.chunk] > 0, pieces)]], [(2,) * (left - 1) + (self.rows, LANES)], after,
                "add_chunk%d_step%d" % (self.chunk, len(self.terms) - 1),
            )
        return self.message

    def run_chain(self, after=()):
        for step, name in enumerate(CHAINS[self.chunk]):
            self.terms.append(swapped(self.tm, self.dp, self.next_message(after if step == 1 else ()), name))
            self.message = None
        return self.terms


def swapped(tm, dp, value, name):
    over_t, over_d = {"core": (0, 1), "y": (0, 2), "x": (1, 0), "z0": (2, 0), "z1": (4, 0)}[name]
    pairs = [(t * dp + d, (t ^ over_t) * dp + (d ^ over_d)) for t in range(tm) for d in range(dp)]
    return lax.ppermute(value, ("tm", "dp"), pairs)


def scattered(part):
    columns = lax.psum_scatter(part, "dp", scatter_dimension=2, tiled=True).astype(jnp.float32)
    return lax.psum_scatter(columns, "tm", scatter_dimension=1, tiled=True)


def body(inputs, grad_stream_out, grad_skip_out, sample_weight, conv_weight, out_weight):
    tm, dp = lax.axis_size("tm"), lax.axis_size("dp")
    batch, length, channels = inputs.shape
    layers = conv_weight.shape[0]
    third = layers // len(CHAINS)
    halo = 2**layers
    samples_all = batch * length * tm * dp
    x, gs, gk = inputs[0], grad_stream_out[0], grad_skip_out[0]
    x_rows, grad_rows = pack(halo, x, gs, gk, sample_weight)
    borders = [around(x_rows, "tm", 1), around(grad_rows, "tm", 1)]
    loaded = load_all(x, gs, gk, sample_weight, conv_weight, out_weight, x_rows)
    in_shards = tm == 8 and dp == 4 and channels // tm % 16 == 0 and 2 * channels == dp * LANES
    other, own, parts = run_layers(in_shards, tm, dp, halo, borders, loaded)
    other = around(other, "tm", -1)
    if not in_shards:
        scale = samples_all / lax.psum(jnp.sum(sample_weight), ("tm", "dp"))
        found = {}
        for chunk, part in enumerate(parts):
            items = items_of(layers, chunk)
            for is_out in (False, True):
                for place, item in enumerate(item for item in items if item[1] == is_out):
                    found[item] = part[int(is_out)][place]
        grad_conv, grad_out = (
            scattered(jnp.stack([found[index, is_out] for index in range(layers)])) * scale for is_out in (False, True)
        )
        return (jnp.concatenate([own, other]) * scale)[None], grad_conv, grad_out
    chunks = [part.run_chain([other] if part is parts[0] else ()) for part in parts]
    conv_rows, out_rows = 2 * channels // tm, channels // tm
    grad_inputs, grad_conv, grad_out = pl.pallas_call(
        functools.partial(last_kernel, [len(terms) for terms in reversed(chunks)], float(samples_all), tm),
        out_shape=[
            jax.ShapeDtypeStruct((length, channels), jnp.float32),
            jax.ShapeDtypeStruct((layers, conv_rows, LANES), jnp.float32),
            jax.ShapeDtypeStruct((layers, out_rows, LANES), jnp.float32),
        ],
        compiler_params=pltpu.CompilerParams(vmem_limit_bytes=ADD_BYTES),
        name="scale_all",
    )(*held([term for terms in reversed(chunks) for term in terms]), *held([other, own]))
    return grad_inputs[None], grad_conv, grad_out


def solution(mesh):
    placed = (
        P("dp", "tm", None),
        P("dp", "tm", None),
        P("dp", "tm", None),
        P("dp", "tm"),
        P(),
        P(),
    )
    return jax.shard_map(
        body,
        mesh=mesh,
        in_specs=placed,
        out_specs=(P("dp", "tm", None), P(None, "tm", "dp"), P(None, "tm", "dp")),
        check_vma=False,
    )
```

```python
import functools

import jax
import jax.numpy as jnp
from jax import lax
from jax.experimental import pallas as pl
from jax.experimental.pallas import tpu as pltpu
from jax.sharding import PartitionSpec as P

LANES = 128
VMEM_BYTES = 24 * 1024 * 1024
ADD_BYTES = 8 * 1024 * 1024
CHAINS = (("x", "z0", "y", "z1"), ("z0", "y", "x", "z1"), ("y", "x", "z0", "z1"))
EXTRA = (16, 0, 0)
NN = (((1,), (0,)), ((), ()))
NT = (((1,), (1,)), ((), ()))
TN = (((0,), (0,)), ((), ()))


def dot(left, right, dims):
    return lax.dot_general(left, right, dims, preferred_element_type=jnp.float32)


def held(arrays, space=pltpu.VMEM):
    return [pltpu.with_memory_space_constraint(x, space) for x in arrays]


def around(x, axis, by):
    count = lax.axis_size(axis)
    return lax.ppermute(x, axis, [(i, (i + by) % count) for i in range(count)])


def column(row, rows):
    return jnp.broadcast_to(row, (LANES, rows)).T


def cost(flops, moved):
    return pl.CostEstimate(flops=flops, bytes_accessed=moved, transcendentals=0)


def pack_kernel(tail_x, tail_gs, tail_gk, weight, x_rows, grad_rows):
    halo, channels = tail_gs.shape
    by_row = column(weight[...], LANES)[LANES - halo :]
    by_row = jnp.concatenate([by_row] * (channels // LANES), axis=1)
    x_rows[...] = tail_x[...]
    grad_rows[0:halo] = (tail_gs[...].astype(jnp.float32) * by_row).astype(jnp.bfloat16)
    grad_rows[halo:] = (tail_gk[...].astype(jnp.float32) * by_row).astype(jnp.bfloat16)


def pack(halo, x, grad_stream_out, grad_skip_out, weight):
    length, channels = x.shape

    def last(rows):
        return pl.BlockSpec((rows, channels), lambda i: (length // rows - 1, 0))

    message = jax.ShapeDtypeStruct((2 * halo, channels), jnp.bfloat16)
    return pl.pallas_call(
        pack_kernel,
        grid=(1,),
        in_specs=[last(2 * halo), last(halo), last(halo), pl.BlockSpec((1, LANES), lambda i: (0, length // LANES - 1))],
        out_specs=[pl.BlockSpec(message.shape, lambda i: (0, 0))] * 2,
        out_shape=[message] * 2,
        compiler_params=pltpu.CompilerParams(vmem_limit_bytes=ADD_BYTES),
        name="pack_borders",
    )(*held((x, grad_stream_out, grad_skip_out, weight), pltpu.HBM))


def load_kernel(
    x, gs, gk, weight, conv_w, out_w, _, x_here, grad_stream, grad_skip, sums, conv_here, out_here,
    gs_raw, gk_raw, weight_here, sems,
):
    pairs = ((weight, weight_here), (gs, gs_raw), (gk, gk_raw), (x, x_here), (conv_w, conv_here), (out_w, out_here))
    copies = [pltpu.make_async_copy(a, b, sems.at[i]) for i, (a, b) in enumerate(pairs)]
    for copy in copies:
        copy.start()
    for copy in copies[:3]:
        copy.wait()
    length, channels = x_here.shape
    by_row = column(weight_here[...], length)
    by_row = jnp.concatenate([by_row] * (channels // LANES), axis=1)
    grad_stream[...] = gs_raw[...].astype(jnp.float32) * by_row
    grad_skip[...] = (gk_raw[...].astype(jnp.float32) * by_row).astype(jnp.bfloat16)
    own_sum = jnp.broadcast_to(jnp.sum(weight_here[...], axis=1, keepdims=True), (1, LANES))
    sums[...] = split_rows(own_sum)
    for copy in copies[3:]:
        copy.wait()


def load_all(x, gs, gk, weight, conv_w, out_w, after):
    shape = x.shape
    vmem, anywhere = pl.BlockSpec(memory_space=pltpu.VMEM), pl.BlockSpec(memory_space=pl.ANY)
    return pl.pallas_call(
        load_kernel,
        in_specs=[anywhere] * 7,
        out_specs=[vmem] * 6,
        out_shape=[
            pltpu.VMEM(shape, jnp.bfloat16),
            pltpu.VMEM(shape, jnp.float32),
            pltpu.VMEM(shape, jnp.bfloat16),
            pltpu.VMEM((16, LANES), jnp.bfloat16),
            pltpu.VMEM(conv_w.shape, jnp.bfloat16),
            pltpu.VMEM(out_w.shape, jnp.bfloat16),
        ],
        scratch_shapes=[
            pltpu.VMEM(shape, jnp.bfloat16),
            pltpu.VMEM(shape, jnp.bfloat16),
            pltpu.VMEM(weight.shape, jnp.float32),
            pltpu.SemaphoreType.DMA((6,)),
        ],
        compiler_params=pltpu.CompilerParams(vmem_limit_bytes=ADD_BYTES),
        cost_estimate=cost(10**7, 6 * 10**6),
        name="load_all",
    )(*held((x, gs, gk, weight, conv_w, out_w), pltpu.HBM), *held([after]))


def split_rows(total):
    high = total.astype(jnp.bfloat16).astype(jnp.float32)
    middle = (total - high).astype(jnp.bfloat16).astype(jnp.float32)
    low = total - high - middle
    row = lax.broadcasted_iota(jnp.int32, (16, LANES), 0)
    rows = jnp.where(row == 0, high, jnp.where(row == 1, middle, jnp.where(row == 2, low, 0.0)))
    return rows.astype(jnp.bfloat16)


def joined_rows(rows):
    return jnp.sum(rows.astype(jnp.float32), axis=0, keepdims=True)


def cut_off(rows, dilation):
    row = lax.broadcasted_iota(jnp.int32, rows.shape, 0)
    return jnp.where(jnp.logical_and(row < dilation, lax.axis_index("tm") == 0), 0.0, rows)


def items_of(layers, chunk):
    third = layers // len(CHAINS)
    high = layers - chunk * third
    return [(index, is_out) for index in reversed(range(high - third, high)) for is_out in (False, True)]


def earlier_rows(plan, index, present, first, last):
    dilation, begin = 2**index, 2 * plan["halo"]
    cut = cut_off(present[begin - dilation : begin], dilation)
    return jnp.concatenate([present[first - dilation : begin - dilation], cut, present[begin : last - dilation]])


def backward(plan, layers, refs_of, conv_w, out_w, grad_proj, grad_stream, past_part, grad_parts):
    halo, length, channels = plan["halo"], plan["length"], plan["channels"]
    own = slice(halo, halo + length)
    items = plan["items"]

    for index in layers:
        dilation, count = 2**index, plan["counts"][index]
        present, earlier, factors, gates = refs_of(index)
        grad_proj[0:count, :channels] = grad_stream[0:count].astype(jnp.bfloat16)
        grad_gated = dot(grad_proj[0:count], out_w[index], NT)
        total = dot(gates[own], grad_proj[0:length], TN)
        plan["store"](total, items.index((index, True)), grad_parts)
        both = factors[halo : halo + count].astype(jnp.float32)
        grad_preact = jnp.concatenate(
            [grad_gated * both[:, :channels], grad_gated * both[:, channels:]], axis=1
        ).astype(jnp.bfloat16)
        spread = dot(grad_preact, conv_w[index], NT)
        past_part[0:count] = spread[:, channels:]
        cut = slice(halo, halo + max(dilation, 8))
        past_part[cut] = cut_off(past_part[cut], dilation)
        rows = plan["counts"][index - 1] if index else length
        grad_stream[0:rows] += spread[0:rows, :channels] + past_part[dilation : dilation + rows]
        past = earlier_rows(plan, index, present, halo, halo + length) if earlier is None else earlier[own]
        total = dot(jnp.concatenate([present[own], past], axis=1), grad_preact[0:length], TN)
        plan["store"](total, items.index((index, False)), grad_parts)


def forward_kernel(plan, prev_x, own_x, conv_w, out_w, all_present, all_earlier, all_factors, all_gates, stream):
    halo, (length, channels) = plan["halo"], own_x.shape
    layers, low = conv_w.shape[0], all_earlier.shape[0]
    pad = 2 ** (layers - 1)
    extent = length + 2 * halo
    begin = 2 * halo
    stream[0:pad] = jnp.zeros((pad, channels), jnp.float32)
    stream[pad : pad + begin] = prev_x[...].astype(jnp.float32)
    stream[pad + begin :] = own_x[...].astype(jnp.float32)
    all_present[0, 0:begin] = prev_x[...]
    all_present[0, begin:] = own_x[...]
    for index in range(layers):
        dilation, start = 2**index, plan["starts"][index]
        present = all_present.at[index]
        if index >= low:
            past = earlier_rows(plan, index, present, start, extent)
        else:
            past = stream[pad + start - dilation : pad + extent - dilation]
            cut = cut_off(past[begin - start : begin - start + 16], dilation)
            past = jnp.concatenate([past[: begin - start], cut, past[begin - start + 16 :]]).astype(jnp.bfloat16)
            all_earlier[index, start:] = past
        preact = dot(jnp.concatenate([present[start:], past], axis=1), conv_w[index], NN)
        filtered = jnp.tanh(preact[:, :channels])
        opening = 0.5 + 0.5 * jnp.tanh(0.5 * preact[:, channels:])
        product = filtered * opening
        gated = product.astype(jnp.bfloat16)
        all_gates[index, start:] = gated
        all_factors[index, start:, :channels] = (opening - filtered * product).astype(jnp.bfloat16)
        all_factors[index, start:, channels:] = (product * (1.0 - opening)).astype(jnp.bfloat16)
        if index < layers - 1:
            after = stream[pad + start :] + dot(gated, out_w[index, :, :channels], NN)
            all_present[index + 1, start:] = after.astype(jnp.bfloat16)
            if index < layers - 2:
                stream[pad + start :] = after


def backward_kernel(plan, first, third, all_present, all_earlier, all_factors, all_gates, conv_w, out_w, *rest):
    refs = rest[: plan["inputs"]]
    *outs, keep, send, grad_stream, grad_proj, past_part = rest[plan["inputs"] + plan["unused"] :]
    halo, length, channels, low = plan["halo"], plan["length"], plan["channels"], all_earlier.shape[0]
    if plan["inputs"] == 4:
        prev_rows, own_grad, own_skip, sums = refs
        *outs, grad_skip = outs
        grad_stream[0:halo] = prev_rows[0:halo].astype(jnp.float32)
        grad_stream[halo:] = own_grad[...]
        grad_skip[0:halo] = prev_rows[halo:]
        grad_skip[halo:] = own_skip[...]
    else:
        grad_before, grad_skip = refs
        grad_stream[...] = grad_before[...]
    grad_proj[:, channels:] = grad_skip[...]

    def refs_of(index):
        earlier = all_earlier.at[index] if index < low else None
        return all_present.at[index], earlier, all_factors.at[index], all_gates.at[index]

    backward(
        plan, list(reversed(range(first, first + third))), refs_of, conv_w, out_w,
        grad_proj, grad_stream, past_part, (keep, send),
    )
    at = 0
    for out in outs:
        out[...] = grad_stream[at : at + out.shape[0]].astype(out.dtype)
        at += out.shape[0]
    if plan["inputs"] == 4:
        plan["finish"](sums, (keep, send))


def store_whole(items, total, item, grad_parts):
    is_out = items[item][1]
    place = sum(kind == is_out for _, kind in items[:item])
    grad_parts[int(is_out)][place] = total.astype(jnp.bfloat16)


def finish_whole(sums, grad_parts):
    pass


def finish_shards(extra, sums, grad_parts):
    for part in grad_parts:
        lead, rows = part.shape[:-2], part.shape[-2]
        for first in range(rows - extra, rows, 16):
            part[(slice(None),) * len(lead) + (slice(first, first + 16),)] = jnp.broadcast_to(
                sums[...], lead + sums.shape
            )


def store_shards(tm, dp, order, bases, total, item, grad_parts):
    keep, send = grad_parts
    t_at, d_at = lax.axis_index("tm"), lax.axis_index("dp")
    core_at = lax.rem(d_at, 2)
    rows = total.shape[0] // tm
    at = pl.ds(bases[item], rows)
    at_bits = bits_of(t_at, d_at, lax.rem, lax.div)
    for y in range(dp // 2):
        near = total[:, (2 * y) * LANES : (2 * y + 1) * LANES]
        far = total[:, (2 * y + 1) * LANES : (2 * y + 2) * LANES]
        mine = jnp.where(core_at == 0, near, far).astype(jnp.bfloat16)
        other = jnp.where(core_at == 0, far, near).astype(jnp.bfloat16)
        for t in range(tm):
            bits = bits_of(t, 2 * y, lambda a, b: a % b, lambda a, b: a // b)
            lead = tuple(lax.rem(bits[name] + at_bits[name], 2) for name in order)
            keep[lead + (at,)] = mine[t * rows : (t + 1) * rows]
            send[lead + (at,)] = other[t * rows : (t + 1) * rows]


def bits_of(t, d, rem, div):
    return {"x": rem(t, 2), "z0": rem(div(t, 2), 2), "z1": div(t, 4), "y": div(d, 2)}


def bases_of(items, tm, channels):
    ends = [0]
    for _, is_out in items:
        ends.append(ends[-1] + (1 if is_out else 2) * channels // tm)
    return ends[:-1], ends[-1]


def run_layers(in_shards, tm, dp, halo, borders, loaded):
    own_x, own_grad, own_skip, sums, conv_w, out_w = loaded
    length, channels = own_x.shape
    layers = conv_w.shape[0]
    third = layers // len(CHAINS)
    low = layers - third
    extent, border = length + 2 * halo, length + halo
    starts = []
    for index in range(layers):
        need = halo if index == layers - 1 else 2 ** (index + 1)
        starts.append(need // 16 * 16)
    counts = [-(-(length + 2 ** (index + 1) - 1) // 16) * 16 for index in range(layers)]
    plan = {"halo": halo, "starts": starts, "counts": counts, "length": length, "channels": channels, "unused": 0}
    plans, shapes = [], []
    for chunk, order in enumerate(CHAINS):
        items = items_of(layers, chunk)
        bases, rows = bases_of(items, tm, channels)
        if in_shards:
            store = functools.partial(store_shards, tm, dp, order, bases)
            finish = functools.partial(finish_shards, EXTRA[chunk])
            shapes.append(2 * [(2,) * len(order) + (rows + EXTRA[chunk], LANES)])
        else:
            store, finish = functools.partial(store_whole, items), finish_whole
            outs = sum(is_out for _, is_out in items)
            shapes.append([(len(items) - outs,) + conv_w.shape[1:], (outs,) + out_w.shape[1:]])
        plans.append(plan | {"items": items, "store": store, "finish": finish})
    vmem, anywhere = pl.BlockSpec(memory_space=pltpu.VMEM), pl.BlockSpec(memory_space=pl.ANY)
    weight_bytes = 2 * (conv_w.size + out_w.size)
    flops = 2 * length * channels * channels
    kept = pl.pallas_call(
        functools.partial(forward_kernel, plan),
        in_specs=[vmem] * 4,
        out_specs=[vmem] * 4,
        out_shape=[
            pltpu.VMEM((layers, extent, channels), jnp.bfloat16),
            pltpu.VMEM((low, extent, channels), jnp.bfloat16),
            pltpu.VMEM((layers, extent, 2 * channels), jnp.bfloat16),
            pltpu.VMEM((layers, extent, channels), jnp.bfloat16),
        ],
        scratch_shapes=[pltpu.VMEM((2 ** (layers - 1) + extent, channels), jnp.float32)],
        compiler_params=pltpu.CompilerParams(vmem_limit_bytes=VMEM_BYTES),
        cost_estimate=cost(flops * 5 * layers, weight_bytes),
        name="forward",
    )(*held((borders[0], own_x, conv_w, out_w)))

    def backward_of(step, inputs, outs, after):
        more = {"inputs": len(inputs), "unused": len(after)}
        return pl.pallas_call(
            functools.partial(backward_kernel, plans[step] | more, layers - (step + 1) * third, third),
            in_specs=[vmem] * (6 + len(inputs)) + [anywhere] * len(after),
            out_specs=[vmem] * (len(outs) + 2),
            out_shape=[pltpu.VMEM((rows, channels), kind) for rows, kind in outs]
            + [pltpu.VMEM(shape, jnp.bfloat16) for shape in shapes[step]],
            scratch_shapes=[
                pltpu.VMEM((border, channels), jnp.float32),
                pltpu.VMEM((border, 2 * channels), jnp.bfloat16),
                pltpu.VMEM((border, channels), jnp.float32),
            ],
            compiler_params=pltpu.CompilerParams(vmem_limit_bytes=VMEM_BYTES),
            cost_estimate=cost(flops * 12 * third, weight_bytes),
            name=("last_third", "middle_third", "first_third")[step],
        )(*held((*kept, conv_w, out_w, *inputs, *after)))

    whole = (border, jnp.float32)
    grad_stream, grad_skip, *last = backward_of(
        0, (borders[1], own_grad, own_skip, sums), [whole, (border, jnp.bfloat16)], []
    )
    parts = [last]
    if in_shards:
        parts[0] = Chunk(tm, dp, 0, *last)
    grad_stream, *middle = backward_of(1, (grad_stream, grad_skip), [whole], [])
    other, own, *first = backward_of(
        2, (grad_stream, grad_skip), [(halo, jnp.bfloat16), (length - halo, jnp.float32)],
        [parts[0].next_message()] if in_shards else [],
    )
    parts += [middle, first]
    if in_shards:
        for step in (1, 2):
            parts[step] = Chunk(tm, dp, step, *parts[step])
    return other, own, parts


def add_kernel(count, groups, *refs):
    arrays, outs = refs[:count], refs[-len(groups) :]
    for out, pieces in zip(outs, groups):
        lead = (slice(None),) * (len(out.shape) - 2)
        for first, rows, with_total, terms in pieces:
            body = rows - 16 if with_total else rows
            value = 0.0
            for array, at, begin in terms:
                value = value + arrays[array][at + lead + (slice(begin, begin + body),)].astype(jnp.float32)
            out[lead + (slice(first, first + body),)] = value.astype(out.dtype)
            if with_total:
                total = 0.0
                for array, at, begin in terms:
                    rows_at = slice(begin + body, begin + rows)
                    total = total + joined_rows(arrays[array][at + (0,) * len(lead) + (rows_at,)])
                slab = split_rows(total)
                out[lead + (slice(first + body, first + rows),)] = jnp.broadcast_to(slab, out.shape[:-2] + slab.shape)


def add_up(arrays, groups, shapes, after, name):
    vmem = pl.BlockSpec(memory_space=pltpu.VMEM)
    return pl.pallas_call(
        functools.partial(add_kernel, len(arrays), groups),
        in_specs=[vmem] * len(arrays) + [pl.BlockSpec(memory_space=pl.ANY)] * len(after),
        out_specs=[vmem] * len(groups),
        out_shape=[pltpu.VMEM(shape, jnp.bfloat16) for shape in shapes],
        compiler_params=pltpu.CompilerParams(vmem_limit_bytes=ADD_BYTES),
        name=name,
    )(*held(arrays), *held(after))


def first_block(array, first, rows):
    return array[(0,) * (len(array.shape) - 2) + (slice(first, first + rows),)].astype(jnp.float32)


def first_block(array, first, rows):
    return array[(0,) * (len(array.shape) - 2) + (slice(first, first + rows),)].astype(jnp.float32)


def last_kernel(counts, samples_all, tm, *refs):
    chunks = []
    for count in counts:
        chunks.insert(0, refs[:count])
        refs = refs[count:]
    other, own, grad_inputs, grad_conv, grad_out = refs
    layers, channels = grad_conv.shape[0], own.shape[1]
    total = 0.0
    for term in chunks[0]:
        total = total + jnp.sum(first_block(term, term.shape[-2] - 16, 16), axis=0, keepdims=True)
    scale = samples_all / total
    for chunk, terms in enumerate(chunks):
        items = items_of(layers, chunk)
        for (index, is_out), base in zip(items, bases_of(items, tm, channels)[0]):
            out = grad_out if is_out else grad_conv
            value = 0.0
            for term in terms:
                value = value + first_block(term, base, out.shape[1])
            out[index] = value * scale
    for first in range(0, channels, LANES):
        lanes = slice(first, first + LANES)
        grad_inputs[0 : own.shape[0], lanes] = own[:, lanes] * scale
        grad_inputs[own.shape[0] :, lanes] = other[:, lanes].astype(jnp.float32) * scale


class Chunk:
    def __init__(self, tm, dp, chunk, keep, send):
        self.tm, self.dp, self.chunk, self.rows = tm, dp, chunk, keep.shape[-2]
        self.message = None
        self.terms = [keep, swapped(tm, dp, send, "core")]

    def next_message(self, after=()):
        if self.message is None:
            left = len(CHAINS[self.chunk]) + 2 - len(self.terms)
            pieces = []
            for i, v in enumerate(self.terms):
                pieces.append((i, (0,) * (len(v.shape) - 2 - left) + (1,), 0))
            (self.message,) = add_up(
                self.terms, [[(0, self.rows, EXTRA[self.chunk] > 0, pieces)]], [(2,) * (left - 1) + (self.rows, LANES)], after,
                "add_chunk%d_step%d" % (self.chunk, len(self.terms) - 1),
            )
        return self.message

    def run_chain(self, after=()):
        for step, name in enumerate(CHAINS[self.chunk]):
            self.terms.append(swapped(self.tm, self.dp, self.next_message(after if step == 1 else ()), name))
            self.message = None
        return self.terms


def swapped(tm, dp, value, name):
    over_t, over_d = {"core": (0, 1), "y": (0, 2), "x": (1, 0), "z0": (2, 0), "z1": (4, 0)}[name]
    pairs = [(t * dp + d, (t ^ over_t) * dp + (d ^ over_d)) for t in range(tm) for d in range(dp)]
    return lax.ppermute(value, ("tm", "dp"), pairs)


def scattered(part):
    columns = lax.psum_scatter(part, "dp", scatter_dimension=2, tiled=True).astype(jnp.float32)
    return lax.psum_scatter(columns, "tm", scatter_dimension=1, tiled=True)


def body(inputs, grad_stream_out, grad_skip_out, sample_weight, conv_weight, out_weight):
    tm, dp = lax.axis_size("tm"), lax.axis_size("dp")
    batch, length, channels = inputs.shape
    layers = conv_weight.shape[0]
    third = layers // len(CHAINS)
    halo = 2**layers
    samples_all = batch * length * tm * dp
    x, gs, gk = inputs[0], grad_stream_out[0], grad_skip_out[0]
    x_rows, grad_rows = pack(halo, x, gs, gk, sample_weight)
    borders = [around(x_rows, "tm", 1), around(grad_rows, "tm", 1)]
    loaded = load_all(x, gs, gk, sample_weight, conv_weight, out_weight, x_rows)
    in_shards = tm == 8 and dp == 4 and channels // tm % 16 == 0 and 2 * channels == dp * LANES
    other, own, parts = run_layers(in_shards, tm, dp, halo, borders, loaded)
    other = around(other, "tm", -1)
    if not in_shards:
        scale = samples_all / lax.psum(jnp.sum(sample_weight), ("tm", "dp"))
        found = {}
        for chunk, part in enumerate(parts):
            items = items_of(layers, chunk)
            for is_out in (False, True):
                for place, item in enumerate(item for item in items if item[1] == is_out):
                    found[item] = part[int(is_out)][place]
        grad_conv, grad_out = (
            scattered(jnp.stack([found[index, is_out] for index in range(layers)])) * scale for is_out in (False, True)
        )
        return (jnp.concatenate([own, other]) * scale)[None], grad_conv, grad_out
    chunks = [part.run_chain([other] if part is parts[0] else ()) for part in parts]
    conv_rows, out_rows = 2 * channels // tm, channels // tm
    grad_inputs, grad_conv, grad_out = pl.pallas_call(
        functools.partial(last_kernel, [len(terms) for terms in reversed(chunks)], float(samples_all), tm),
        out_shape=[
            jax.ShapeDtypeStruct((length, channels), jnp.float32),
            jax.ShapeDtypeStruct((layers, conv_rows, LANES), jnp.float32),
            jax.ShapeDtypeStruct((layers, out_rows, LANES), jnp.float32),
        ],
        compiler_params=pltpu.CompilerParams(vmem_limit_bytes=ADD_BYTES),
        name="scale_all",
    )(*held([term for terms in reversed(chunks) for term in terms]), *held([other, own]))
    return grad_inputs[None], grad_conv, grad_out


def solution(mesh):
    placed = (
        P("dp", "tm", None),
        P("dp", "tm", None),
        P("dp", "tm", None),
        P("dp", "tm"),
        P(),
        P(),
    )
    return jax.shard_map(
        body,
        mesh=mesh,
        in_specs=placed,
        out_specs=(P("dp", "tm", None), P(None, "tm", "dp"), P(None, "tm", "dp")),
        check_vma=False,
    )
```

```python
import functools

import jax
import jax.numpy as jnp
from jax import lax
from jax.experimental import pallas as pl
from jax.experimental.pallas import tpu as pltpu
from jax.sharding import PartitionSpec as P

LANES = 128
VMEM_BYTES = 24 * 1024 * 1024
ADD_BYTES = 8 * 1024 * 1024
CHAINS = (("x", "z0", "y", "z1"), ("z0", "y", "x", "z1"), ("y", "x", "z0", "z1"))
EXTRA = (16, 0, 0)
NN = (((1,), (0,)), ((), ()))
NT = (((1,), (1,)), ((), ()))
TN = (((0,), (0,)), ((), ()))


def dot(left, right, dims):
    return lax.dot_general(left, right, dims, preferred_element_type=jnp.float32)


def held(arrays, space=pltpu.VMEM):
    return [pltpu.with_memory_space_constraint(x, space) for x in arrays]


def around(x, axis, by):
    count = lax.axis_size(axis)
    return lax.ppermute(x, axis, [(i, (i + by) % count) for i in range(count)])


def column(row, rows):
    return jnp.broadcast_to(row, (LANES, rows)).T


def cost(flops, moved):
    return pl.CostEstimate(flops=flops, bytes_accessed=moved, transcendentals=0)


def take_kernel(x, rows, sem):
    copy = pltpu.make_async_copy(x.at[pl.ds(x.shape[0] - rows.shape[0], rows.shape[0])], rows, sem)
    copy.start()
    copy.wait()


def last_rows(x, rows):
    return pl.pallas_call(
        take_kernel,
        in_specs=[pl.BlockSpec(memory_space=pl.ANY)],
        out_specs=pl.BlockSpec(memory_space=pltpu.VMEM),
        out_shape=pltpu.VMEM((rows, x.shape[1]), x.dtype),
        scratch_shapes=[pltpu.SemaphoreType.DMA],
        compiler_params=pltpu.CompilerParams(vmem_limit_bytes=ADD_BYTES),
        name="take_border",
    )(*held([x], pltpu.HBM))


def load_kernel(
    x, gs, gk, weight, conv_w, out_w, _, x_here, grad_stream, grad_skip, sums, conv_here, out_here, grad_rows,
    gs_raw, gk_raw, weight_here, sems,
):
    pairs = ((weight, weight_here), (gs, gs_raw), (gk, gk_raw), (x, x_here), (conv_w, conv_here), (out_w, out_here))
    copies = [pltpu.make_async_copy(a, b, sems.at[i]) for i, (a, b) in enumerate(pairs)]
    for copy in copies:
        copy.start()
    for copy in copies[:3]:
        copy.wait()
    length, channels = x_here.shape
    by_row = column(weight_here[...], length)
    by_row = jnp.concatenate([by_row] * (channels // LANES), axis=1)
    grad_stream[...] = gs_raw[...].astype(jnp.float32) * by_row
    grad_skip[...] = (gk_raw[...].astype(jnp.float32) * by_row).astype(jnp.bfloat16)
    halo = grad_rows.shape[0] // 2
    grad_rows[0:halo] = grad_stream[length - halo :].astype(jnp.bfloat16)
    grad_rows[halo:] = grad_skip[length - halo :]
    own_sum = jnp.broadcast_to(jnp.sum(weight_here[...], axis=1, keepdims=True), (1, LANES))
    sums[...] = split_rows(own_sum)
    for copy in copies[3:]:
        copy.wait()


def load_all(halo, x, gs, gk, weight, conv_w, out_w, after):
    shape = x.shape
    vmem, anywhere = pl.BlockSpec(memory_space=pltpu.VMEM), pl.BlockSpec(memory_space=pl.ANY)
    return pl.pallas_call(
        load_kernel,
        in_specs=[anywhere] * 7,
        out_specs=[vmem] * 7,
        out_shape=[
            pltpu.VMEM(shape, jnp.bfloat16),
            pltpu.VMEM(shape, jnp.float32),
            pltpu.VMEM(shape, jnp.bfloat16),
            pltpu.VMEM((16, LANES), jnp.bfloat16),
            pltpu.VMEM(conv_w.shape, jnp.bfloat16),
            pltpu.VMEM(out_w.shape, jnp.bfloat16),
            pltpu.VMEM((2 * halo, shape[1]), jnp.bfloat16),
        ],
        scratch_shapes=[
            pltpu.VMEM(shape, jnp.bfloat16),
            pltpu.VMEM(shape, jnp.bfloat16),
            pltpu.VMEM(weight.shape, jnp.float32),
            pltpu.SemaphoreType.DMA((6,)),
        ],
        compiler_params=pltpu.CompilerParams(vmem_limit_bytes=ADD_BYTES),
        cost_estimate=cost(10**7, 6 * 10**6),
        name="load_all",
    )(*held((x, gs, gk, weight, conv_w, out_w), pltpu.HBM), *held([after]))


def split_rows(total):
    high = total.astype(jnp.bfloat16).astype(jnp.float32)
    middle = (total - high).astype(jnp.bfloat16).astype(jnp.float32)
    low = total - high - middle
    row = lax.broadcasted_iota(jnp.int32, (16, LANES), 0)
    rows = jnp.where(row == 0, high, jnp.where(row == 1, middle, jnp.where(row == 2, low, 0.0)))
    return rows.astype(jnp.bfloat16)


def joined_rows(rows):
    return jnp.sum(rows.astype(jnp.float32), axis=0, keepdims=True)


def cut_off(rows, dilation):
    row = lax.broadcasted_iota(jnp.int32, rows.shape, 0)
    return jnp.where(jnp.logical_and(row < dilation, lax.axis_index("tm") == 0), 0.0, rows)


def items_of(layers, chunk):
    third = layers // len(CHAINS)
    high = layers - chunk * third
    return [(index, is_out) for index in reversed(range(high - third, high)) for is_out in (False, True)]


def earlier_rows(plan, index, present, first, last):
    dilation, begin = 2**index, 2 * plan["halo"]
    cut = cut_off(present[begin - dilation : begin], dilation)
    return jnp.concatenate([present[first - dilation : begin - dilation], cut, present[begin : last - dilation]])


def backward(plan, layers, refs_of, conv_w, out_w, grad_proj, grad_stream, past_part, grad_parts):
    halo, length, channels = plan["halo"], plan["length"], plan["channels"]
    own = slice(halo, halo + length)
    items = plan["items"]

    for index in layers:
        dilation, count = 2**index, plan["counts"][index]
        present, earlier, factors, gates = refs_of(index)
        grad_proj[0:count, :channels] = grad_stream[0:count].astype(jnp.bfloat16)
        grad_gated = dot(grad_proj[0:count], out_w[index], NT)
        total = dot(gates[own], grad_proj[0:length], TN)
        plan["store"](total, items.index((index, True)), grad_parts)
        both = factors[halo : halo + count].astype(jnp.float32)
        grad_preact = jnp.concatenate(
            [grad_gated * both[:, :channels], grad_gated * both[:, channels:]], axis=1
        ).astype(jnp.bfloat16)
        spread = dot(grad_preact, conv_w[index], NT)
        past_part[0:count] = spread[:, channels:]
        cut = slice(halo, halo + max(dilation, 8))
        past_part[cut] = cut_off(past_part[cut], dilation)
        rows = plan["counts"][index - 1] if index else length
        grad_stream[0:rows] += spread[0:rows, :channels] + past_part[dilation : dilation + rows]
        past = earlier_rows(plan, index, present, halo, halo + length) if earlier is None else earlier[own]
        total = dot(jnp.concatenate([present[own], past], axis=1), grad_preact[0:length], TN)
        plan["store"](total, items.index((index, False)), grad_parts)


def forward_kernel(plan, prev_x, own_x, conv_w, out_w, all_present, all_earlier, all_factors, all_gates, stream):
    halo, (length, channels) = plan["halo"], own_x.shape
    layers, low = conv_w.shape[0], all_earlier.shape[0]
    pad = 2 ** (layers - 1)
    extent = length + 2 * halo
    begin = 2 * halo
    stream[0:pad] = jnp.zeros((pad, channels), jnp.float32)
    stream[pad : pad + begin] = prev_x[...].astype(jnp.float32)
    stream[pad + begin :] = own_x[...].astype(jnp.float32)
    all_present[0, 0:begin] = prev_x[...]
    all_present[0, begin:] = own_x[...]
    for index in range(layers):
        dilation, start = 2**index, plan["starts"][index]
        present = all_present.at[index]
        if index >= low:
            past = earlier_rows(plan, index, present, start, extent)
        else:
            past = stream[pad + start - dilation : pad + extent - dilation]
            cut = cut_off(past[begin - start : begin - start + 16], dilation)
            past = jnp.concatenate([past[: begin - start], cut, past[begin - start + 16 :]]).astype(jnp.bfloat16)
            all_earlier[index, start:] = past
        preact = dot(jnp.concatenate([present[start:], past], axis=1), conv_w[index], NN)
        filtered = jnp.tanh(preact[:, :channels])
        opening = 0.5 + 0.5 * jnp.tanh(0.5 * preact[:, channels:])
        product = filtered * opening
        gated = product.astype(jnp.bfloat16)
        all_gates[index, start:] = gated
        all_factors[index, start:, :channels] = (opening - filtered * product).astype(jnp.bfloat16)
        all_factors[index, start:, channels:] = (product * (1.0 - opening)).astype(jnp.bfloat16)
        if index < layers - 1:
            after = stream[pad + start :] + dot(gated, out_w[index, :, :channels], NN)
            all_present[index + 1, start:] = after.astype(jnp.bfloat16)
            if index < layers - 2:
                stream[pad + start :] = after


def backward_kernel(plan, first, third, all_present, all_earlier, all_factors, all_gates, conv_w, out_w, *rest):
    refs = rest[: plan["inputs"]]
    *outs, keep, send, grad_stream, grad_proj, past_part = rest[plan["inputs"] + plan["unused"] :]
    halo, length, channels, low = plan["halo"], plan["length"], plan["channels"], all_earlier.shape[0]
    if plan["inputs"] == 4:
        prev_rows, own_grad, own_skip, sums = refs
        *outs, grad_skip = outs
        grad_stream[0:halo] = prev_rows[0:halo].astype(jnp.float32)
        grad_stream[halo:] = own_grad[...]
        grad_skip[0:halo] = prev_rows[halo:]
        grad_skip[halo:] = own_skip[...]
    else:
        grad_before, grad_skip = refs
        grad_stream[...] = grad_before[...]
    grad_proj[:, channels:] = grad_skip[...]

    def refs_of(index):
        earlier = all_earlier.at[index] if index < low else None
        return all_present.at[index], earlier, all_factors.at[index], all_gates.at[index]

    backward(
        plan, list(reversed(range(first, first + third))), refs_of, conv_w, out_w,
        grad_proj, grad_stream, past_part, (keep, send),
    )
    at = 0
    for out in outs:
        out[...] = grad_stream[at : at + out.shape[0]].astype(out.dtype)
        at += out.shape[0]
    if plan["inputs"] == 4:
        plan["finish"](sums, (keep, send))


def store_whole(items, total, item, grad_parts):
    is_out = items[item][1]
    place = sum(kind == is_out for _, kind in items[:item])
    grad_parts[int(is_out)][place] = total.astype(jnp.bfloat16)


def finish_whole(sums, grad_parts):
    pass


def finish_shards(extra, sums, grad_parts):
    for part in grad_parts:
        lead, rows = part.shape[:-2], part.shape[-2]
        for first in range(rows - extra, rows, 16):
            part[(slice(None),) * len(lead) + (slice(first, first + 16),)] = jnp.broadcast_to(
                sums[...], lead + sums.shape
            )


def store_shards(tm, dp, order, bases, total, item, grad_parts):
    keep, send = grad_parts
    t_at, d_at = lax.axis_index("tm"), lax.axis_index("dp")
    core_at = lax.rem(d_at, 2)
    rows = total.shape[0] // tm
    at = pl.ds(bases[item], rows)
    at_bits = bits_of(t_at, d_at, lax.rem, lax.div)
    for y in range(dp // 2):
        near = total[:, (2 * y) * LANES : (2 * y + 1) * LANES]
        far = total[:, (2 * y + 1) * LANES : (2 * y + 2) * LANES]
        mine = jnp.where(core_at == 0, near, far).astype(jnp.bfloat16)
        other = jnp.where(core_at == 0, far, near).astype(jnp.bfloat16)
        for t in range(tm):
            bits = bits_of(t, 2 * y, lambda a, b: a % b, lambda a, b: a // b)
            lead = tuple(lax.rem(bits[name] + at_bits[name], 2) for name in order)
            keep[lead + (at,)] = mine[t * rows : (t + 1) * rows]
            send[lead + (at,)] = other[t * rows : (t + 1) * rows]


def bits_of(t, d, rem, div):
    return {"x": rem(t, 2), "z0": rem(div(t, 2), 2), "z1": div(t, 4), "y": div(d, 2)}


def bases_of(items, tm, channels):
    ends = [0]
    for _, is_out in items:
        ends.append(ends[-1] + (1 if is_out else 2) * channels // tm)
    return ends[:-1], ends[-1]


def run_layers(in_shards, tm, dp, halo, borders, loaded):
    own_x, own_grad, own_skip, sums, conv_w, out_w = loaded
    length, channels = own_x.shape
    layers = conv_w.shape[0]
    third = layers // len(CHAINS)
    low = layers - third
    extent, border = length + 2 * halo, length + halo
    starts = []
    for index in range(layers):
        need = halo if index == layers - 1 else 2 ** (index + 1)
        starts.append(need // 16 * 16)
    counts = [-(-(length + 2 ** (index + 1) - 1) // 16) * 16 for index in range(layers)]
    plan = {"halo": halo, "starts": starts, "counts": counts, "length": length, "channels": channels, "unused": 0}
    plans, shapes = [], []
    for chunk, order in enumerate(CHAINS):
        items = items_of(layers, chunk)
        bases, rows = bases_of(items, tm, channels)
        if in_shards:
            store = functools.partial(store_shards, tm, dp, order, bases)
            finish = functools.partial(finish_shards, EXTRA[chunk])
            shapes.append(2 * [(2,) * len(order) + (rows + EXTRA[chunk], LANES)])
        else:
            store, finish = functools.partial(store_whole, items), finish_whole
            outs = sum(is_out for _, is_out in items)
            shapes.append([(len(items) - outs,) + conv_w.shape[1:], (outs,) + out_w.shape[1:]])
        plans.append(plan | {"items": items, "store": store, "finish": finish})
    vmem, anywhere = pl.BlockSpec(memory_space=pltpu.VMEM), pl.BlockSpec(memory_space=pl.ANY)
    weight_bytes = 2 * (conv_w.size + out_w.size)
    flops = 2 * length * channels * channels
    kept = pl.pallas_call(
        functools.partial(forward_kernel, plan),
        in_specs=[vmem] * 4,
        out_specs=[vmem] * 4,
        out_shape=[
            pltpu.VMEM((layers, extent, channels), jnp.bfloat16),
            pltpu.VMEM((low, extent, channels), jnp.bfloat16),
            pltpu.VMEM((layers, extent, 2 * channels), jnp.bfloat16),
            pltpu.VMEM((layers, extent, channels), jnp.bfloat16),
        ],
        scratch_shapes=[pltpu.VMEM((2 ** (layers - 1) + extent, channels), jnp.float32)],
        compiler_params=pltpu.CompilerParams(vmem_limit_bytes=VMEM_BYTES),
        cost_estimate=cost(flops * 5 * layers, weight_bytes),
        name="forward",
    )(*held((borders[0], own_x, conv_w, out_w)))

    def backward_of(step, inputs, outs, after):
        more = {"inputs": len(inputs), "unused": len(after)}
        return pl.pallas_call(
            functools.partial(backward_kernel, plans[step] | more, layers - (step + 1) * third, third),
            in_specs=[vmem] * (6 + len(inputs)) + [anywhere] * len(after),
            out_specs=[vmem] * (len(outs) + 2),
            out_shape=[pltpu.VMEM((rows, channels), kind) for rows, kind in outs]
            + [pltpu.VMEM(shape, jnp.bfloat16) for shape in shapes[step]],
            scratch_shapes=[
                pltpu.VMEM((border, channels), jnp.float32),
                pltpu.VMEM((border, 2 * channels), jnp.bfloat16),
                pltpu.VMEM((border, channels), jnp.float32),
            ],
            compiler_params=pltpu.CompilerParams(vmem_limit_bytes=VMEM_BYTES),
            cost_estimate=cost(flops * 12 * third, weight_bytes),
            name=("last_third", "middle_third", "first_third")[step],
        )(*held((*kept, conv_w, out_w, *inputs, *after)))

    whole = (border, jnp.float32)
    grad_stream, grad_skip, *last = backward_of(
        0, (borders[1], own_grad, own_skip, sums), [whole, (border, jnp.bfloat16)], []
    )
    parts = [last]
    if in_shards:
        parts[0] = Chunk(tm, dp, 0, *last)
    grad_stream, *middle = backward_of(1, (grad_stream, grad_skip), [whole], [])
    other, own, *first = backward_of(
        2, (grad_stream, grad_skip), [(halo, jnp.bfloat16), (length - halo, jnp.float32)],
        [parts[0].next_message()] if in_shards else [],
    )
    parts += [middle, first]
    if in_shards:
        for step in (1, 2):
            parts[step] = Chunk(tm, dp, step, *parts[step])
    return other, own, parts


def add_kernel(count, groups, *refs):
    arrays, outs = refs[:count], refs[-len(groups) :]
    for out, pieces in zip(outs, groups):
        lead = (slice(None),) * (len(out.shape) - 2)
        for first, rows, with_total, terms in pieces:
            body = rows - 16 if with_total else rows
            value = 0.0
            for array, at, begin in terms:
                value = value + arrays[array][at + lead + (slice(begin, begin + body),)].astype(jnp.float32)
            out[lead + (slice(first, first + body),)] = value.astype(out.dtype)
            if with_total:
                total = 0.0
                for array, at, begin in terms:
                    rows_at = slice(begin + body, begin + rows)
                    total = total + joined_rows(arrays[array][at + (0,) * len(lead) + (rows_at,)])
                slab = split_rows(total)
                out[lead + (slice(first + body, first + rows),)] = jnp.broadcast_to(slab, out.shape[:-2] + slab.shape)


def add_up(arrays, groups, shapes, after, name):
    vmem = pl.BlockSpec(memory_space=pltpu.VMEM)
    return pl.pallas_call(
        functools.partial(add_kernel, len(arrays), groups),
        in_specs=[vmem] * len(arrays) + [pl.BlockSpec(memory_space=pl.ANY)] * len(after),
        out_specs=[vmem] * len(groups),
        out_shape=[pltpu.VMEM(shape, jnp.bfloat16) for shape in shapes],
        compiler_params=pltpu.CompilerParams(vmem_limit_bytes=ADD_BYTES),
        name=name,
    )(*held(arrays), *held(after))


def first_block(array, first, rows):
    return array[(0,) * (len(array.shape) - 2) + (slice(first, first + rows),)].astype(jnp.float32)


def first_block(array, first, rows):
    return array[(0,) * (len(array.shape) - 2) + (slice(first, first + rows),)].astype(jnp.float32)


def last_kernel(counts, samples_all, tm, *refs):
    chunks = []
    for count in counts:
        chunks.insert(0, refs[:count])
        refs = refs[count:]
    other, own, *results, grad_inputs, grad_conv, grad_out, sems = refs
    layers, channels = grad_conv.shape[0], own.shape[1]
    total = 0.0
    for term in chunks[0]:
        total = total + jnp.sum(first_block(term, term.shape[-2] - 16, 16), axis=0, keepdims=True)
    scale = samples_all / total
    copies = [
        pltpu.make_async_copy(here, result, sems.at[i])
        for i, (here, result) in enumerate(zip((grad_inputs, grad_conv, grad_out), results))
    ]
    for first in range(0, channels, LANES):
        lanes = slice(first, first + LANES)
        grad_inputs[0 : own.shape[0], lanes] = own[:, lanes] * scale
        grad_inputs[own.shape[0] :, lanes] = other[:, lanes].astype(jnp.float32) * scale
    copies[0].start()
    for chunk, terms in enumerate(chunks):
        items = items_of(layers, chunk)
        for (index, is_out), base in zip(items, bases_of(items, tm, channels)[0]):
            out = grad_out if is_out else grad_conv
            value = 0.0
            for term in terms:
                value = value + first_block(term, base, out.shape[1])
            out[index] = value * scale
    for copy in copies[1:]:
        copy.start()
    for copy in copies:
        copy.wait()


class Chunk:
    def __init__(self, tm, dp, chunk, keep, send):
        self.tm, self.dp, self.chunk, self.rows = tm, dp, chunk, keep.shape[-2]
        self.message = None
        self.terms = [keep, swapped(tm, dp, send, "core")]

    def next_message(self, after=()):
        if self.message is None:
            left = len(CHAINS[self.chunk]) + 2 - len(self.terms)
            pieces = []
            for i, v in enumerate(self.terms):
                pieces.append((i, (0,) * (len(v.shape) - 2 - left) + (1,), 0))
            (self.message,) = add_up(
                self.terms, [[(0, self.rows, EXTRA[self.chunk] > 0, pieces)]], [(2,) * (left - 1) + (self.rows, LANES)], after,
                "add_chunk%d_step%d" % (self.chunk, len(self.terms) - 1),
            )
        return self.message

    def run_chain(self, after=()):
        for step, name in enumerate(CHAINS[self.chunk]):
            self.terms.append(swapped(self.tm, self.dp, self.next_message(after if step == 1 else ()), name))
            self.message = None
        return self.terms


def swapped(tm, dp, value, name):
    over_t, over_d = {"core": (0, 1), "y": (0, 2), "x": (1, 0), "z0": (2, 0), "z1": (4, 0)}[name]
    pairs = [(t * dp + d, (t ^ over_t) * dp + (d ^ over_d)) for t in range(tm) for d in range(dp)]
    return lax.ppermute(value, ("tm", "dp"), pairs)


def scattered(part):
    columns = lax.psum_scatter(part, "dp", scatter_dimension=2, tiled=True).astype(jnp.float32)
    return lax.psum_scatter(columns, "tm", scatter_dimension=1, tiled=True)


def body(inputs, grad_stream_out, grad_skip_out, sample_weight, conv_weight, out_weight):
    tm, dp = lax.axis_size("tm"), lax.axis_size("dp")
    batch, length, channels = inputs.shape
    layers = conv_weight.shape[0]
    third = layers // len(CHAINS)
    halo = 2**layers
    samples_all = batch * length * tm * dp
    x, gs, gk = inputs[0], grad_stream_out[0], grad_skip_out[0]
    x_rows = last_rows(x, 2 * halo)
    prev_x = around(x_rows, "tm", 1)
    *loaded, grad_rows = load_all(halo, x, gs, gk, sample_weight, conv_weight, out_weight, x_rows)
    borders = [prev_x, around(grad_rows, "tm", 1)]
    in_shards = tm == 8 and dp == 4 and channels // tm % 16 == 0 and 2 * channels == dp * LANES
    other, own, parts = run_layers(in_shards, tm, dp, halo, borders, loaded)
    other = around(other, "tm", -1)
    if not in_shards:
        scale = samples_all / lax.psum(jnp.sum(sample_weight), ("tm", "dp"))
        found = {}
        for chunk, part in enumerate(parts):
            items = items_of(layers, chunk)
            for is_out in (False, True):
                for place, item in enumerate(item for item in items if item[1] == is_out):
                    found[item] = part[int(is_out)][place]
        grad_conv, grad_out = (
            scattered(jnp.stack([found[index, is_out] for index in range(layers)])) * scale for is_out in (False, True)
        )
        return (jnp.concatenate([own, other]) * scale)[None], grad_conv, grad_out
    chunks = [part.run_chain([other] if part is parts[0] else ()) for part in parts]
    conv_rows, out_rows = 2 * channels // tm, channels // tm
    shapes = [(length, channels), (layers, conv_rows, LANES), (layers, out_rows, LANES)]
    terms = [term for group in reversed(chunks) for term in group]
    grad_inputs, grad_conv, grad_out = pl.pallas_call(
        functools.partial(last_kernel, [len(group) for group in reversed(chunks)], float(samples_all), tm),
        in_specs=[pl.BlockSpec(memory_space=pltpu.VMEM)] * (len(terms) + 2),
        out_specs=[pl.BlockSpec(memory_space=pl.ANY)] * len(shapes),
        out_shape=[jax.ShapeDtypeStruct(shape, jnp.float32) for shape in shapes],
        scratch_shapes=[pltpu.VMEM(shape, jnp.float32) for shape in shapes] + [pltpu.SemaphoreType.DMA((len(shapes),))],
        compiler_params=pltpu.CompilerParams(vmem_limit_bytes=ADD_BYTES),
        name="scale_all",
    )(*held(terms), *held([other, own]))
    return grad_inputs[None], grad_conv, grad_out


def solution(mesh):
    placed = (
        P("dp", "tm", None),
        P("dp", "tm", None),
        P("dp", "tm", None),
        P("dp", "tm"),
        P(),
        P(),
    )
    return jax.shard_map(
        body,
        mesh=mesh,
        in_specs=placed,
        out_specs=(P("dp", "tm", None), P(None, "tm", "dp"), P(None, "tm", "dp")),
        check_vma=False,
    )
```

```python
import functools

import jax
import jax.numpy as jnp
from jax import lax
from jax.experimental import pallas as pl
from jax.experimental.pallas import tpu as pltpu
from jax.sharding import PartitionSpec as P

LANES = 128
VMEM_BYTES = 24 * 1024 * 1024
ADD_BYTES = 8 * 1024 * 1024
CHAINS = (("x", "z0", "y", "z1"), ("z0", "y", "x", "z1"), ("y", "x", "z0", "z1"))
EXTRA = (16, 0, 0)
NN = (((1,), (0,)), ((), ()))
NT = (((1,), (1,)), ((), ()))
TN = (((0,), (0,)), ((), ()))


def dot(left, right, dims):
    return lax.dot_general(left, right, dims, preferred_element_type=jnp.float32)


def held(arrays, space=pltpu.VMEM):
    return [pltpu.with_memory_space_constraint(x, space) for x in arrays]


def around(x, axis, by):
    count = lax.axis_size(axis)
    return lax.ppermute(x, axis, [(i, (i + by) % count) for i in range(count)])


def column(row, rows):
    return jnp.broadcast_to(row, (LANES, rows)).T


def cost(flops, moved):
    return pl.CostEstimate(flops=flops, bytes_accessed=moved, transcendentals=0)


def pack_kernel(tail_x, tail_gs, tail_gk, weight, x_rows, grad_rows):
    halo, channels = tail_gs.shape
    by_row = column(weight[...], LANES)[LANES - halo :]
    by_row = jnp.concatenate([by_row] * (channels // LANES), axis=1)
    x_rows[...] = tail_x[...]
    grad_rows[0:halo] = (tail_gs[...].astype(jnp.float32) * by_row).astype(jnp.bfloat16)
    grad_rows[halo:] = (tail_gk[...].astype(jnp.float32) * by_row).astype(jnp.bfloat16)


def pack(halo, x, grad_stream_out, grad_skip_out, weight):
    length, channels = x.shape

    def last(rows):
        return pl.BlockSpec((rows, channels), lambda i: (length // rows - 1, 0))

    message = jax.ShapeDtypeStruct((2 * halo, channels), jnp.bfloat16)
    return pl.pallas_call(
        pack_kernel,
        grid=(1,),
        in_specs=[last(2 * halo), last(halo), last(halo), pl.BlockSpec((1, LANES), lambda i: (0, length // LANES - 1))],
        out_specs=[pl.BlockSpec(message.shape, lambda i: (0, 0))] * 2,
        out_shape=[message] * 2,
        compiler_params=pltpu.CompilerParams(vmem_limit_bytes=ADD_BYTES),
        name="pack_borders",
    )(*held((x, grad_stream_out, grad_skip_out, weight), pltpu.HBM))


def load_kernel(
    x, gs, gk, weight, conv_w, out_w, _, x_here, grad_stream, grad_skip, sums, conv_here, out_here,
    gs_raw, gk_raw, weight_here, sems,
):
    pairs = ((weight, weight_here), (gs, gs_raw), (gk, gk_raw), (x, x_here), (conv_w, conv_here), (out_w, out_here))
    copies = [pltpu.make_async_copy(a, b, sems.at[i]) for i, (a, b) in enumerate(pairs)]
    for copy in copies:
        copy.start()
    for copy in copies[:3]:
        copy.wait()
    length, channels = x_here.shape
    by_row = column(weight_here[...], length)
    by_row = jnp.concatenate([by_row] * (channels // LANES), axis=1)
    grad_stream[...] = gs_raw[...].astype(jnp.float32) * by_row
    grad_skip[...] = (gk_raw[...].astype(jnp.float32) * by_row).astype(jnp.bfloat16)
    own_sum = jnp.broadcast_to(jnp.sum(weight_here[...], axis=1, keepdims=True), (1, LANES))
    sums[...] = split_rows(own_sum)
    for copy in copies[3:]:
        copy.wait()


def load_all(x, gs, gk, weight, conv_w, out_w, after):
    shape = x.shape
    vmem, anywhere = pl.BlockSpec(memory_space=pltpu.VMEM), pl.BlockSpec(memory_space=pl.ANY)
    return pl.pallas_call(
        load_kernel,
        in_specs=[anywhere] * 7,
        out_specs=[vmem] * 6,
        out_shape=[
            pltpu.VMEM(shape, jnp.bfloat16),
            pltpu.VMEM(shape, jnp.float32),
            pltpu.VMEM(shape, jnp.bfloat16),
            pltpu.VMEM((16, LANES), jnp.bfloat16),
            pltpu.VMEM(conv_w.shape, jnp.bfloat16),
            pltpu.VMEM(out_w.shape, jnp.bfloat16),
        ],
        scratch_shapes=[
            pltpu.VMEM(shape, jnp.bfloat16),
            pltpu.VMEM(shape, jnp.bfloat16),
            pltpu.VMEM(weight.shape, jnp.float32),
            pltpu.SemaphoreType.DMA((6,)),
        ],
        compiler_params=pltpu.CompilerParams(vmem_limit_bytes=ADD_BYTES),
        cost_estimate=cost(10**7, 6 * 10**6),
        name="load_all",
    )(*held((x, gs, gk, weight, conv_w, out_w), pltpu.HBM), *held([after]))


def split_rows(total):
    high = total.astype(jnp.bfloat16).astype(jnp.float32)
    middle = (total - high).astype(jnp.bfloat16).astype(jnp.float32)
    low = total - high - middle
    row = lax.broadcasted_iota(jnp.int32, (16, LANES), 0)
    rows = jnp.where(row == 0, high, jnp.where(row == 1, middle, jnp.where(row == 2, low, 0.0)))
    return rows.astype(jnp.bfloat16)


def joined_rows(rows):
    return jnp.sum(rows.astype(jnp.float32), axis=0, keepdims=True)


def cut_off(rows, dilation):
    row = lax.broadcasted_iota(jnp.int32, rows.shape, 0)
    return jnp.where(jnp.logical_and(row < dilation, lax.axis_index("tm") == 0), 0.0, rows)


def items_of(layers, chunk):
    third = layers // len(CHAINS)
    high = layers - chunk * third
    return [(index, is_out) for index in reversed(range(high - third, high)) for is_out in (False, True)]


def earlier_rows(plan, index, present, first, last):
    dilation, begin = 2**index, 2 * plan["halo"]
    cut = cut_off(present[begin - dilation : begin], dilation)
    return jnp.concatenate([present[first - dilation : begin - dilation], cut, present[begin : last - dilation]])


def moved_on(dilation, spread, past_part, grad_stream, halo, rows):
    count, channels = spread.shape[0], grad_stream.shape[1]
    past_part[0:count] = spread[:, channels:]
    cut = slice(halo, halo + max(dilation, 8))
    past_part[cut] = cut_off(past_part[cut], dilation)
    grad_stream[0:rows] += spread[0:rows, :channels] + past_part[dilation : dilation + rows]


def inputs_kernel(halo, preact, grad_before, conv_w, other, own, grad_stream, past_part):
    grad_stream[...] = grad_before[...]
    moved_on(1, dot(preact[...], conv_w[0], NT), past_part, grad_stream, halo, grad_stream.shape[0])
    other[...] = grad_stream[0:halo].astype(other.dtype)
    own[...] = grad_stream[halo:]


def backward(plan, layers, refs_of, conv_w, out_w, grad_proj, grad_stream, past_part, grad_parts, last_preact):
    halo, length, channels = plan["halo"], plan["length"], plan["channels"]
    own = slice(halo, halo + length)
    items = plan["items"]

    for index in layers:
        dilation, count = 2**index, plan["counts"][index]
        present, earlier, factors, gates = refs_of(index)
        grad_proj[0:count, :channels] = grad_stream[0:count].astype(jnp.bfloat16)
        grad_gated = dot(grad_proj[0:count], out_w[index], NT)
        both = factors[halo : halo + count].astype(jnp.float32)
        grad_preact = jnp.concatenate(
            [grad_gated * both[:, :channels], grad_gated * both[:, channels:]], axis=1
        ).astype(jnp.bfloat16)
        if index:
            moved_on(dilation, dot(grad_preact, conv_w[index], NT), past_part, grad_stream, halo, plan["counts"][index - 1])
        else:
            last_preact[...] = grad_preact
        total = dot(gates[own], grad_proj[0:length], TN)
        plan["store"](total, items.index((index, True)), grad_parts)
        past = earlier_rows(plan, index, present, halo, halo + length) if earlier is None else earlier[own]
        total = dot(jnp.concatenate([present[own], past], axis=1), grad_preact[0:length], TN)
        plan["store"](total, items.index((index, False)), grad_parts)


def forward_kernel(plan, prev_x, own_x, conv_w, out_w, all_present, all_earlier, all_factors, all_gates, stream):
    halo, (length, channels) = plan["halo"], own_x.shape
    layers, low = conv_w.shape[0], all_earlier.shape[0]
    pad = 2 ** (layers - 1)
    extent = length + 2 * halo
    begin = 2 * halo
    stream[0:pad] = jnp.zeros((pad, channels), jnp.float32)
    stream[pad : pad + begin] = prev_x[...].astype(jnp.float32)
    stream[pad + begin :] = own_x[...].astype(jnp.float32)
    all_present[0, 0:begin] = prev_x[...]
    all_present[0, begin:] = own_x[...]
    for index in range(layers):
        dilation, start = 2**index, plan["starts"][index]
        present = all_present.at[index]
        if index >= low:
            past = earlier_rows(plan, index, present, start, extent)
        else:
            past = stream[pad + start - dilation : pad + extent - dilation]
            cut = cut_off(past[begin - start : begin - start + 16], dilation)
            past = jnp.concatenate([past[: begin - start], cut, past[begin - start + 16 :]]).astype(jnp.bfloat16)
            all_earlier[index, start:] = past
        preact = dot(jnp.concatenate([present[start:], past], axis=1), conv_w[index], NN)
        filtered = jnp.tanh(preact[:, :channels])
        opening = 0.5 + 0.5 * jnp.tanh(0.5 * preact[:, channels:])
        product = filtered * opening
        gated = product.astype(jnp.bfloat16)
        all_gates[index, start:] = gated
        all_factors[index, start:, :channels] = (opening - filtered * product).astype(jnp.bfloat16)
        all_factors[index, start:, channels:] = (product * (1.0 - opening)).astype(jnp.bfloat16)
        if index < layers - 1:
            after = stream[pad + start :] + dot(gated, out_w[index, :, :channels], NN)
            all_present[index + 1, start:] = after.astype(jnp.bfloat16)
            if index < layers - 2:
                stream[pad + start :] = after


def backward_kernel(plan, first, third, all_present, all_earlier, all_factors, all_gates, conv_w, out_w, *rest):
    refs = rest[: plan["inputs"]]
    *outs, keep, send, grad_stream, grad_proj, past_part = rest[plan["inputs"] + plan["unused"] :]
    halo, length, channels, low = plan["halo"], plan["length"], plan["channels"], all_earlier.shape[0]
    if plan["inputs"] == 4:
        prev_rows, own_grad, own_skip, sums = refs
        *outs, grad_skip = outs
        grad_stream[0:halo] = prev_rows[0:halo].astype(jnp.float32)
        grad_stream[halo:] = own_grad[...]
        grad_skip[0:halo] = prev_rows[halo:]
        grad_skip[halo:] = own_skip[...]
    else:
        grad_before, grad_skip = refs
        grad_stream[...] = grad_before[...]
    grad_proj[:, channels:] = grad_skip[...]

    def refs_of(index):
        earlier = all_earlier.at[index] if index < low else None
        return all_present.at[index], earlier, all_factors.at[index], all_gates.at[index]

    backward(
        plan, list(reversed(range(first, first + third))), refs_of, conv_w, out_w,
        grad_proj, grad_stream, past_part, (keep, send), outs[-1],
    )
    outs[0][...] = grad_stream[0 : outs[0].shape[0]]
    if plan["inputs"] == 4:
        plan["finish"](sums, (keep, send))


def store_whole(items, total, item, grad_parts):
    is_out = items[item][1]
    place = sum(kind == is_out for _, kind in items[:item])
    grad_parts[int(is_out)][place] = total.astype(jnp.bfloat16)


def finish_whole(sums, grad_parts):
    pass


def finish_shards(extra, sums, grad_parts):
    for part in grad_parts:
        lead, rows = part.shape[:-2], part.shape[-2]
        for first in range(rows - extra, rows, 16):
            part[(slice(None),) * len(lead) + (slice(first, first + 16),)] = jnp.broadcast_to(
                sums[...], lead + sums.shape
            )


def store_shards(tm, dp, order, bases, total, item, grad_parts):
    keep, send = grad_parts
    t_at, d_at = lax.axis_index("tm"), lax.axis_index("dp")
    core_at = lax.rem(d_at, 2)
    rows = total.shape[0] // tm
    at = pl.ds(bases[item], rows)
    at_bits = bits_of(t_at, d_at, lax.rem, lax.div)
    for y in range(dp // 2):
        near = total[:, (2 * y) * LANES : (2 * y + 1) * LANES]
        far = total[:, (2 * y + 1) * LANES : (2 * y + 2) * LANES]
        mine = jnp.where(core_at == 0, near, far).astype(jnp.bfloat16)
        other = jnp.where(core_at == 0, far, near).astype(jnp.bfloat16)
        for t in range(tm):
            bits = bits_of(t, 2 * y, lambda a, b: a % b, lambda a, b: a // b)
            lead = tuple(lax.rem(bits[name] + at_bits[name], 2) for name in order)
            keep[lead + (at,)] = mine[t * rows : (t + 1) * rows]
            send[lead + (at,)] = other[t * rows : (t + 1) * rows]


def bits_of(t, d, rem, div):
    return {"x": rem(t, 2), "z0": rem(div(t, 2), 2), "z1": div(t, 4), "y": div(d, 2)}


def bases_of(items, tm, channels):
    ends = [0]
    for _, is_out in items:
        ends.append(ends[-1] + (1 if is_out else 2) * channels // tm)
    return ends[:-1], ends[-1]


def run_layers(in_shards, tm, dp, halo, borders, loaded):
    own_x, own_grad, own_skip, sums, conv_w, out_w = loaded
    length, channels = own_x.shape
    layers = conv_w.shape[0]
    third = layers // len(CHAINS)
    low = layers - third
    extent, border = length + 2 * halo, length + halo
    starts = []
    for index in range(layers):
        need = halo if index == layers - 1 else 2 ** (index + 1)
        starts.append(need // 16 * 16)
    counts = [-(-(length + 2 ** (index + 1) - 1) // 16) * 16 for index in range(layers)]
    plan = {"halo": halo, "starts": starts, "counts": counts, "length": length, "channels": channels, "unused": 0}
    plans, shapes = [], []
    for chunk, order in enumerate(CHAINS):
        items = items_of(layers, chunk)
        bases, rows = bases_of(items, tm, channels)
        if in_shards:
            store = functools.partial(store_shards, tm, dp, order, bases)
            finish = functools.partial(finish_shards, EXTRA[chunk])
            shapes.append(2 * [(2,) * len(order) + (rows + EXTRA[chunk], LANES)])
        else:
            store, finish = functools.partial(store_whole, items), finish_whole
            outs = sum(is_out for _, is_out in items)
            shapes.append([(len(items) - outs,) + conv_w.shape[1:], (outs,) + out_w.shape[1:]])
        plans.append(plan | {"items": items, "store": store, "finish": finish})
    vmem, anywhere = pl.BlockSpec(memory_space=pltpu.VMEM), pl.BlockSpec(memory_space=pl.ANY)
    weight_bytes = 2 * (conv_w.size + out_w.size)
    flops = 2 * length * channels * channels
    kept = pl.pallas_call(
        functools.partial(forward_kernel, plan),
        in_specs=[vmem] * 4,
        out_specs=[vmem] * 4,
        out_shape=[
            pltpu.VMEM((layers, extent, channels), jnp.bfloat16),
            pltpu.VMEM((low, extent, channels), jnp.bfloat16),
            pltpu.VMEM((layers, extent, 2 * channels), jnp.bfloat16),
            pltpu.VMEM((layers, extent, channels), jnp.bfloat16),
        ],
        scratch_shapes=[pltpu.VMEM((2 ** (layers - 1) + extent, channels), jnp.float32)],
        compiler_params=pltpu.CompilerParams(vmem_limit_bytes=VMEM_BYTES),
        cost_estimate=cost(flops * 5 * layers, weight_bytes),
        name="forward",
    )(*held((borders[0], own_x, conv_w, out_w)))

    def backward_of(step, inputs, outs, after):
        more = {"inputs": len(inputs), "unused": len(after)}
        return pl.pallas_call(
            functools.partial(backward_kernel, plans[step] | more, layers - (step + 1) * third, third),
            in_specs=[vmem] * (6 + len(inputs)) + [anywhere] * len(after),
            out_specs=[vmem] * (len(outs) + 2),
            out_shape=[pltpu.VMEM((rows, wide), kind) for rows, wide, kind in outs]
            + [pltpu.VMEM(shape, jnp.bfloat16) for shape in shapes[step]],
            scratch_shapes=[
                pltpu.VMEM((border, channels), jnp.float32),
                pltpu.VMEM((border, 2 * channels), jnp.bfloat16),
                pltpu.VMEM((border, channels), jnp.float32),
            ],
            compiler_params=pltpu.CompilerParams(vmem_limit_bytes=VMEM_BYTES),
            cost_estimate=cost(flops * 12 * third, weight_bytes),
            name=("last_third", "middle_third", "first_third")[step],
        )(*held((*kept, conv_w, out_w, *inputs, *after)))

    whole = (border, channels, jnp.float32)
    grad_stream, grad_skip, *last = backward_of(
        0, (borders[1], own_grad, own_skip, sums), [whole, (border, channels, jnp.bfloat16)], []
    )
    parts = [last]
    if in_shards:
        parts[0] = Chunk(tm, dp, 0, *last)
    grad_stream, *middle = backward_of(1, (grad_stream, grad_skip), [whole], [])
    grad_stream, preact, *first = backward_of(
        2, (grad_stream, grad_skip), [(length, channels, jnp.float32), (counts[0], 2 * channels, jnp.bfloat16)],
        [parts[0].next_message()] if in_shards else [],
    )
    other, own = pl.pallas_call(
        functools.partial(inputs_kernel, halo),
        in_specs=[vmem] * 3,
        out_specs=[vmem] * 2,
        out_shape=[pltpu.VMEM((halo, channels), jnp.bfloat16), pltpu.VMEM((length - halo, channels), jnp.float32)],
        scratch_shapes=[pltpu.VMEM((length, channels), jnp.float32), pltpu.VMEM((counts[0], channels), jnp.float32)],
        compiler_params=pltpu.CompilerParams(vmem_limit_bytes=ADD_BYTES),
        cost_estimate=cost(flops * 4, weight_bytes // layers),
        name="to_inputs",
    )(*held((preact, grad_stream, conv_w)))
    parts += [middle, first]
    if in_shards:
        for step in (1, 2):
            parts[step] = Chunk(tm, dp, step, *parts[step])
    return other, own, parts


def add_kernel(count, groups, *refs):
    arrays, outs = refs[:count], refs[-len(groups) :]
    for out, pieces in zip(outs, groups):
        lead = (slice(None),) * (len(out.shape) - 2)
        for first, rows, with_total, terms in pieces:
            body = rows - 16 if with_total else rows
            value = 0.0
            for array, at, begin in terms:
                value = value + arrays[array][at + lead + (slice(begin, begin + body),)].astype(jnp.float32)
            out[lead + (slice(first, first + body),)] = value.astype(out.dtype)
            if with_total:
                total = 0.0
                for array, at, begin in terms:
                    rows_at = slice(begin + body, begin + rows)
                    total = total + joined_rows(arrays[array][at + (0,) * len(lead) + (rows_at,)])
                slab = split_rows(total)
                out[lead + (slice(first + body, first + rows),)] = jnp.broadcast_to(slab, out.shape[:-2] + slab.shape)


def add_up(arrays, groups, shapes, after, name):
    vmem = pl.BlockSpec(memory_space=pltpu.VMEM)
    return pl.pallas_call(
        functools.partial(add_kernel, len(arrays), groups),
        in_specs=[vmem] * len(arrays) + [pl.BlockSpec(memory_space=pl.ANY)] * len(after),
        out_specs=[vmem] * len(groups),
        out_shape=[pltpu.VMEM(shape, jnp.bfloat16) for shape in shapes],
        compiler_params=pltpu.CompilerParams(vmem_limit_bytes=ADD_BYTES),
        name=name,
    )(*held(arrays), *held(after))


def first_block(array, first, rows):
    return array[(0,) * (len(array.shape) - 2) + (slice(first, first + rows),)].astype(jnp.float32)


def first_block(array, first, rows):
    return array[(0,) * (len(array.shape) - 2) + (slice(first, first + rows),)].astype(jnp.float32)


def last_kernel(counts, samples_all, tm, *refs):
    chunks = []
    for count in counts:
        chunks.insert(0, refs[:count])
        refs = refs[count:]
    other, own, grad_inputs, grad_conv, grad_out = refs
    layers, channels = grad_conv.shape[0], own.shape[1]
    total = 0.0
    for term in chunks[0]:
        total = total + jnp.sum(first_block(term, term.shape[-2] - 16, 16), axis=0, keepdims=True)
    scale = samples_all / total
    for chunk, terms in enumerate(chunks):
        items = items_of(layers, chunk)
        for (index, is_out), base in zip(items, bases_of(items, tm, channels)[0]):
            out = grad_out if is_out else grad_conv
            value = 0.0
            for term in terms:
                value = value + first_block(term, base, out.shape[1])
            out[index] = value * scale
    for first in range(0, channels, LANES):
        lanes = slice(first, first + LANES)
        grad_inputs[0 : own.shape[0], lanes] = own[:, lanes] * scale
        grad_inputs[own.shape[0] :, lanes] = other[:, lanes].astype(jnp.float32) * scale


class Chunk:
    def __init__(self, tm, dp, chunk, keep, send):
        self.tm, self.dp, self.chunk, self.rows = tm, dp, chunk, keep.shape[-2]
        self.message = None
        self.terms = [keep, swapped(tm, dp, send, "core")]

    def next_message(self, after=()):
        if self.message is None:
            left = len(CHAINS[self.chunk]) + 2 - len(self.terms)
            pieces = []
            for i, v in enumerate(self.terms):
                pieces.append((i, (0,) * (len(v.shape) - 2 - left) + (1,), 0))
            (self.message,) = add_up(
                self.terms, [[(0, self.rows, EXTRA[self.chunk] > 0, pieces)]], [(2,) * (left - 1) + (self.rows, LANES)], after,
                "add_chunk%d_step%d" % (self.chunk, len(self.terms) - 1),
            )
        return self.message

    def run_chain(self, after=()):
        for step, name in enumerate(CHAINS[self.chunk]):
            self.terms.append(swapped(self.tm, self.dp, self.next_message(after if step == 1 else ()), name))
            self.message = None
        return self.terms


def swapped(tm, dp, value, name):
    over_t, over_d = {"core": (0, 1), "y": (0, 2), "x": (1, 0), "z0": (2, 0), "z1": (4, 0)}[name]
    pairs = [(t * dp + d, (t ^ over_t) * dp + (d ^ over_d)) for t in range(tm) for d in range(dp)]
    return lax.ppermute(value, ("tm", "dp"), pairs)


def scattered(part):
    columns = lax.psum_scatter(part, "dp", scatter_dimension=2, tiled=True).astype(jnp.float32)
    return lax.psum_scatter(columns, "tm", scatter_dimension=1, tiled=True)


def body(inputs, grad_stream_out, grad_skip_out, sample_weight, conv_weight, out_weight):
    tm, dp = lax.axis_size("tm"), lax.axis_size("dp")
    batch, length, channels = inputs.shape
    layers = conv_weight.shape[0]
    third = layers // len(CHAINS)
    halo = 2**layers
    samples_all = batch * length * tm * dp
    x, gs, gk = inputs[0], grad_stream_out[0], grad_skip_out[0]
    x_rows, grad_rows = pack(halo, x, gs, gk, sample_weight)
    borders = [around(x_rows, "tm", 1), around(grad_rows, "tm", 1)]
    loaded = load_all(x, gs, gk, sample_weight, conv_weight, out_weight, x_rows)
    in_shards = tm == 8 and dp == 4 and channels // tm % 16 == 0 and 2 * channels == dp * LANES
    other, own, parts = run_layers(in_shards, tm, dp, halo, borders, loaded)
    other = around(other, "tm", -1)
    if not in_shards:
        scale = samples_all / lax.psum(jnp.sum(sample_weight), ("tm", "dp"))
        found = {}
        for chunk, part in enumerate(parts):
            items = items_of(layers, chunk)
            for is_out in (False, True):
                for place, item in enumerate(item for item in items if item[1] == is_out):
                    found[item] = part[int(is_out)][place]
        grad_conv, grad_out = (
            scattered(jnp.stack([found[index, is_out] for index in range(layers)])) * scale for is_out in (False, True)
        )
        return (jnp.concatenate([own, other]) * scale)[None], grad_conv, grad_out
    chunks = [part.run_chain([other] if part is parts[0] else ()) for part in parts]
    conv_rows, out_rows = 2 * channels // tm, channels // tm
    grad_inputs, grad_conv, grad_out = pl.pallas_call(
        functools.partial(last_kernel, [len(terms) for terms in reversed(chunks)], float(samples_all), tm),
        out_shape=[
            jax.ShapeDtypeStruct((length, channels), jnp.float32),
            jax.ShapeDtypeStruct((layers, conv_rows, LANES), jnp.float32),
            jax.ShapeDtypeStruct((layers, out_rows, LANES), jnp.float32),
        ],
        compiler_params=pltpu.CompilerParams(vmem_limit_bytes=ADD_BYTES),
        name="scale_all",
    )(*held([term for terms in reversed(chunks) for term in terms]), *held([other, own]))
    return grad_inputs[None], grad_conv, grad_out


def solution(mesh):
    placed = (
        P("dp", "tm", None),
        P("dp", "tm", None),
        P("dp", "tm", None),
        P("dp", "tm"),
        P(),
        P(),
    )
    return jax.shard_map(
        body,
        mesh=mesh,
        in_specs=placed,
        out_specs=(P("dp", "tm", None), P(None, "tm", "dp"), P(None, "tm", "dp")),
        check_vma=False,
    )
```

```python
import functools

import jax
import jax.numpy as jnp
from jax import lax
from jax.experimental import pallas as pl
from jax.experimental.pallas import tpu as pltpu
from jax.sharding import PartitionSpec as P

LANES = 128
VMEM_BYTES = 24 * 1024 * 1024
ADD_BYTES = 8 * 1024 * 1024
CHAINS = (("x", "z0", "y", "z1"), ("z0", "y", "x", "z1"), ("y", "x", "z0", "z1"))
EXTRA = (16, 0, 0)
NN = (((1,), (0,)), ((), ()))
NT = (((1,), (1,)), ((), ()))
TN = (((0,), (0,)), ((), ()))


def dot(left, right, dims):
    return lax.dot_general(left, right, dims, preferred_element_type=jnp.float32)


def held(arrays, space=pltpu.VMEM):
    return [pltpu.with_memory_space_constraint(x, space) for x in arrays]


def around(x, axis, by):
    count = lax.axis_size(axis)
    return lax.ppermute(x, axis, [(i, (i + by) % count) for i in range(count)])


def column(row, rows):
    return jnp.broadcast_to(row, (LANES, rows)).T


def cost(flops, moved):
    return pl.CostEstimate(flops=flops, bytes_accessed=moved, transcendentals=0)


def pack_kernel(tail_x, tail_gs, tail_gk, weight, x_rows, grad_rows):
    halo, channels = tail_gs.shape
    by_row = column(weight[...], LANES)[LANES - halo :]
    by_row = jnp.concatenate([by_row] * (channels // LANES), axis=1)
    x_rows[...] = tail_x[...]
    grad_rows[0:halo] = (tail_gs[...].astype(jnp.float32) * by_row).astype(jnp.bfloat16)
    grad_rows[halo:] = (tail_gk[...].astype(jnp.float32) * by_row).astype(jnp.bfloat16)


def pack(halo, x, grad_stream_out, grad_skip_out, weight):
    length, channels = x.shape

    def last(rows):
        return pl.BlockSpec((rows, channels), lambda i: (length // rows - 1, 0))

    message = jax.ShapeDtypeStruct((2 * halo, channels), jnp.bfloat16)
    return pl.pallas_call(
        pack_kernel,
        grid=(1,),
        in_specs=[last(2 * halo), last(halo), last(halo), pl.BlockSpec((1, LANES), lambda i: (0, length // LANES - 1))],
        out_specs=[pl.BlockSpec(message.shape, lambda i: (0, 0))] * 2,
        out_shape=[message] * 2,
        compiler_params=pltpu.CompilerParams(vmem_limit_bytes=ADD_BYTES),
        name="pack_borders",
    )(*held((x, grad_stream_out, grad_skip_out, weight), pltpu.HBM))


def load_kernel(
    x, gs, gk, weight, conv_w, out_w, _, x_here, grad_stream, grad_skip, sums, conv_here, out_here,
    gs_raw, gk_raw, weight_here, sems,
):
    pairs = ((weight, weight_here), (gs, gs_raw), (gk, gk_raw), (x, x_here), (conv_w, conv_here), (out_w, out_here))
    copies = [pltpu.make_async_copy(a, b, sems.at[i]) for i, (a, b) in enumerate(pairs)]
    for copy in copies:
        copy.start()
    for copy in copies[:3]:
        copy.wait()
    length, channels = x_here.shape
    by_row = column(weight_here[...], length)
    by_row = jnp.concatenate([by_row] * (channels // LANES), axis=1)
    grad_stream[...] = gs_raw[...].astype(jnp.float32) * by_row
    grad_skip[...] = (gk_raw[...].astype(jnp.float32) * by_row).astype(jnp.bfloat16)
    own_sum = jnp.broadcast_to(jnp.sum(weight_here[...], axis=1, keepdims=True), (1, LANES))
    sums[...] = split_rows(own_sum)
    for copy in copies[3:]:
        copy.wait()


def load_all(x, gs, gk, weight, conv_w, out_w, after):
    shape = x.shape
    vmem, anywhere = pl.BlockSpec(memory_space=pltpu.VMEM), pl.BlockSpec(memory_space=pl.ANY)
    return pl.pallas_call(
        load_kernel,
        in_specs=[anywhere] * 7,
        out_specs=[vmem] * 6,
        out_shape=[
            pltpu.VMEM(shape, jnp.bfloat16),
            pltpu.VMEM(shape, jnp.float32),
            pltpu.VMEM(shape, jnp.bfloat16),
            pltpu.VMEM((16, LANES), jnp.bfloat16),
            pltpu.VMEM(conv_w.shape, jnp.bfloat16),
            pltpu.VMEM(out_w.shape, jnp.bfloat16),
        ],
        scratch_shapes=[
            pltpu.VMEM(shape, jnp.bfloat16),
            pltpu.VMEM(shape, jnp.bfloat16),
            pltpu.VMEM(weight.shape, jnp.float32),
            pltpu.SemaphoreType.DMA((6,)),
        ],
        compiler_params=pltpu.CompilerParams(vmem_limit_bytes=ADD_BYTES),
        cost_estimate=cost(10**7, 6 * 10**6),
        name="load_all",
    )(*held((x, gs, gk, weight, conv_w, out_w), pltpu.HBM), *held([after]))


def split_rows(total):
    high = total.astype(jnp.bfloat16).astype(jnp.float32)
    middle = (total - high).astype(jnp.bfloat16).astype(jnp.float32)
    low = total - high - middle
    row = lax.broadcasted_iota(jnp.int32, (16, LANES), 0)
    rows = jnp.where(row == 0, high, jnp.where(row == 1, middle, jnp.where(row == 2, low, 0.0)))
    return rows.astype(jnp.bfloat16)


def joined_rows(rows):
    return jnp.sum(rows.astype(jnp.float32), axis=0, keepdims=True)


def cut_off(rows, dilation):
    row = lax.broadcasted_iota(jnp.int32, rows.shape, 0)
    return jnp.where(jnp.logical_and(row < dilation, lax.axis_index("tm") == 0), 0.0, rows)


def items_of(layers, chunk):
    third = layers // len(CHAINS)
    high = layers - chunk * third
    return [(index, is_out) for index in reversed(range(high - third, high)) for is_out in (False, True)]


def earlier_rows(plan, index, present, first, last):
    dilation, begin = 2**index, 2 * plan["halo"]
    cut = cut_off(present[begin - dilation : begin], dilation)
    return jnp.concatenate([present[first - dilation : begin - dilation], cut, present[begin : last - dilation]])


def moved_on(dilation, spread, past_part, grad_stream, halo, rows):
    count, channels = spread.shape[0], grad_stream.shape[1]
    past_part[0:count] = spread[:, channels:]
    cut = slice(halo, halo + max(dilation, 8))
    past_part[cut] = cut_off(past_part[cut], dilation)
    grad_stream[0:rows] += spread[0:rows, :channels] + past_part[dilation : dilation + rows]


def inputs_kernel(halo, preact, grad_before, conv_w, other, own, grad_stream, past_part):
    grad_stream[...] = grad_before[...]
    moved_on(1, dot(preact[...], conv_w[0], NT), past_part, grad_stream, halo, grad_stream.shape[0])
    other[...] = grad_stream[0:halo].astype(other.dtype)
    own[...] = grad_stream[halo:]


def backward(plan, layers, refs_of, conv_w, out_w, grad_proj, grad_stream, past_part, grad_parts, last_preact):
    halo, length, channels = plan["halo"], plan["length"], plan["channels"]
    own = slice(halo, halo + length)
    items = plan["items"]

    for index in layers:
        dilation, count = 2**index, plan["counts"][index]
        present, earlier, factors, gates = refs_of(index)
        grad_proj[0:count, :channels] = grad_stream[0:count].astype(jnp.bfloat16)
        grad_gated = dot(grad_proj[0:count], out_w[index], NT)
        total = dot(gates[own], grad_proj[0:length], TN)
        plan["store"](total, items.index((index, True)), grad_parts)
        both = factors[halo : halo + count].astype(jnp.float32)
        grad_preact = jnp.concatenate(
            [grad_gated * both[:, :channels], grad_gated * both[:, channels:]], axis=1
        ).astype(jnp.bfloat16)
        if index:
            moved_on(dilation, dot(grad_preact, conv_w[index], NT), past_part, grad_stream, halo, plan["counts"][index - 1])
        else:
            last_preact[...] = grad_preact
        past = earlier_rows(plan, index, present, halo, halo + length) if earlier is None else earlier[own]
        total = dot(jnp.concatenate([present[own], past], axis=1), grad_preact[0:length], TN)
        plan["store"](total, items.index((index, False)), grad_parts)


def forward_kernel(plan, prev_x, own_x, conv_w, out_w, all_present, all_earlier, all_factors, all_gates, stream):
    halo, (length, channels) = plan["halo"], own_x.shape
    layers, low = conv_w.shape[0], all_earlier.shape[0]
    pad = 2 ** (layers - 1)
    extent = length + 2 * halo
    begin = 2 * halo
    stream[0:pad] = jnp.zeros((pad, channels), jnp.float32)
    stream[pad : pad + begin] = prev_x[...].astype(jnp.float32)
    stream[pad + begin :] = own_x[...].astype(jnp.float32)
    all_present[0, 0:begin] = prev_x[...]
    all_present[0, begin:] = own_x[...]
    for index in range(layers):
        dilation, start = 2**index, plan["starts"][index]
        present = all_present.at[index]
        if index >= low:
            past = earlier_rows(plan, index, present, start, extent)
        else:
            past = stream[pad + start - dilation : pad + extent - dilation]
            cut = cut_off(past[begin - start : begin - start + 16], dilation)
            past = jnp.concatenate([past[: begin - start], cut, past[begin - start + 16 :]]).astype(jnp.bfloat16)
            all_earlier[index, start:] = past
        preact = dot(jnp.concatenate([present[start:], past], axis=1), conv_w[index], NN)
        filtered = jnp.tanh(preact[:, :channels])
        opening = 0.5 + 0.5 * jnp.tanh(0.5 * preact[:, channels:])
        product = filtered * opening
        gated = product.astype(jnp.bfloat16)
        all_gates[index, start:] = gated
        all_factors[index, start:, :channels] = (opening - filtered * product).astype(jnp.bfloat16)
        all_factors[index, start:, channels:] = (product * (1.0 - opening)).astype(jnp.bfloat16)
        if index < layers - 1:
            after = stream[pad + start :] + dot(gated, out_w[index, :, :channels], NN)
            all_present[index + 1, start:] = after.astype(jnp.bfloat16)
            if index < layers - 2:
                stream[pad + start :] = after


def backward_kernel(plan, first, third, all_present, all_earlier, all_factors, all_gates, conv_w, out_w, *rest):
    refs = rest[: plan["inputs"]]
    *outs, keep, send, grad_stream, grad_proj, past_part = rest[plan["inputs"] + plan["unused"] :]
    halo, length, channels, low = plan["halo"], plan["length"], plan["channels"], all_earlier.shape[0]
    if plan["inputs"] == 4:
        prev_rows, own_grad, own_skip, sums = refs
        *outs, grad_skip = outs
        grad_stream[0:halo] = prev_rows[0:halo].astype(jnp.float32)
        grad_stream[halo:] = own_grad[...]
        grad_skip[0:halo] = prev_rows[halo:]
        grad_skip[halo:] = own_skip[...]
    else:
        grad_before, grad_skip = refs
        grad_stream[...] = grad_before[...]
    grad_proj[:, channels:] = grad_skip[...]

    def refs_of(index):
        earlier = all_earlier.at[index] if index < low else None
        return all_present.at[index], earlier, all_factors.at[index], all_gates.at[index]

    backward(
        plan, list(reversed(range(first, first + third))), refs_of, conv_w, out_w,
        grad_proj, grad_stream, past_part, (keep, send), outs[-1],
    )
    outs[0][...] = grad_stream[0 : outs[0].shape[0]]
    if plan["inputs"] == 4:
        plan["finish"](sums, (keep, send))


def store_whole(items, total, item, grad_parts):
    is_out = items[item][1]
    place = sum(kind == is_out for _, kind in items[:item])
    grad_parts[int(is_out)][place] = total.astype(jnp.bfloat16)


def finish_whole(sums, grad_parts):
    pass


def finish_shards(extra, sums, grad_parts):
    for part in grad_parts:
        lead, rows = part.shape[:-2], part.shape[-2]
        for first in range(rows - extra, rows, 16):
            part[(slice(None),) * len(lead) + (slice(first, first + 16),)] = jnp.broadcast_to(
                sums[...], lead + sums.shape
            )


def store_shards(tm, dp, order, bases, total, item, grad_parts):
    keep, send = grad_parts
    t_at, d_at = lax.axis_index("tm"), lax.axis_index("dp")
    core_at = lax.rem(d_at, 2)
    rows = total.shape[0] // tm
    at = pl.ds(bases[item], rows)
    at_bits = bits_of(t_at, d_at, lax.rem, lax.div)
    for y in range(dp // 2):
        near = total[:, (2 * y) * LANES : (2 * y + 1) * LANES]
        far = total[:, (2 * y + 1) * LANES : (2 * y + 2) * LANES]
        mine = jnp.where(core_at == 0, near, far).astype(jnp.bfloat16)
        other = jnp.where(core_at == 0, far, near).astype(jnp.bfloat16)
        for t in range(tm):
            bits = bits_of(t, 2 * y, lambda a, b: a % b, lambda a, b: a // b)
            lead = tuple(lax.rem(bits[name] + at_bits[name], 2) for name in order)
            keep[lead + (at,)] = mine[t * rows : (t + 1) * rows]
            send[lead + (at,)] = other[t * rows : (t + 1) * rows]


def bits_of(t, d, rem, div):
    return {"x": rem(t, 2), "z0": rem(div(t, 2), 2), "z1": div(t, 4), "y": div(d, 2)}


def bases_of(items, tm, channels):
    ends = [0]
    for _, is_out in items:
        ends.append(ends[-1] + (1 if is_out else 2) * channels // tm)
    return ends[:-1], ends[-1]


def run_layers(in_shards, tm, dp, halo, borders, loaded):
    own_x, own_grad, own_skip, sums, conv_w, out_w = loaded
    length, channels = own_x.shape
    layers = conv_w.shape[0]
    third = layers // len(CHAINS)
    low = layers - third
    extent, border = length + 2 * halo, length + halo
    starts = []
    for index in range(layers):
        need = halo if index == layers - 1 else 2 ** (index + 1)
        starts.append(need // 16 * 16)
    counts = [-(-(length + 2 ** (index + 1) - 1) // 16) * 16 for index in range(layers)]
    plan = {"halo": halo, "starts": starts, "counts": counts, "length": length, "channels": channels, "unused": 0}
    plans, shapes = [], []
    for chunk, order in enumerate(CHAINS):
        items = items_of(layers, chunk)
        bases, rows = bases_of(items, tm, channels)
        if in_shards:
            store = functools.partial(store_shards, tm, dp, order, bases)
            finish = functools.partial(finish_shards, EXTRA[chunk])
            shapes.append(2 * [(2,) * len(order) + (rows + EXTRA[chunk], LANES)])
        else:
            store, finish = functools.partial(store_whole, items), finish_whole
            outs = sum(is_out for _, is_out in items)
            shapes.append([(len(items) - outs,) + conv_w.shape[1:], (outs,) + out_w.shape[1:]])
        plans.append(plan | {"items": items, "store": store, "finish": finish})
    vmem, anywhere = pl.BlockSpec(memory_space=pltpu.VMEM), pl.BlockSpec(memory_space=pl.ANY)
    weight_bytes = 2 * (conv_w.size + out_w.size)
    flops = 2 * length * channels * channels
    kept = pl.pallas_call(
        functools.partial(forward_kernel, plan),
        in_specs=[vmem] * 4,
        out_specs=[vmem] * 4,
        out_shape=[
            pltpu.VMEM((layers, extent, channels), jnp.bfloat16),
            pltpu.VMEM((low, extent, channels), jnp.bfloat16),
            pltpu.VMEM((layers, extent, 2 * channels), jnp.bfloat16),
            pltpu.VMEM((layers, extent, channels), jnp.bfloat16),
        ],
        scratch_shapes=[pltpu.VMEM((2 ** (layers - 1) + extent, channels), jnp.float32)],
        compiler_params=pltpu.CompilerParams(vmem_limit_bytes=VMEM_BYTES),
        cost_estimate=cost(flops * 5 * layers, weight_bytes),
        name="forward",
    )(*held((borders[0], own_x, conv_w, out_w)))

    def backward_of(step, inputs, outs, after):
        more = {"inputs": len(inputs), "unused": len(after)}
        return pl.pallas_call(
            functools.partial(backward_kernel, plans[step] | more, layers - (step + 1) * third, third),
            in_specs=[vmem] * (6 + len(inputs)) + [anywhere] * len(after),
            out_specs=[vmem] * (len(outs) + 2),
            out_shape=[pltpu.VMEM((rows, wide), kind) for rows, wide, kind in outs]
            + [pltpu.VMEM(shape, jnp.bfloat16) for shape in shapes[step]],
            scratch_shapes=[
                pltpu.VMEM((border, channels), jnp.float32),
                pltpu.VMEM((border, 2 * channels), jnp.bfloat16),
                pltpu.VMEM((border, channels), jnp.float32),
            ],
            compiler_params=pltpu.CompilerParams(vmem_limit_bytes=VMEM_BYTES),
            cost_estimate=cost(flops * 12 * third, weight_bytes),
            name=("last_third", "middle_third", "first_third")[step],
        )(*held((*kept, conv_w, out_w, *inputs, *after)))

    whole = (border, channels, jnp.float32)
    grad_stream, grad_skip, *last = backward_of(
        0, (borders[1], own_grad, own_skip, sums), [whole, (border, channels, jnp.bfloat16)], []
    )
    parts = [last]
    if in_shards:
        parts[0] = Chunk(tm, dp, 0, *last)
    grad_stream, *middle = backward_of(1, (grad_stream, grad_skip), [whole], [])
    grad_stream, preact, *first = backward_of(
        2, (grad_stream, grad_skip), [(length, channels, jnp.float32), (counts[0], 2 * channels, jnp.bfloat16)],
        [parts[0].next_message()] if in_shards else [],
    )
    other, own = pl.pallas_call(
        functools.partial(inputs_kernel, halo),
        in_specs=[vmem] * 3,
        out_specs=[vmem] * 2,
        out_shape=[pltpu.VMEM((halo, channels), jnp.bfloat16), pltpu.VMEM((length - halo, channels), jnp.float32)],
        scratch_shapes=[pltpu.VMEM((length, channels), jnp.float32), pltpu.VMEM((counts[0], channels), jnp.float32)],
        compiler_params=pltpu.CompilerParams(vmem_limit_bytes=ADD_BYTES),
        cost_estimate=cost(flops * 4, weight_bytes // layers),
        name="to_inputs",
    )(*held((preact, grad_stream, conv_w)))
    parts += [middle, first]
    if in_shards:
        for step in (1, 2):
            parts[step] = Chunk(tm, dp, step, *parts[step])
    return other, own, parts


def add_kernel(count, groups, *refs):
    arrays, outs = refs[:count], refs[-len(groups) :]
    for out, pieces in zip(outs, groups):
        lead = (slice(None),) * (len(out.shape) - 2)
        for first, rows, with_total, terms in pieces:
            body = rows - 16 if with_total else rows
            value = 0.0
            for array, at, begin in terms:
                value = value + arrays[array][at + lead + (slice(begin, begin + body),)].astype(jnp.float32)
            out[lead + (slice(first, first + body),)] = value.astype(out.dtype)
            if with_total:
                total = 0.0
                for array, at, begin in terms:
                    rows_at = slice(begin + body, begin + rows)
                    total = total + joined_rows(arrays[array][at + (0,) * len(lead) + (rows_at,)])
                slab = split_rows(total)
                out[lead + (slice(first + body, first + rows),)] = jnp.broadcast_to(slab, out.shape[:-2] + slab.shape)


def add_up(arrays, groups, shapes, after, name):
    vmem = pl.BlockSpec(memory_space=pltpu.VMEM)
    return pl.pallas_call(
        functools.partial(add_kernel, len(arrays), groups),
        in_specs=[vmem] * len(arrays) + [pl.BlockSpec(memory_space=pl.ANY)] * len(after),
        out_specs=[vmem] * len(groups),
        out_shape=[pltpu.VMEM(shape, jnp.bfloat16) for shape in shapes],
        compiler_params=pltpu.CompilerParams(vmem_limit_bytes=ADD_BYTES),
        name=name,
    )(*held(arrays), *held(after))


def first_block(array, first, rows):
    return array[(0,) * (len(array.shape) - 2) + (slice(first, first + rows),)].astype(jnp.float32)


def first_block(array, first, rows):
    return array[(0,) * (len(array.shape) - 2) + (slice(first, first + rows),)].astype(jnp.float32)


def last_kernel(counts, samples_all, tm, *refs):
    chunks = []
    for count in counts:
        chunks.insert(0, refs[:count])
        refs = refs[count:]
    other, own, grad_inputs, grad_conv, grad_out = refs
    layers, channels = grad_conv.shape[0], own.shape[1]
    total = 0.0
    for term in chunks[0]:
        total = total + jnp.sum(first_block(term, term.shape[-2] - 16, 16), axis=0, keepdims=True)
    scale = samples_all / total
    for chunk, terms in enumerate(chunks):
        items = items_of(layers, chunk)
        for (index, is_out), base in zip(items, bases_of(items, tm, channels)[0]):
            out = grad_out if is_out else grad_conv
            value = 0.0
            for term in terms:
                value = value + first_block(term, base, out.shape[1])
            out[index] = value * scale
    for first in range(0, channels, LANES):
        lanes = slice(first, first + LANES)
        grad_inputs[0 : own.shape[0], lanes] = own[:, lanes] * scale
        grad_inputs[own.shape[0] :, lanes] = other[:, lanes].astype(jnp.float32) * scale


class Chunk:
    def __init__(self, tm, dp, chunk, keep, send):
        self.tm, self.dp, self.chunk, self.rows = tm, dp, chunk, keep.shape[-2]
        self.message = None
        self.terms = [keep, swapped(tm, dp, send, "core")]

    def next_message(self, after=()):
        if self.message is None:
            left = len(CHAINS[self.chunk]) + 2 - len(self.terms)
            pieces = []
            for i, v in enumerate(self.terms):
                pieces.append((i, (0,) * (len(v.shape) - 2 - left) + (1,), 0))
            (self.message,) = add_up(
                self.terms, [[(0, self.rows, EXTRA[self.chunk] > 0, pieces)]], [(2,) * (left - 1) + (self.rows, LANES)], after,
                "add_chunk%d_step%d" % (self.chunk, len(self.terms) - 1),
            )
        return self.message

    def run_chain(self, after=()):
        for step, name in enumerate(CHAINS[self.chunk]):
            self.terms.append(swapped(self.tm, self.dp, self.next_message(after if step == 1 else ()), name))
            self.message = None
        return self.terms


def swapped(tm, dp, value, name):
    over_t, over_d = {"core": (0, 1), "y": (0, 2), "x": (1, 0), "z0": (2, 0), "z1": (4, 0)}[name]
    pairs = [(t * dp + d, (t ^ over_t) * dp + (d ^ over_d)) for t in range(tm) for d in range(dp)]
    return lax.ppermute(value, ("tm", "dp"), pairs)


def scattered(part):
    columns = lax.psum_scatter(part, "dp", scatter_dimension=2, tiled=True).astype(jnp.float32)
    return lax.psum_scatter(columns, "tm", scatter_dimension=1, tiled=True)


def body(inputs, grad_stream_out, grad_skip_out, sample_weight, conv_weight, out_weight):
    tm, dp = lax.axis_size("tm"), lax.axis_size("dp")
    batch, length, channels = inputs.shape
    layers = conv_weight.shape[0]
    third = layers // len(CHAINS)
    halo = 2**layers
    samples_all = batch * length * tm * dp
    x, gs, gk = inputs[0], grad_stream_out[0], grad_skip_out[0]
    x_rows, grad_rows = pack(halo, x, gs, gk, sample_weight)
    borders = [around(x_rows, "tm", 1), around(grad_rows, "tm", 1)]
    loaded = load_all(x, gs, gk, sample_weight, conv_weight, out_weight, x_rows)
    in_shards = tm == 8 and dp == 4 and channels // tm % 16 == 0 and 2 * channels == dp * LANES
    other, own, parts = run_layers(in_shards, tm, dp, halo, borders, loaded)
    other = around(other, "tm", -1)
    if not in_shards:
        scale = samples_all / lax.psum(jnp.sum(sample_weight), ("tm", "dp"))
        found = {}
        for chunk, part in enumerate(parts):
            items = items_of(layers, chunk)
            for is_out in (False, True):
                for place, item in enumerate(item for item in items if item[1] == is_out):
                    found[item] = part[int(is_out)][place]
        grad_conv, grad_out = (
            scattered(jnp.stack([found[index, is_out] for index in range(layers)])) * scale for is_out in (False, True)
        )
        return (jnp.concatenate([own, other]) * scale)[None], grad_conv, grad_out
    chunks = [part.run_chain([other] if part is parts[0] else ()) for part in parts]
    conv_rows, out_rows = 2 * channels // tm, channels // tm
    grad_inputs, grad_conv, grad_out = pl.pallas_call(
        functools.partial(last_kernel, [len(terms) for terms in reversed(chunks)], float(samples_all), tm),
        out_shape=[
            jax.ShapeDtypeStruct((length, channels), jnp.float32),
            jax.ShapeDtypeStruct((layers, conv_rows, LANES), jnp.float32),
            jax.ShapeDtypeStruct((layers, out_rows, LANES), jnp.float32),
        ],
        compiler_params=pltpu.CompilerParams(vmem_limit_bytes=ADD_BYTES),
        name="scale_all",
    )(*held([term for terms in reversed(chunks) for term in terms]), *held([other, own]))
    return grad_inputs[None], grad_conv, grad_out


def solution(mesh):
    placed = (
        P("dp", "tm", None),
        P("dp", "tm", None),
        P("dp", "tm", None),
        P("dp", "tm"),
        P(),
        P(),
    )
    return jax.shard_map(
        body,
        mesh=mesh,
        in_specs=placed,
        out_specs=(P("dp", "tm", None), P(None, "tm", "dp"), P(None, "tm", "dp")),
        check_vma=False,
    )
```

```python
import functools

import jax
import jax.numpy as jnp
from jax import lax
from jax.experimental import pallas as pl
from jax.experimental.pallas import tpu as pltpu
from jax.sharding import PartitionSpec as P

LANES = 128
VMEM_BYTES = 24 * 1024 * 1024
ADD_BYTES = 8 * 1024 * 1024
CHAINS = (("x", "z0", "y", "z1"), ("z0", "y", "x", "z1"), ("y", "x", "z0", "z1"))
EXTRA = (16, 0, 0)
NN = (((1,), (0,)), ((), ()))
NT = (((1,), (1,)), ((), ()))
TN = (((0,), (0,)), ((), ()))


def dot(left, right, dims):
    return lax.dot_general(left, right, dims, preferred_element_type=jnp.float32)


def held(arrays, space=pltpu.VMEM):
    return [pltpu.with_memory_space_constraint(x, space) for x in arrays]


def around(x, axis, by):
    count = lax.axis_size(axis)
    return lax.ppermute(x, axis, [(i, (i + by) % count) for i in range(count)])


def column(row, rows):
    return jnp.broadcast_to(row, (LANES, rows)).T


def cost(flops, moved):
    return pl.CostEstimate(flops=flops, bytes_accessed=moved, transcendentals=0)


def pack_kernel(tail_x, tail_gs, tail_gk, weight, x_rows, grad_rows):
    halo, channels = tail_gs.shape
    by_row = column(weight[...], LANES)[LANES - halo :]
    by_row = jnp.concatenate([by_row] * (channels // LANES), axis=1)
    x_rows[...] = tail_x[...]
    grad_rows[0:halo] = (tail_gs[...].astype(jnp.float32) * by_row).astype(jnp.bfloat16)
    grad_rows[halo:] = (tail_gk[...].astype(jnp.float32) * by_row).astype(jnp.bfloat16)


def pack(halo, x, grad_stream_out, grad_skip_out, weight):
    length, channels = x.shape

    def last(rows):
        return pl.BlockSpec((rows, channels), lambda i: (length // rows - 1, 0))

    message = jax.ShapeDtypeStruct((2 * halo, channels), jnp.bfloat16)
    return pl.pallas_call(
        pack_kernel,
        grid=(1,),
        in_specs=[last(2 * halo), last(halo), last(halo), pl.BlockSpec((1, LANES), lambda i: (0, length // LANES - 1))],
        out_specs=[pl.BlockSpec(message.shape, lambda i: (0, 0))] * 2,
        out_shape=[message] * 2,
        compiler_params=pltpu.CompilerParams(vmem_limit_bytes=ADD_BYTES),
        name="pack_borders",
    )(*held((x, grad_stream_out, grad_skip_out, weight), pltpu.HBM))


def load_kernel(
    x, gs, gk, weight, conv_w, out_w, _, x_here, grad_stream, grad_skip, sums, conv_here, out_here,
    gs_raw, gk_raw, weight_here, sems,
):
    pairs = ((weight, weight_here), (gs, gs_raw), (gk, gk_raw), (x, x_here), (conv_w, conv_here), (out_w, out_here))
    copies = [pltpu.make_async_copy(a, b, sems.at[i]) for i, (a, b) in enumerate(pairs)]
    for copy in copies:
        copy.start()
    for copy in copies[:3]:
        copy.wait()
    length, channels = x_here.shape
    by_row = column(weight_here[...], length)
    by_row = jnp.concatenate([by_row] * (channels // LANES), axis=1)
    grad_stream[...] = gs_raw[...].astype(jnp.float32) * by_row
    grad_skip[...] = (gk_raw[...].astype(jnp.float32) * by_row).astype(jnp.bfloat16)
    own_sum = jnp.broadcast_to(jnp.sum(weight_here[...], axis=1, keepdims=True), (1, LANES))
    sums[...] = split_rows(own_sum)
    for copy in copies[3:]:
        copy.wait()


def load_all(x, gs, gk, weight, conv_w, out_w, after):
    shape = x.shape
    vmem, anywhere = pl.BlockSpec(memory_space=pltpu.VMEM), pl.BlockSpec(memory_space=pl.ANY)
    return pl.pallas_call(
        load_kernel,
        in_specs=[anywhere] * 7,
        out_specs=[vmem] * 6,
        out_shape=[
            pltpu.VMEM(shape, jnp.bfloat16),
            pltpu.VMEM(shape, jnp.float32),
            pltpu.VMEM(shape, jnp.bfloat16),
            pltpu.VMEM((16, LANES), jnp.bfloat16),
            pltpu.VMEM(conv_w.shape, jnp.bfloat16),
            pltpu.VMEM(out_w.shape, jnp.bfloat16),
        ],
        scratch_shapes=[
            pltpu.VMEM(shape, jnp.bfloat16),
            pltpu.VMEM(shape, jnp.bfloat16),
            pltpu.VMEM(weight.shape, jnp.float32),
            pltpu.SemaphoreType.DMA((6,)),
        ],
        compiler_params=pltpu.CompilerParams(vmem_limit_bytes=ADD_BYTES),
        cost_estimate=cost(10**7, 6 * 10**6),
        name="load_all",
    )(*held((x, gs, gk, weight, conv_w, out_w), pltpu.HBM), *held([after]))


def split_rows(total):
    high = total.astype(jnp.bfloat16).astype(jnp.float32)
    middle = (total - high).astype(jnp.bfloat16).astype(jnp.float32)
    low = total - high - middle
    row = lax.broadcasted_iota(jnp.int32, (16, LANES), 0)
    rows = jnp.where(row == 0, high, jnp.where(row == 1, middle, jnp.where(row == 2, low, 0.0)))
    return rows.astype(jnp.bfloat16)


def joined_rows(rows):
    return jnp.sum(rows.astype(jnp.float32), axis=0, keepdims=True)


def cut_off(rows, dilation):
    row = lax.broadcasted_iota(jnp.int32, rows.shape, 0)
    return jnp.where(jnp.logical_and(row < dilation, lax.axis_index("tm") == 0), 0.0, rows)


def items_of(layers, chunk):
    third = layers // len(CHAINS)
    high = layers - chunk * third
    return [(index, is_out) for index in reversed(range(high - third, high)) for is_out in (False, True)]


def earlier_rows(plan, index, present, first, last):
    dilation, begin = 2**index, 2 * plan["halo"]
    cut = cut_off(present[begin - dilation : begin], dilation)
    return jnp.concatenate([present[first - dilation : begin - dilation], cut, present[begin : last - dilation]])


def moved_on(dilation, spread, past_part, grad_stream, halo, rows):
    count, channels = spread.shape[0], grad_stream.shape[1]
    past_part[0:count] = spread[:, channels:]
    cut = slice(halo, halo + max(dilation, 8))
    past_part[cut] = cut_off(past_part[cut], dilation)
    grad_stream[0:rows] += spread[0:rows, :channels] + past_part[dilation : dilation + rows]


def inputs_kernel(halo, preact, grad_before, conv_w, other, own, grad_stream, past_part):
    grad_stream[...] = grad_before[...]
    moved_on(1, dot(preact[...], conv_w[0], NT), past_part, grad_stream, halo, grad_stream.shape[0])
    other[...] = grad_stream[0:halo].astype(other.dtype)
    own[...] = grad_stream[halo:]


def backward(plan, layers, refs_of, conv_w, out_w, grad_proj, grad_stream, past_part, grad_parts, last_preact):
    halo, length, channels = plan["halo"], plan["length"], plan["channels"]
    own = slice(halo, halo + length)
    items = plan["items"]

    for index in layers:
        dilation, count = 2**index, plan["counts"][index]
        present, earlier, factors, gates = refs_of(index)
        grad_proj[0:count, :channels] = grad_stream[0:count].astype(jnp.bfloat16)
        grad_gated = dot(grad_proj[0:count], out_w[index], NT)
        total = dot(gates[own], grad_proj[0:length], TN)
        plan["store"](total, items.index((index, True)), grad_parts)
        both = factors[halo : halo + count].astype(jnp.float32)
        grad_preact = jnp.concatenate(
            [grad_gated * both[:, :channels], grad_gated * both[:, channels:]], axis=1
        ).astype(jnp.bfloat16)
        if index:
            moved_on(dilation, dot(grad_preact, conv_w[index], NT), past_part, grad_stream, halo, plan["counts"][index - 1])
        else:
            last_preact[...] = grad_preact
        past = earlier_rows(plan, index, present, halo, halo + length) if earlier is None else earlier[own]
        total = dot(jnp.concatenate([present[own], past], axis=1), grad_preact[0:length], TN)
        plan["store"](total, items.index((index, False)), grad_parts)


def forward_kernel(plan, prev_x, own_x, conv_w, out_w, all_present, all_earlier, all_factors, all_gates, stream):
    halo, (length, channels) = plan["halo"], own_x.shape
    layers, low = conv_w.shape[0], all_earlier.shape[0]
    pad = 2 ** (layers - 1)
    extent = length + 2 * halo
    begin = 2 * halo
    stream[0:pad] = jnp.zeros((pad, channels), jnp.float32)
    stream[pad : pad + begin] = prev_x[...].astype(jnp.float32)
    stream[pad + begin :] = own_x[...].astype(jnp.float32)
    all_present[0, 0:begin] = prev_x[...]
    all_present[0, begin:] = own_x[...]
    for index in range(layers):
        dilation, start = 2**index, plan["starts"][index]
        present = all_present.at[index]
        if index >= low:
            past = earlier_rows(plan, index, present, start, extent)
        else:
            past = stream[pad + start - dilation : pad + extent - dilation]
            cut = cut_off(past[begin - start : begin - start + 16], dilation)
            past = jnp.concatenate([past[: begin - start], cut, past[begin - start + 16 :]]).astype(jnp.bfloat16)
            all_earlier[index, start:] = past
        preact = dot(jnp.concatenate([present[start:], past], axis=1), conv_w[index], NN)
        filtered = jnp.tanh(preact[:, :channels])
        opening = 0.5 + 0.5 * jnp.tanh(0.5 * preact[:, channels:])
        product = filtered * opening
        gated = product.astype(jnp.bfloat16)
        all_gates[index, start:] = gated
        if index < layers - 1:
            projected = dot(gated, out_w[index, :, :channels], NN)
        all_factors[index, start:, :channels] = (opening - filtered * product).astype(jnp.bfloat16)
        all_factors[index, start:, channels:] = (product * (1.0 - opening)).astype(jnp.bfloat16)
        if index < layers - 1:
            after = stream[pad + start :] + projected
            all_present[index + 1, start:] = after.astype(jnp.bfloat16)
            if index < layers - 2:
                stream[pad + start :] = after


def backward_kernel(plan, first, third, all_present, all_earlier, all_factors, all_gates, conv_w, out_w, *rest):
    refs = rest[: plan["inputs"]]
    *outs, keep, send, grad_stream, grad_proj, past_part = rest[plan["inputs"] + plan["unused"] :]
    halo, length, channels, low = plan["halo"], plan["length"], plan["channels"], all_earlier.shape[0]
    if plan["inputs"] == 4:
        prev_rows, own_grad, own_skip, sums = refs
        *outs, grad_skip = outs
        grad_stream[0:halo] = prev_rows[0:halo].astype(jnp.float32)
        grad_stream[halo:] = own_grad[...]
        grad_skip[0:halo] = prev_rows[halo:]
        grad_skip[halo:] = own_skip[...]
    else:
        grad_before, grad_skip = refs
        grad_stream[...] = grad_before[...]
    grad_proj[:, channels:] = grad_skip[...]

    def refs_of(index):
        earlier = all_earlier.at[index] if index < low else None
        return all_present.at[index], earlier, all_factors.at[index], all_gates.at[index]

    backward(
        plan, list(reversed(range(first, first + third))), refs_of, conv_w, out_w,
        grad_proj, grad_stream, past_part, (keep, send), outs[-1],
    )
    outs[0][...] = grad_stream[0 : outs[0].shape[0]]
    if plan["inputs"] == 4:
        plan["finish"](sums, (keep, send))


def store_whole(items, total, item, grad_parts):
    is_out = items[item][1]
    place = sum(kind == is_out for _, kind in items[:item])
    grad_parts[int(is_out)][place] = total.astype(jnp.bfloat16)


def finish_whole(sums, grad_parts):
    pass


def finish_shards(extra, sums, grad_parts):
    for part in grad_parts:
        lead, rows = part.shape[:-2], part.shape[-2]
        for first in range(rows - extra, rows, 16):
            part[(slice(None),) * len(lead) + (slice(first, first + 16),)] = jnp.broadcast_to(
                sums[...], lead + sums.shape
            )


def store_shards(tm, dp, order, bases, total, item, grad_parts):
    keep, send = grad_parts
    t_at, d_at = lax.axis_index("tm"), lax.axis_index("dp")
    core_at = lax.rem(d_at, 2)
    rows = total.shape[0] // tm
    at = pl.ds(bases[item], rows)
    at_bits = bits_of(t_at, d_at, lax.rem, lax.div)
    for y in range(dp // 2):
        near = total[:, (2 * y) * LANES : (2 * y + 1) * LANES]
        far = total[:, (2 * y + 1) * LANES : (2 * y + 2) * LANES]
        mine = jnp.where(core_at == 0, near, far).astype(jnp.bfloat16)
        other = jnp.where(core_at == 0, far, near).astype(jnp.bfloat16)
        for t in range(tm):
            bits = bits_of(t, 2 * y, lambda a, b: a % b, lambda a, b: a // b)
            lead = tuple(lax.rem(bits[name] + at_bits[name], 2) for name in order)
            keep[lead + (at,)] = mine[t * rows : (t + 1) * rows]
            send[lead + (at,)] = other[t * rows : (t + 1) * rows]


def bits_of(t, d, rem, div):
    return {"x": rem(t, 2), "z0": rem(div(t, 2), 2), "z1": div(t, 4), "y": div(d, 2)}


def bases_of(items, tm, channels):
    ends = [0]
    for _, is_out in items:
        ends.append(ends[-1] + (1 if is_out else 2) * channels // tm)
    return ends[:-1], ends[-1]


def run_layers(in_shards, tm, dp, halo, borders, loaded):
    own_x, own_grad, own_skip, sums, conv_w, out_w = loaded
    length, channels = own_x.shape
    layers = conv_w.shape[0]
    third = layers // len(CHAINS)
    low = layers - third
    extent, border = length + 2 * halo, length + halo
    starts = []
    for index in range(layers):
        need = halo if index == layers - 1 else 2 ** (index + 1)
        starts.append(need // 16 * 16)
    counts = [-(-(length + 2 ** (index + 1) - 1) // 16) * 16 for index in range(layers)]
    plan = {"halo": halo, "starts": starts, "counts": counts, "length": length, "channels": channels, "unused": 0}
    plans, shapes = [], []
    for chunk, order in enumerate(CHAINS):
        items = items_of(layers, chunk)
        bases, rows = bases_of(items, tm, channels)
        if in_shards:
            store = functools.partial(store_shards, tm, dp, order, bases)
            finish = functools.partial(finish_shards, EXTRA[chunk])
            shapes.append(2 * [(2,) * len(order) + (rows + EXTRA[chunk], LANES)])
        else:
            store, finish = functools.partial(store_whole, items), finish_whole
            outs = sum(is_out for _, is_out in items)
            shapes.append([(len(items) - outs,) + conv_w.shape[1:], (outs,) + out_w.shape[1:]])
        plans.append(plan | {"items": items, "store": store, "finish": finish})
    vmem, anywhere = pl.BlockSpec(memory_space=pltpu.VMEM), pl.BlockSpec(memory_space=pl.ANY)
    weight_bytes = 2 * (conv_w.size + out_w.size)
    flops = 2 * length * channels * channels
    kept = pl.pallas_call(
        functools.partial(forward_kernel, plan),
        in_specs=[vmem] * 4,
        out_specs=[vmem] * 4,
        out_shape=[
            pltpu.VMEM((layers, extent, channels), jnp.bfloat16),
            pltpu.VMEM((low, extent, channels), jnp.bfloat16),
            pltpu.VMEM((layers, extent, 2 * channels), jnp.bfloat16),
            pltpu.VMEM((layers, extent, channels), jnp.bfloat16),
        ],
        scratch_shapes=[pltpu.VMEM((2 ** (layers - 1) + extent, channels), jnp.float32)],
        compiler_params=pltpu.CompilerParams(vmem_limit_bytes=VMEM_BYTES),
        cost_estimate=cost(flops * 5 * layers, weight_bytes),
        name="forward",
    )(*held((borders[0], own_x, conv_w, out_w)))

    def backward_of(step, inputs, outs, after):
        more = {"inputs": len(inputs), "unused": len(after)}
        return pl.pallas_call(
            functools.partial(backward_kernel, plans[step] | more, layers - (step + 1) * third, third),
            in_specs=[vmem] * (6 + len(inputs)) + [anywhere] * len(after),
            out_specs=[vmem] * (len(outs) + 2),
            out_shape=[pltpu.VMEM((rows, wide), kind) for rows, wide, kind in outs]
            + [pltpu.VMEM(shape, jnp.bfloat16) for shape in shapes[step]],
            scratch_shapes=[
                pltpu.VMEM((border, channels), jnp.float32),
                pltpu.VMEM((border, 2 * channels), jnp.bfloat16),
                pltpu.VMEM((border, channels), jnp.float32),
            ],
            compiler_params=pltpu.CompilerParams(vmem_limit_bytes=VMEM_BYTES),
            cost_estimate=cost(flops * 12 * third, weight_bytes),
            name=("last_third", "middle_third", "first_third")[step],
        )(*held((*kept, conv_w, out_w, *inputs, *after)))

    whole = (border, channels, jnp.float32)
    grad_stream, grad_skip, *last = backward_of(
        0, (borders[1], own_grad, own_skip, sums), [whole, (border, channels, jnp.bfloat16)], []
    )
    parts = [last]
    if in_shards:
        parts[0] = Chunk(tm, dp, 0, *last)
    grad_stream, *middle = backward_of(1, (grad_stream, grad_skip), [whole], [])
    grad_stream, preact, *first = backward_of(
        2, (grad_stream, grad_skip), [(length, channels, jnp.float32), (counts[0], 2 * channels, jnp.bfloat16)],
        [parts[0].next_message()] if in_shards else [],
    )
    other, own = pl.pallas_call(
        functools.partial(inputs_kernel, halo),
        in_specs=[vmem] * 3,
        out_specs=[vmem] * 2,
        out_shape=[pltpu.VMEM((halo, channels), jnp.bfloat16), pltpu.VMEM((length - halo, channels), jnp.float32)],
        scratch_shapes=[pltpu.VMEM((length, channels), jnp.float32), pltpu.VMEM((counts[0], channels), jnp.float32)],
        compiler_params=pltpu.CompilerParams(vmem_limit_bytes=ADD_BYTES),
        cost_estimate=cost(flops * 4, weight_bytes // layers),
        name="to_inputs",
    )(*held((preact, grad_stream, conv_w)))
    parts += [middle, first]
    if in_shards:
        for step in (1, 2):
            parts[step] = Chunk(tm, dp, step, *parts[step])
    return other, own, parts


def add_kernel(count, groups, *refs):
    arrays, outs = refs[:count], refs[-len(groups) :]
    for out, pieces in zip(outs, groups):
        lead = (slice(None),) * (len(out.shape) - 2)
        for first, rows, with_total, terms in pieces:
            body = rows - 16 if with_total else rows
            value = 0.0
            for array, at, begin in terms:
                value = value + arrays[array][at + lead + (slice(begin, begin + body),)].astype(jnp.float32)
            out[lead + (slice(first, first + body),)] = value.astype(out.dtype)
            if with_total:
                total = 0.0
                for array, at, begin in terms:
                    rows_at = slice(begin + body, begin + rows)
                    total = total + joined_rows(arrays[array][at + (0,) * len(lead) + (rows_at,)])
                slab = split_rows(total)
                out[lead + (slice(first + body, first + rows),)] = jnp.broadcast_to(slab, out.shape[:-2] + slab.shape)


def add_up(arrays, groups, shapes, after, name):
    vmem = pl.BlockSpec(memory_space=pltpu.VMEM)
    return pl.pallas_call(
        functools.partial(add_kernel, len(arrays), groups),
        in_specs=[vmem] * len(arrays) + [pl.BlockSpec(memory_space=pl.ANY)] * len(after),
        out_specs=[vmem] * len(groups),
        out_shape=[pltpu.VMEM(shape, jnp.bfloat16) for shape in shapes],
        compiler_params=pltpu.CompilerParams(vmem_limit_bytes=ADD_BYTES),
        name=name,
    )(*held(arrays), *held(after))


def first_block(array, first, rows):
    return array[(0,) * (len(array.shape) - 2) + (slice(first, first + rows),)].astype(jnp.float32)


def first_block(array, first, rows):
    return array[(0,) * (len(array.shape) - 2) + (slice(first, first + rows),)].astype(jnp.float32)


def last_kernel(counts, samples_all, tm, *refs):
    chunks = []
    for count in counts:
        chunks.insert(0, refs[:count])
        refs = refs[count:]
    other, own, grad_inputs, grad_conv, grad_out = refs
    layers, channels = grad_conv.shape[0], own.shape[1]
    total = 0.0
    for term in chunks[0]:
        total = total + jnp.sum(first_block(term, term.shape[-2] - 16, 16), axis=0, keepdims=True)
    scale = samples_all / total
    for chunk, terms in enumerate(chunks):
        items = items_of(layers, chunk)
        for (index, is_out), base in zip(items, bases_of(items, tm, channels)[0]):
            out = grad_out if is_out else grad_conv
            value = 0.0
            for term in terms:
                value = value + first_block(term, base, out.shape[1])
            out[index] = value * scale
    for first in range(0, channels, LANES):
        lanes = slice(first, first + LANES)
        grad_inputs[0 : own.shape[0], lanes] = own[:, lanes] * scale
        grad_inputs[own.shape[0] :, lanes] = other[:, lanes].astype(jnp.float32) * scale


class Chunk:
    def __init__(self, tm, dp, chunk, keep, send):
        self.tm, self.dp, self.chunk, self.rows = tm, dp, chunk, keep.shape[-2]
        self.message = None
        self.terms = [keep, swapped(tm, dp, send, "core")]

    def next_message(self, after=()):
        if self.message is None:
            left = len(CHAINS[self.chunk]) + 2 - len(self.terms)
            pieces = []
            for i, v in enumerate(self.terms):
                pieces.append((i, (0,) * (len(v.shape) - 2 - left) + (1,), 0))
            (self.message,) = add_up(
                self.terms, [[(0, self.rows, EXTRA[self.chunk] > 0, pieces)]], [(2,) * (left - 1) + (self.rows, LANES)], after,
                "add_chunk%d_step%d" % (self.chunk, len(self.terms) - 1),
            )
        return self.message

    def run_chain(self, after=()):
        for step, name in enumerate(CHAINS[self.chunk]):
            self.terms.append(swapped(self.tm, self.dp, self.next_message(after if step == 1 else ()), name))
            self.message = None
        return self.terms


def swapped(tm, dp, value, name):
    over_t, over_d = {"core": (0, 1), "y": (0, 2), "x": (1, 0), "z0": (2, 0), "z1": (4, 0)}[name]
    pairs = [(t * dp + d, (t ^ over_t) * dp + (d ^ over_d)) for t in range(tm) for d in range(dp)]
    return lax.ppermute(value, ("tm", "dp"), pairs)


def scattered(part):
    columns = lax.psum_scatter(part, "dp", scatter_dimension=2, tiled=True).astype(jnp.float32)
    return lax.psum_scatter(columns, "tm", scatter_dimension=1, tiled=True)


def body(inputs, grad_stream_out, grad_skip_out, sample_weight, conv_weight, out_weight):
    tm, dp = lax.axis_size("tm"), lax.axis_size("dp")
    batch, length, channels = inputs.shape
    layers = conv_weight.shape[0]
    third = layers // len(CHAINS)
    halo = 2**layers
    samples_all = batch * length * tm * dp
    x, gs, gk = inputs[0], grad_stream_out[0], grad_skip_out[0]
    x_rows, grad_rows = pack(halo, x, gs, gk, sample_weight)
    borders = [around(x_rows, "tm", 1), around(grad_rows, "tm", 1)]
    loaded = load_all(x, gs, gk, sample_weight, conv_weight, out_weight, x_rows)
    in_shards = tm == 8 and dp == 4 and channels // tm % 16 == 0 and 2 * channels == dp * LANES
    other, own, parts = run_layers(in_shards, tm, dp, halo, borders, loaded)
    other = around(other, "tm", -1)
    if not in_shards:
        scale = samples_all / lax.psum(jnp.sum(sample_weight), ("tm", "dp"))
        found = {}
        for chunk, part in enumerate(parts):
            items = items_of(layers, chunk)
            for is_out in (False, True):
                for place, item in enumerate(item for item in items if item[1] == is_out):
                    found[item] = part[int(is_out)][place]
        grad_conv, grad_out = (
            scattered(jnp.stack([found[index, is_out] for index in range(layers)])) * scale for is_out in (False, True)
        )
        return (jnp.concatenate([own, other]) * scale)[None], grad_conv, grad_out
    chunks = [part.run_chain([other] if part is parts[0] else ()) for part in parts]
    conv_rows, out_rows = 2 * channels // tm, channels // tm
    grad_inputs, grad_conv, grad_out = pl.pallas_call(
        functools.partial(last_kernel, [len(terms) for terms in reversed(chunks)], float(samples_all), tm),
        out_shape=[
            jax.ShapeDtypeStruct((length, channels), jnp.float32),
            jax.ShapeDtypeStruct((layers, conv_rows, LANES), jnp.float32),
            jax.ShapeDtypeStruct((layers, out_rows, LANES), jnp.float32),
        ],
        compiler_params=pltpu.CompilerParams(vmem_limit_bytes=ADD_BYTES),
        name="scale_all",
    )(*held([term for terms in reversed(chunks) for term in terms]), *held([other, own]))
    return grad_inputs[None], grad_conv, grad_out


def solution(mesh):
    placed = (
        P("dp", "tm", None),
        P("dp", "tm", None),
        P("dp", "tm", None),
        P("dp", "tm"),
        P(),
        P(),
    )
    return jax.shard_map(
        body,
        mesh=mesh,
        in_specs=placed,
        out_specs=(P("dp", "tm", None), P(None, "tm", "dp"), P(None, "tm", "dp")),
        check_vma=False,
    )
```

```python
import functools

import jax
import jax.numpy as jnp
from jax import lax
from jax.experimental import pallas as pl
from jax.experimental.pallas import tpu as pltpu
from jax.sharding import PartitionSpec as P

LANES = 128
VMEM_BYTES = 24 * 1024 * 1024
ADD_BYTES = 8 * 1024 * 1024
CHAINS = (("x", "z0", "y", "z1"), ("z0", "y", "x", "z1"), ("y", "x", "z0", "z1"))
EXTRA = (16, 0, 0)
NN = (((1,), (0,)), ((), ()))
NT = (((1,), (1,)), ((), ()))
TN = (((0,), (0,)), ((), ()))


def dot(left, right, dims):
    return lax.dot_general(left, right, dims, preferred_element_type=jnp.float32)


def held(arrays, space=pltpu.VMEM):
    return [pltpu.with_memory_space_constraint(x, space) for x in arrays]


def around(x, axis, by):
    count = lax.axis_size(axis)
    return lax.ppermute(x, axis, [(i, (i + by) % count) for i in range(count)])


def column(row, rows):
    return jnp.broadcast_to(row, (LANES, rows)).T


def cost(flops, moved):
    return pl.CostEstimate(flops=flops, bytes_accessed=moved, transcendentals=0)


def pack_kernel(tail_x, tail_gs, tail_gk, weight, x_rows, grad_rows):
    halo, channels = tail_gs.shape
    by_row = column(weight[...], LANES)[LANES - halo :]
    by_row = jnp.concatenate([by_row] * (channels // LANES), axis=1)
    x_rows[...] = tail_x[...]
    grad_rows[0:halo] = (tail_gs[...].astype(jnp.float32) * by_row).astype(jnp.bfloat16)
    grad_rows[halo:] = (tail_gk[...].astype(jnp.float32) * by_row).astype(jnp.bfloat16)


def pack(halo, x, grad_stream_out, grad_skip_out, weight):
    length, channels = x.shape

    def last(rows):
        return pl.BlockSpec((rows, channels), lambda i: (length // rows - 1, 0))

    message = jax.ShapeDtypeStruct((2 * halo, channels), jnp.bfloat16)
    return pl.pallas_call(
        pack_kernel,
        grid=(1,),
        in_specs=[last(2 * halo), last(halo), last(halo), pl.BlockSpec((1, LANES), lambda i: (0, length // LANES - 1))],
        out_specs=[pl.BlockSpec(message.shape, lambda i: (0, 0))] * 2,
        out_shape=[message] * 2,
        compiler_params=pltpu.CompilerParams(vmem_limit_bytes=ADD_BYTES),
        name="pack_borders",
    )(*held((x, grad_stream_out, grad_skip_out, weight), pltpu.HBM))


def load_kernel(
    x, gs, gk, weight, conv_w, out_w, _, x_here, grad_stream, grad_skip, sums, conv_here, out_here,
    gs_raw, gk_raw, weight_here, sems,
):
    pairs = ((weight, weight_here), (gs, gs_raw), (gk, gk_raw), (x, x_here), (conv_w, conv_here), (out_w, out_here))
    copies = [pltpu.make_async_copy(a, b, sems.at[i]) for i, (a, b) in enumerate(pairs)]
    for copy in copies:
        copy.start()
    for copy in copies[:3]:
        copy.wait()
    length, channels = x_here.shape
    by_row = column(weight_here[...], length)
    by_row = jnp.concatenate([by_row] * (channels // LANES), axis=1)
    grad_stream[...] = gs_raw[...].astype(jnp.float32) * by_row
    grad_skip[...] = (gk_raw[...].astype(jnp.float32) * by_row).astype(jnp.bfloat16)
    own_sum = jnp.broadcast_to(jnp.sum(weight_here[...], axis=1, keepdims=True), (1, LANES))
    sums[...] = split_rows(own_sum)
    for copy in copies[3:]:
        copy.wait()


def load_all(x, gs, gk, weight, conv_w, out_w, after):
    shape = x.shape
    vmem, anywhere = pl.BlockSpec(memory_space=pltpu.VMEM), pl.BlockSpec(memory_space=pl.ANY)
    return pl.pallas_call(
        load_kernel,
        in_specs=[anywhere] * 7,
        out_specs=[vmem] * 6,
        out_shape=[
            pltpu.VMEM(shape, jnp.bfloat16),
            pltpu.VMEM(shape, jnp.float32),
            pltpu.VMEM(shape, jnp.bfloat16),
            pltpu.VMEM((16, LANES), jnp.bfloat16),
            pltpu.VMEM(conv_w.shape, jnp.bfloat16),
            pltpu.VMEM(out_w.shape, jnp.bfloat16),
        ],
        scratch_shapes=[
            pltpu.VMEM(shape, jnp.bfloat16),
            pltpu.VMEM(shape, jnp.bfloat16),
            pltpu.VMEM(weight.shape, jnp.float32),
            pltpu.SemaphoreType.DMA((6,)),
        ],
        compiler_params=pltpu.CompilerParams(vmem_limit_bytes=ADD_BYTES),
        cost_estimate=cost(10**7, 6 * 10**6),
        name="load_all",
    )(*held((x, gs, gk, weight, conv_w, out_w), pltpu.HBM), *held([after]))


def split_rows(total):
    high = total.astype(jnp.bfloat16).astype(jnp.float32)
    middle = (total - high).astype(jnp.bfloat16).astype(jnp.float32)
    low = total - high - middle
    row = lax.broadcasted_iota(jnp.int32, (16, LANES), 0)
    rows = jnp.where(row == 0, high, jnp.where(row == 1, middle, jnp.where(row == 2, low, 0.0)))
    return rows.astype(jnp.bfloat16)


def joined_rows(rows):
    return jnp.sum(rows.astype(jnp.float32), axis=0, keepdims=True)


def cut_off(rows, dilation):
    row = lax.broadcasted_iota(jnp.int32, rows.shape, 0)
    return jnp.where(jnp.logical_and(row < dilation, lax.axis_index("tm") == 0), 0.0, rows)


def items_of(layers, chunk):
    third = layers // len(CHAINS)
    high = layers - chunk * third
    return [(index, is_out) for index in reversed(range(high - third, high)) for is_out in (False, True)]


def earlier_rows(plan, index, present, first, last):
    dilation, begin = 2**index, 2 * plan["halo"]
    cut = cut_off(present[begin - dilation : begin], dilation)
    return jnp.concatenate([present[first - dilation : begin - dilation], cut, present[begin : last - dilation]])


def moved_on(dilation, spread, past_part, grad_stream, halo, rows):
    count, channels = spread.shape[0], grad_stream.shape[1]
    past_part[0:count] = spread[:, channels:]
    cut = slice(halo, halo + max(dilation, 8))
    past_part[cut] = cut_off(past_part[cut], dilation)
    grad_stream[0:rows] += spread[0:rows, :channels] + past_part[dilation : dilation + rows]


def inputs_kernel(halo, preact, grad_before, conv_w, other, own, grad_stream, past_part):
    grad_stream[...] = grad_before[...]
    moved_on(1, dot(preact[...], conv_w[0], NT), past_part, grad_stream, halo, grad_stream.shape[0])
    other[...] = grad_stream[0:halo].astype(other.dtype)
    own[...] = grad_stream[halo:]


def backward(plan, layers, refs_of, conv_w, out_w, grad_proj, grad_stream, past_part, grad_parts, last_preact):
    halo, length, channels = plan["halo"], plan["length"], plan["channels"]
    own = slice(halo, halo + length)
    items = plan["items"]

    for index in layers:
        dilation, count = 2**index, plan["counts"][index]
        present, earlier, factors, gates = refs_of(index)
        grad_proj[0:count, :channels] = grad_stream[0:count].astype(jnp.bfloat16)
        grad_gated = dot(grad_proj[0:count], out_w[index], NT)
        total = dot(gates[own], grad_proj[0:length], TN)
        plan["store"](total, items.index((index, True)), grad_parts)
        both = factors[halo : halo + count].astype(jnp.float32)
        grad_preact = jnp.concatenate(
            [grad_gated * both[:, :channels], grad_gated * both[:, channels:]], axis=1
        ).astype(jnp.bfloat16)
        if index:
            spread = dot(grad_preact, conv_w[index], NT)
        else:
            last_preact[...] = grad_preact
        past = earlier_rows(plan, index, present, halo, halo + length) if earlier is None else earlier[own]
        total = dot(jnp.concatenate([present[own], past], axis=1), grad_preact[0:length], TN)
        if index:
            moved_on(dilation, spread, past_part, grad_stream, halo, plan["counts"][index - 1])
        plan["store"](total, items.index((index, False)), grad_parts)


def forward_kernel(plan, prev_x, own_x, conv_w, out_w, all_present, all_earlier, all_factors, all_gates, stream):
    halo, (length, channels) = plan["halo"], own_x.shape
    layers, low = conv_w.shape[0], all_earlier.shape[0]
    pad = 2 ** (layers - 1)
    extent = length + 2 * halo
    begin = 2 * halo
    stream[0:pad] = jnp.zeros((pad, channels), jnp.float32)
    stream[pad : pad + begin] = prev_x[...].astype(jnp.float32)
    stream[pad + begin :] = own_x[...].astype(jnp.float32)
    all_present[0, 0:begin] = prev_x[...]
    all_present[0, begin:] = own_x[...]
    for index in range(layers):
        dilation, start = 2**index, plan["starts"][index]
        present = all_present.at[index]
        if index >= low:
            past = earlier_rows(plan, index, present, start, extent)
        else:
            past = stream[pad + start - dilation : pad + extent - dilation]
            cut = cut_off(past[begin - start : begin - start + 16], dilation)
            past = jnp.concatenate([past[: begin - start], cut, past[begin - start + 16 :]]).astype(jnp.bfloat16)
            all_earlier[index, start:] = past
        preact = dot(jnp.concatenate([present[start:], past], axis=1), conv_w[index], NN)
        filtered = jnp.tanh(preact[:, :channels])
        opening = 0.5 + 0.5 * jnp.tanh(0.5 * preact[:, channels:])
        product = filtered * opening
        gated = product.astype(jnp.bfloat16)
        all_gates[index, start:] = gated
        all_factors[index, start:, :channels] = (opening - filtered * product).astype(jnp.bfloat16)
        all_factors[index, start:, channels:] = (product * (1.0 - opening)).astype(jnp.bfloat16)
        if index < layers - 1:
            after = stream[pad + start :] + dot(gated, out_w[index, :, :channels], NN)
            all_present[index + 1, start:] = after.astype(jnp.bfloat16)
            if index < layers - 2:
                stream[pad + start :] = after


def backward_kernel(plan, first, third, all_present, all_earlier, all_factors, all_gates, conv_w, out_w, *rest):
    refs = rest[: plan["inputs"]]
    *outs, keep, send, grad_stream, grad_proj, past_part = rest[plan["inputs"] + plan["unused"] :]
    halo, length, channels, low = plan["halo"], plan["length"], plan["channels"], all_earlier.shape[0]
    if plan["inputs"] == 4:
        prev_rows, own_grad, own_skip, sums = refs
        *outs, grad_skip = outs
        grad_stream[0:halo] = prev_rows[0:halo].astype(jnp.float32)
        grad_stream[halo:] = own_grad[...]
        grad_skip[0:halo] = prev_rows[halo:]
        grad_skip[halo:] = own_skip[...]
    else:
        grad_before, grad_skip = refs
        grad_stream[...] = grad_before[...]
    grad_proj[:, channels:] = grad_skip[...]

    def refs_of(index):
        earlier = all_earlier.at[index] if index < low else None
        return all_present.at[index], earlier, all_factors.at[index], all_gates.at[index]

    backward(
        plan, list(reversed(range(first, first + third))), refs_of, conv_w, out_w,
        grad_proj, grad_stream, past_part, (keep, send), outs[-1],
    )
    outs[0][...] = grad_stream[0 : outs[0].shape[0]]
    if plan["inputs"] == 4:
        plan["finish"](sums, (keep, send))


def store_whole(items, total, item, grad_parts):
    is_out = items[item][1]
    place = sum(kind == is_out for _, kind in items[:item])
    grad_parts[int(is_out)][place] = total.astype(jnp.bfloat16)


def finish_whole(sums, grad_parts):
    pass


def finish_shards(extra, sums, grad_parts):
    for part in grad_parts:
        lead, rows = part.shape[:-2], part.shape[-2]
        for first in range(rows - extra, rows, 16):
            part[(slice(None),) * len(lead) + (slice(first, first + 16),)] = jnp.broadcast_to(
                sums[...], lead + sums.shape
            )


def store_shards(tm, dp, order, bases, total, item, grad_parts):
    keep, send = grad_parts
    t_at, d_at = lax.axis_index("tm"), lax.axis_index("dp")
    core_at = lax.rem(d_at, 2)
    rows = total.shape[0] // tm
    at = pl.ds(bases[item], rows)
    at_bits = bits_of(t_at, d_at, lax.rem, lax.div)
    for y in range(dp // 2):
        near = total[:, (2 * y) * LANES : (2 * y + 1) * LANES]
        far = total[:, (2 * y + 1) * LANES : (2 * y + 2) * LANES]
        mine = jnp.where(core_at == 0, near, far).astype(jnp.bfloat16)
        other = jnp.where(core_at == 0, far, near).astype(jnp.bfloat16)
        for t in range(tm):
            bits = bits_of(t, 2 * y, lambda a, b: a % b, lambda a, b: a // b)
            lead = tuple(lax.rem(bits[name] + at_bits[name], 2) for name in order)
            keep[lead + (at,)] = mine[t * rows : (t + 1) * rows]
            send[lead + (at,)] = other[t * rows : (t + 1) * rows]


def bits_of(t, d, rem, div):
    return {"x": rem(t, 2), "z0": rem(div(t, 2), 2), "z1": div(t, 4), "y": div(d, 2)}


def bases_of(items, tm, channels):
    ends = [0]
    for _, is_out in items:
        ends.append(ends[-1] + (1 if is_out else 2) * channels // tm)
    return ends[:-1], ends[-1]


def run_layers(in_shards, tm, dp, halo, borders, loaded):
    own_x, own_grad, own_skip, sums, conv_w, out_w = loaded
    length, channels = own_x.shape
    layers = conv_w.shape[0]
    third = layers // len(CHAINS)
    low = layers - third
    extent, border = length + 2 * halo, length + halo
    starts = []
    for index in range(layers):
        need = halo if index == layers - 1 else 2 ** (index + 1)
        starts.append(need // 16 * 16)
    counts = [-(-(length + 2 ** (index + 1) - 1) // 16) * 16 for index in range(layers)]
    plan = {"halo": halo, "starts": starts, "counts": counts, "length": length, "channels": channels, "unused": 0}
    plans, shapes = [], []
    for chunk, order in enumerate(CHAINS):
        items = items_of(layers, chunk)
        bases, rows = bases_of(items, tm, channels)
        if in_shards:
            store = functools.partial(store_shards, tm, dp, order, bases)
            finish = functools.partial(finish_shards, EXTRA[chunk])
            shapes.append(2 * [(2,) * len(order) + (rows + EXTRA[chunk], LANES)])
        else:
            store, finish = functools.partial(store_whole, items), finish_whole
            outs = sum(is_out for _, is_out in items)
            shapes.append([(len(items) - outs,) + conv_w.shape[1:], (outs,) + out_w.shape[1:]])
        plans.append(plan | {"items": items, "store": store, "finish": finish})
    vmem, anywhere = pl.BlockSpec(memory_space=pltpu.VMEM), pl.BlockSpec(memory_space=pl.ANY)
    weight_bytes = 2 * (conv_w.size + out_w.size)
    flops = 2 * length * channels * channels
    kept = pl.pallas_call(
        functools.partial(forward_kernel, plan),
        in_specs=[vmem] * 4,
        out_specs=[vmem] * 4,
        out_shape=[
            pltpu.VMEM((layers, extent, channels), jnp.bfloat16),
            pltpu.VMEM((low, extent, channels), jnp.bfloat16),
            pltpu.VMEM((layers, extent, 2 * channels), jnp.bfloat16),
            pltpu.VMEM((layers, extent, channels), jnp.bfloat16),
        ],
        scratch_shapes=[pltpu.VMEM((2 ** (layers - 1) + extent, channels), jnp.float32)],
        compiler_params=pltpu.CompilerParams(vmem_limit_bytes=VMEM_BYTES),
        cost_estimate=cost(flops * 5 * layers, weight_bytes),
        name="forward",
    )(*held((borders[0], own_x, conv_w, out_w)))

    def backward_of(step, inputs, outs, after):
        more = {"inputs": len(inputs), "unused": len(after)}
        return pl.pallas_call(
            functools.partial(backward_kernel, plans[step] | more, layers - (step + 1) * third, third),
            in_specs=[vmem] * (6 + len(inputs)) + [anywhere] * len(after),
            out_specs=[vmem] * (len(outs) + 2),
            out_shape=[pltpu.VMEM((rows, wide), kind) for rows, wide, kind in outs]
            + [pltpu.VMEM(shape, jnp.bfloat16) for shape in shapes[step]],
            scratch_shapes=[
                pltpu.VMEM((border, channels), jnp.float32),
                pltpu.VMEM((border, 2 * channels), jnp.bfloat16),
                pltpu.VMEM((border, channels), jnp.float32),
            ],
            compiler_params=pltpu.CompilerParams(vmem_limit_bytes=VMEM_BYTES),
            cost_estimate=cost(flops * 12 * third, weight_bytes),
            name=("last_third", "middle_third", "first_third")[step],
        )(*held((*kept, conv_w, out_w, *inputs, *after)))

    whole = (border, channels, jnp.float32)
    grad_stream, grad_skip, *last = backward_of(
        0, (borders[1], own_grad, own_skip, sums), [whole, (border, channels, jnp.bfloat16)], []
    )
    parts = [last]
    if in_shards:
        parts[0] = Chunk(tm, dp, 0, *last)
    grad_stream, *middle = backward_of(1, (grad_stream, grad_skip), [whole], [])
    grad_stream, preact, *first = backward_of(
        2, (grad_stream, grad_skip), [(length, channels, jnp.float32), (counts[0], 2 * channels, jnp.bfloat16)],
        [parts[0].next_message()] if in_shards else [],
    )
    other, own = pl.pallas_call(
        functools.partial(inputs_kernel, halo),
        in_specs=[vmem] * 3,
        out_specs=[vmem] * 2,
        out_shape=[pltpu.VMEM((halo, channels), jnp.bfloat16), pltpu.VMEM((length - halo, channels), jnp.float32)],
        scratch_shapes=[pltpu.VMEM((length, channels), jnp.float32), pltpu.VMEM((counts[0], channels), jnp.float32)],
        compiler_params=pltpu.CompilerParams(vmem_limit_bytes=ADD_BYTES),
        cost_estimate=cost(flops * 4, weight_bytes // layers),
        name="to_inputs",
    )(*held((preact, grad_stream, conv_w)))
    parts += [middle, first]
    if in_shards:
        for step in (1, 2):
            parts[step] = Chunk(tm, dp, step, *parts[step])
    return other, own, parts


def add_kernel(count, groups, *refs):
    arrays, outs = refs[:count], refs[-len(groups) :]
    for out, pieces in zip(outs, groups):
        lead = (slice(None),) * (len(out.shape) - 2)
        for first, rows, with_total, terms in pieces:
            body = rows - 16 if with_total else rows
            value = 0.0
            for array, at, begin in terms:
                value = value + arrays[array][at + lead + (slice(begin, begin + body),)].astype(jnp.float32)
            out[lead + (slice(first, first + body),)] = value.astype(out.dtype)
            if with_total:
                total = 0.0
                for array, at, begin in terms:
                    rows_at = slice(begin + body, begin + rows)
                    total = total + joined_rows(arrays[array][at + (0,) * len(lead) + (rows_at,)])
                slab = split_rows(total)
                out[lead + (slice(first + body, first + rows),)] = jnp.broadcast_to(slab, out.shape[:-2] + slab.shape)


def add_up(arrays, groups, shapes, after, name):
    vmem = pl.BlockSpec(memory_space=pltpu.VMEM)
    return pl.pallas_call(
        functools.partial(add_kernel, len(arrays), groups),
        in_specs=[vmem] * len(arrays) + [pl.BlockSpec(memory_space=pl.ANY)] * len(after),
        out_specs=[vmem] * len(groups),
        out_shape=[pltpu.VMEM(shape, jnp.bfloat16) for shape in shapes],
        compiler_params=pltpu.CompilerParams(vmem_limit_bytes=ADD_BYTES),
        name=name,
    )(*held(arrays), *held(after))


def first_block(array, first, rows):
    return array[(0,) * (len(array.shape) - 2) + (slice(first, first + rows),)].astype(jnp.float32)


def first_block(array, first, rows):
    return array[(0,) * (len(array.shape) - 2) + (slice(first, first + rows),)].astype(jnp.float32)


def last_kernel(counts, samples_all, tm, *refs):
    chunks = []
    for count in counts:
        chunks.insert(0, refs[:count])
        refs = refs[count:]
    other, own, grad_inputs, grad_conv, grad_out = refs
    layers, channels = grad_conv.shape[0], own.shape[1]
    total = 0.0
    for term in chunks[0]:
        total = total + jnp.sum(first_block(term, term.shape[-2] - 16, 16), axis=0, keepdims=True)
    scale = samples_all / total
    for chunk, terms in enumerate(chunks):
        items = items_of(layers, chunk)
        for (index, is_out), base in zip(items, bases_of(items, tm, channels)[0]):
            out = grad_out if is_out else grad_conv
            value = 0.0
            for term in terms:
                value = value + first_block(term, base, out.shape[1])
            out[index] = value * scale
    for first in range(0, channels, LANES):
        lanes = slice(first, first + LANES)
        grad_inputs[0 : own.shape[0], lanes] = own[:, lanes] * scale
        grad_inputs[own.shape[0] :, lanes] = other[:, lanes].astype(jnp.float32) * scale


class Chunk:
    def __init__(self, tm, dp, chunk, keep, send):
        self.tm, self.dp, self.chunk, self.rows = tm, dp, chunk, keep.shape[-2]
        self.message = None
        self.terms = [keep, swapped(tm, dp, send, "core")]

    def next_message(self, after=()):
        if self.message is None:
            left = len(CHAINS[self.chunk]) + 2 - len(self.terms)
            pieces = []
            for i, v in enumerate(self.terms):
                pieces.append((i, (0,) * (len(v.shape) - 2 - left) + (1,), 0))
            (self.message,) = add_up(
                self.terms, [[(0, self.rows, EXTRA[self.chunk] > 0, pieces)]], [(2,) * (left - 1) + (self.rows, LANES)], after,
                "add_chunk%d_step%d" % (self.chunk, len(self.terms) - 1),
            )
        return self.message

    def run_chain(self, after=()):
        for step, name in enumerate(CHAINS[self.chunk]):
            self.terms.append(swapped(self.tm, self.dp, self.next_message(after if step == 1 else ()), name))
            self.message = None
        return self.terms


def swapped(tm, dp, value, name):
    over_t, over_d = {"core": (0, 1), "y": (0, 2), "x": (1, 0), "z0": (2, 0), "z1": (4, 0)}[name]
    pairs = [(t * dp + d, (t ^ over_t) * dp + (d ^ over_d)) for t in range(tm) for d in range(dp)]
    return lax.ppermute(value, ("tm", "dp"), pairs)


def scattered(part):
    columns = lax.psum_scatter(part, "dp", scatter_dimension=2, tiled=True).astype(jnp.float32)
    return lax.psum_scatter(columns, "tm", scatter_dimension=1, tiled=True)


def body(inputs, grad_stream_out, grad_skip_out, sample_weight, conv_weight, out_weight):
    tm, dp = lax.axis_size("tm"), lax.axis_size("dp")
    batch, length, channels = inputs.shape
    layers = conv_weight.shape[0]
    third = layers // len(CHAINS)
    halo = 2**layers
    samples_all = batch * length * tm * dp
    x, gs, gk = inputs[0], grad_stream_out[0], grad_skip_out[0]
    x_rows, grad_rows = pack(halo, x, gs, gk, sample_weight)
    borders = [around(x_rows, "tm", 1), around(grad_rows, "tm", 1)]
    loaded = load_all(x, gs, gk, sample_weight, conv_weight, out_weight, x_rows)
    in_shards = tm == 8 and dp == 4 and channels // tm % 16 == 0 and 2 * channels == dp * LANES
    other, own, parts = run_layers(in_shards, tm, dp, halo, borders, loaded)
    other = around(other, "tm", -1)
    if not in_shards:
        scale = samples_all / lax.psum(jnp.sum(sample_weight), ("tm", "dp"))
        found = {}
        for chunk, part in enumerate(parts):
            items = items_of(layers, chunk)
            for is_out in (False, True):
                for place, item in enumerate(item for item in items if item[1] == is_out):
                    found[item] = part[int(is_out)][place]
        grad_conv, grad_out = (
            scattered(jnp.stack([found[index, is_out] for index in range(layers)])) * scale for is_out in (False, True)
        )
        return (jnp.concatenate([own, other]) * scale)[None], grad_conv, grad_out
    chunks = [part.run_chain([other] if part is parts[0] else ()) for part in parts]
    conv_rows, out_rows = 2 * channels // tm, channels // tm
    grad_inputs, grad_conv, grad_out = pl.pallas_call(
        functools.partial(last_kernel, [len(terms) for terms in reversed(chunks)], float(samples_all), tm),
        out_shape=[
            jax.ShapeDtypeStruct((length, channels), jnp.float32),
            jax.ShapeDtypeStruct((layers, conv_rows, LANES), jnp.float32),
            jax.ShapeDtypeStruct((layers, out_rows, LANES), jnp.float32),
        ],
        compiler_params=pltpu.CompilerParams(vmem_limit_bytes=ADD_BYTES),
        name="scale_all",
    )(*held([term for terms in reversed(chunks) for term in terms]), *held([other, own]))
    return grad_inputs[None], grad_conv, grad_out


def solution(mesh):
    placed = (
        P("dp", "tm", None),
        P("dp", "tm", None),
        P("dp", "tm", None),
        P("dp", "tm"),
        P(),
        P(),
    )
    return jax.shard_map(
        body,
        mesh=mesh,
        in_specs=placed,
        out_specs=(P("dp", "tm", None), P(None, "tm", "dp"), P(None, "tm", "dp")),
        check_vma=False,
    )
```
